32 devices in a mesh: dp: 8 (over z, x), ctx: 4 (over y, core).
Axes of the slice: x: 2, y: 2, z: 4, core: 2. Of those that a mesh axis runs over, the one named last changes fastest.
Arguments:
- tokens: float32 [8, 1024, 1024], P('dp', 'ctx'), may hold values from -6 to 6
- segment_ids: int32 [8, 1024], P('dp'), may hold values from 0 to 6, as said below
- cotangent: float32 [8, 1024, 1024], P('dp', 'ctx'), may hold values from -12 to 12
- in_weight: float32 [1024, 4352], P('dp'), may hold values from -0.1875 to 0.1875
- dt_weight: float32 [32, 1024], P(None, 'dp'), may hold values from -0.1875 to 0.1875
- out_weight: float32 [2048, 1024], P('dp'), may hold values from -0.125 to 0.125
- conv_params: float32 [5, 2304], P(None, 'dp'), may hold values from -0.5 to 0.5
- gains: float32 [3072], P('dp'), may hold values from 0.5 to 1.5
- head_params: float32 [3, 32], replicated, may hold values from -9 to 1.5
- in_first: float32 [1024, 4352], P('dp')
- in_second: float32 [1024, 4352], P('dp'), as said below
- dt_first: float32 [32, 1024], P(None, 'dp')
- dt_second: float32 [32, 1024], P(None, 'dp'), as said below
- out_first: float32 [2048, 1024], P('dp')
- out_second: float32 [2048, 1024], P('dp'), as said below
- conv_first: float32 [5, 2304], P(None, 'dp')
- conv_second: float32 [5, 2304], P(None, 'dp'), as said below
- gain_first: float32 [3072], P('dp')
- gain_second: float32 [3072], P('dp'), as said below
- head_first: float32 [3, 32], replicated
- head_second: float32 [3, 32], replicated, as said below
Outputs:
- block_output: float32 [8, 1024, 1024], P('dp', 'ctx')
- input_grad: float32 [8, 1024, 1024], P('dp', 'ctx')
- in_weight_new: float32 [1024, 4352], P('dp')
- in_first_new: float32 [1024, 4352], P('dp')
- in_second_new: float32 [1024, 4352], P('dp')
- dt_weight_new: float32 [32, 1024], P(None, 'dp')
- dt_first_new: float32 [32, 1024], P(None, 'dp')
- dt_second_new: float32 [32, 1024], P(None, 'dp')
- out_weight_new: float32 [2048, 1024], P('dp')
- out_first_new: float32 [2048, 1024], P('dp')
- out_second_new: float32 [2048, 1024], P('dp')
- conv_params_new: float32 [5, 2304], P(None, 'dp')
- conv_first_new: float32 [5, 2304], P(None, 'dp')
- conv_second_new: float32 [5, 2304], P(None, 'dp')
- gains_new: float32 [3072], P('dp')
- gain_first_new: float32 [3072], P('dp')
- gain_second_new: float32 [3072], P('dp')
- head_params_new: float32 [3, 32], replicated
- head_first_new: float32 [3, 32], replicated
- head_second_new: float32 [3, 32], replicated
The draws below stay inside these ranges and needn't reach their ends.
Inputs may be any that keep to these rules, and one draw needn't show every extreme that they name: `segment_ids`: along each row the ids never fall; in each row one document starts within the first 256 positions and ends within the last 256. `in_second`: Positive. `dt_second`: Positive. `out_second`: Positive. `conv_second`: Positive. `gain_second`: Positive. `head_second`: Positive.
All inputs are finite; a program needn't handle non-finite values.
Results may differ from the reference program's by a relative error of at most 0.009.
The reference program's roundings to bfloat16 on the way count: a program that leaves them out, or rounds other values in their place, can miss the bound.
Values may be sent and summed in bfloat16 or wider, within the bound.
No kernel may reach another device: no remote copies, remote signals or barrier semaphores. Data moves between devices by JAX's collectives and lax.ppermute only.
A program may use at most 256 MiB of HBM per device.

```python
import math
import jax
import jax.numpy as jnp
from jax import lax

D = 1024
INNER = 2048
HEADS = 32
HEAD_DIM = 64
STATE = 128
CONV = 4
GROUP = 256
STEP = 10
SEQS = 8
LENGTH = 1024
TOKENS = 8192
PROJ = 4352
CONVDIM = 2304
GAINS = 3072


def first_moment(key, array_shape, factor):
    values = jnp.clip(jax.random.normal(key, array_shape, jnp.float32), -4.0, 4.0)
    return values * (0.11 * factor * math.sqrt(TOKENS))


def second_moment(key, array_shape, factor):
    values = jnp.exp(jax.random.uniform(key, array_shape, jnp.float32, 0.0, 1.386))
    return values * (0.053 * factor * factor * TOKENS)


def draw_segment_ids(key, part):
    key = jax.random.fold_in(key, 1)
    sub_keys = jax.random.split(key, 4)
    doc_start = jax.random.randint(sub_keys[0], (SEQS, 1), 1, GROUP)
    doc_end = jax.random.randint(sub_keys[1], (SEQS, 1), LENGTH - GROUP + 1, LENGTH)
    early_cuts = jax.random.randint(sub_keys[2], (SEQS, 2), 0, doc_start)
    late_cuts = jax.random.randint(sub_keys[3], (SEQS, 2), doc_end, LENGTH)
    bounds = jnp.concatenate([doc_start, doc_end, early_cuts, late_cuts], axis=1)
    positions = jnp.arange(LENGTH, dtype=jnp.int32)
    return jnp.sum((bounds[:, :, None] <= positions[None, None, :]).astype(jnp.int32), axis=1).astype(jnp.int32)


def draw_cotangent(key, part):
    key = jax.random.fold_in(key, 2)
    seq_pos = jnp.arange(SEQS, dtype=jnp.float32)[:, None, None] / max(SEQS - 1, 1)
    places = jnp.arange(LENGTH, dtype=jnp.float32)[None, :, None] / (LENGTH - 1)
    values = jnp.clip(jax.random.normal(key, (SEQS, LENGTH, D), jnp.float32), -5.0, 5.0)
    row_scale = (0.5 + seq_pos) * (0.5 + places)
    return values * row_scale


def draw_head_params(key, part):
    key = jax.random.fold_in(key, 3)
    sub_keys = jax.random.split(key, 3)
    decay_log = jax.random.uniform(sub_keys[0], (HEADS,), jnp.float32, 0.0, 1.4)
    step_bias = jax.random.uniform(sub_keys[1], (HEADS,), jnp.float32, -8.0, -4.5)
    skip_gain = jax.random.uniform(sub_keys[2], (HEADS,), jnp.float32, 0.5, 1.5)
    return jnp.stack([decay_log, step_bias, skip_gain])


def draw_in_first(key, part):
    key = jax.random.fold_in(key, 11)
    return first_moment(key, (D, PROJ), 0.5)


def draw_in_second(key, part):
    key = jax.random.fold_in(key, 12)
    return second_moment(key, (D, PROJ), 0.5)


def draw_dt_first(key, part):
    key = jax.random.fold_in(key, 13)
    return first_moment(key, (HEADS, D), 0.5)


def draw_dt_second(key, part):
    key = jax.random.fold_in(key, 14)
    return second_moment(key, (HEADS, D), 0.5)


def draw_out_first(key, part):
    key = jax.random.fold_in(key, 15)
    return first_moment(key, (INNER, D), 1.0)


def draw_out_second(key, part):
    key = jax.random.fold_in(key, 16)
    return second_moment(key, (INNER, D), 1.0)


def draw_conv_first(key, part):
    key = jax.random.fold_in(key, 17)
    return first_moment(key, (CONV + 1, CONVDIM), 0.5)


def draw_conv_second(key, part):
    key = jax.random.fold_in(key, 18)
    return second_moment(key, (CONV + 1, CONVDIM), 0.5)


def draw_gain_first(key, part):
    key = jax.random.fold_in(key, 19)
    return first_moment(key, (GAINS,), 0.5)


def draw_gain_second(key, part):
    key = jax.random.fold_in(key, 20)
    return second_moment(key, (GAINS,), 0.5)


def draw_head_first(key, part):
    key = jax.random.fold_in(key, 21)
    return first_moment(key, (3, HEADS), 4.0)


def draw_head_second(key, part):
    key = jax.random.fold_in(key, 22)
    return second_moment(key, (3, HEADS), 4.0)


def shard_levels(rng, shape, cuts, low, top_value):
    gain = 1.0
    for axis_at, shards_of in cuts:
        heights = jax.random.uniform(jax.random.fold_in(jax.random.fold_in(rng, 6), axis_at), (shards_of,), jnp.float32, low / len(cuts), top_value / len(cuts))
        gain = gain * jnp.repeat(jnp.exp(heights), shape[axis_at] // shards_of).reshape((-1,) + (1,) * (len(shape) - 1 - axis_at))
    return gain


def scatter_about(stream_key, shape, scale, most, shards=(), kind=jnp.bfloat16):
    values = jax.random.normal(stream_key, shape, jnp.float32) * scale
    if len(shards) > 0:
        values = shard_levels(stream_key, shape, shards, -0.22, 0.18) * values
    return jnp.clip(values, min=-most, max=most).astype(kind)


def setup_inputs(seed: int = 0) -> dict:
    streams_of = jax.random.split(jax.random.key(seed), 22)
    tokens = scatter_about(streams_of[0], (SEQS, LENGTH, D), 1.0, 6.0, ((0, 8), (1, 4)), jnp.float32)
    segment_ids = draw_segment_ids(jax.random.fold_in(streams_of[21], 71), 0)
    cotangent = draw_cotangent(jax.random.fold_in(streams_of[21], 71), 0)
    in_weight = scatter_about(streams_of[3], (D, PROJ), D ** -0.5, 0.1875, ((0, 8),), jnp.float32)
    dt_weight = scatter_about(streams_of[4], (HEADS, D), D ** -0.5, 0.1875, ((1, 8),), jnp.float32)
    out_weight = scatter_about(streams_of[5], (INNER, D), INNER ** -0.5, 0.125, ((0, 8),), jnp.float32)
    conv_params = jnp.clip(jax.random.uniform(streams_of[6], (CONV + 1, CONVDIM), jnp.float32, -0.5, 0.5) * shard_levels(streams_of[6], (CONV + 1, CONVDIM), ((1, 8),), -0.4, 0.0), -0.5, 0.5)
    gains = jnp.clip(1.0 + 0.1 * jax.random.normal(streams_of[7], (GAINS,), jnp.float32), 0.5, 1.5)
    head_params = draw_head_params(jax.random.fold_in(streams_of[21], 71), 0)
    in_first = draw_in_first(jax.random.fold_in(streams_of[21], 71), 0)
    in_second = draw_in_second(jax.random.fold_in(streams_of[21], 71), 0)
    dt_first = draw_dt_first(jax.random.fold_in(streams_of[21], 71), 0)
    dt_second = draw_dt_second(jax.random.fold_in(streams_of[21], 71), 0)
    out_first = draw_out_first(jax.random.fold_in(streams_of[21], 71), 0)
    out_second = draw_out_second(jax.random.fold_in(streams_of[21], 71), 0)
    conv_first = draw_conv_first(jax.random.fold_in(streams_of[21], 71), 0)
    conv_second = draw_conv_second(jax.random.fold_in(streams_of[21], 71), 0)
    gain_first = draw_gain_first(jax.random.fold_in(streams_of[21], 71), 0)
    gain_second = draw_gain_second(jax.random.fold_in(streams_of[21], 71), 0)
    head_first = draw_head_first(jax.random.fold_in(streams_of[21], 71), 0)
    head_second = draw_head_second(jax.random.fold_in(streams_of[21], 71), 0)
    return dict(tokens=tokens, segment_ids=segment_ids, cotangent=cotangent, in_weight=in_weight, dt_weight=dt_weight, out_weight=out_weight, conv_params=conv_params, gains=gains, head_params=head_params, in_first=in_first, in_second=in_second, dt_first=dt_first, dt_second=dt_second, out_first=out_first, out_second=out_second, conv_first=conv_first, conv_second=conv_second, gain_first=gain_first, gain_second=gain_second, head_first=head_first, head_second=head_second)


HIGHEST = lax.Precision.HIGHEST
NORM_EPS = 1e-05
BETA_ONE = 0.9
BETA_TWO = 0.95
ADAM_EPS = 1e-08
WEIGHT_DECAY = 0.1

@jax.custom_vjp
def low(v):
    return lax.optimization_barrier(v.astype(jnp.bfloat16)).astype(jnp.float32)

@jax.custom_vjp
def low_back(v):
    return v

def low_keep(v):
    return (low(v), None)

def low_pass(kept, grad):
    return (grad,)

def back_keep(v):
    return (v, None)

def back_low(kept, grad):
    return (low(grad),)
low.defvjp(low_keep, low_pass)
low_back.defvjp(back_keep, back_low)

def matmul(left, right):
    return jnp.dot(left, right, precision=HIGHEST, preferred_element_type=jnp.float32)

def ssd_block(carry_pair, block_data):
    state_now, seg_prev = carry_pair
    head_values, write_map, read_map, step_size, alpha, seg_ids = block_data
    log_decay = jnp.cumsum(alpha, axis=0)
    positions = jnp.arange(seg_ids.shape[0])
    visible = ((seg_ids[:, None] == seg_ids[None, :]) & (positions[:, None] >= positions[None, :]))[:, :, None]
    log_gap = log_decay[:, None, :] - log_decay[None, :, :]
    decay_map = jnp.where(visible, jnp.exp(jnp.where(visible, log_gap, 0.0)), 0.0)
    scores = matmul(read_map, write_map.T)
    weights = scores[:, :, None] * decay_map * step_size[None, :, :]
    inner_out = jnp.einsum('tsh,shp->thp', weights, head_values, precision=HIGHEST)
    enter_scale = jnp.where((seg_ids == seg_prev)[:, None], jnp.exp(log_decay), 0.0)
    inner_out = inner_out + enter_scale[:, :, None] * jnp.einsum('tn,hpn->thp', read_map, state_now, precision=HIGHEST)
    tail_scale = jnp.where((seg_ids == seg_ids[-1])[:, None], jnp.exp(log_decay[-1][None, :] - log_decay), 0.0) * step_size
    local_state = jnp.einsum('sh,shp,sn->hpn', tail_scale, head_values, write_map, precision=HIGHEST)
    carry_keep = jnp.where(seg_ids[-1] == seg_prev, jnp.exp(log_decay[-1]), 0.0)
    return ((carry_keep[:, None, None] * state_now + local_state, seg_ids[-1]), inner_out)

def sequence_forward(params, block_in, seg_ids):
    w_in, w_dt, w_out, conv_weights, gain_all, head_rows = params
    hidden = low(block_in * lax.rsqrt(lax.optimization_barrier(jnp.mean(block_in * block_in, axis=-1, keepdims=True)) + NORM_EPS) * gain_all[:D])
    projected = low(low_back(matmul(hidden, w_in)))
    step_raw = low_back(matmul(hidden, w_dt.T))
    gate_half = projected[:, :INNER]
    conv_in = projected[:, INNER:]
    padded = jnp.concatenate([jnp.zeros((CONV - 1, conv_in.shape[1]), jnp.float32), conv_in], axis=0)
    padded_ids = jnp.concatenate([jnp.full((CONV - 1,), -1, jnp.int32), seg_ids], axis=0)
    conv_sum = conv_weights[CONV]
    for tap_index in range(CONV):
        same_doc = (padded_ids[tap_index:tap_index + LENGTH] == seg_ids)[:, None]
        conv_sum = conv_sum + conv_weights[tap_index] * jnp.where(same_doc, padded[tap_index:tap_index + LENGTH], 0.0)
    mixed_out = low(jax.nn.silu(conv_sum))
    head_values = mixed_out[:, :INNER].reshape(LENGTH, HEADS, HEAD_DIM)
    write_map = mixed_out[:, INNER:INNER + STATE]
    read_map = mixed_out[:, INNER + STATE:]
    step_size = jax.nn.softplus(step_raw + head_rows[1])
    alpha = -step_size * jnp.exp(head_rows[0])
    block_count = LENGTH // GROUP

    def by_block(value):
        return value.reshape((block_count, GROUP) + value.shape[1:])
    start_pair = (jnp.zeros((HEADS, HEAD_DIM, STATE), jnp.float32), jnp.array(-1, jnp.int32))
    _, inner_out = lax.scan(jax.checkpoint(ssd_block), start_pair, (by_block(head_values), by_block(write_map), by_block(read_map), by_block(step_size), by_block(alpha), by_block(seg_ids)))
    inner_out = inner_out.reshape(LENGTH, HEADS, HEAD_DIM) + head_rows[2][:, None] * head_values
    gated_out = inner_out.reshape(LENGTH, INNER) * jax.nn.silu(gate_half)
    normed = low(gated_out * lax.rsqrt(lax.optimization_barrier(jnp.mean(gated_out * gated_out, axis=-1, keepdims=True)) + NORM_EPS) * gain_all[D:])
    branch = low_back(matmul(normed, w_out))
    return block_in + branch

def adam_step(weight, moment_one, second, gradient, step_rate, decay_rate):
    moment_new = BETA_ONE * moment_one + (1.0 - BETA_ONE) * gradient
    second_new = BETA_TWO * second + (1.0 - BETA_TWO) * gradient * gradient
    first_hat = moment_new / (1.0 - BETA_ONE ** STEP)
    second_hat = second_new / (1.0 - BETA_TWO ** STEP)
    weight_new = weight - step_rate * (first_hat / (jnp.sqrt(second_hat) + ADAM_EPS) + decay_rate * weight)
    return (weight_new, moment_new, second_new)

def reference(tokens, segment_ids, cotangent, in_weight, dt_weight, out_weight, conv_params, gains, head_params, in_first, in_second, dt_first, dt_second, out_first, out_second, conv_first, conv_second, gain_first, gain_second, head_first, head_second):
    params = (low(in_weight), low(dt_weight), low(out_weight), low(conv_params), low(gains), head_params)

    def one_sequence(totals, inputs):
        block_in, seg_ids, cot_rows = inputs

        def forward_here(param_set, block_rows):
            return sequence_forward(param_set, block_rows, seg_ids)
        block_out, pull_back = jax.vjp(forward_here, params, block_in)
        grad_sums, grad_in = pull_back(cot_rows)
        return (jax.tree.map(jnp.add, totals, grad_sums), (block_out, grad_in))
    zero_grads = jax.tree.map(jnp.zeros_like, params)
    totals, (block_output, input_grad) = lax.scan(one_sequence, zero_grads, (tokens, segment_ids, cotangent))
    in_grad, dt_grad, out_grad, conv_grad, gain_grad, head_grad = totals
    in_new = adam_step(in_weight, in_first, in_second, in_grad, 0.03, WEIGHT_DECAY)
    dt_new = adam_step(dt_weight, dt_first, dt_second, dt_grad, 0.03, WEIGHT_DECAY)
    out_new = adam_step(out_weight, out_first, out_second, out_grad, 0.02, WEIGHT_DECAY)
    conv_new = adam_step(conv_params, conv_first, conv_second, conv_grad, 0.3, 0.0)
    gain_new = adam_step(gains, gain_first, gain_second, gain_grad, 0.5, 0.0)
    head_new = adam_step(head_params, head_first, head_second, head_grad, 2.0, 0.0)
    return (block_output, input_grad, in_new[0], in_new[1], in_new[2], dt_new[0], dt_new[1], dt_new[2], out_new[0], out_new[1], out_new[2], conv_new[0], conv_new[1], conv_new[2], gain_new[0], gain_new[1], gain_new[2], head_new[0], head_new[1], head_new[2])
```

```python
import jax
import jax.numpy as jnp
from jax import lax
from jax.experimental import pallas as pl
from jax.experimental.pallas import tpu as pltpu
from jax.sharding import PartitionSpec as P

INNER = 2048
HEADS = 32
HEAD_DIM = 64
STATE = 128
CONV = 4
STEP = 10

F32 = jnp.float32
BF16 = jnp.bfloat16
HIGHEST = lax.Precision.HIGHEST
NORM_EPS = 1e-05
BETA_ONE = 0.9
BETA_TWO = 0.95
ADAM_EPS = 1e-08
WEIGHT_DECAY = 0.1
VMEM_LIMIT = 56 * 1024 * 1024


def nn(a, b, precision=None):
    return lax.dot_general(
        a, b, (((1,), (0,)), ((), ())), precision=precision, preferred_element_type=F32
    )


def nt(a, b, precision=None):
    return lax.dot_general(
        a, b, (((1,), (1,)), ((), ())), precision=precision, preferred_element_type=F32
    )


def tn(a, b, precision=None):
    return lax.dot_general(
        a, b, (((0,), (0,)), ((), ())), precision=precision, preferred_element_type=F32
    )


def halves(value):
    high = value.astype(BF16)
    return high, (value - high.astype(F32)).astype(BF16)


def spread(value, width):
    heads = value.shape[1]
    row = lax.broadcasted_iota(jnp.int32, (heads, width), 0)
    col = lax.broadcasted_iota(jnp.int32, (heads, width), 1)
    table = jnp.where(col // HEAD_DIM == row, 1.0, 0.0).astype(BF16)
    high, low = halves(value)
    return nn(high, table) + nn(low, table)


def gather_heads(value, heads):
    width = value.shape[1]
    row = lax.broadcasted_iota(jnp.int32, (width, heads), 0)
    col = lax.broadcasted_iota(jnp.int32, (width, heads), 1)
    table = jnp.where(row // HEAD_DIM == col, 1.0, 0.0).astype(BF16)
    high, low = halves(value)
    return nn(high, table) + nn(low, table)


def softplus(value):
    return jnp.maximum(value, 0.0) + jnp.log1p(jnp.exp(-jnp.abs(value)))


def sigmoid(value):
    return 1.0 / (1.0 + jnp.exp(-value))


def silu_grad(value):
    sig = sigmoid(value)
    return sig * (1.0 + value * (1.0 - sig))


def triangle(size, lower):
    row = lax.broadcasted_iota(jnp.int32, (size, size), 0)
    col = lax.broadcasted_iota(jnp.int32, (size, size), 1)
    keep = row >= col if lower else row <= col
    return jnp.where(keep, 1.0, 0.0).astype(F32)


def params(*semantics):
    return pltpu.CompilerParams(
        dimension_semantics=semantics or None, vmem_limit_bytes=VMEM_LIMIT
    )


def norm_kernel(tok_ref, gain_ref, hid_ref):
    tok = tok_ref[...]
    scale = lax.rsqrt(jnp.mean(tok * tok, axis=-1, keepdims=True) + NORM_EPS)
    hid_ref[...] = (tok * scale * gain_ref[...]).astype(BF16)


def scan_forward_kernel(
    perm_ref,
    hid_ref,
    w1_ref,
    wdt_ref,
    conv_ref,
    hrow_ref,
    hcol_ref,
    segc_ref,
    segr_ref,
    mixed_ref,
    convin_ref,
    convsum_ref,
    inner_ref,
    raw_ref,
    stepc_ref,
    logc_ref,
    stepr_ref,
    logr_ref,
    start_ref,
    ext_ref,
    seg_ref,
    state_ref,
):
    step = pl.program_id(0)
    span = hid_ref.shape[1]
    heads = wdt_ref.shape[0]
    width = heads * HEAD_DIM

    @pl.when(step == 0)
    def _():
        ext_ref[0:8] = jnp.zeros((8, ext_ref.shape[1]), F32)
        state_ref[...] = jnp.zeros_like(state_ref)

    hid = hid_ref[0]
    proj = nn(hid, w1_ref[...]).astype(BF16)
    convin_ref[...] = proj
    ext_ref[8 : 8 + span] = proj.astype(F32)
    seg_ref[...] = segc_ref[pl.ds(pl.multiple_of(step * span, 8), span + 8), :]
    seg_here = seg_ref[8 : 8 + span]
    total = conv_ref[CONV : CONV + 1]
    for tap in range(CONV):
        at = 8 - (CONV - 1) + tap
        same = seg_ref[at : at + span] == seg_here
        total = total + conv_ref[tap : tap + 1] * jnp.where(same, ext_ref[at : at + span], 0.0)
    ext_ref[0:8] = ext_ref[span : span + 8]
    convsum_ref[...] = total
    mixed = (total * sigmoid(total)).astype(BF16)
    mixed_ref[...] = mixed

    raw_c = nt(hid, wdt_ref[...]) + hrow_ref[1:2]
    raw_r = nt(wdt_ref[...], hid) + hcol_ref[:, 1:2]
    step_c = softplus(raw_c)
    step_r = softplus(raw_r)
    log_c = nn(triangle(span, True), -step_c * jnp.exp(hrow_ref[0:1]), HIGHEST)
    log_r = nn(-step_r * jnp.exp(hcol_ref[:, 0:1]), triangle(span, False), HIGHEST)
    raw_ref[...] = raw_c
    stepc_ref[...] = step_c
    logc_ref[...] = log_c
    stepr_ref[...] = step_r
    logr_ref[...] = log_r

    values = mixed[:, :width]
    write = mixed[:, width : width + STATE]
    read = mixed[:, width + STATE :]
    row = lax.broadcasted_iota(jnp.int32, (span, span), 0)
    col = lax.broadcasted_iota(jnp.int32, (span, span), 1)
    visible = (seg_here == segr_ref[...]) & (row >= col)
    scores = jnp.where(visible, nt(read, write), 0.0)
    lane = lax.broadcasted_iota(jnp.int32, (span, 2 * HEAD_DIM), 1)

    seg_prev = seg_ref[7:8]
    seg_last = seg_ref[span + 7 : span + 8]
    last = log_c[span - 1 : span]
    enter = jnp.where(seg_here == seg_prev, jnp.exp(log_c), 0.0)
    tail = jnp.where(seg_here == seg_last, jnp.exp(last - log_c), 0.0) * step_c
    keep = jnp.where(seg_last == seg_prev, jnp.exp(last), 0.0)
    state = state_ref[...]
    start_ref[0] = state
    values_f = values.astype(F32)
    base = spread(enter, width) * nn(read, state.astype(BF16)) + spread(
        hrow_ref[2:3] + jnp.zeros((8, heads), F32), width
    )[0:1] * values_f
    for pair in range(heads // 2):
        lanes = slice(pair * 2 * HEAD_DIM, (pair + 1) * 2 * HEAD_DIM)
        pieces = []
        for head in (2 * pair, 2 * pair + 1):
            gap = jnp.minimum(log_c[:, head : head + 1] - log_r[head : head + 1], 0.0)
            weights = scores * jnp.exp(gap) * step_r[head : head + 1]
            pieces.append(nn(weights.astype(BF16), values[:, lanes]))
        inner_ref[:, lanes] = base[:, lanes] + jnp.where(lane < HEAD_DIM, pieces[0], pieces[1])
    moved = (spread(tail, width) * values_f).astype(BF16)
    state_ref[...] = spread(keep + jnp.zeros((8, heads), F32), width)[0:1] * state + tn(
        write, moved
    )


def gate_kernel(perm_ref, hid_ref, wg_ref, inner_ref, cot_ref, wout_ref, gain_ref, gate_ref, ng_ref, stat_ref):
    gate = nn(hid_ref[0], wg_ref[...]).astype(BF16)
    gate_ref[...] = gate
    gate = gate.astype(F32)
    grad = nt(cot_ref[0], wout_ref[...])
    ng_ref[...] = grad
    gated = inner_ref[...] * (gate * sigmoid(gate))
    ones = jnp.ones((8, gated.shape[1]), F32)
    squares = nt(ones, gated * gated, HIGHEST)
    crossed = nt(ones, gated * (grad * gain_ref[...]), HIGHEST)
    at = lax.broadcasted_iota(jnp.int32, squares.shape, 0)
    stat_ref[...] = jnp.where(at == 0, squares, crossed)


def norm_back_kernel(
    perm_ref,
    hid_ref,
    inner_ref,
    gate_ref,
    ng_ref,
    stat_ref,
    gain_ref,
    cot_ref,
    wout_ref,
    mixed_ref,
    block_ref,
    outg_ref,
    ing_ref,
    dy_ref,
    dgate_ref,
    sums_ref,
    outacc_ref,
    inacc_ref,
):
    step = pl.program_id(0)
    span, width = inner_ref.shape

    @pl.when(step == 0)
    def _():
        outacc_ref[...] = jnp.zeros_like(outacc_ref)
        inacc_ref[...] = jnp.zeros_like(inacc_ref)
        sums_ref[...] = jnp.zeros_like(sums_ref)

    row = lax.broadcasted_iota(jnp.int32, (span, span), 0)
    col = lax.broadcasted_iota(jnp.int32, (span, span), 1)
    eye = jnp.where(row == col, 1.0, 0.0).astype(F32)
    stats = nt(eye, stat_ref[...], HIGHEST)
    inv = lax.rsqrt(stats[:, 0:1] * (1.0 / INNER) + NORM_EPS)
    cross = stats[:, 1:2]
    gate = gate_ref[...].astype(F32)
    sig = sigmoid(gate)
    silu = gate * sig
    inner = inner_ref[...]
    gated = inner * silu
    unit = gated * inv
    normed = (unit * gain_ref[...]).astype(BF16)
    cot = cot_ref[0]
    block_ref[0] = nn(normed, wout_ref[...]).astype(BF16)
    outacc_ref[...] += tn(normed, cot)
    grad = ng_ref[...]
    dgated = inv * (grad * gain_ref[...] - unit * (cross * inv * (1.0 / INNER)))
    dy = dgated * silu
    dy_ref[...] = dy
    dgate = (dgated * inner * (sig * (1.0 + gate * (1.0 - sig)))).astype(BF16)
    dgate_ref[...] = dgate
    inacc_ref[...] += tn(hid_ref[0], dgate)
    gain_sum = jnp.sum(grad * unit, axis=0, keepdims=True)
    skip_sum = jnp.sum(dy * mixed_ref[...].astype(F32), axis=0, keepdims=True)
    at = lax.broadcasted_iota(jnp.int32, (8, width), 0)
    sums_ref[...] += jnp.where(at == 0, gain_sum, jnp.where(at == 1, skip_sum, 0.0))

    @pl.when(step == pl.num_programs(0) - 1)
    def _():
        outg_ref[...] = outacc_ref[...].astype(BF16)
        ing_ref[...] = inacc_ref[...].astype(BF16)


def scan_back_kernel(
    perm_ref,
    hid_ref,
    dy_ref,
    mixed_ref,
    convin_ref,
    convsum_ref,
    raw_ref,
    stepc_ref,
    logc_ref,
    stepr_ref,
    logr_ref,
    start_ref,
    conv_ref,
    hrow_ref,
    segc_ref,
    segr_ref,
    ing_ref,
    dval_ref,
    dbc_ref,
    dstep_ref,
    convg_ref,
    dtg_ref,
    headg_ref,
    ext_ref,
    seg_ref,
    grad_ref,
    inacc_ref,
    dx_ref,
):
    step = pl.program_id(0)
    chunk = pl.num_programs(0) - 1 - step
    span = hid_ref.shape[1]
    heads = stepc_ref.shape[1]
    width = heads * HEAD_DIM

    @pl.when(step == 0)
    def _():
        ext_ref[span : span + 8] = jnp.zeros((8, width), F32)
        grad_ref[...] = jnp.zeros_like(grad_ref)
        inacc_ref[...] = jnp.zeros_like(inacc_ref)
        convg_ref[...] = jnp.zeros_like(convg_ref)
        dtg_ref[...] = jnp.zeros_like(dtg_ref)
        headg_ref[...] = jnp.zeros_like(headg_ref)

    seg_ref[...] = segc_ref[pl.ds(pl.multiple_of(chunk * span, 8), span + 16), :]
    seg_here = seg_ref[8 : 8 + span]
    seg_prev = seg_ref[7:8]
    seg_last = seg_ref[span + 7 : span + 8]
    mixed = mixed_ref[...]
    values = mixed[:, :width]
    write = mixed[:, width : width + STATE]
    read = mixed[:, width + STATE :]
    values_f = values.astype(F32)
    dy = dy_ref[...]
    dy_low = dy.astype(BF16)
    step_c = stepc_ref[...]
    log_c = logc_ref[...]
    step_r = stepr_ref[...]
    log_r = logr_ref[...]
    last = log_c[span - 1 : span]
    enter = jnp.where(seg_here == seg_prev, jnp.exp(log_c), 0.0)
    tail_raw = jnp.where(seg_here == seg_last, jnp.exp(last - log_c), 0.0)
    tail = tail_raw * step_c
    keep = jnp.where(seg_last == seg_prev, jnp.exp(last), 0.0)
    enter_w = spread(enter, width)
    tail_w = spread(tail, width)
    wide = spread(
        jnp.concatenate([hrow_ref[2:3] + jnp.zeros((8, heads), F32), keep + jnp.zeros((8, heads), F32)], axis=0),
        width,
    )
    skip_w = wide[0:1]
    keep_w = wide[8:9]
    state = start_ref[0]
    state_low = state.astype(BF16)
    later = grad_ref[...]
    later_low = later.astype(BF16)

    row = lax.broadcasted_iota(jnp.int32, (span, span), 0)
    col = lax.broadcasted_iota(jnp.int32, (span, span), 1)
    visible = (seg_here == segr_ref[...]) & (row >= col)
    scores = jnp.where(visible, nt(read, write), 0.0)
    lane = lax.broadcasted_iota(jnp.int32, (span, 2 * HEAD_DIM), 1)
    head_at = lax.broadcasted_iota(jnp.int32, (8, span), 0)
    lane_at = lax.broadcasted_iota(jnp.int32, (span, heads), 1)

    entered = enter_w * dy
    entered_low = entered.astype(BF16)
    inter = enter_w * nn(read, state_low)
    from_later = nn(write, later_low)
    moved_low = (tail_w * values_f).astype(BF16)
    dread = nt(entered_low, state_low)
    dwrite = nt(moved_low, later_low)
    dlog_c = gather_heads(dy * inter, heads)
    tail_dot = gather_heads(values_f * from_later, heads)
    dlog_c = dlog_c - tail_dot * tail
    dstep_c = tail_dot * tail_raw
    carried = gather_heads(jnp.sum(later * state, axis=0, keepdims=True) + jnp.zeros((8, width), F32), heads)[0:1]
    at_last = lax.broadcasted_iota(jnp.int32, (span, heads), 0) == span - 1
    dlog_c = dlog_c + jnp.where(
        at_last, jnp.sum(tail_dot * tail, axis=0, keepdims=True) + keep * carried, 0.0
    )
    grad_ref[...] = keep_w * later + tn(read, entered_low)
    dx_ref[...] = tail_w * from_later + skip_w * dy

    dscores = jnp.zeros((span, span), F32)
    dstep_r = jnp.zeros((8, span), F32)
    for pair in range(heads // 2):
        lanes = slice(pair * 2 * HEAD_DIM, (pair + 1) * 2 * HEAD_DIM)
        dy_pair = dy_low[:, lanes]
        pieces = []
        for head in (2 * pair, 2 * pair + 1):
            mine = lane < HEAD_DIM if head % 2 == 0 else lane >= HEAD_DIM
            gap = jnp.minimum(log_c[:, head : head + 1] - log_r[head : head + 1], 0.0)
            decay = jnp.exp(gap)
            outer = nt(jnp.where(mine, dy_pair, jnp.zeros_like(dy_pair)), values[:, lanes])
            fade = decay * step_r[head : head + 1]
            dscores = dscores + outer * fade
            flow = outer * scores
            base = flow * decay
            dstep_r = dstep_r + jnp.where(head_at == head, jnp.sum(base, axis=0, keepdims=True), 0.0)
            dlog_c = dlog_c + jnp.where(
                lane_at == head, jnp.sum(flow * fade, axis=1, keepdims=True), 0.0
            )
            pieces.append(tn((scores * fade).astype(BF16), dy_pair))
        dx_ref[:, lanes] += jnp.where(lane < HEAD_DIM, pieces[0], pieces[1])
    dscores = jnp.where(visible, dscores, 0.0).astype(BF16)
    dread = dread + nn(dscores, write)
    dwrite = dwrite + tn(dscores, read)
    dbc_ref[:, :STATE] = dwrite.astype(BF16)
    dbc_ref[:, STATE:] = dread.astype(BF16)

    upper = triangle(span, False)
    eye = jnp.where(row == col, 1.0, 0.0).astype(F32)
    dalpha = nn(upper, dlog_c, HIGHEST) - nt(upper, dstep_r * step_r, HIGHEST)[:, :heads]
    dstep = dstep_c + nt(eye, dstep_r, HIGHEST)[:, :heads]
    rate = jnp.exp(hrow_ref[0:1])
    draw = (dstep - rate * dalpha) * sigmoid(raw_ref[...])
    draw_low = draw.astype(BF16)
    dstep_ref[...] = draw_low
    hid = hid_ref[0]
    dtg_ref[...] += tn(draw_low, hid)
    rate_sum = jnp.sum(-dalpha * step_c * rate, axis=0, keepdims=True)
    bias_sum = jnp.sum(draw, axis=0, keepdims=True)
    at = lax.broadcasted_iota(jnp.int32, (8, heads), 0)
    headg_ref[...] += jnp.where(at == 0, rate_sum, jnp.where(at == 1, bias_sum, 0.0))

    ext_ref[0:span] = dx_ref[...] * silu_grad(convsum_ref[...])
    back = jnp.zeros((span, width), F32)
    conv_in = convin_ref[...].astype(F32)
    at = lax.broadcasted_iota(jnp.int32, (8, width), 0)
    sums = jnp.where(at == CONV, jnp.sum(ext_ref[0:span], axis=0, keepdims=True), 0.0)
    for tap in range(CONV):
        ahead = CONV - 1 - tap
        same = seg_ref[8 + ahead : 8 + ahead + span] == seg_here
        term = jnp.where(same, ext_ref[ahead : ahead + span], 0.0)
        back = back + conv_ref[tap : tap + 1] * term
        sums = sums + jnp.where(at == tap, jnp.sum(conv_in * term, axis=0, keepdims=True), 0.0)
    convg_ref[...] += sums
    ext_ref[span : span + 8] = ext_ref[0:8]
    dval = back.astype(BF16)
    dval_ref[...] = dval
    inacc_ref[...] += tn(hid, dval)

    @pl.when(step == pl.num_programs(0) - 1)
    def _():
        ing_ref[...] = inacc_ref[...].astype(BF16)


def hidden_back_kernel(perm_ref, dgate_ref, dval_ref, dstep_ref, wg_ref, wv_ref, wdt_ref, out_ref):
    total = nt(dgate_ref[...], wg_ref[...]) + nt(dval_ref[...], wv_ref[...])
    out_ref[0] = (total + nn(dstep_ref[...], wdt_ref[...])).astype(BF16)


def maps_back_kernel(dbc_ref, convsum_ref, convin_ref, conv_ref, segc_ref, hid_ref, dmap_ref, convg_ref, ing_ref, ext_ref):
    size, width = dmap_ref.shape
    ext_ref[0:size] = dbc_ref[...] * silu_grad(convsum_ref[...])
    ext_ref[size : size + 8] = jnp.zeros((8, width), F32)
    back = jnp.zeros((size, width), F32)
    conv_in = convin_ref[...].astype(F32)
    at = lax.broadcasted_iota(jnp.int32, (8, width), 0)
    sums = jnp.where(at == CONV, jnp.sum(ext_ref[0:size], axis=0, keepdims=True), 0.0)
    seg_here = segc_ref[8 : 8 + size]
    for tap in range(CONV):
        ahead = CONV - 1 - tap
        same = segc_ref[8 + ahead : 8 + ahead + size] == seg_here
        term = jnp.where(same, ext_ref[ahead : ahead + size], 0.0)
        back = back + conv_ref[tap : tap + 1] * term
        sums = sums + jnp.where(at == tap, jnp.sum(conv_in * term, axis=0, keepdims=True), 0.0)
    convg_ref[...] = sums
    dmap = back.astype(BF16)
    dmap_ref[...] = dmap
    ing_ref[...] = tn(hid_ref[...], dmap).astype(BF16)


def input_back_kernel(hg_ref, dmap_ref, wbc_ref, tok_ref, gain_ref, cot_ref, out_ref, gsum_ref):
    grad = hg_ref[...] + nt(dmap_ref[...], wbc_ref[...])
    tok = tok_ref[...]
    scale = lax.rsqrt(jnp.mean(tok * tok, axis=-1, keepdims=True) + NORM_EPS)
    unit = tok * scale
    gsum_ref[...] = jnp.sum(grad * unit, axis=0, keepdims=True) + jnp.zeros(gsum_ref.shape, F32)
    scaled = grad * gain_ref[...]
    mean = jnp.mean(scaled * unit, axis=-1, keepdims=True)
    out_ref[...] = cot_ref[...] + scale * (scaled - unit * mean)


def swap(value, axis, bit):
    count = lax.axis_size(axis)
    return lax.ppermute(value, axis, [(at, at ^ bit) for at in range(count)])


def gather_ctx(value):
    two = jnp.stack([value, swap(value, "ctx", 2)])
    return jnp.concatenate([two, swap(two, "ctx", 1)])


def scatter_ctx(value):
    near = value[0:2].astype(F32) + swap(value[2:4], "ctx", 1).astype(F32)
    return near[0] + swap(near[1].astype(BF16), "ctx", 2).astype(F32)


def sum_ctx(value):
    pair = value.astype(F32) + swap(value, "ctx", 1).astype(F32)
    pair = pair.astype(BF16)
    return pair.astype(F32) + swap(pair, "ctx", 2).astype(F32)


def adam_step(weight, moment_one, second, gradient, step_rate, decay_rate):
    moment_new = BETA_ONE * moment_one + (1.0 - BETA_ONE) * gradient
    second_new = BETA_TWO * second + (1.0 - BETA_TWO) * gradient * gradient
    first_hat = moment_new / (1.0 - BETA_ONE**STEP)
    second_hat = second_new / (1.0 - BETA_TWO**STEP)
    weight_new = weight - step_rate * (
        first_hat / (jnp.sqrt(second_hat) + ADAM_EPS) + decay_rate * weight
    )
    return (weight_new, moment_new, second_new)


def full(shape):
    return pl.BlockSpec(shape, lambda *_: (0,) * len(shape))


def shape_of(*shape, dtype=F32):
    return jax.ShapeDtypeStruct(shape, dtype)


def shards(
    tokens,
    segment_ids,
    cotangent,
    in_weight,
    dt_weight,
    out_weight,
    conv_params,
    gains,
    head_params,
    in_first,
    in_second,
    dt_first,
    dt_second,
    out_first,
    out_second,
    conv_first,
    conv_second,
    gain_first,
    gain_second,
    head_first,
    head_second,
):
    _, span, model = tokens.shape
    length = segment_ids.shape[1]
    ndp, nctx = lax.axis_size("dp"), lax.axis_size("ctx")
    d, c = lax.axis_index("dp"), lax.axis_index("ctx")
    heads = HEADS // nctx
    width = INNER // nctx
    maps = 2 * STATE
    wide = width + maps
    chunks = nctx
    rows_in = in_weight.shape[0]
    rows_out = out_weight.shape[0]
    cols_out = model // nctx
    conv_cols = conv_params.shape[1]
    gain_len = gains.shape[0]
    dt_cols = dt_weight.shape[1]

    tok = tokens[0]
    lanes = max(-(-max(gain_len, conv_cols, dt_cols) // 128) * 128, 128)

    def padded(value):
        return jnp.pad(value.astype(BF16), ((0, 0), (0, lanes - value.shape[1])))

    small = jnp.concatenate(
        [padded(dt_weight), padded(conv_params), padded(gains[None]), jnp.zeros((10, lanes), BF16)]
    )
    small_all = lax.all_gather(small, "dp", axis=0)
    gain_full = small_all[:, HEADS + CONV + 1, :gain_len].astype(F32).reshape(1, -1)
    conv_full = jnp.moveaxis(
        small_all[:, HEADS : HEADS + CONV + 1, :conv_cols].astype(F32), 0, 1
    ).reshape(CONV + 1, -1)
    dt_mine = lax.dynamic_slice_in_dim(small_all[:, :HEADS, :dt_cols], c * heads, heads, 1)
    dt_mine = jnp.moveaxis(dt_mine, 0, 1).reshape(heads, model)
    gain_pre = gain_full[:, :model]
    gain_mine = lax.dynamic_slice_in_dim(gain_full, model + c * width, width, 1)
    conv_mine = jnp.concatenate(
        [lax.dynamic_slice_in_dim(conv_full, c * width, width, 1), conv_full[:, INNER:]], axis=1
    )
    conv_mine = jnp.pad(conv_mine, ((0, 8 - CONV - 1), (0, 0)))

    value_part = lax.dynamic_slice_in_dim(in_weight, INNER + c * width, width, 1)
    w1 = lax.all_gather(
        jnp.concatenate([value_part, in_weight[:, 2 * INNER :]], axis=1).astype(BF16),
        "dp",
        axis=0,
        tiled=True,
    )
    wout = lax.all_gather(
        lax.dynamic_slice_in_dim(out_weight, c * cols_out, cols_out, 1).astype(BF16),
        "dp",
        axis=0,
        tiled=True,
    )
    wout = lax.all_to_all(wout, "ctx", split_axis=0, concat_axis=1, tiled=True)
    wg = lax.all_gather(
        lax.dynamic_slice_in_dim(in_weight, c * width, width, 1).astype(BF16),
        "dp",
        axis=0,
        tiled=True,
    )

    order = jnp.asarray([0, 2, 1, 3], jnp.int32)
    perm = order[jnp.arange(nctx, dtype=jnp.int32) ^ c]
    cot_all = gather_ctx(cotangent[0].astype(BF16))
    hid_own = pl.pallas_call(
        norm_kernel, out_shape=shape_of(span, model, dtype=BF16), compiler_params=params(), name="pre_norm"
    )(tok, gain_pre)
    hid_all = gather_ctx(hid_own)

    ids = segment_ids[0]
    seg_col = jnp.pad(ids, (8, 8), constant_values=-1)[:, None]
    seg_row = segment_ids
    head_mine = lax.dynamic_slice_in_dim(head_params, c * heads, heads, 1)
    head_col = head_mine.T

    slot_rows = pl.BlockSpec((1, span, model), lambda i, p: (p[i], 0, 0))
    rows = lambda cols: pl.BlockSpec((span, cols), lambda i, p: (i, 0))
    row_of = pl.BlockSpec((heads, span), lambda i, p: (0, i))

    mixed, conv_in, conv_sum, inner, raw, step_c, log_c, step_r, log_r, starts = pl.pallas_call(
        scan_forward_kernel,
        grid_spec=pltpu.PrefetchScalarGridSpec(
            num_scalar_prefetch=1,
            grid=(chunks,),
            in_specs=[
                slot_rows,
                full((model, wide)),
                full((heads, model)),
                full((8, wide)),
                full((3, heads)),
                full((heads, 3)),
                full((length + 16, 1)),
                pl.BlockSpec((1, span), lambda i, p: (0, i)),
            ],
            out_specs=[
                rows(wide),
                rows(wide),
                rows(wide),
                rows(width),
                rows(heads),
                rows(heads),
                rows(heads),
                row_of,
                row_of,
                pl.BlockSpec((1, STATE, width), lambda i, p: (i, 0, 0)),
            ],
            scratch_shapes=[
                pltpu.VMEM((span + 8, wide), F32),
                pltpu.VMEM((span + 8, 1), jnp.int32),
                pltpu.VMEM((STATE, width), F32),
            ],
        ),
        out_shape=[
            shape_of(length, wide, dtype=BF16),
            shape_of(length, wide, dtype=BF16),
            shape_of(length, wide),
            shape_of(length, width),
            shape_of(length, heads),
            shape_of(length, heads),
            shape_of(length, heads),
            shape_of(heads, length),
            shape_of(heads, length),
            shape_of(chunks, STATE, width),
        ],
        compiler_params=params("arbitrary"),
        name="scan_forward",
    )(perm, hid_all, w1, dt_mine, conv_mine, head_mine, head_col, seg_col, seg_row)

    gate, normed_grad, stats = pl.pallas_call(
        gate_kernel,
        grid_spec=pltpu.PrefetchScalarGridSpec(
            num_scalar_prefetch=1,
            grid=(chunks,),
            in_specs=[
                slot_rows,
                full((model, width)),
                rows(width),
                slot_rows,
                full((width, model)),
                full((1, width)),
            ],
            out_specs=[rows(width), rows(width), pl.BlockSpec((8, span), lambda i, p: (0, i))],
        ),
        out_shape=[
            shape_of(length, width, dtype=BF16),
            shape_of(length, width),
            shape_of(8, length),
        ],
        compiler_params=params("arbitrary"),
        name="gate",
    )(perm, hid_all, wg, inner, cot_all, wout, gain_mine)
    stats = stats + swap(stats, "ctx", 1)
    stats = stats + swap(stats, "ctx", 2)

    block_part, out_grad, gate_in_grad, dy, dgate, col_sums = pl.pallas_call(
        norm_back_kernel,
        grid_spec=pltpu.PrefetchScalarGridSpec(
            num_scalar_prefetch=1,
            grid=(chunks,),
            in_specs=[
                slot_rows,
                rows(width),
                rows(width),
                rows(width),
                pl.BlockSpec((8, span), lambda i, p: (0, i)),
                full((1, width)),
                slot_rows,
                full((width, model)),
                rows(width),
            ],
            out_specs=[
                slot_rows,
                full((width, model)),
                full((model, width)),
                rows(width),
                rows(width),
                full((8, width)),
            ],
            scratch_shapes=[pltpu.VMEM((width, model), F32), pltpu.VMEM((model, width), F32)],
        ),
        out_shape=[
            shape_of(nctx, span, model, dtype=BF16),
            shape_of(width, model, dtype=BF16),
            shape_of(model, width, dtype=BF16),
            shape_of(length, width),
            shape_of(length, width, dtype=BF16),
            shape_of(8, width),
        ],
        compiler_params=params("arbitrary"),
        name="norm_back",
    )(perm, hid_all, inner, gate, normed_grad, stats, gain_mine, cot_all, wout, mixed)

    block_output = tok + scatter_ctx(block_part)
    out_cols = lax.all_to_all(out_grad, "ctx", split_axis=1, concat_axis=0, tiled=True)
    out_shard = lax.psum_scatter(out_cols, "dp", scatter_dimension=0, tiled=True)
    gate_shard = lax.psum_scatter(gate_in_grad, "dp", scatter_dimension=0, tiled=True)

    back = lambda cols: pl.BlockSpec((span, cols), lambda i, p: (chunks - 1 - i, 0))
    back_row = pl.BlockSpec((heads, span), lambda i, p: (0, chunks - 1 - i))
    value_in_grad, dval, dbc, dstep, conv_grad, dt_grad, head_grad = pl.pallas_call(
        scan_back_kernel,
        grid_spec=pltpu.PrefetchScalarGridSpec(
            num_scalar_prefetch=1,
            grid=(chunks,),
            in_specs=[
                pl.BlockSpec((1, span, model), lambda i, p: (p[chunks - 1 - i], 0, 0)),
                back(width),
                back(wide),
                back(width),
                back(width),
                back(heads),
                back(heads),
                back(heads),
                back_row,
                back_row,
                pl.BlockSpec((1, STATE, width), lambda i, p: (chunks - 1 - i, 0, 0)),
                full((8, width)),
                full((3, heads)),
                full((length + 16, 1)),
                pl.BlockSpec((1, span), lambda i, p: (0, chunks - 1 - i)),
            ],
            out_specs=[
                full((model, width)),
                back(width),
                back(maps),
                back(heads),
                full((8, width)),
                full((heads, model)),
                full((8, heads)),
            ],
            scratch_shapes=[
                pltpu.VMEM((span + 8, width), F32),
                pltpu.VMEM((span + 16, 1), jnp.int32),
                pltpu.VMEM((STATE, width), F32),
                pltpu.VMEM((model, width), F32),
                pltpu.VMEM((span, width), F32),
            ],
        ),
        out_shape=[
            shape_of(model, width, dtype=BF16),
            shape_of(length, width, dtype=BF16),
            shape_of(length, maps, dtype=BF16),
            shape_of(length, heads, dtype=BF16),
            shape_of(8, width),
            shape_of(heads, model),
            shape_of(8, heads),
        ],
        compiler_params=params("arbitrary"),
        name="scan_back",
    )(
        perm, hid_all, dy, mixed, conv_in, conv_sum, raw, step_c, log_c, step_r, log_r, starts,
        conv_mine, head_mine, seg_col, seg_row,
    )
    value_shard = lax.psum_scatter(value_in_grad, "dp", scatter_dimension=0, tiled=True)
    dbc_total = sum_ctx(dbc)

    hidden_part = pl.pallas_call(
        hidden_back_kernel,
        grid_spec=pltpu.PrefetchScalarGridSpec(
            num_scalar_prefetch=1,
            grid=(chunks,),
            in_specs=[
                rows(width),
                rows(width),
                rows(heads),
                full((model, width)),
                full((model, width)),
                full((heads, model)),
            ],
            out_specs=[slot_rows],
        ),
        out_shape=[shape_of(nctx, span, model, dtype=BF16)],
        compiler_params=params("arbitrary"),
        name="hidden_back",
    )(perm, dgate, dval, dstep, wg, w1, dt_mine)[0]
    hidden_grad = scatter_ctx(hidden_part)

    hid_order = jnp.concatenate(
        [lax.dynamic_index_in_dim(hid_all, perm[at], 0, keepdims=False) for at in range(nctx)]
    )
    dmap, map_conv_grad, map_in_grad = pl.pallas_call(
        maps_back_kernel,
        out_shape=[
            shape_of(length, maps, dtype=BF16),
            shape_of(8, maps),
            shape_of(model, maps, dtype=BF16),
        ],
        scratch_shapes=[pltpu.VMEM((length + 8, maps), F32)],
        compiler_params=params(),
        name="maps_back",
    )(dbc_total, conv_sum[:, width:], conv_in[:, width:], conv_mine[:, width:], seg_col, hid_order)
    map_rows = rows_in // nctx
    map_part = lax.dynamic_index_in_dim(
        map_in_grad.reshape(ndp, nctx, map_rows, maps), c, 1, keepdims=False
    )
    map_shard = lax.psum_scatter(map_part, "dp", scatter_dimension=0, tiled=True)[0]

    input_grad, gain_sum = pl.pallas_call(
        input_back_kernel,
        out_shape=[shape_of(span, model), shape_of(8, model)],
        compiler_params=params(),
        name="input_back",
    )(
        hidden_grad,
        lax.dynamic_slice_in_dim(dmap, c * span, span, 0),
        w1[:, width:],
        tok,
        gain_pre,
        cotangent[0],
    )

    def row_block(value):
        return jnp.pad(value, ((0, 0), (0, width - value.shape[1])))

    half = model // width
    packed = jnp.concatenate(
        [conv_grad, col_sums, row_block(map_conv_grad), row_block(head_grad)]
        + [dt_grad[:, at * width : (at + 1) * width] for at in range(half)]
        + [gain_sum[:, at * width : (at + 1) * width] for at in range(half)]
    )
    packed = lax.all_gather(lax.psum(packed, "dp"), "ctx", axis=0)
    conv_total = jnp.concatenate(
        [packed[at, : CONV + 1] for at in range(nctx)] + [packed[0, 16 : 16 + CONV + 1, :maps]], axis=1
    )
    conv_total = lax.dynamic_slice_in_dim(conv_total, d * conv_cols, conv_cols, 1)
    dt_total = jnp.concatenate(
        [packed[:, 32 + 8 * at : 40 + 8 * at].reshape(HEADS, width) for at in range(half)], axis=1
    )
    dt_total = lax.dynamic_slice_in_dim(dt_total, d * dt_cols, dt_cols, 1)
    first_gain = 32 + 8 * half
    pre_total = [
        jnp.sum(packed[:, first_gain + 8 * at], axis=0) for at in range(half)
    ]
    gain_total = jnp.concatenate(pre_total + [packed[:, 8].reshape(-1)])
    gain_total = lax.dynamic_slice_in_dim(gain_total, d * gain_len, gain_len, 0)
    head_total = jnp.stack(
        [
            packed[:, 24, :heads].reshape(-1),
            packed[:, 25, :heads].reshape(-1),
            jnp.sum(packed[:, 9].reshape(HEADS, HEAD_DIM), axis=1),
        ]
    )

    columns = lax.all_gather(jnp.stack([gate_shard, value_shard]).astype(BF16), "ctx", axis=0)
    map_total = lax.all_gather(map_shard.astype(BF16), "ctx", axis=0, tiled=True)
    in_total = jnp.concatenate(
        [columns[at, 0] for at in range(nctx)] + [columns[at, 1] for at in range(nctx)] + [map_total],
        axis=1,
    ).astype(F32)
    out_total = lax.all_gather(out_shard.astype(BF16), "ctx", axis=1, tiled=True).astype(F32)

    in_new = adam_step(in_weight, in_first, in_second, in_total, 0.03, WEIGHT_DECAY)
    dt_new = adam_step(dt_weight, dt_first, dt_second, dt_total, 0.03, WEIGHT_DECAY)
    out_new = adam_step(out_weight, out_first, out_second, out_total, 0.02, WEIGHT_DECAY)
    conv_new = adam_step(conv_params, conv_first, conv_second, conv_total, 0.3, 0.0)
    gain_new = adam_step(gains, gain_first, gain_second, gain_total, 0.5, 0.0)
    head_new = adam_step(head_params, head_first, head_second, head_total, 2.0, 0.0)
    return (block_output[None], input_grad[None]) + in_new + dt_new + out_new + conv_new + gain_new + head_new


def solution(mesh):
    tokens, rows, cols = P("dp", "ctx", None), P("dp", None), P(None, "dp")
    return jax.shard_map(
        shards,
        mesh=mesh,
        in_specs=(tokens, rows, tokens, rows, cols, rows, cols, P("dp"), P())
        + (rows, rows, cols, cols, rows, rows, cols, cols, P("dp"), P("dp"), P(), P()),
        out_specs=(tokens, tokens)
        + (rows,) * 3
        + (cols,) * 3
        + (rows,) * 3
        + (cols,) * 3
        + (P("dp"),) * 3
        + (P(),) * 3,
        check_vma=False,
    )
```

```python
import jax
import jax.numpy as jnp
from jax import lax
from jax.experimental import pallas as pl
from jax.experimental.pallas import tpu as pltpu
from jax.sharding import PartitionSpec as P

INNER = 2048
HEADS = 32
HEAD_DIM = 64
STATE = 128
CONV = 4
STEP = 10

F32 = jnp.float32
BF16 = jnp.bfloat16
HIGHEST = lax.Precision.HIGHEST
NORM_EPS = 1e-05
BETA_ONE = 0.9
BETA_TWO = 0.95
ADAM_EPS = 1e-08
WEIGHT_DECAY = 0.1
VMEM_LIMIT = 56 * 1024 * 1024


def nn(a, b, precision=None):
    return lax.dot_general(
        a, b, (((1,), (0,)), ((), ())), precision=precision, preferred_element_type=F32
    )


def nt(a, b, precision=None):
    return lax.dot_general(
        a, b, (((1,), (1,)), ((), ())), precision=precision, preferred_element_type=F32
    )


def tn(a, b, precision=None):
    return lax.dot_general(
        a, b, (((0,), (0,)), ((), ())), precision=precision, preferred_element_type=F32
    )


def halves(value):
    high = value.astype(BF16)
    return high, (value - high.astype(F32)).astype(BF16)


def spread(value, width):
    heads = value.shape[1]
    row = lax.broadcasted_iota(jnp.int32, (heads, width), 0)
    col = lax.broadcasted_iota(jnp.int32, (heads, width), 1)
    table = jnp.where(col // HEAD_DIM == row, 1.0, 0.0).astype(BF16)
    high, low = halves(value)
    return nn(high, table) + nn(low, table)


def gather_heads(value, heads):
    width = value.shape[1]
    row = lax.broadcasted_iota(jnp.int32, (width, heads), 0)
    col = lax.broadcasted_iota(jnp.int32, (width, heads), 1)
    table = jnp.where(row // HEAD_DIM == col, 1.0, 0.0).astype(BF16)
    high, low = halves(value)
    return nn(high, table) + nn(low, table)


def softplus(value):
    return jnp.maximum(value, 0.0) + jnp.log1p(jnp.exp(-jnp.abs(value)))


def sigmoid(value):
    return 1.0 / (1.0 + jnp.exp(-value))


def silu_grad(value):
    sig = sigmoid(value)
    return sig * (1.0 + value * (1.0 - sig))


def triangle(size, lower):
    row = lax.broadcasted_iota(jnp.int32, (size, size), 0)
    col = lax.broadcasted_iota(jnp.int32, (size, size), 1)
    keep = row >= col if lower else row <= col
    return jnp.where(keep, 1.0, 0.0).astype(F32)


def params(*semantics):
    return pltpu.CompilerParams(
        dimension_semantics=semantics or None, vmem_limit_bytes=VMEM_LIMIT
    )


def place(pieces, at_ref, target, sems, first=0):
    copies = []
    for index, piece in enumerate(pieces):
        rows = piece.shape[0]
        start = pl.multiple_of(at_ref[index] * rows, 16)
        copies.append(
            pltpu.make_async_copy(piece, target.at[pl.ds(start, rows), :], sems.at[first + index])
        )
    for copy in copies:
        copy.start()
    return copies


def part_rows(total, own_bit, keep_ref, send_ref):
    count, rows, _ = keep_ref.shape
    for at in range(count):
        low = total[2 * at * rows : (2 * at + 1) * rows].astype(BF16)
        high = total[(2 * at + 1) * rows : (2 * at + 2) * rows].astype(BF16)
        keep_ref[at] = jnp.where(own_bit == 0, low, high)
        send_ref[at] = jnp.where(own_bit == 0, high, low)


def norm_kernel(tok_ref, gain_ref, hid_ref):
    tok = tok_ref[...]
    scale = lax.rsqrt(jnp.mean(tok * tok, axis=-1, keepdims=True) + NORM_EPS)
    hid_ref[...] = (tok * scale * gain_ref[...]).astype(BF16)


def scan_forward_kernel(
    perm_ref,
    at_ref,
    hid_ref,
    w1_pieces,
    wdt_ref,
    conv_ref,
    hrow_ref,
    hcol_ref,
    segc_ref,
    segr_ref,
    mixed_ref,
    convin_ref,
    convsum_ref,
    inner_ref,
    raw_ref,
    stepc_ref,
    logc_ref,
    stepr_ref,
    logr_ref,
    start_ref,
    ext_ref,
    seg_ref,
    state_ref,
    w1_ref,
    sems,
):
    step = pl.program_id(0)
    span = hid_ref.shape[1]
    heads = wdt_ref.shape[0]
    width = heads * HEAD_DIM

    @pl.when(step == 0)
    def _():
        copies = place(w1_pieces, at_ref, w1_ref, sems)
        ext_ref[0:8] = jnp.zeros((8, ext_ref.shape[1]), F32)
        state_ref[...] = jnp.zeros_like(state_ref)
        for copy in copies:
            copy.wait()

    hid = hid_ref[0]
    proj = nn(hid, w1_ref[...]).astype(BF16)
    convin_ref[...] = proj
    ext_ref[8 : 8 + span] = proj.astype(F32)
    seg_ref[...] = segc_ref[pl.ds(pl.multiple_of(step * span, 8), span + 8), :]
    seg_here = seg_ref[8 : 8 + span]
    total = conv_ref[CONV : CONV + 1]
    for tap in range(CONV):
        at = 8 - (CONV - 1) + tap
        same = seg_ref[at : at + span] == seg_here
        total = total + conv_ref[tap : tap + 1] * jnp.where(same, ext_ref[at : at + span], 0.0)
    ext_ref[0:8] = ext_ref[span : span + 8]
    convsum_ref[...] = total
    mixed = (total * sigmoid(total)).astype(BF16)
    mixed_ref[...] = mixed

    raw_c = nt(hid, wdt_ref[...]) + hrow_ref[1:2]
    raw_r = nt(wdt_ref[...], hid) + hcol_ref[:, 1:2]
    step_c = softplus(raw_c)
    step_r = softplus(raw_r)
    log_c = nn(triangle(span, True), -step_c * jnp.exp(hrow_ref[0:1]), HIGHEST)
    log_r = nn(-step_r * jnp.exp(hcol_ref[:, 0:1]), triangle(span, False), HIGHEST)
    raw_ref[...] = raw_c
    stepc_ref[...] = step_c
    logc_ref[...] = log_c
    stepr_ref[...] = step_r
    logr_ref[...] = log_r

    values = mixed[:, :width]
    write = mixed[:, width : width + STATE]
    read = mixed[:, width + STATE :]
    row = lax.broadcasted_iota(jnp.int32, (span, span), 0)
    col = lax.broadcasted_iota(jnp.int32, (span, span), 1)
    visible = (seg_here == segr_ref[...]) & (row >= col)
    scores = jnp.where(visible, nt(read, write), 0.0)
    lane = lax.broadcasted_iota(jnp.int32, (span, 2 * HEAD_DIM), 1)

    seg_prev = seg_ref[7:8]
    seg_last = seg_ref[span + 7 : span + 8]
    last = log_c[span - 1 : span]
    enter = jnp.where(seg_here == seg_prev, jnp.exp(log_c), 0.0)
    tail = jnp.where(seg_here == seg_last, jnp.exp(last - log_c), 0.0) * step_c
    keep = jnp.where(seg_last == seg_prev, jnp.exp(last), 0.0)
    state = state_ref[...]
    start_ref[0] = state
    values_f = values.astype(F32)
    base = spread(enter, width) * nn(read, state.astype(BF16)) + spread(
        hrow_ref[2:3] + jnp.zeros((8, heads), F32), width
    )[0:1] * values_f
    for pair in range(heads // 2):
        lanes = slice(pair * 2 * HEAD_DIM, (pair + 1) * 2 * HEAD_DIM)
        pieces = []
        for head in (2 * pair, 2 * pair + 1):
            gap = jnp.minimum(log_c[:, head : head + 1] - log_r[head : head + 1], 0.0)
            weights = scores * jnp.exp(gap) * step_r[head : head + 1]
            pieces.append(nn(weights.astype(BF16), values[:, lanes]))
        inner_ref[:, lanes] = base[:, lanes] + jnp.where(lane < HEAD_DIM, pieces[0], pieces[1])
    moved = (spread(tail, width) * values_f).astype(BF16)
    state_ref[...] = spread(keep + jnp.zeros((8, heads), F32), width)[0:1] * state + tn(
        write, moved
    )


def gate_kernel(
    perm_ref,
    at_ref,
    hid_ref,
    wg_pieces,
    inner_ref,
    cot_ref,
    wout_ref,
    gain_ref,
    gate_ref,
    ng_ref,
    stat_ref,
    wg_ref,
    sems,
):
    @pl.when(pl.program_id(0) == 0)
    def _():
        for copy in place(wg_pieces, at_ref, wg_ref, sems):
            copy.wait()

    gate = nn(hid_ref[0], wg_ref[...]).astype(BF16)
    gate_ref[...] = gate
    gate = gate.astype(F32)
    grad = nt(cot_ref[0], wout_ref[...])
    ng_ref[...] = grad
    gated = inner_ref[...] * (gate * sigmoid(gate))
    ones = jnp.ones((8, gated.shape[1]), F32)
    squares = nt(ones, gated * gated, HIGHEST)
    crossed = nt(ones, gated * (grad * gain_ref[...]), HIGHEST)
    at = lax.broadcasted_iota(jnp.int32, squares.shape, 0)
    stat_ref[...] = jnp.where(at == 0, squares, crossed)


def norm_back_kernel(
    perm_ref,
    here_ref,
    hid_ref,
    inner_ref,
    gate_ref,
    ng_ref,
    stat_ref,
    gain_ref,
    cot_ref,
    wout_ref,
    mixed_ref,
    block_ref,
    outg_refs,
    keep_ref,
    send_ref,
    dy_ref,
    dgate_ref,
    sums_ref,
    outacc_ref,
    inacc_ref,
):
    step = pl.program_id(0)
    span, width = inner_ref.shape

    @pl.when(step == 0)
    def _():
        outacc_ref[...] = jnp.zeros_like(outacc_ref)
        inacc_ref[...] = jnp.zeros_like(inacc_ref)
        sums_ref[...] = jnp.zeros_like(sums_ref)

    row = lax.broadcasted_iota(jnp.int32, (span, span), 0)
    col = lax.broadcasted_iota(jnp.int32, (span, span), 1)
    eye = jnp.where(row == col, 1.0, 0.0).astype(F32)
    stats = nt(eye, stat_ref[...], HIGHEST)
    inv = lax.rsqrt(stats[:, 0:1] * (1.0 / INNER) + NORM_EPS)
    cross = stats[:, 1:2]
    gate = gate_ref[...].astype(F32)
    sig = sigmoid(gate)
    silu = gate * sig
    inner = inner_ref[...]
    gated = inner * silu
    unit = gated * inv
    normed = (unit * gain_ref[...]).astype(BF16)
    cot = cot_ref[0]
    block_ref[0] = nn(normed, wout_ref[...]).astype(BF16)
    outacc_ref[...] += tn(normed, cot)
    grad = ng_ref[...]
    dgated = inv * (grad * gain_ref[...] - unit * (cross * inv * (1.0 / INNER)))
    dy = dgated * silu
    dy_ref[...] = dy
    dgate = (dgated * inner * (sig * (1.0 + gate * (1.0 - sig)))).astype(BF16)
    dgate_ref[...] = dgate
    inacc_ref[...] += tn(hid_ref[0], dgate)
    gain_sum = jnp.sum(grad * unit, axis=0, keepdims=True)
    skip_sum = jnp.sum(dy * mixed_ref[...].astype(F32), axis=0, keepdims=True)
    at = lax.broadcasted_iota(jnp.int32, (8, width), 0)
    sums_ref[...] += jnp.where(at == 0, gain_sum, jnp.where(at == 1, skip_sum, 0.0))

    @pl.when(step == pl.num_programs(0) - 1)
    def _():
        cols = outg_refs[0].shape[1]
        for at, outg_ref in enumerate(outg_refs):
            start = pl.multiple_of((here_ref[2] ^ at) * cols, 128)
            outg_ref[...] = outacc_ref[:, pl.ds(start, cols)].astype(BF16)
        part_rows(inacc_ref, here_ref[0], keep_ref, send_ref)


def scan_back_kernel(
    perm_ref,
    here_ref,
    hid_ref,
    dy_ref,
    mixed_ref,
    convin_ref,
    convsum_ref,
    raw_ref,
    stepc_ref,
    logc_ref,
    stepr_ref,
    logr_ref,
    start_ref,
    conv_ref,
    hrow_ref,
    segc_ref,
    segr_ref,
    keep_ref,
    send_ref,
    dval_ref,
    dbc_ref,
    dstep_ref,
    convg_ref,
    dtg_ref,
    headg_ref,
    ext_ref,
    seg_ref,
    grad_ref,
    inacc_ref,
    dx_ref,
):
    step = pl.program_id(0)
    chunk = pl.num_programs(0) - 1 - step
    span = hid_ref.shape[1]
    heads = stepc_ref.shape[1]
    width = heads * HEAD_DIM

    @pl.when(step == 0)
    def _():
        ext_ref[span : span + 8] = jnp.zeros((8, width), F32)
        grad_ref[...] = jnp.zeros_like(grad_ref)
        inacc_ref[...] = jnp.zeros_like(inacc_ref)
        convg_ref[...] = jnp.zeros_like(convg_ref)
        dtg_ref[...] = jnp.zeros_like(dtg_ref)
        headg_ref[...] = jnp.zeros_like(headg_ref)

    seg_ref[...] = segc_ref[pl.ds(pl.multiple_of(chunk * span, 8), span + 16), :]
    seg_here = seg_ref[8 : 8 + span]
    seg_prev = seg_ref[7:8]
    seg_last = seg_ref[span + 7 : span + 8]
    mixed = mixed_ref[...]
    values = mixed[:, :width]
    write = mixed[:, width : width + STATE]
    read = mixed[:, width + STATE :]
    values_f = values.astype(F32)
    dy = dy_ref[...]
    dy_low = dy.astype(BF16)
    step_c = stepc_ref[...]
    log_c = logc_ref[...]
    step_r = stepr_ref[...]
    log_r = logr_ref[...]
    last = log_c[span - 1 : span]
    enter = jnp.where(seg_here == seg_prev, jnp.exp(log_c), 0.0)
    tail_raw = jnp.where(seg_here == seg_last, jnp.exp(last - log_c), 0.0)
    tail = tail_raw * step_c
    keep = jnp.where(seg_last == seg_prev, jnp.exp(last), 0.0)
    enter_w = spread(enter, width)
    tail_w = spread(tail, width)
    wide = spread(
        jnp.concatenate([hrow_ref[2:3] + jnp.zeros((8, heads), F32), keep + jnp.zeros((8, heads), F32)], axis=0),
        width,
    )
    skip_w = wide[0:1]
    keep_w = wide[8:9]
    state = start_ref[0]
    state_low = state.astype(BF16)
    later = grad_ref[...]
    later_low = later.astype(BF16)

    row = lax.broadcasted_iota(jnp.int32, (span, span), 0)
    col = lax.broadcasted_iota(jnp.int32, (span, span), 1)
    visible = (seg_here == segr_ref[...]) & (row >= col)
    scores = jnp.where(visible, nt(read, write), 0.0)
    lane = lax.broadcasted_iota(jnp.int32, (span, 2 * HEAD_DIM), 1)
    head_at = lax.broadcasted_iota(jnp.int32, (8, span), 0)
    lane_at = lax.broadcasted_iota(jnp.int32, (span, heads), 1)

    entered = enter_w * dy
    entered_low = entered.astype(BF16)
    inter = enter_w * nn(read, state_low)
    from_later = nn(write, later_low)
    moved_low = (tail_w * values_f).astype(BF16)
    dread = nt(entered_low, state_low)
    dwrite = nt(moved_low, later_low)
    dlog_c = gather_heads(dy * inter, heads)
    tail_dot = gather_heads(values_f * from_later, heads)
    dlog_c = dlog_c - tail_dot * tail
    dstep_c = tail_dot * tail_raw
    carried = gather_heads(jnp.sum(later * state, axis=0, keepdims=True) + jnp.zeros((8, width), F32), heads)[0:1]
    at_last = lax.broadcasted_iota(jnp.int32, (span, heads), 0) == span - 1
    dlog_c = dlog_c + jnp.where(
        at_last, jnp.sum(tail_dot * tail, axis=0, keepdims=True) + keep * carried, 0.0
    )
    grad_ref[...] = keep_w * later + tn(read, entered_low)
    dx_ref[...] = tail_w * from_later + skip_w * dy

    dscores = jnp.zeros((span, span), F32)
    dstep_r = jnp.zeros((8, span), F32)
    for pair in range(heads // 2):
        lanes = slice(pair * 2 * HEAD_DIM, (pair + 1) * 2 * HEAD_DIM)
        dy_pair = dy_low[:, lanes]
        pieces = []
        for head in (2 * pair, 2 * pair + 1):
            mine = lane < HEAD_DIM if head % 2 == 0 else lane >= HEAD_DIM
            gap = jnp.minimum(log_c[:, head : head + 1] - log_r[head : head + 1], 0.0)
            decay = jnp.exp(gap)
            outer = nt(jnp.where(mine, dy_pair, jnp.zeros_like(dy_pair)), values[:, lanes])
            fade = decay * step_r[head : head + 1]
            dscores = dscores + outer * fade
            flow = outer * scores
            base = flow * decay
            dstep_r = dstep_r + jnp.where(head_at == head, jnp.sum(base, axis=0, keepdims=True), 0.0)
            dlog_c = dlog_c + jnp.where(
                lane_at == head, jnp.sum(flow * fade, axis=1, keepdims=True), 0.0
            )
            pieces.append(tn((scores * fade).astype(BF16), dy_pair))
        dx_ref[:, lanes] += jnp.where(lane < HEAD_DIM, pieces[0], pieces[1])
    dscores = jnp.where(visible, dscores, 0.0).astype(BF16)
    dread = dread + nn(dscores, write)
    dwrite = dwrite + tn(dscores, read)
    dbc_ref[:, :STATE] = dwrite.astype(BF16)
    dbc_ref[:, STATE:] = dread.astype(BF16)

    upper = triangle(span, False)
    eye = jnp.where(row == col, 1.0, 0.0).astype(F32)
    dalpha = nn(upper, dlog_c, HIGHEST) - nt(upper, dstep_r * step_r, HIGHEST)[:, :heads]
    dstep = dstep_c + nt(eye, dstep_r, HIGHEST)[:, :heads]
    rate = jnp.exp(hrow_ref[0:1])
    draw = (dstep - rate * dalpha) * sigmoid(raw_ref[...])
    draw_low = draw.astype(BF16)
    dstep_ref[...] = draw_low
    hid = hid_ref[0]
    dtg_ref[...] += tn(draw_low, hid)
    rate_sum = jnp.sum(-dalpha * step_c * rate, axis=0, keepdims=True)
    bias_sum = jnp.sum(draw, axis=0, keepdims=True)
    at = lax.broadcasted_iota(jnp.int32, (8, heads), 0)
    headg_ref[...] += jnp.where(at == 0, rate_sum, jnp.where(at == 1, bias_sum, 0.0))

    ext_ref[0:span] = dx_ref[...] * silu_grad(convsum_ref[...])
    back = jnp.zeros((span, width), F32)
    conv_in = convin_ref[...].astype(F32)
    at = lax.broadcasted_iota(jnp.int32, (8, width), 0)
    sums = jnp.where(at == CONV, jnp.sum(ext_ref[0:span], axis=0, keepdims=True), 0.0)
    for tap in range(CONV):
        ahead = CONV - 1 - tap
        same = seg_ref[8 + ahead : 8 + ahead + span] == seg_here
        term = jnp.where(same, ext_ref[ahead : ahead + span], 0.0)
        back = back + conv_ref[tap : tap + 1] * term
        sums = sums + jnp.where(at == tap, jnp.sum(conv_in * term, axis=0, keepdims=True), 0.0)
    convg_ref[...] += sums
    ext_ref[span : span + 8] = ext_ref[0:8]
    dval = back.astype(BF16)
    dval_ref[...] = dval
    inacc_ref[...] += tn(hid, dval)

    @pl.when(step == pl.num_programs(0) - 1)
    def _():
        part_rows(inacc_ref, here_ref[0], keep_ref, send_ref)


def hidden_back_kernel(
    perm_ref,
    at_ref,
    dgate_ref,
    dval_ref,
    dstep_ref,
    wg_pieces,
    w1_pieces,
    wdt_ref,
    hid_ref,
    gain_ref,
    out_ref,
    gsum_ref,
    wg_ref,
    wv_ref,
    sems,
):
    @pl.when(pl.program_id(0) == 0)
    def _():
        copies = place(wg_pieces, at_ref, wg_ref, sems)
        copies += place(w1_pieces, at_ref, wv_ref, sems, len(wg_pieces))
        gsum_ref[...] = jnp.zeros_like(gsum_ref)
        for copy in copies:
            copy.wait()

    width = wg_ref.shape[1]
    total = nt(dgate_ref[...], wg_ref[...]) + nt(dval_ref[...], wv_ref[:, :width])
    total = total + nn(dstep_ref[...], wdt_ref[...])
    out_ref[0] = total.astype(BF16)
    unit = hid_ref[0].astype(F32) / gain_ref[...]
    gsum_ref[...] += jnp.sum(total * unit, axis=0, keepdims=True) + jnp.zeros(gsum_ref.shape, F32)


def maps_back_kernel(
    perm_ref,
    at_ref,
    here_ref,
    dbc_ref,
    convsum_ref,
    convin_ref,
    conv_ref,
    segc_ref,
    hid_ref,
    w1_pieces,
    gain_ref,
    convg_ref,
    keep_ref,
    send_ref,
    own_ref,
    gsum_ref,
    ext_ref,
    acc_ref,
    dmap_ref,
    w1_ref,
    sems,
):
    copies = place(w1_pieces, at_ref, w1_ref, sems)
    size, width = dmap_ref.shape
    ext_ref[0:size] = dbc_ref[...] * silu_grad(convsum_ref[...])
    ext_ref[size : size + 8] = jnp.zeros((8, width), F32)
    back = jnp.zeros((size, width), F32)
    conv_in = convin_ref[...].astype(F32)
    at = lax.broadcasted_iota(jnp.int32, (8, width), 0)
    sums = jnp.where(at == CONV, jnp.sum(ext_ref[0:size], axis=0, keepdims=True), 0.0)
    seg_here = segc_ref[8 : 8 + size]
    for tap in range(CONV):
        ahead = CONV - 1 - tap
        same = segc_ref[8 + ahead : 8 + ahead + size] == seg_here
        term = jnp.where(same, ext_ref[ahead : ahead + size], 0.0)
        back = back + conv_ref[tap : tap + 1] * term
        sums = sums + jnp.where(at == tap, jnp.sum(conv_in * term, axis=0, keepdims=True), 0.0)
    convg_ref[...] = sums
    dmap_ref[...] = back.astype(BF16)
    pieces, span, _ = hid_ref.shape
    total = None
    for index in range(pieces):
        part = tn(hid_ref[perm_ref[index]], dmap_ref[index * span : (index + 1) * span])
        total = part if total is None else total + part
    acc_ref[...] = total
    count, rows, _ = keep_ref.shape
    for at_block in range(count):
        start = pl.multiple_of((2 * at_block * pieces + here_ref[2]) * rows, 8)
        low = acc_ref[pl.ds(start, rows), :].astype(BF16)
        start = pl.multiple_of(((2 * at_block + 1) * pieces + here_ref[2]) * rows, 8)
        high = acc_ref[pl.ds(start, rows), :].astype(BF16)
        keep_ref[at_block] = jnp.where(here_ref[0] == 0, low, high)
        send_ref[at_block] = jnp.where(here_ref[0] == 0, high, low)
    own = dmap_ref[pl.ds(pl.multiple_of(here_ref[2] * span, 16), span), :]
    for copy in copies:
        copy.wait()
    grad = nt(own, w1_ref[:, w1_ref.shape[1] - width :])
    own_ref[...] = grad
    unit = hid_ref[0].astype(F32) / gain_ref[...]
    gsum_ref[...] = jnp.sum(grad * unit, axis=0, keepdims=True) + jnp.zeros(gsum_ref.shape, F32)


def input_back_kernel(hg_ref, own_ref, tok_ref, gain_ref, cot_ref, out_ref):
    grad = hg_ref[...] + own_ref[...]
    tok = tok_ref[...]
    scale = lax.rsqrt(jnp.mean(tok * tok, axis=-1, keepdims=True) + NORM_EPS)
    unit = tok * scale
    scaled = grad * gain_ref[...]
    mean = jnp.mean(scaled * unit, axis=-1, keepdims=True)
    out_ref[...] = cot_ref[...] + scale * (scaled - unit * mean)


def split_kernel(here_ref, part_refs, keep_ref, send_ref):
    rows = keep_ref.shape[1]
    for at, part_ref in enumerate(part_refs):
        place_at = here_ref[2] ^ at
        low, high = part_ref[0:rows], part_ref[rows : 2 * rows]
        keep_ref[pl.ds(place_at, 1)] = jnp.where(here_ref[0] == 0, low, high)[None]
        send_ref[pl.ds(place_at, 1)] = jnp.where(here_ref[0] == 0, high, low)[None]


def pair_sum_kernel(here_ref, keep_ref, came_ref, out_refs):
    for at, out_ref in enumerate(out_refs):
        index = pl.ds(here_ref[1] ^ at, 1)
        out_ref[...] = (keep_ref[index].astype(F32) + came_ref[index].astype(F32))[0].astype(BF16)


def adam_in_kernel(
    here_ref, weight_ref, first_ref, second_ref, gate_refs, value_refs, map_refs, *rest
):
    new_refs, (cols_ref, maps_ref) = rest[:3], rest[3:]
    step = pl.program_id(0)
    pieces = len(gate_refs)
    rows, width = gate_refs[0].shape
    block = weight_ref.shape[1]
    per = width // block

    @pl.when(step == 0)
    def _():
        for at in range(pieces):
            owner = here_ref[2] ^ at
            cols_ref[pl.ds(owner, 1)] = gate_refs[at][...][None]
            cols_ref[pl.ds(pieces + owner, 1)] = value_refs[at][...][None]
            some = map_refs[at].shape[0]
            maps_ref[pl.ds(pl.multiple_of(owner * some, some), some), :] = map_refs[at][...]

    last = pl.num_programs(0) - 1

    @pl.when(step < last)
    def _():
        grad = cols_ref[step // per, :, pl.ds(pl.multiple_of((step % per) * block, 128), block)]
        news = adam_step(weight_ref[...], first_ref[...], second_ref[...], grad.astype(F32), 0.03, WEIGHT_DECAY)
        for ref, new in zip(new_refs, news):
            ref[...] = new

    @pl.when(step == last)
    def _():
        news = adam_step(
            weight_ref[...], first_ref[...], second_ref[...], maps_ref[...].astype(F32), 0.03, WEIGHT_DECAY
        )
        for ref, new in zip(new_refs, news):
            ref[...] = new


def swap(value, axis, bit):
    count = lax.axis_size(axis)
    return lax.ppermute(value, axis, [(at, at ^ bit) for at in range(count)])


def gather_ctx(value):
    two = jnp.stack([value, swap(value, "ctx", 2)])
    return jnp.concatenate([two, swap(two, "ctx", 1)])


def scatter_ctx(value):
    near = value[0:2].astype(F32) + swap(value[2:4], "ctx", 1).astype(F32)
    return near[0] + swap(near[1].astype(BF16), "ctx", 2).astype(F32)


def sum_ctx(value):
    pair = value.astype(F32) + swap(value, "ctx", 1).astype(F32)
    pair = pair.astype(BF16)
    return pair.astype(F32) + swap(pair, "ctx", 2).astype(F32)


def gather_dp(value):
    count, here = lax.axis_size("dp"), lax.axis_index("dp")
    if count > 8 or count & (count - 1) or value.shape[0] % 16:
        return [lax.all_gather(value, "dp", axis=0, tiled=True)], jnp.zeros((1,), jnp.int32)
    pieces = [(value, 0)] + [(swap(value, "dp", bit), bit) for bit in range(2, count, 2)]
    if count > 1:
        pieces += [(swap(piece, "dp", 1), bit + 1) for piece, bit in pieces]
    return [piece for piece, _ in pieces], here ^ jnp.asarray([bit for _, bit in pieces], jnp.int32)


def scatter_dp(keep, send, here, name):
    count, rows, cols = keep.shape
    if 2 * count != lax.axis_size("dp"):
        return keep[0]
    came = swap(send, "dp", 1)
    if count > 4 or rows % 16:
        part = keep.astype(F32) + came.astype(F32)
        stride, high = 2, here[1]
        while part.shape[0] > 1:
            size = min(4, part.shape[0])
            low = part.astype(BF16).reshape(part.shape[0] // size, size, rows, cols)
            part = 0.0
            for at in range(size):
                term = lax.dynamic_index_in_dim(low, (high % size) ^ at, 1, keepdims=False)
                part = part + (swap(term, "dp", stride * at) if at else term).astype(F32)
            stride, high = stride * size, high // size
        return part[0].astype(BF16)
    parts = pl.pallas_call(
        pair_sum_kernel,
        in_specs=[pl.BlockSpec(memory_space=pltpu.SMEM)] + [pl.BlockSpec(memory_space=pltpu.VMEM)] * 2,
        out_shape=[[shape_of(rows, cols, dtype=BF16)] * count],
        compiler_params=params(),
        name="pair_sum_" + name,
    )(here, keep, came)[0]
    total = parts[0].astype(F32)
    for at in range(1, count):
        total = total + swap(parts[at], "dp", 2 * at).astype(F32)
    return total.astype(BF16)


def fan_ctx(value):
    return [value] + [swap(value, "ctx", bit) for bit in range(1, lax.axis_size("ctx"))]


def adam_step(weight, moment_one, second, gradient, step_rate, decay_rate):
    moment_new = BETA_ONE * moment_one + (1.0 - BETA_ONE) * gradient
    second_new = BETA_TWO * second + (1.0 - BETA_TWO) * gradient * gradient
    first_hat = moment_new / (1.0 - BETA_ONE**STEP)
    second_hat = second_new / (1.0 - BETA_TWO**STEP)
    weight_new = weight - step_rate * (
        first_hat / (jnp.sqrt(second_hat) + ADAM_EPS) + decay_rate * weight
    )
    return (weight_new, moment_new, second_new)


def full(shape):
    return pl.BlockSpec(shape, lambda *_: (0,) * len(shape))


def shape_of(*shape, dtype=F32):
    return jax.ShapeDtypeStruct(shape, dtype)


def shards(
    tokens,
    segment_ids,
    cotangent,
    in_weight,
    dt_weight,
    out_weight,
    conv_params,
    gains,
    head_params,
    in_first,
    in_second,
    dt_first,
    dt_second,
    out_first,
    out_second,
    conv_first,
    conv_second,
    gain_first,
    gain_second,
    head_first,
    head_second,
):
    _, span, model = tokens.shape
    length = segment_ids.shape[1]
    ndp, nctx = lax.axis_size("dp"), lax.axis_size("ctx")
    d, c = lax.axis_index("dp"), lax.axis_index("ctx")
    heads = HEADS // nctx
    width = INNER // nctx
    maps = 2 * STATE
    wide = width + maps
    chunks = nctx
    rows_in = in_weight.shape[0]
    rows_out = out_weight.shape[0]
    cols_out = model // nctx
    conv_cols = conv_params.shape[1]
    gain_len = gains.shape[0]
    dt_cols = dt_weight.shape[1]

    tok = tokens[0]
    lanes = max(-(-max(gain_len, conv_cols, dt_cols) // 128) * 128, 128)

    def padded(value):
        return jnp.pad(value.astype(BF16), ((0, 0), (0, lanes - value.shape[1])))

    small = jnp.concatenate(
        [padded(dt_weight), padded(conv_params), padded(gains[None]), jnp.zeros((10, lanes), BF16)]
    )
    small_all = lax.all_gather(small, "dp", axis=0)
    gain_full = small_all[:, HEADS + CONV + 1, :gain_len].astype(F32).reshape(1, -1)
    conv_full = jnp.moveaxis(
        small_all[:, HEADS : HEADS + CONV + 1, :conv_cols].astype(F32), 0, 1
    ).reshape(CONV + 1, -1)
    dt_mine = lax.dynamic_slice_in_dim(small_all[:, :HEADS, :dt_cols], c * heads, heads, 1)
    dt_mine = jnp.moveaxis(dt_mine, 0, 1).reshape(heads, model)
    gain_pre = gain_full[:, :model]
    gain_mine = lax.dynamic_slice_in_dim(gain_full, model + c * width, width, 1)
    conv_mine = jnp.concatenate(
        [lax.dynamic_slice_in_dim(conv_full, c * width, width, 1), conv_full[:, INNER:]], axis=1
    )
    conv_mine = jnp.pad(conv_mine, ((0, 8 - CONV - 1), (0, 0)))

    value_part = lax.dynamic_slice_in_dim(in_weight, INNER + c * width, width, 1)
    w1, at_rows = gather_dp(
        jnp.concatenate([value_part, in_weight[:, 2 * INNER :]], axis=1).astype(BF16)
    )
    wout = lax.all_gather(
        lax.dynamic_slice_in_dim(out_weight, c * cols_out, cols_out, 1).astype(BF16),
        "dp",
        axis=0,
        tiled=True,
    )
    wout = lax.all_to_all(wout, "ctx", split_axis=0, concat_axis=1, tiled=True)
    wg, _ = gather_dp(lax.dynamic_slice_in_dim(in_weight, c * width, width, 1).astype(BF16))
    here = jnp.stack([d & 1, d >> 1, c]).astype(jnp.int32)

    order = jnp.asarray([0, 2, 1, 3], jnp.int32)
    perm = order[jnp.arange(nctx, dtype=jnp.int32) ^ c]
    cot_all = gather_ctx(cotangent[0].astype(BF16))
    hid_own = pl.pallas_call(
        norm_kernel, out_shape=shape_of(span, model, dtype=BF16), compiler_params=params(), name="pre_norm"
    )(tok, gain_pre)
    hid_all = gather_ctx(hid_own)

    ids = segment_ids[0]
    seg_col = jnp.pad(ids, (8, 8), constant_values=-1)[:, None]
    seg_row = segment_ids
    head_mine = lax.dynamic_slice_in_dim(head_params, c * heads, heads, 1)
    head_col = head_mine.T

    anywhere = lambda pieces: [pl.BlockSpec(memory_space=pl.ANY)] * len(pieces)
    blocks_of = lambda rows, cols: [shape_of(ndp // 2, rows, cols, dtype=BF16)] * 2
    slot_rows = pl.BlockSpec((1, span, model), lambda i, p, *_: (p[i], 0, 0))
    rows = lambda cols: pl.BlockSpec((span, cols), lambda i, *_: (i, 0))
    row_of = pl.BlockSpec((heads, span), lambda i, *_: (0, i))

    mixed, conv_in, conv_sum, inner, raw, step_c, log_c, step_r, log_r, starts = pl.pallas_call(
        scan_forward_kernel,
        grid_spec=pltpu.PrefetchScalarGridSpec(
            num_scalar_prefetch=2,
            grid=(chunks,),
            in_specs=[
                slot_rows,
                anywhere(w1),
                full((heads, model)),
                full((8, wide)),
                full((3, heads)),
                full((heads, 3)),
                full((length + 16, 1)),
                pl.BlockSpec((1, span), lambda i, *_: (0, i)),
            ],
            out_specs=[
                rows(wide),
                rows(wide),
                rows(wide),
                rows(width),
                rows(heads),
                rows(heads),
                rows(heads),
                row_of,
                row_of,
                pl.BlockSpec((1, STATE, width), lambda i, *_: (i, 0, 0)),
            ],
            scratch_shapes=[
                pltpu.VMEM((span + 8, wide), F32),
                pltpu.VMEM((span + 8, 1), jnp.int32),
                pltpu.VMEM((STATE, width), F32),
                pltpu.VMEM((model, wide), BF16),
                pltpu.SemaphoreType.DMA((len(w1),)),
            ],
        ),
        out_shape=[
            shape_of(length, wide, dtype=BF16),
            shape_of(length, wide, dtype=BF16),
            shape_of(length, wide),
            shape_of(length, width),
            shape_of(length, heads),
            shape_of(length, heads),
            shape_of(length, heads),
            shape_of(heads, length),
            shape_of(heads, length),
            shape_of(chunks, STATE, width),
        ],
        compiler_params=params("arbitrary"),
        name="scan_forward",
    )(perm, at_rows, hid_all, w1, dt_mine, conv_mine, head_mine, head_col, seg_col, seg_row)

    gate, normed_grad, stats = pl.pallas_call(
        gate_kernel,
        grid_spec=pltpu.PrefetchScalarGridSpec(
            num_scalar_prefetch=2,
            grid=(chunks,),
            in_specs=[
                slot_rows,
                anywhere(wg),
                rows(width),
                slot_rows,
                full((width, model)),
                full((1, width)),
            ],
            out_specs=[rows(width), rows(width), pl.BlockSpec((8, span), lambda i, *_: (0, i))],
            scratch_shapes=[pltpu.VMEM((model, width), BF16), pltpu.SemaphoreType.DMA((len(wg),))],
        ),
        out_shape=[
            shape_of(length, width, dtype=BF16),
            shape_of(length, width),
            shape_of(8, length),
        ],
        compiler_params=params("arbitrary"),
        name="gate",
    )(perm, at_rows, hid_all, wg, inner, cot_all, wout, gain_mine)
    stats = sum(fan_ctx(stats))

    block_part, out_grads, gate_keep, gate_send, dy, dgate, col_sums = pl.pallas_call(
        norm_back_kernel,
        grid_spec=pltpu.PrefetchScalarGridSpec(
            num_scalar_prefetch=2,
            grid=(chunks,),
            in_specs=[
                slot_rows,
                rows(width),
                rows(width),
                rows(width),
                pl.BlockSpec((8, span), lambda i, *_: (0, i)),
                full((1, width)),
                slot_rows,
                full((width, model)),
                rows(width),
            ],
            out_specs=[
                slot_rows,
                [full((width, cols_out))] * nctx,
                full((ndp // 2, rows_in, width)),
                full((ndp // 2, rows_in, width)),
                rows(width),
                rows(width),
                full((8, width)),
            ],
            scratch_shapes=[pltpu.VMEM((width, model), F32), pltpu.VMEM((model, width), F32)],
        ),
        out_shape=[
            shape_of(nctx, span, model, dtype=BF16),
            [shape_of(width, cols_out, dtype=BF16)] * nctx,
            *blocks_of(rows_in, width),
            shape_of(length, width),
            shape_of(length, width, dtype=BF16),
            shape_of(8, width),
        ],
        compiler_params=params("arbitrary"),
        name="norm_back",
    )(perm, here, hid_all, inner, gate, normed_grad, stats, gain_mine, cot_all, wout, mixed)

    block_output = tok + scatter_ctx(block_part)
    gate_shard = scatter_dp(gate_keep, gate_send, here, "gate")
    if ndp == 2 * nctx:
        out_grads = [
            swap(part, "ctx", bit) if bit else part for bit, part in enumerate(out_grads)
        ]
        out_keep, out_send = pl.pallas_call(
            split_kernel,
            in_specs=[
                pl.BlockSpec(memory_space=pltpu.SMEM),
                [pl.BlockSpec(memory_space=pltpu.VMEM)] * nctx,
            ],
            out_shape=blocks_of(rows_out, cols_out),
            compiler_params=params(),
            name="out_split",
        )(here, out_grads)
        out_shard = scatter_dp(out_keep, out_send, here, "out")
    else:
        natural = [lax.dynamic_index_in_dim(jnp.stack(out_grads), c ^ at, 0, False) for at in range(nctx)]
        out_grad = lax.all_to_all(
            jnp.concatenate(natural, axis=1), "ctx", split_axis=1, concat_axis=0, tiled=True
        )
        out_shard = lax.psum_scatter(out_grad, "dp", scatter_dimension=0, tiled=True)

    back = lambda cols: pl.BlockSpec((span, cols), lambda i, *_: (chunks - 1 - i, 0))
    back_row = pl.BlockSpec((heads, span), lambda i, *_: (0, chunks - 1 - i))
    value_keep, value_send, dval, dbc, dstep, conv_grad, dt_grad, head_grad = pl.pallas_call(
        scan_back_kernel,
        grid_spec=pltpu.PrefetchScalarGridSpec(
            num_scalar_prefetch=2,
            grid=(chunks,),
            in_specs=[
                pl.BlockSpec((1, span, model), lambda i, p, *_: (p[chunks - 1 - i], 0, 0)),
                back(width),
                back(wide),
                back(width),
                back(width),
                back(heads),
                back(heads),
                back(heads),
                back_row,
                back_row,
                pl.BlockSpec((1, STATE, width), lambda i, *_: (chunks - 1 - i, 0, 0)),
                full((8, width)),
                full((3, heads)),
                full((length + 16, 1)),
                pl.BlockSpec((1, span), lambda i, *_: (0, chunks - 1 - i)),
            ],
            out_specs=[
                full((ndp // 2, rows_in, width)),
                full((ndp // 2, rows_in, width)),
                back(width),
                back(maps),
                back(heads),
                full((8, width)),
                full((heads, model)),
                full((8, heads)),
            ],
            scratch_shapes=[
                pltpu.VMEM((span + 8, width), F32),
                pltpu.VMEM((span + 16, 1), jnp.int32),
                pltpu.VMEM((STATE, width), F32),
                pltpu.VMEM((model, width), F32),
                pltpu.VMEM((span, width), F32),
            ],
        ),
        out_shape=[
            *blocks_of(rows_in, width),
            shape_of(length, width, dtype=BF16),
            shape_of(length, maps, dtype=BF16),
            shape_of(length, heads, dtype=BF16),
            shape_of(8, width),
            shape_of(heads, model),
            shape_of(8, heads),
        ],
        compiler_params=params("arbitrary"),
        name="scan_back",
    )(
        perm, here, hid_all, dy, mixed, conv_in, conv_sum, raw, step_c, log_c, step_r, log_r, starts,
        conv_mine, head_mine, seg_col, seg_row,
    )
    value_shard = scatter_dp(value_keep, value_send, here, "value")
    dbc_total = sum_ctx(dbc)

    hidden_part, gain_sum = pl.pallas_call(
        hidden_back_kernel,
        grid_spec=pltpu.PrefetchScalarGridSpec(
            num_scalar_prefetch=2,
            grid=(chunks,),
            in_specs=[
                rows(width),
                rows(width),
                rows(heads),
                anywhere(wg),
                anywhere(w1),
                full((heads, model)),
                slot_rows,
                full((1, model)),
            ],
            out_specs=[slot_rows, full((8, model))],
            scratch_shapes=[
                pltpu.VMEM((model, width), BF16),
                pltpu.VMEM((model, wide), BF16),
                pltpu.SemaphoreType.DMA((len(wg) + len(w1),)),
            ],
        ),
        out_shape=[shape_of(nctx, span, model, dtype=BF16), shape_of(8, model)],
        compiler_params=params("arbitrary"),
        name="hidden_back",
    )(perm, at_rows, dgate, dval, dstep, wg, w1, dt_mine, hid_all, gain_pre)
    hidden_grad = scatter_ctx(hidden_part)

    map_rows = rows_in // nctx
    in_smem = pl.BlockSpec(memory_space=pltpu.SMEM)
    in_vmem = pl.BlockSpec(memory_space=pltpu.VMEM)
    map_conv_grad, map_keep, map_send, hidden_own, gain_own = pl.pallas_call(
        maps_back_kernel,
        in_specs=[in_smem] * 3 + [in_vmem] * 6 + [anywhere(w1), in_vmem],
        out_shape=[
            shape_of(8, maps),
            *blocks_of(map_rows, maps),
            shape_of(span, model),
            shape_of(8, model),
        ],
        scratch_shapes=[
            pltpu.VMEM((length + 8, maps), F32),
            pltpu.VMEM((model, maps), F32),
            pltpu.VMEM((length, maps), BF16),
            pltpu.VMEM((model, wide), BF16),
            pltpu.SemaphoreType.DMA((len(w1),)),
        ],
        compiler_params=params(),
        name="maps_back",
    )(
        perm,
        at_rows,
        here,
        dbc_total,
        conv_sum[:, width:],
        conv_in[:, width:],
        conv_mine[:, width:],
        seg_col,
        hid_all,
        w1,
        gain_pre,
    )
    map_shard = scatter_dp(map_keep, map_send, here, "map")

    input_grad = pl.pallas_call(
        input_back_kernel,
        out_shape=shape_of(span, model),
        compiler_params=params(),
        name="input_back",
    )(hidden_grad, hidden_own, tok, gain_pre, cotangent[0])

    def row_block(value):
        return jnp.pad(value, ((0, 0), (0, width - value.shape[1])))

    half = model // width
    gain_sum = gain_sum + gain_own
    packed = jnp.concatenate(
        [conv_grad[: CONV + 1], col_sums[:2], row_block(head_grad[:2]), row_block(map_conv_grad[: CONV + 1])]
        + [gain_sum[:1, at * width : (at + 1) * width] for at in range(half)]
        + [dt_grad[:, at * width : (at + 1) * width] for at in range(half)]
    )
    packed = jnp.pad(packed, ((0, -packed.shape[0] % 8), (0, 0)))
    if ndp > 8 or ndp & (ndp - 1):
        packed = lax.psum(packed, "dp")
    else:
        packed = packed + swap(packed, "dp", 1)
        others = [swap(packed, "dp", bit) for bit in range(2, ndp, 2)]
        others = jnp.stack([packed] + others)[here[1] ^ jnp.arange(ndp // 2)]
        packed = sum(others[at] for at in range(ndp // 2))
    packed = jnp.stack(fan_ctx(packed))[c ^ jnp.arange(nctx)]
    map_at = CONV + 5
    gain_at = map_at + CONV + 1
    dt_at = gain_at + half
    conv_total = jnp.concatenate(
        [packed[at, : CONV + 1] for at in range(nctx)] + [packed[0, map_at:gain_at, :maps]], axis=1
    )
    conv_total = lax.dynamic_slice_in_dim(conv_total, d * conv_cols, conv_cols, 1)
    dt_total = jnp.concatenate(
        [packed[:, dt_at + heads * at : dt_at + heads * (at + 1)].reshape(HEADS, width) for at in range(half)],
        axis=1,
    )
    dt_total = lax.dynamic_slice_in_dim(dt_total, d * dt_cols, dt_cols, 1)
    pre_total = jnp.sum(packed[:, gain_at:dt_at], axis=0).reshape(-1)
    gain_total = jnp.concatenate([pre_total, packed[:, CONV + 1].reshape(-1)])
    gain_total = lax.dynamic_slice_in_dim(gain_total, d * gain_len, gain_len, 0)
    head_total = jnp.concatenate(
        [
            jnp.moveaxis(packed[:, CONV + 3 : CONV + 5, :heads], 0, 1).reshape(2, HEADS),
            jnp.sum(packed[:, CONV + 2].reshape(HEADS, HEAD_DIM), axis=1)[None],
        ]
    )

    gates, values, maps_in, outs = [
        fan_ctx(shard) for shard in (gate_shard, value_shard, map_shard, out_shard)
    ]
    if rows_in % 64 == 0:
        block = maps
        steps = in_weight.shape[1] // block
        part = pl.BlockSpec((rows_in, block), lambda i, *_: (0, i))
        in_new = pl.pallas_call(
            adam_in_kernel,
            grid_spec=pltpu.PrefetchScalarGridSpec(
                num_scalar_prefetch=1,
                grid=(steps,),
                in_specs=[part] * 3
                + [
                    [full((rows_in, width))] * nctx,
                    [full((rows_in, width))] * nctx,
                    [full((map_rows, maps))] * nctx,
                ],
                out_specs=[part] * 3,
                scratch_shapes=[
                    pltpu.VMEM((2 * nctx, rows_in, width), BF16),
                    pltpu.VMEM((rows_in, maps), BF16),
                ],
            ),
            out_shape=[shape_of(*in_weight.shape)] * 3,
            compiler_params=params("arbitrary"),
            name="adam_in",
        )(here, in_weight, in_first, in_second, gates, values, maps_in)
        in_new = tuple(in_new)
    else:
        natural = lambda parts: [
            lax.dynamic_index_in_dim(jnp.stack(parts), c ^ at, 0, False) for at in range(nctx)
        ]
        in_total = jnp.concatenate(
            natural(gates) + natural(values) + [jnp.concatenate(natural(maps_in))], axis=1
        ).astype(F32)
        in_new = adam_step(in_weight, in_first, in_second, in_total, 0.03, WEIGHT_DECAY)
    out_total = jnp.stack(outs)[c ^ jnp.arange(nctx)]
    out_total = jnp.concatenate([out_total[at] for at in range(nctx)], axis=1).astype(F32)

    dt_new = adam_step(dt_weight, dt_first, dt_second, dt_total, 0.03, WEIGHT_DECAY)
    out_new = adam_step(out_weight, out_first, out_second, out_total, 0.02, WEIGHT_DECAY)
    conv_new = adam_step(conv_params, conv_first, conv_second, conv_total, 0.3, 0.0)
    gain_new = adam_step(gains, gain_first, gain_second, gain_total, 0.5, 0.0)
    head_new = adam_step(head_params, head_first, head_second, head_total, 2.0, 0.0)
    return (block_output[None], input_grad[None]) + in_new + dt_new + out_new + conv_new + gain_new + head_new


def solution(mesh):
    tokens, rows, cols = P("dp", "ctx", None), P("dp", None), P(None, "dp")
    return jax.shard_map(
        shards,
        mesh=mesh,
        in_specs=(tokens, rows, tokens, rows, cols, rows, cols, P("dp"), P())
        + (rows, rows, cols, cols, rows, rows, cols, cols, P("dp"), P("dp"), P(), P()),
        out_specs=(tokens, tokens)
        + (rows,) * 3
        + (cols,) * 3
        + (rows,) * 3
        + (cols,) * 3
        + (P("dp"),) * 3
        + (P(),) * 3,
        check_vma=False,
    )
```

```python
import functools

import jax
import jax.numpy as jnp
from jax import lax
from jax.experimental import pallas as pl
from jax.experimental.pallas import tpu as pltpu
from jax.sharding import PartitionSpec as P

INNER = 2048
HEADS = 32
HEAD_DIM = 64
STATE = 128
CONV = 4
STEP = 10

F32 = jnp.float32
BF16 = jnp.bfloat16
HIGHEST = lax.Precision.HIGHEST
NORM_EPS = 1e-05
BETA_ONE = 0.9
BETA_TWO = 0.95
ADAM_EPS = 1e-08
WEIGHT_DECAY = 0.1
VMEM_LIMIT = 56 * 1024 * 1024


def nn(a, b, precision=None):
    return lax.dot_general(
        a, b, (((1,), (0,)), ((), ())), precision=precision, preferred_element_type=F32
    )


def nt(a, b, precision=None):
    return lax.dot_general(
        a, b, (((1,), (1,)), ((), ())), precision=precision, preferred_element_type=F32
    )


def tn(a, b, precision=None):
    return lax.dot_general(
        a, b, (((0,), (0,)), ((), ())), precision=precision, preferred_element_type=F32
    )


def halves(value):
    high = value.astype(BF16)
    return high, (value - high.astype(F32)).astype(BF16)


def spread(value, width):
    heads = value.shape[1]
    row = lax.broadcasted_iota(jnp.int32, (heads, width), 0)
    col = lax.broadcasted_iota(jnp.int32, (heads, width), 1)
    table = jnp.where(col // HEAD_DIM == row, 1.0, 0.0).astype(BF16)
    high, low = halves(value)
    return nn(high, table) + nn(low, table)


def gather_heads(value, heads):
    width = value.shape[1]
    row = lax.broadcasted_iota(jnp.int32, (width, heads), 0)
    col = lax.broadcasted_iota(jnp.int32, (width, heads), 1)
    table = jnp.where(row // HEAD_DIM == col, 1.0, 0.0).astype(BF16)
    high, low = halves(value)
    return nn(high, table) + nn(low, table)


def softplus(value):
    return jnp.maximum(value, 0.0) + jnp.log1p(jnp.exp(-jnp.abs(value)))


def sigmoid(value):
    return 1.0 / (1.0 + jnp.exp(-value))


def silu_grad(value):
    sig = sigmoid(value)
    return sig * (1.0 + value * (1.0 - sig))


def triangle(size, lower):
    row = lax.broadcasted_iota(jnp.int32, (size, size), 0)
    col = lax.broadcasted_iota(jnp.int32, (size, size), 1)
    keep = row >= col if lower else row <= col
    return jnp.where(keep, 1.0, 0.0).astype(F32)


def params(*semantics):
    return pltpu.CompilerParams(
        dimension_semantics=semantics or None, vmem_limit_bytes=VMEM_LIMIT
    )


def place(pieces, at_ref, sems, targets):
    copies = []
    for index, piece in enumerate(pieces):
        for block in range(piece.shape[0]):
            for first, rows, target in targets:
                copies.append(
                    pltpu.make_async_copy(
                        piece.at[block, first : first + rows],
                        target(at_ref[index] + block),
                        sems.at[len(copies)],
                    )
                )
    for copy in copies:
        copy.start()
    return copies


def copies_of(pieces, targets):
    return sum(piece.shape[0] for piece in pieces) * targets


def rows_of(ref, rows):
    return lambda at: ref.at[pl.ds(pl.multiple_of(at * rows, 16), rows)]


def part_of(block, own_bit, keep_ref, send_ref, first=0):
    for at in range(keep_ref.shape[0]):
        low, high = block(2 * at).astype(BF16), block(2 * at + 1).astype(BF16)
        rows = slice(first, first + low.shape[0])
        keep_ref[at, rows] = jnp.where(own_bit == 0, low, high)
        send_ref[at, rows] = jnp.where(own_bit == 0, high, low)


def pick_heads(ref, base, ctx, heads):
    first = pl.multiple_of(base + (ctx >> 1) * 2 * HEAD_DIM, 2 * HEAD_DIM)
    wide = ref[:, pl.ds(first, 2 * HEAD_DIM)]
    low = lax.broadcasted_iota(jnp.int32, wide.shape, 1) < HEAD_DIM
    odd = (ctx & 1) == 1
    out = []
    for pair in range(heads // 2):
        parts = []
        for head in (2 * pair, 2 * pair + 1):
            first = pl.multiple_of(base + head * 4 * HEAD_DIM + (ctx >> 1) * 2 * HEAD_DIM, 2 * HEAD_DIM)
            parts.append(ref[:, pl.ds(first, 2 * HEAD_DIM)])
        even = jnp.where(low, parts[0], pltpu.roll(parts[1], HEAD_DIM, 1))
        other = jnp.where(low, pltpu.roll(parts[0], HEAD_DIM, 1), parts[1])
        out.append(jnp.where(odd, other, even))
    return out


def pack_kernel(here_ref, win_ref, wout_ref, dt_ref, conv_ref, gain_ref, cot_ref, w1_ref, g2_ref, cotl_ref, tmp_ref):
    ctx = here_ref[2]
    rows = win_ref.shape[0]
    heads = HEADS // 4
    width = heads * HEAD_DIM
    for at, part in enumerate(pick_heads(win_ref, INNER, ctx, heads)):
        w1_ref[0:rows, at * 128 : (at + 1) * 128] = part.astype(BF16)
    w1_ref[0:rows, width:] = win_ref[:, 2 * INNER :].astype(BF16)
    tmp_ref[...] = jnp.zeros_like(tmp_ref)
    row = lax.broadcasted_iota(jnp.int32, (heads, HEADS), 0)
    col = lax.broadcasted_iota(jnp.int32, (heads, HEADS), 1)
    table = jnp.where(col == 4 * row + ctx, 1.0, 0.0).astype(BF16)
    tmp_ref[0:heads, 384 : 384 + dt_ref.shape[1]] = nn(table, dt_ref[...].astype(BF16))
    tmp_ref[8 : 8 + CONV + 1, 0 : conv_ref.shape[1]] = conv_ref[...]
    tmp_ref[8 + CONV + 1 : 8 + CONV + 2, 0 : gain_ref.shape[1]] = gain_ref[...]
    w1_ref[rows : rows + 16, :] = tmp_ref[...].astype(BF16)
    for at, part in enumerate(pick_heads(win_ref, 0, ctx, heads)):
        g2_ref[0:rows, at * 128 : (at + 1) * 128] = part.astype(BF16)
    if g2_ref.shape[0] > rows:
        some = wout_ref.shape[0] // 4
        mine = wout_ref[pl.ds(pl.multiple_of(ctx * some, 8), some), :].astype(BF16)
        g2_ref[rows : rows + some] = mine[:, :width]
        g2_ref[rows + some : rows + 2 * some] = mine[:, width:]
    cotl_ref[...] = cot_ref[...].astype(BF16)


def scan_forward_kernel(
    here_ref,
    at_ref,
    tok_pieces,
    w1_pieces,
    hrow_ref,
    hcol_ref,
    segc_ref,
    segr_ref,
    hid_ref,
    conv_ref,
    gpre_ref,
    gmine_ref,
    wdt_ref,
    w1_ref,
    mixed_ref,
    convin_ref,
    convsum_ref,
    inner_ref,
    raw_ref,
    stepc_ref,
    logc_ref,
    stepr_ref,
    logr_ref,
    start_ref,
    ext_ref,
    seg_ref,
    state_ref,
    small_ref,
    tok_ref,
    conv_all,
    gain_all,
    sems,
    tok_sems,
):
    step = pl.program_id(0)
    span, model = hid_ref.shape
    heads = wdt_ref.shape[0]
    width = heads * HEAD_DIM
    shards = small_ref.shape[0]
    rows = model // shards

    @pl.when(step == 0)
    def _():
        copies = place(
            w1_pieces,
            at_ref,
            sems,
            [(0, rows, rows_of(w1_ref, rows)), (rows, 16, lambda at: small_ref.at[at])],
        )
        tokens = [
            pltpu.make_async_copy(piece, tok_ref.at[here_ref[2] ^ index], tok_sems.at[index])
            for index, piece in enumerate(tok_pieces)
        ]
        for copy in tokens:
            copy.start()
        ext_ref[0:8] = jnp.zeros((8, ext_ref.shape[1]), F32)
        state_ref[...] = jnp.zeros_like(state_ref)
        conv_all[...] = jnp.zeros_like(conv_all)
        for copy in copies:
            copy.wait()
        conv_cols = conv_all.shape[1] // shards
        gain_len = gain_all.shape[1] // shards
        for shard in range(shards):
            small = small_ref[shard].astype(F32)
            wdt_ref[:, shard * rows : (shard + 1) * rows] = small[0:8, 384 : 384 + rows].astype(BF16)
            conv_all[0 : CONV + 1, shard * conv_cols : (shard + 1) * conv_cols] = small[
                8 : 8 + CONV + 1, :conv_cols
            ]
            gain_all[:, shard * gain_len : (shard + 1) * gain_len] = small[13:14, :gain_len]
        for at, part in enumerate(pick_heads(conv_all, 0, here_ref[2], heads)):
            conv_ref[:, at * 128 : (at + 1) * 128] = part
        conv_ref[:, width:] = conv_all[:, INNER:]
        gpre_ref[...] = gain_all[:, :model]
        for at, part in enumerate(pick_heads(gain_all, model, here_ref[2], heads)):
            gmine_ref[:, at * 128 : (at + 1) * 128] = part
        for copy in tokens:
            copy.wait()

    tok = tok_ref[step]
    scale = lax.rsqrt(jnp.mean(tok * tok, axis=-1, keepdims=True) + NORM_EPS)
    hid = (tok * scale * gpre_ref[...]).astype(BF16)
    hid_ref[...] = hid
    proj = nn(hid, w1_ref[...]).astype(BF16)
    convin_ref[...] = proj
    ext_ref[8 : 8 + span] = proj.astype(F32)
    seg_ref[...] = segc_ref[pl.ds(pl.multiple_of(step * span, 8), span + 8), :]
    seg_here = seg_ref[8 : 8 + span]
    total = conv_ref[CONV : CONV + 1]
    for tap in range(CONV):
        at = 8 - (CONV - 1) + tap
        same = seg_ref[at : at + span] == seg_here
        total = total + conv_ref[tap : tap + 1] * jnp.where(same, ext_ref[at : at + span], 0.0)
    ext_ref[0:8] = ext_ref[span : span + 8]
    convsum_ref[...] = total
    mixed = (total * sigmoid(total)).astype(BF16)
    mixed_ref[...] = mixed

    raw_c = nt(hid, wdt_ref[...]) + hrow_ref[1:2]
    raw_r = nt(wdt_ref[...], hid) + hcol_ref[:, 1:2]
    step_c = softplus(raw_c)
    step_r = softplus(raw_r)
    log_c = nn(triangle(span, True), -step_c * jnp.exp(hrow_ref[0:1]), HIGHEST)
    log_r = nn(-step_r * jnp.exp(hcol_ref[:, 0:1]), triangle(span, False), HIGHEST)
    raw_ref[...] = raw_c
    stepc_ref[...] = step_c
    logc_ref[...] = log_c
    stepr_ref[...] = step_r
    logr_ref[...] = log_r

    values = mixed[:, :width]
    write = mixed[:, width : width + STATE]
    read = mixed[:, width + STATE :]
    row = lax.broadcasted_iota(jnp.int32, (span, span), 0)
    col = lax.broadcasted_iota(jnp.int32, (span, span), 1)
    visible = (seg_here == segr_ref[...]) & (row >= col)
    scores = jnp.where(visible, nt(read, write), 0.0)
    lane = lax.broadcasted_iota(jnp.int32, (span, 2 * HEAD_DIM), 1)

    seg_prev = seg_ref[7:8]
    seg_last = seg_ref[span + 7 : span + 8]
    last = log_c[span - 1 : span]
    enter = jnp.where(seg_here == seg_prev, jnp.exp(log_c), 0.0)
    tail = jnp.where(seg_here == seg_last, jnp.exp(last - log_c), 0.0) * step_c
    keep = jnp.where(seg_last == seg_prev, jnp.exp(last), 0.0)
    state = state_ref[...]
    start_ref[0] = state
    values_f = values.astype(F32)
    base = spread(enter, width) * nn(read, state.astype(BF16)) + spread(
        hrow_ref[2:3] + jnp.zeros((8, heads), F32), width
    )[0:1] * values_f
    for pair in range(heads // 2):
        lanes = slice(pair * 2 * HEAD_DIM, (pair + 1) * 2 * HEAD_DIM)
        pieces = []
        for head in (2 * pair, 2 * pair + 1):
            gap = jnp.minimum(log_c[:, head : head + 1] - log_r[head : head + 1], 0.0)
            weights = scores * jnp.exp(gap) * step_r[head : head + 1]
            pieces.append(nn(weights.astype(BF16), values[:, lanes]))
        inner_ref[:, lanes] = base[:, lanes] + jnp.where(lane < HEAD_DIM, pieces[0], pieces[1])
    moved = (spread(tail, width) * values_f).astype(BF16)
    state_ref[...] = spread(keep + jnp.zeros((8, heads), F32), width)[0:1] * state + tn(
        write, moved
    )


def gate_kernel(
    here_ref,
    at_ref,
    hid_ref,
    g2_pieces,
    cot_pieces,
    inner_ref,
    gain_ref,
    wg_ref,
    wout_ref,
    cot_ref,
    gate_ref,
    ng_ref,
    stat_ref,
    sems,
    cot_sems,
):
    step = pl.program_id(0)
    rows = wg_ref.shape[0] // (wout_ref.shape[0] // HEAD_DIM)
    width = wg_ref.shape[1]

    @pl.when(step == 0)
    def _():
        some = rows_of(wout_ref, HEAD_DIM)
        copies = place(
            g2_pieces,
            at_ref,
            sems,
            [
                (0, rows, rows_of(wg_ref, rows)),
                (rows, HEAD_DIM, lambda at: some(at).at[:, 0:width]),
                (rows + HEAD_DIM, HEAD_DIM, lambda at: some(at).at[:, width : 2 * width]),
            ],
        )
        cots = [
            pltpu.make_async_copy(piece, cot_ref.at[here_ref[2] ^ index], cot_sems.at[index])
            for index, piece in enumerate(cot_pieces)
        ]
        for copy in cots:
            copy.start()
        for copy in copies + cots:
            copy.wait()

    gate = nn(hid_ref[...], wg_ref[...]).astype(BF16)
    gate_ref[...] = gate
    gate = gate.astype(F32)
    grad = nt(cot_ref[step], wout_ref[...])
    ng_ref[...] = grad
    gated = inner_ref[...] * (gate * sigmoid(gate))
    ones = jnp.ones((8, gated.shape[1]), F32)
    squares = nt(ones, gated * gated, HIGHEST)
    crossed = nt(ones, gated * (grad * gain_ref[...]), HIGHEST)
    at = lax.broadcasted_iota(jnp.int32, squares.shape, 0)
    stat_ref[...] = jnp.where(at == 0, squares, crossed)


def norm_back_kernel(
    perm_ref,
    here_ref,
    hid_ref,
    inner_ref,
    gate_ref,
    ng_ref,
    stat_ref,
    gain_ref,
    mixed_ref,
    wout_ref,
    cot_ref,
    block_ref,
    keep_ref,
    send_ref,
    dy_ref,
    dgate_ref,
    sums_ref,
    outacc_ref,
    inacc_ref,
):
    step = pl.program_id(0)
    span, width = inner_ref.shape

    @pl.when(step == 0)
    def _():
        outacc_ref[...] = jnp.zeros_like(outacc_ref)
        inacc_ref[...] = jnp.zeros_like(inacc_ref)
        sums_ref[...] = jnp.zeros_like(sums_ref)

    row = lax.broadcasted_iota(jnp.int32, (span, span), 0)
    col = lax.broadcasted_iota(jnp.int32, (span, span), 1)
    eye = jnp.where(row == col, 1.0, 0.0).astype(F32)
    stats = nt(eye, stat_ref[...], HIGHEST)
    inv = lax.rsqrt(stats[:, 0:1] * (1.0 / INNER) + NORM_EPS)
    cross = stats[:, 1:2]
    gate = gate_ref[...].astype(F32)
    sig = sigmoid(gate)
    silu = gate * sig
    inner = inner_ref[...]
    gated = inner * silu
    unit = gated * inv
    normed = (unit * gain_ref[...]).astype(BF16)
    cot = cot_ref[step]
    block_ref[0] = nn(normed, wout_ref[...]).astype(BF16)
    outacc_ref[...] += tn(normed, cot)
    grad = ng_ref[...]
    dgated = inv * (grad * gain_ref[...] - unit * (cross * inv * (1.0 / INNER)))
    dy = dgated * silu
    dy_ref[...] = dy
    dgate = (dgated * inner * (sig * (1.0 + gate * (1.0 - sig)))).astype(BF16)
    dgate_ref[...] = dgate
    inacc_ref[...] += tn(hid_ref[...], dgate)
    gain_sum = jnp.sum(grad * unit, axis=0, keepdims=True)
    skip_sum = jnp.sum(dy * mixed_ref[...].astype(F32), axis=0, keepdims=True)
    at = lax.broadcasted_iota(jnp.int32, (8, width), 0)
    sums_ref[...] += jnp.where(at == 0, gain_sum, jnp.where(at == 1, skip_sum, 0.0))

    @pl.when(step == pl.num_programs(0) - 1)
    def _():
        own = here_ref[0]
        rows = inacc_ref.shape[0] // (2 * keep_ref.shape[0])
        part_of(lambda at: inacc_ref[at * rows : (at + 1) * rows], own, keep_ref, send_ref)
        outs = lambda at: outacc_ref[at * HEAD_DIM : (at + 1) * HEAD_DIM]
        part_of(lambda at: outs(at)[:, :width], own, keep_ref, send_ref, rows)
        part_of(lambda at: outs(at)[:, width:], own, keep_ref, send_ref, rows + HEAD_DIM)


def scan_back_kernel(
    perm_ref,
    here_ref,
    hid_ref,
    dy_ref,
    mixed_ref,
    convin_ref,
    convsum_ref,
    raw_ref,
    stepc_ref,
    logc_ref,
    stepr_ref,
    logr_ref,
    start_ref,
    conv_ref,
    hrow_ref,
    segc_ref,
    segr_ref,
    keep_ref,
    send_ref,
    dval_ref,
    dbc_ref,
    dstep_ref,
    convg_ref,
    dtg_ref,
    headg_ref,
    ext_ref,
    seg_ref,
    grad_ref,
    inacc_ref,
    dx_ref,
):
    step = pl.program_id(0)
    chunk = pl.num_programs(0) - 1 - step
    span = hid_ref.shape[0]
    heads = stepc_ref.shape[1]
    width = heads * HEAD_DIM

    @pl.when(step == 0)
    def _():
        ext_ref[span : span + 8] = jnp.zeros((8, width), F32)
        grad_ref[...] = jnp.zeros_like(grad_ref)
        inacc_ref[...] = jnp.zeros_like(inacc_ref)
        convg_ref[...] = jnp.zeros_like(convg_ref)
        dtg_ref[...] = jnp.zeros_like(dtg_ref)
        headg_ref[...] = jnp.zeros_like(headg_ref)

    seg_ref[...] = segc_ref[pl.ds(pl.multiple_of(chunk * span, 8), span + 16), :]
    seg_here = seg_ref[8 : 8 + span]
    seg_prev = seg_ref[7:8]
    seg_last = seg_ref[span + 7 : span + 8]
    mixed = mixed_ref[...]
    values = mixed[:, :width]
    write = mixed[:, width : width + STATE]
    read = mixed[:, width + STATE :]
    values_f = values.astype(F32)
    dy = dy_ref[...]
    dy_low = dy.astype(BF16)
    step_c = stepc_ref[...]
    log_c = logc_ref[...]
    step_r = stepr_ref[...]
    log_r = logr_ref[...]
    last = log_c[span - 1 : span]
    enter = jnp.where(seg_here == seg_prev, jnp.exp(log_c), 0.0)
    tail_raw = jnp.where(seg_here == seg_last, jnp.exp(last - log_c), 0.0)
    tail = tail_raw * step_c
    keep = jnp.where(seg_last == seg_prev, jnp.exp(last), 0.0)
    enter_w = spread(enter, width)
    tail_w = spread(tail, width)
    wide = spread(
        jnp.concatenate([hrow_ref[2:3] + jnp.zeros((8, heads), F32), keep + jnp.zeros((8, heads), F32)], axis=0),
        width,
    )
    skip_w = wide[0:1]
    keep_w = wide[8:9]
    state = start_ref[0]
    state_low = state.astype(BF16)
    later = grad_ref[...]
    later_low = later.astype(BF16)

    row = lax.broadcasted_iota(jnp.int32, (span, span), 0)
    col = lax.broadcasted_iota(jnp.int32, (span, span), 1)
    visible = (seg_here == segr_ref[...]) & (row >= col)
    scores = jnp.where(visible, nt(read, write), 0.0)
    lane = lax.broadcasted_iota(jnp.int32, (span, 2 * HEAD_DIM), 1)
    head_at = lax.broadcasted_iota(jnp.int32, (8, span), 0)
    lane_at = lax.broadcasted_iota(jnp.int32, (span, heads), 1)

    entered = enter_w * dy
    entered_low = entered.astype(BF16)
    inter = enter_w * nn(read, state_low)
    from_later = nn(write, later_low)
    moved_low = (tail_w * values_f).astype(BF16)
    dread = nt(entered_low, state_low)
    dwrite = nt(moved_low, later_low)
    dlog_c = gather_heads(dy * inter, heads)
    tail_dot = gather_heads(values_f * from_later, heads)
    dlog_c = dlog_c - tail_dot * tail
    dstep_c = tail_dot * tail_raw
    carried = gather_heads(jnp.sum(later * state, axis=0, keepdims=True) + jnp.zeros((8, width), F32), heads)[0:1]
    at_last = lax.broadcasted_iota(jnp.int32, (span, heads), 0) == span - 1
    dlog_c = dlog_c + jnp.where(
        at_last, jnp.sum(tail_dot * tail, axis=0, keepdims=True) + keep * carried, 0.0
    )
    grad_ref[...] = keep_w * later + tn(read, entered_low)
    dx_ref[...] = tail_w * from_later + skip_w * dy

    dscores = jnp.zeros((span, span), F32)
    dstep_r = jnp.zeros((8, span), F32)
    for pair in range(heads // 2):
        lanes = slice(pair * 2 * HEAD_DIM, (pair + 1) * 2 * HEAD_DIM)
        dy_pair = dy_low[:, lanes]
        pieces = []
        for head in (2 * pair, 2 * pair + 1):
            mine = lane < HEAD_DIM if head % 2 == 0 else lane >= HEAD_DIM
            gap = jnp.minimum(log_c[:, head : head + 1] - log_r[head : head + 1], 0.0)
            decay = jnp.exp(gap)
            outer = nt(jnp.where(mine, dy_pair, jnp.zeros_like(dy_pair)), values[:, lanes])
            fade = decay * step_r[head : head + 1]
            dscores = dscores + outer * fade
            flow = outer * scores
            base = flow * decay
            dstep_r = dstep_r + jnp.where(head_at == head, jnp.sum(base, axis=0, keepdims=True), 0.0)
            dlog_c = dlog_c + jnp.where(
                lane_at == head, jnp.sum(flow * fade, axis=1, keepdims=True), 0.0
            )
            pieces.append(tn((scores * fade).astype(BF16), dy_pair))
        dx_ref[:, lanes] += jnp.where(lane < HEAD_DIM, pieces[0], pieces[1])
    dscores = jnp.where(visible, dscores, 0.0).astype(BF16)
    dread = dread + nn(dscores, write)
    dwrite = dwrite + tn(dscores, read)
    dbc_ref[:, :STATE] = dwrite.astype(BF16)
    dbc_ref[:, STATE:] = dread.astype(BF16)

    upper = triangle(span, False)
    eye = jnp.where(row == col, 1.0, 0.0).astype(F32)
    dalpha = nn(upper, dlog_c, HIGHEST) - nt(upper, dstep_r * step_r, HIGHEST)[:, :heads]
    dstep = dstep_c + nt(eye, dstep_r, HIGHEST)[:, :heads]
    rate = jnp.exp(hrow_ref[0:1])
    draw = (dstep - rate * dalpha) * sigmoid(raw_ref[...])
    draw_low = draw.astype(BF16)
    dstep_ref[...] = draw_low
    hid = hid_ref[...]
    dtg_ref[...] += tn(draw_low, hid)
    rate_sum = jnp.sum(-dalpha * step_c * rate, axis=0, keepdims=True)
    bias_sum = jnp.sum(draw, axis=0, keepdims=True)
    at = lax.broadcasted_iota(jnp.int32, (8, heads), 0)
    headg_ref[...] += jnp.where(at == 0, rate_sum, jnp.where(at == 1, bias_sum, 0.0))

    ext_ref[0:span] = dx_ref[...] * silu_grad(convsum_ref[...])
    back = jnp.zeros((span, width), F32)
    conv_in = convin_ref[...].astype(F32)
    at = lax.broadcasted_iota(jnp.int32, (8, width), 0)
    sums = jnp.where(at == CONV, jnp.sum(ext_ref[0:span], axis=0, keepdims=True), 0.0)
    for tap in range(CONV):
        ahead = CONV - 1 - tap
        same = seg_ref[8 + ahead : 8 + ahead + span] == seg_here
        term = jnp.where(same, ext_ref[ahead : ahead + span], 0.0)
        back = back + conv_ref[tap : tap + 1] * term
        sums = sums + jnp.where(at == tap, jnp.sum(conv_in * term, axis=0, keepdims=True), 0.0)
    convg_ref[...] += sums
    ext_ref[span : span + 8] = ext_ref[0:8]
    dval = back.astype(BF16)
    dval_ref[...] = dval
    inacc_ref[...] += tn(hid, dval)

    @pl.when(step == pl.num_programs(0) - 1)
    def _():
        rows = inacc_ref.shape[0] // (2 * keep_ref.shape[0])
        part_of(lambda at: inacc_ref[at * rows : (at + 1) * rows], here_ref[0], keep_ref, send_ref)


def hidden_back_kernel(
    perm_ref,
    dgate_ref,
    dval_ref,
    dstep_ref,
    wg_ref,
    wv_ref,
    wdt_ref,
    hid_ref,
    gain_ref,
    out_ref,
    gsum_ref,
):
    @pl.when(pl.program_id(0) == 0)
    def _():
        gsum_ref[...] = jnp.zeros_like(gsum_ref)

    total = nt(dgate_ref[...], wg_ref[...]) + nt(dval_ref[...], wv_ref[...])
    total = total + nn(dstep_ref[...], wdt_ref[...])
    out_ref[0] = total.astype(BF16)
    unit = hid_ref[...].astype(F32) / gain_ref[...]
    gsum_ref[...] += jnp.sum(total * unit, axis=0, keepdims=True) + jnp.zeros(gsum_ref.shape, F32)


def maps_back_kernel(
    here_ref,
    dbc_ref,
    convsum_ref,
    convin_ref,
    conv_ref,
    segc_ref,
    hid_ref,
    w1_ref,
    gain_ref,
    convg_ref,
    sums_ref,
    headg_ref,
    dtg_ref,
    gall_ref,
    keep_ref,
    send_ref,
    own_ref,
    ext_ref,
    acc_ref,
    dmap_ref,
    small_ref,
):
    size, width = dmap_ref.shape
    ext_ref[0:size] = dbc_ref[...] * silu_grad(convsum_ref[...])
    ext_ref[size : size + 8] = jnp.zeros((8, width), F32)
    back = jnp.zeros((size, width), F32)
    conv_in = convin_ref[...].astype(F32)
    at = lax.broadcasted_iota(jnp.int32, (8, width), 0)
    sums = jnp.where(at == CONV, jnp.sum(ext_ref[0:size], axis=0, keepdims=True), 0.0)
    seg_here = segc_ref[8 : 8 + size]
    for tap in range(CONV):
        ahead = CONV - 1 - tap
        same = segc_ref[8 + ahead : 8 + ahead + size] == seg_here
        term = jnp.where(same, ext_ref[ahead : ahead + size], 0.0)
        back = back + conv_ref[tap : tap + 1] * term
        sums = sums + jnp.where(at == tap, jnp.sum(conv_in * term, axis=0, keepdims=True), 0.0)
    dmap_ref[...] = back.astype(BF16)
    ctx = here_ref[2]
    acc_ref[...] = tn(hid_ref[...], dmap_ref[...])
    span = own_ref.shape[0]
    own = pl.ds(pl.multiple_of(ctx * span, 16), span)
    grad = nt(dmap_ref[own, :], w1_ref[:, w1_ref.shape[1] - width :])
    own_ref[...] = grad
    unit = hid_ref[own, :].astype(F32) / gain_ref[...]
    gain_sum = gall_ref[0:1] + jnp.sum(grad * unit, axis=0, keepdims=True)
    half = small_ref.shape[1]
    heads = headg_ref.shape[1]
    small_ref[...] = jnp.zeros_like(small_ref)
    small_ref[0 : CONV + 1] = convg_ref[0 : CONV + 1]
    small_ref[CONV + 1 : CONV + 3] = sums_ref[0:2]
    small_ref[7:8, 0:heads] = headg_ref[0:1]
    small_ref[7:8, 128 : 128 + heads] = headg_ref[1:2]
    small_ref[8 : 8 + CONV + 1, 0:width] = sums[0 : CONV + 1]
    small_ref[13:14] = gain_sum[:, :half]
    small_ref[14:15] = gain_sum[:, half:]
    small_ref[15:16] = small_ref[7:8] - small_ref[7:8].astype(BF16).astype(F32)
    small_ref[16:24] = dtg_ref[:, :half]
    small_ref[24:32] = dtg_ref[:, half:]
    small = small_ref[...].astype(BF16)
    count = keep_ref.shape[0] // 32 - 1
    block = acc_ref.shape[0] // (2 * count)
    some = block // 4
    keep_ref[0:32] = small
    send_ref[0:32] = small
    for at in range(count):
        start = pl.multiple_of(2 * at * block + ctx * some, 8)
        low = acc_ref[pl.ds(start, some), :].astype(BF16)
        start = pl.multiple_of((2 * at + 1) * block + ctx * some, 8)
        high = acc_ref[pl.ds(start, some), :].astype(BF16)
        keep_ref[32 + 32 * at : 64 + 32 * at, 0:width] = jnp.where(here_ref[0] == 0, low, high)
        send_ref[32 + 32 * at : 64 + 32 * at, 0:width] = jnp.where(here_ref[0] == 0, high, low)


def input_back_kernel(hg_ref, own_ref, tok_ref, gain_ref, cot_ref, out_ref):
    grad = hg_ref[...] + own_ref[...]
    tok = tok_ref[...]
    scale = lax.rsqrt(jnp.mean(tok * tok, axis=-1, keepdims=True) + NORM_EPS)
    unit = tok * scale
    scaled = grad * gain_ref[...]
    mean = jnp.mean(scaled * unit, axis=-1, keepdims=True)
    out_ref[...] = cot_ref[...] + scale * (scaled - unit * mean)


def pair_sum_kernel(here_ref, keep_ref, came_ref, out_refs):
    for at, out_ref in enumerate(out_refs):
        index = pl.ds(here_ref[1] ^ at, 1)
        out_ref[...] = (keep_ref[index].astype(F32) + came_ref[index].astype(F32))[0].astype(BF16)


def pair_sum_late_kernel(here_ref, keep_ref, came_ref, mkeep_ref, mcame_ref, out_refs):
    rows, width = keep_ref.shape[1:]
    small = (mkeep_ref[0:32].astype(F32) + mcame_ref[0:32].astype(F32))
    row = lax.broadcasted_iota(jnp.int32, small.shape, 0)
    head = small[7:8] + small[15:16]
    rest = head - head.astype(BF16).astype(F32)
    small = jnp.where(row == 7, head, jnp.where(row == 15, rest, small)).astype(BF16)
    for at, out_ref in enumerate(out_refs):
        block = here_ref[1] ^ at
        index = pl.ds(block, 1)
        out_ref[0:rows] = (keep_ref[index].astype(F32) + came_ref[index].astype(F32))[0].astype(BF16)
        out_ref[rows : rows + 32] = small
        index = pl.ds(pl.multiple_of(32 + 32 * block, 32), 32)
        out_ref[rows + 32 : rows + 64] = (
            mkeep_ref[index].astype(F32) + mcame_ref[index].astype(F32)
        ).astype(BF16)


def sum_kernel(late, part_refs, out_ref):
    terms = [ref[...].astype(F32) for ref in part_refs]
    while len(terms) > 1:
        terms = [terms[at] + terms[at + 1] for at in range(0, len(terms), 2)]
    total = terms[0]
    if late:
        first = out_ref.shape[0] - 64
        row = lax.broadcasted_iota(jnp.int32, total.shape, 0)
        head = total[first + 7 : first + 8] + total[first + 15 : first + 16]
        rest = head - head.astype(BF16).astype(F32)
        total = jnp.where(row == first + 7, head, jnp.where(row == first + 15, rest, total))
    out_ref[...] = total.astype(out_ref.dtype)


def adam_kernel(
    here_ref,
    win_ref,
    wfirst_ref,
    wsecond_ref,
    oin_ref,
    ofirst_ref,
    osecond_ref,
    early_refs,
    late_refs,
    win_new,
    wfirst_new,
    wsecond_new,
    out_new,
    ofirst_new,
    osecond_new,
    early_ref,
    late_ref,
):
    step = pl.program_id(0)
    pieces = len(early_refs)
    rows = win_ref.shape[0]
    width = early_ref.shape[2]
    block = pieces * HEAD_DIM

    @pl.when(step == 0)
    def _():
        for at in range(pieces):
            owner = pl.ds(here_ref[2] ^ at, 1)
            early_ref[owner] = early_refs[at][...][None]
            late_ref[owner] = late_refs[at][...][None]

    here = pl.ds(pl.multiple_of(step * rows, rows), rows)
    low = lax.broadcasted_iota(jnp.int32, (rows, 2 * HEAD_DIM), 1) < HEAD_DIM

    def update(lanes, grad):
        news = adam_step(
            win_ref[:, lanes], wfirst_ref[:, lanes], wsecond_ref[:, lanes], grad, 0.03, WEIGHT_DECAY
        )
        win_new[:, lanes], wfirst_new[:, lanes], wsecond_new[:, lanes] = news

    for base, ref in ((0, early_ref), (INNER, late_ref)):
        for pair in range(width // (2 * HEAD_DIM)):
            lanes = slice(pair * 2 * HEAD_DIM, (pair + 1) * 2 * HEAD_DIM)
            for at in range(0, pieces, 2):
                first = ref[at, here, lanes].astype(F32)
                second = ref[at + 1, here, lanes].astype(F32)
                start = base + 2 * pair * block + at * HEAD_DIM
                even = jnp.where(low, first, pltpu.roll(second, HEAD_DIM, 1))
                update(slice(start, start + 2 * HEAD_DIM), even)
                start = start + block
                odd = jnp.where(low, pltpu.roll(first, HEAD_DIM, 1), second)
                update(slice(start, start + 2 * HEAD_DIM), odd)
    first = late_ref.shape[1] - 32
    update(slice(2 * INNER, 2 * INNER + 2 * STATE), late_ref[step, first : first + 32, 0 : 2 * STATE].astype(F32))
    first = rows * pieces
    for at in range(2):
        lanes = slice(at * width, (at + 1) * width)
        grad = early_ref[step, first + at * HEAD_DIM : first + (at + 1) * HEAD_DIM].astype(F32)
        news = adam_step(
            oin_ref[:, lanes], ofirst_ref[:, lanes], osecond_ref[:, lanes], grad, 0.02, WEIGHT_DECAY
        )
        out_new[:, lanes], ofirst_new[:, lanes], osecond_new[:, lanes] = news


def swap(value, axis, bit):
    count = lax.axis_size(axis)
    return lax.ppermute(value, axis, [(at, at ^ bit) for at in range(count)])


def gather_ctx(value):
    far = swap(value, "ctx", 2)
    return [value, swap(value, "ctx", 1), far, swap(far, "ctx", 1)]


def scatter_ctx(value):
    near = value[0:2].astype(F32) + swap(value[2:4], "ctx", 1).astype(F32)
    return near[0] + swap(near[1].astype(BF16), "ctx", 2).astype(F32)


def sum_ctx(value):
    pair = value.astype(F32) + swap(value, "ctx", 1).astype(F32)
    pair = pair.astype(BF16)
    return pair.astype(F32) + swap(pair, "ctx", 2).astype(F32)


def gather_dp(value):
    count, here = lax.axis_size("dp"), lax.axis_index("dp")
    if count != 8:
        return [lax.all_gather(value, "dp", axis=0)], jnp.zeros((1,), jnp.int32)
    value = value[None]
    pieces = [(value, 0)] + [(swap(value, "dp", bit), bit) for bit in range(2, count, 2)]
    pieces += [(swap(piece, "dp", 1), bit + 1) for piece, bit in pieces]
    return [piece for piece, _ in pieces], here ^ jnp.asarray([bit for _, bit in pieces], jnp.int32)


def spread_dp(parts):
    return [parts[0]] + [swap(part, "dp", 2 * at) for at, part in enumerate(parts) if at]


def fan_ctx(value):
    return [value] + [swap(value, "ctx", bit) for bit in range(1, lax.axis_size("ctx"))]


def adam_step(weight, moment_one, second, gradient, step_rate, decay_rate):
    moment_new = BETA_ONE * moment_one + (1.0 - BETA_ONE) * gradient
    second_new = BETA_TWO * second + (1.0 - BETA_TWO) * gradient * gradient
    first_hat = moment_new / (1.0 - BETA_ONE**STEP)
    second_hat = second_new / (1.0 - BETA_TWO**STEP)
    weight_new = weight - step_rate * (
        first_hat / (jnp.sqrt(second_hat) + ADAM_EPS) + decay_rate * weight
    )
    return (weight_new, moment_new, second_new)


def full(shape):
    return pl.BlockSpec(shape, lambda *_: (0,) * len(shape))


def shape_of(*shape, dtype=F32):
    return jax.ShapeDtypeStruct(shape, dtype)


def shards(
    tokens,
    segment_ids,
    cotangent,
    in_weight,
    dt_weight,
    out_weight,
    conv_params,
    gains,
    head_params,
    in_first,
    in_second,
    dt_first,
    dt_second,
    out_first,
    out_second,
    conv_first,
    conv_second,
    gain_first,
    gain_second,
    head_first,
    head_second,
):
    _, span, model = tokens.shape
    length = segment_ids.shape[1]
    ndp, nctx = lax.axis_size("dp"), lax.axis_size("ctx")
    d, c = lax.axis_index("dp"), lax.axis_index("ctx")
    heads = HEADS // nctx
    width = INNER // nctx
    maps = 2 * STATE
    wide = width + maps
    chunks = nctx
    rows_in = in_weight.shape[0]
    conv_cols = conv_params.shape[1]
    gain_len = gains.shape[0]
    dt_cols = dt_weight.shape[1]
    near = ndp == heads
    high = heads // 2
    block_in = model // heads
    tok = tokens[0]
    bits = jnp.stack([d & 1, d >> 1, c] if near else [0 * d, 0 * d, c]).astype(jnp.int32)
    order = jnp.asarray([0, 2, 1, 3], jnp.int32)
    perm = order[jnp.arange(nctx, dtype=jnp.int32) ^ c]
    smem = pl.BlockSpec(memory_space=pltpu.SMEM)
    vmem = pl.BlockSpec(memory_space=pltpu.VMEM)
    anywhere = lambda pieces: [pl.BlockSpec(memory_space=pl.ANY)] * len(pieces)

    w1, g2, cot_low = pl.pallas_call(
        pack_kernel,
        in_specs=[smem] + [vmem] * 6,
        out_shape=[
            shape_of(rows_in + 16, wide, dtype=BF16),
            shape_of(rows_in + (2 * HEAD_DIM if near else 0), width, dtype=BF16),
            shape_of(span, model, dtype=BF16),
        ],
        scratch_shapes=[pltpu.VMEM((16, wide), F32)],
        compiler_params=params(),
        name="pack",
    )(bits, in_weight, out_weight, dt_weight, conv_params, gains[None], cotangent[0])
    toks = gather_ctx(tok)
    w1, at_rows = gather_dp(w1)
    if near:
        g2, at_g2 = gather_dp(g2)
    else:
        wg = lax.all_gather(g2, "dp", axis=0, tiled=True).reshape(heads, block_in, width)
        wout = lax.all_gather(out_weight.astype(BF16), "dp", axis=0, tiled=True)
        wout = lax.dynamic_index_in_dim(wout.reshape(heads, nctx, HEAD_DIM, model), c, 1, False)
        g2 = [jnp.concatenate([wg, wout[:, :, :width], wout[:, :, width:]], axis=1)]
        at_g2 = at_rows
    cots = gather_ctx(cot_low)

    ids = segment_ids[0]
    seg_col = jnp.pad(ids, (8, 8), constant_values=-1)[:, None]
    seg_row = segment_ids
    head_mine = lax.dynamic_index_in_dim(head_params.reshape(3, heads, nctx), c, 2, False)
    head_col = head_mine.T

    rows = lambda cols: pl.BlockSpec((span, cols), lambda i, *_: (i, 0))
    row_of = pl.BlockSpec((heads, span), lambda i, *_: (0, i))
    slot_rows = pl.BlockSpec((1, span, model), lambda i, p, *_: (p[i], 0, 0))
    shards_in = sum(piece.shape[0] for piece in w1)

    (
        hid, conv_mine, gain_pre, gain_mine, dt_mine, w1, mixed, conv_in, conv_sum, inner, raw,
        step_c, log_c, step_r, log_r, starts,
    ) = pl.pallas_call(
        scan_forward_kernel,
        grid_spec=pltpu.PrefetchScalarGridSpec(
            num_scalar_prefetch=2,
            grid=(chunks,),
            in_specs=[
                anywhere(toks),
                anywhere(w1),
                full((3, heads)),
                full((heads, 3)),
                full((length + 16, 1)),
                pl.BlockSpec((1, span), lambda i, *_: (0, i)),
            ],
            out_specs=[
                rows(model),
                full((8, wide)),
                full((1, model)),
                full((1, width)),
                full((heads, model)),
                full((model, wide)),
                rows(wide),
                rows(wide),
                rows(wide),
                rows(width),
                rows(heads),
                rows(heads),
                rows(heads),
                row_of,
                row_of,
                pl.BlockSpec((1, STATE, width), lambda i, *_: (i, 0, 0)),
            ],
            scratch_shapes=[
                pltpu.VMEM((span + 8, wide), F32),
                pltpu.VMEM((span + 8, 1), jnp.int32),
                pltpu.VMEM((STATE, width), F32),
                pltpu.VMEM((shards_in, 16, wide), BF16),
                pltpu.VMEM((nctx, span, model), F32),
                pltpu.VMEM((8, INNER + maps), F32),
                pltpu.VMEM((1, model + INNER), F32),
                pltpu.SemaphoreType.DMA((copies_of(w1, 2),)),
                pltpu.SemaphoreType.DMA((nctx,)),
            ],
        ),
        out_shape=[
            shape_of(length, model, dtype=BF16),
            shape_of(8, wide),
            shape_of(1, model),
            shape_of(1, width),
            shape_of(heads, model, dtype=BF16),
            shape_of(model, wide, dtype=BF16),
            shape_of(length, wide, dtype=BF16),
            shape_of(length, wide, dtype=BF16),
            shape_of(length, wide),
            shape_of(length, width),
            shape_of(length, heads),
            shape_of(length, heads),
            shape_of(length, heads),
            shape_of(heads, length),
            shape_of(heads, length),
            shape_of(chunks, STATE, width),
        ],
        compiler_params=params("arbitrary"),
        name="scan_forward",
    )(bits, at_rows, toks, w1, head_mine, head_col, seg_col, seg_row)

    wg, wout, cot_all, gate, normed_grad, stats = pl.pallas_call(
        gate_kernel,
        grid_spec=pltpu.PrefetchScalarGridSpec(
            num_scalar_prefetch=2,
            grid=(chunks,),
            in_specs=[rows(model), anywhere(g2), anywhere(cots), rows(width), full((1, width))],
            out_specs=[
                full((model, width)),
                full((width, model)),
                full((nctx, span, model)),
                rows(width),
                rows(width),
                pl.BlockSpec((8, span), lambda i, *_: (0, i)),
            ],
            scratch_shapes=[
                pltpu.SemaphoreType.DMA((copies_of(g2, 3),)),
                pltpu.SemaphoreType.DMA((nctx,)),
            ],
        ),
        out_shape=[
            shape_of(model, width, dtype=BF16),
            shape_of(width, model, dtype=BF16),
            shape_of(nctx, span, model, dtype=BF16),
            shape_of(length, width, dtype=BF16),
            shape_of(length, width),
            shape_of(8, length),
        ],
        compiler_params=params("arbitrary"),
        name="gate",
    )(bits, at_g2, hid, g2, cots, inner, gain_mine)
    stats = sum(fan_ctx(stats))

    early_rows = block_in + 2 * HEAD_DIM
    block_part, early_keep, early_send, dy, dgate, col_sums = pl.pallas_call(
        norm_back_kernel,
        grid_spec=pltpu.PrefetchScalarGridSpec(
            num_scalar_prefetch=2,
            grid=(chunks,),
            in_specs=[
                rows(model),
                rows(width),
                rows(width),
                rows(width),
                pl.BlockSpec((8, span), lambda i, *_: (0, i)),
                full((1, width)),
                rows(width),
                full((width, model)),
                full((nctx, span, model)),
            ],
            out_specs=[
                slot_rows,
                full((high, early_rows, width)),
                full((high, early_rows, width)),
                rows(width),
                rows(width),
                full((8, width)),
            ],
            scratch_shapes=[pltpu.VMEM((width, model), F32), pltpu.VMEM((model, width), F32)],
        ),
        out_shape=[
            shape_of(nctx, span, model, dtype=BF16),
            shape_of(high, early_rows, width, dtype=BF16),
            shape_of(high, early_rows, width, dtype=BF16),
            shape_of(length, width),
            shape_of(length, width, dtype=BF16),
            shape_of(8, width),
        ],
        compiler_params=params("arbitrary"),
        name="norm_back",
    )(perm, bits, hid, inner, gate, normed_grad, stats, gain_mine, mixed, wout, cot_all)
    block_output = tok + scatter_ctx(block_part)
    if near:
        early_came = swap(early_send, "dp", 1)

    back = lambda cols: pl.BlockSpec((span, cols), lambda i, *_: (chunks - 1 - i, 0))
    back_row = pl.BlockSpec((heads, span), lambda i, *_: (0, chunks - 1 - i))
    late_keep, late_send, dval, dbc, dstep, conv_grad, dt_grad, head_grad = pl.pallas_call(
        scan_back_kernel,
        grid_spec=pltpu.PrefetchScalarGridSpec(
            num_scalar_prefetch=2,
            grid=(chunks,),
            in_specs=[
                back(model),
                back(width),
                back(wide),
                back(width),
                back(width),
                back(heads),
                back(heads),
                back(heads),
                back_row,
                back_row,
                pl.BlockSpec((1, STATE, width), lambda i, *_: (chunks - 1 - i, 0, 0)),
                full((8, width)),
                full((3, heads)),
                full((length + 16, 1)),
                pl.BlockSpec((1, span), lambda i, *_: (0, chunks - 1 - i)),
            ],
            out_specs=[
                full((high, block_in, width)),
                full((high, block_in, width)),
                back(width),
                back(maps),
                back(heads),
                full((8, width)),
                full((heads, model)),
                full((8, heads)),
            ],
            scratch_shapes=[
                pltpu.VMEM((span + 8, width), F32),
                pltpu.VMEM((span + 16, 1), jnp.int32),
                pltpu.VMEM((STATE, width), F32),
                pltpu.VMEM((model, width), F32),
                pltpu.VMEM((span, width), F32),
            ],
        ),
        out_shape=[
            shape_of(high, block_in, width, dtype=BF16),
            shape_of(high, block_in, width, dtype=BF16),
            shape_of(length, width, dtype=BF16),
            shape_of(length, maps, dtype=BF16),
            shape_of(length, heads, dtype=BF16),
            shape_of(8, width),
            shape_of(heads, model),
            shape_of(8, heads),
        ],
        compiler_params=params("arbitrary"),
        name="scan_back",
    )(
        perm, bits, hid, dy, mixed, conv_in, conv_sum, raw, step_c, log_c, step_r, log_r, starts,
        conv_mine, head_mine, seg_col, seg_row,
    )
    dbc_total = sum_ctx(dbc)
    if near:
        late_came = swap(late_send, "dp", 1)
        early_parts = pl.pallas_call(
            pair_sum_kernel,
            in_specs=[smem, vmem, vmem],
            out_shape=[[shape_of(early_rows, width, dtype=BF16)] * high],
            compiler_params=params(),
            name="pair_sum_early",
        )(bits, early_keep, early_came)[0]
        early_parts = spread_dp(early_parts)

    hidden_part, gain_sum = pl.pallas_call(
        hidden_back_kernel,
        grid_spec=pltpu.PrefetchScalarGridSpec(
            num_scalar_prefetch=1,
            grid=(chunks,),
            in_specs=[
                rows(width),
                rows(width),
                rows(heads),
                full((model, width)),
                full((model, width)),
                full((heads, model)),
                rows(model),
                full((1, model)),
            ],
            out_specs=[slot_rows, full((8, model))],
        ),
        out_shape=[shape_of(nctx, span, model, dtype=BF16), shape_of(8, model)],
        compiler_params=params("arbitrary"),
        name="hidden_back",
    )(perm, dgate, dval, dstep, wg, w1, dt_mine, hid, gain_pre)
    hidden_grad = scatter_ctx(hidden_part)

    map_rows = 32 + 32 * high
    map_keep, map_send, hidden_own = pl.pallas_call(
        maps_back_kernel,
        in_specs=[smem] + [vmem] * 13,
        out_shape=[
            shape_of(map_rows, width, dtype=BF16),
            shape_of(map_rows, width, dtype=BF16),
            shape_of(span, model),
        ],
        scratch_shapes=[
            pltpu.VMEM((length + 8, maps), F32),
            pltpu.VMEM((model, maps), F32),
            pltpu.VMEM((length, maps), BF16),
            pltpu.VMEM((32, width), F32),
        ],
        compiler_params=params(),
        name="maps_back",
    )(
        bits,
        dbc_total,
        conv_sum[:, width:],
        conv_in[:, width:],
        conv_mine[:, width:],
        seg_col,
        hid,
        w1,
        gain_pre,
        conv_grad,
        col_sums,
        head_grad,
        dt_grad,
        gain_sum,
    )

    input_grad = pl.pallas_call(
        input_back_kernel,
        out_shape=shape_of(span, model),
        compiler_params=params(),
        name="input_back",
    )(hidden_grad, hidden_own, tok, gain_pre, cotangent[0])

    late_rows = block_in + 64
    if near:
        map_came = swap(map_send, "dp", 1)
        late_parts = pl.pallas_call(
            pair_sum_late_kernel,
            in_specs=[smem] + [vmem] * 4,
            out_shape=[[shape_of(late_rows, width, dtype=BF16)] * high],
            compiler_params=params(),
            name="pair_sum_late",
        )(bits, late_keep, late_came, map_keep, map_came)[0]
        late_parts = spread_dp(late_parts)
        early, late = [
            pl.pallas_call(
                functools.partial(sum_kernel, name == "late"),
                in_specs=[[vmem] * high],
                out_shape=shape_of(*parts[0].shape, dtype=BF16),
                compiler_params=params(),
                name="sum_" + name,
            )(parts)
            for name, parts in (("early", early_parts), ("late", late_parts))
        ]
        early, late = fan_ctx(early), fan_ctx(late)
        row_block = lambda ref_rows, cols: pl.BlockSpec((ref_rows, cols), lambda i, *_: (i, 0))
        in_block = row_block(rows_in // nctx, in_weight.shape[1])
        out_block = row_block(out_weight.shape[0] // nctx, model)
        news = pl.pallas_call(
            adam_kernel,
            grid_spec=pltpu.PrefetchScalarGridSpec(
                num_scalar_prefetch=1,
                grid=(nctx,),
                in_specs=[in_block] * 3
                + [out_block] * 3
                + [[full((early_rows, width))] * nctx, [full((late_rows, width))] * nctx],
                out_specs=[in_block] * 3 + [out_block] * 3,
                scratch_shapes=[
                    pltpu.VMEM((nctx, early_rows, width), BF16),
                    pltpu.VMEM((nctx, late_rows, width), BF16),
                ],
            ),
            out_shape=[shape_of(*in_weight.shape)] * 3 + [shape_of(*out_weight.shape)] * 3,
            compiler_params=params("arbitrary"),
            name="adam",
        )(bits, in_weight, in_first, in_second, out_weight, out_first, out_second, early, late)
        in_new, out_new = tuple(news[:3]), tuple(news[3:])
        small = jnp.stack([part[block_in : block_in + 32] for part in late])[c ^ jnp.arange(nctx)]
        small = small.astype(F32)
    else:
        blocks = lambda keep, send: jnp.stack([keep, send], axis=1).reshape((heads,) + keep.shape[1:])
        early = blocks(early_keep, early_send).astype(F32)
        late = blocks(late_keep, late_send).astype(F32)
        part = lambda value: value[32:].reshape(high, 32, width)[:, :, :maps]
        map_blocks = blocks(part(map_keep), part(map_send)).astype(F32)

        def total(value):
            return lax.psum_scatter(value, "dp", scatter_dimension=0, tiled=True)

        def spaced(value):
            place_at = (jnp.arange(nctx) == c).astype(F32).reshape((1, nctx, 1, 1))
            value = value[:, None] * place_at
            return lax.psum(total(value.reshape(-1, value.shape[-1])), "ctx")

        def by_head(value):
            value = lax.all_gather(total(value.reshape(model, width)), "ctx", axis=0)
            value = value.reshape(nctx, rows_in, heads, HEAD_DIM)
            return jnp.transpose(value, (1, 2, 0, 3)).reshape(rows_in, INNER)

        in_total = jnp.concatenate(
            [by_head(early[:, :block_in]), by_head(late), spaced(map_blocks)], axis=1
        )
        out_total = spaced(
            jnp.concatenate([early[:, block_in : block_in + HEAD_DIM], early[:, block_in + HEAD_DIM :]], axis=2)
        )
        in_new = adam_step(in_weight, in_first, in_second, in_total, 0.03, WEIGHT_DECAY)
        out_new = adam_step(out_weight, out_first, out_second, out_total, 0.02, WEIGHT_DECAY)
        small = lax.all_gather(lax.psum(map_keep[:32].astype(F32), "dp"), "ctx", axis=0)

    def in_order(value):
        return jnp.swapaxes(value.reshape(nctx, -1, heads, HEAD_DIM), 0, 1).swapaxes(1, 2).reshape(-1, INNER)

    columns = in_order(small[:, : CONV + 2])
    conv_total = jnp.concatenate([columns[: CONV + 1], small[0, 8 : 8 + CONV + 1, :maps]], axis=1)
    conv_total = lax.dynamic_slice_in_dim(conv_total, d * conv_cols, conv_cols, 1)
    dt_total = small[:, 16:32].reshape(nctx, 2, heads, width)
    dt_total = jnp.transpose(dt_total, (2, 0, 1, 3)).reshape(HEADS, model)
    dt_total = lax.dynamic_slice_in_dim(dt_total, d * dt_cols, dt_cols, 1)
    pre_total = jnp.sum(small[:, 13:15], axis=0).reshape(-1)
    gain_total = jnp.concatenate([pre_total, columns[CONV + 1]])
    gain_total = lax.dynamic_slice_in_dim(gain_total, d * gain_len, gain_len, 0)
    head_row = small[:, 7] + small[:, 15]
    head_total = jnp.stack(
        [
            head_row[:, :heads].T.reshape(-1),
            head_row[:, 128 : 128 + heads].T.reshape(-1),
            jnp.sum(small[:, CONV + 2].reshape(nctx, heads, HEAD_DIM), axis=2).T.reshape(-1),
        ]
    )

    dt_new = adam_step(dt_weight, dt_first, dt_second, dt_total, 0.03, WEIGHT_DECAY)
    conv_new = adam_step(conv_params, conv_first, conv_second, conv_total, 0.3, 0.0)
    gain_new = adam_step(gains, gain_first, gain_second, gain_total, 0.5, 0.0)
    head_new = adam_step(head_params, head_first, head_second, head_total, 2.0, 0.0)
    return (block_output[None], input_grad[None]) + in_new + dt_new + out_new + conv_new + gain_new + head_new


def solution(mesh):
    tokens, rows, cols = P("dp", "ctx", None), P("dp", None), P(None, "dp")
    return jax.shard_map(
        shards,
        mesh=mesh,
        in_specs=(tokens, rows, tokens, rows, cols, rows, cols, P("dp"), P())
        + (rows, rows, cols, cols, rows, rows, cols, cols, P("dp"), P("dp"), P(), P()),
        out_specs=(tokens, tokens)
        + (rows,) * 3
        + (cols,) * 3
        + (rows,) * 3
        + (cols,) * 3
        + (P("dp"),) * 3
        + (P(),) * 3,
        check_vma=False,
    )
```

```python
import functools

import jax
import jax.numpy as jnp
from jax import lax
from jax.experimental import pallas as pl
from jax.experimental.pallas import tpu as pltpu
from jax.sharding import PartitionSpec as P

INNER = 2048
HEADS = 32
HEAD_DIM = 64
STATE = 128
CONV = 4
STEP = 10

F32 = jnp.float32
BF16 = jnp.bfloat16
HIGHEST = lax.Precision.HIGHEST
NORM_EPS = 1e-05
BETA_ONE = 0.9
BETA_TWO = 0.95
ADAM_EPS = 1e-08
WEIGHT_DECAY = 0.1
VMEM_LIMIT = 56 * 1024 * 1024


def nn(a, b, precision=None):
    return lax.dot_general(
        a, b, (((1,), (0,)), ((), ())), precision=precision, preferred_element_type=F32
    )


def nt(a, b, precision=None):
    return lax.dot_general(
        a, b, (((1,), (1,)), ((), ())), precision=precision, preferred_element_type=F32
    )


def tn(a, b, precision=None):
    return lax.dot_general(
        a, b, (((0,), (0,)), ((), ())), precision=precision, preferred_element_type=F32
    )


def halves(value):
    high = value.astype(BF16)
    return high, (value - high.astype(F32)).astype(BF16)


def spread(value, width):
    heads = value.shape[1]
    row = lax.broadcasted_iota(jnp.int32, (heads, width), 0)
    col = lax.broadcasted_iota(jnp.int32, (heads, width), 1)
    table = jnp.where(col // HEAD_DIM == row, 1.0, 0.0).astype(BF16)
    high, low = halves(value)
    return nn(high, table) + nn(low, table)


def gather_heads(value, heads):
    width = value.shape[1]
    row = lax.broadcasted_iota(jnp.int32, (width, heads), 0)
    col = lax.broadcasted_iota(jnp.int32, (width, heads), 1)
    table = jnp.where(row // HEAD_DIM == col, 1.0, 0.0).astype(BF16)
    high, low = halves(value)
    return nn(high, table) + nn(low, table)


def softplus(value):
    return jnp.maximum(value, 0.0) + jnp.log1p(jnp.exp(-jnp.abs(value)))


def sigmoid(value):
    return 1.0 / (1.0 + jnp.exp(-value))


def silu_grad(value):
    sig = sigmoid(value)
    return sig * (1.0 + value * (1.0 - sig))


def diagonal(size):
    row = lax.broadcasted_iota(jnp.int32, (size, size), 0)
    return row == lax.broadcasted_iota(jnp.int32, (size, size), 1)


def triangle(size, lower):
    row = lax.broadcasted_iota(jnp.int32, (size, size), 0)
    col = lax.broadcasted_iota(jnp.int32, (size, size), 1)
    keep = row >= col if lower else row <= col
    return jnp.where(keep, 1.0, 0.0).astype(F32)


def cost(micros):
    return pl.CostEstimate(
        flops=int(micros * 1.1e9), bytes_accessed=int(micros * 3.6e6), transcendentals=0
    )


def params(*semantics):
    return pltpu.CompilerParams(
        dimension_semantics=semantics or None, vmem_limit_bytes=VMEM_LIMIT
    )


def place(pieces, at_ref, sems, targets):
    copies = []
    for index, piece in enumerate(pieces):
        for block in range(piece.shape[0]):
            for first, rows, target in targets:
                copies.append(
                    pltpu.make_async_copy(
                        piece.at[block, first : first + rows],
                        target(at_ref[index] + block),
                        sems.at[len(copies)],
                    )
                )
    for copy in copies:
        copy.start()
    return copies


def copies_of(pieces, targets):
    return sum(piece.shape[0] for piece in pieces) * targets


def rows_of(ref, rows):
    return lambda at: ref.at[pl.ds(pl.multiple_of(at * rows, 16), rows)]


def part_of(block, own_bit, keep_ref, send_ref, first=0):
    for at in range(keep_ref.shape[0]):
        low, high = block(2 * at).astype(BF16), block(2 * at + 1).astype(BF16)
        rows = slice(first, first + low.shape[0])
        keep_ref[at, rows] = jnp.where(own_bit == 0, low, high)
        send_ref[at, rows] = jnp.where(own_bit == 0, high, low)


def pick_heads(ref, base, ctx, heads):
    first = pl.multiple_of(base + (ctx >> 1) * 2 * HEAD_DIM, 2 * HEAD_DIM)
    wide = ref[:, pl.ds(first, 2 * HEAD_DIM)]
    low = lax.broadcasted_iota(jnp.int32, wide.shape, 1) < HEAD_DIM
    odd = (ctx & 1) == 1
    out = []
    for pair in range(heads // 2):
        parts = []
        for head in (2 * pair, 2 * pair + 1):
            first = pl.multiple_of(base + head * 4 * HEAD_DIM + (ctx >> 1) * 2 * HEAD_DIM, 2 * HEAD_DIM)
            parts.append(ref[:, pl.ds(first, 2 * HEAD_DIM)])
        even = jnp.where(low, parts[0], pltpu.roll(parts[1], HEAD_DIM, 1))
        other = jnp.where(low, pltpu.roll(parts[0], HEAD_DIM, 1), parts[1])
        out.append(jnp.where(odd, other, even))
    return out


def pack_kernel(here_ref, win_ref, wout_ref, dt_ref, conv_ref, gain_ref, w1_ref, g2_ref, tmp_ref):
    ctx = here_ref[2]
    rows = win_ref.shape[0]
    heads = HEADS // 4
    width = heads * HEAD_DIM
    for at, part in enumerate(pick_heads(win_ref, INNER, ctx, heads)):
        w1_ref[0:rows, at * 128 : (at + 1) * 128] = part.astype(BF16)
    w1_ref[0:rows, width:] = win_ref[:, 2 * INNER :].astype(BF16)
    tmp_ref[...] = jnp.zeros_like(tmp_ref)
    row = lax.broadcasted_iota(jnp.int32, (heads, HEADS), 0)
    col = lax.broadcasted_iota(jnp.int32, (heads, HEADS), 1)
    table = jnp.where(col == 4 * row + ctx, 1.0, 0.0).astype(BF16)
    tmp_ref[0:heads, 384 : 384 + dt_ref.shape[1]] = nn(table, dt_ref[...].astype(BF16))
    tmp_ref[8 : 8 + CONV + 1, 0 : conv_ref.shape[1]] = conv_ref[...]
    tmp_ref[8 + CONV + 1 : 8 + CONV + 2, 0 : gain_ref.shape[0]] = gain_ref[...].reshape(1, -1)
    w1_ref[rows : rows + 16, :] = tmp_ref[...].astype(BF16)
    for at, part in enumerate(pick_heads(win_ref, 0, ctx, heads)):
        g2_ref[0:rows, at * 128 : (at + 1) * 128] = part.astype(BF16)
    if g2_ref.shape[0] > rows:
        some = wout_ref.shape[0] // 4
        mine = wout_ref[pl.ds(pl.multiple_of(ctx * some, 8), some), :].astype(BF16)
        g2_ref[rows : rows + some] = mine[:, :width]
        g2_ref[rows + some : rows + 2 * some] = mine[:, width:]


def scan_forward_kernel(
    here_ref,
    at_ref,
    tok_pieces,
    w1_pieces,
    hrow_ref,
    hcol_ref,
    segc_ref,
    segr_ref,
    hid_ref,
    conv_ref,
    gpre_ref,
    gmine_ref,
    wdt_ref,
    w1_ref,
    mixed_ref,
    convin_ref,
    convsum_ref,
    inner_ref,
    raw_ref,
    stepc_ref,
    logc_ref,
    stepr_ref,
    logr_ref,
    start_ref,
    ext_ref,
    seg_ref,
    state_ref,
    small_ref,
    tok_ref,
    conv_all,
    gain_all,
    sems,
    tok_sems,
):
    step = pl.program_id(0)
    span, model = hid_ref.shape
    heads = wdt_ref.shape[0]
    width = heads * HEAD_DIM
    shards = small_ref.shape[0]
    rows = model // shards

    @pl.when(step == 0)
    def _():
        copies = place(
            w1_pieces,
            at_ref,
            sems,
            [(0, rows, rows_of(w1_ref, rows)), (rows, 16, lambda at: small_ref.at[at])],
        )
        tokens = [
            pltpu.make_async_copy(piece, tok_ref.at[here_ref[2] ^ index], tok_sems.at[index])
            for index, piece in enumerate(tok_pieces)
        ]
        for copy in tokens:
            copy.start()
        ext_ref[0:8] = jnp.zeros((8, ext_ref.shape[1]), F32)
        state_ref[...] = jnp.zeros_like(state_ref)
        conv_all[...] = jnp.zeros_like(conv_all)
        for copy in copies:
            copy.wait()
        conv_cols = conv_all.shape[1] // shards
        gain_len = gain_all.shape[1] // shards
        for shard in range(shards):
            small = small_ref[shard].astype(F32)
            wdt_ref[:, shard * rows : (shard + 1) * rows] = small[0:8, 384 : 384 + rows].astype(BF16)
            conv_all[0 : CONV + 1, shard * conv_cols : (shard + 1) * conv_cols] = small[
                8 : 8 + CONV + 1, :conv_cols
            ]
            gain_all[:, shard * gain_len : (shard + 1) * gain_len] = small[13:14, :gain_len]
        for at, part in enumerate(pick_heads(conv_all, 0, here_ref[2], heads)):
            conv_ref[:, at * 128 : (at + 1) * 128] = part
        conv_ref[:, width:] = conv_all[:, INNER:]
        gpre_ref[...] = gain_all[:, :model]
        for at, part in enumerate(pick_heads(gain_all, model, here_ref[2], heads)):
            gmine_ref[:, at * 128 : (at + 1) * 128] = part
        for copy in tokens:
            copy.wait()

    tok = tok_ref[step]
    scale = lax.rsqrt(jnp.mean(tok * tok, axis=-1, keepdims=True) + NORM_EPS)
    hid = (tok * scale * gpre_ref[...]).astype(BF16)
    hid_ref[...] = hid
    proj = nn(hid, w1_ref[...]).astype(BF16)
    convin_ref[...] = proj
    ext_ref[8 : 8 + span] = proj.astype(F32)
    seg_ref[...] = segc_ref[pl.ds(pl.multiple_of(step * span, 8), span + 8), :]
    seg_here = seg_ref[8 : 8 + span]
    total = conv_ref[CONV : CONV + 1]
    for tap in range(CONV):
        at = 8 - (CONV - 1) + tap
        same = seg_ref[at : at + span] == seg_here
        total = total + conv_ref[tap : tap + 1] * jnp.where(same, ext_ref[at : at + span], 0.0)
    ext_ref[0:8] = ext_ref[span : span + 8]
    convsum_ref[...] = total
    mixed = (total * sigmoid(total)).astype(BF16)
    mixed_ref[...] = mixed

    raw_c = nt(hid, wdt_ref[...]) + hrow_ref[1:2]
    raw_r = nt(wdt_ref[...], hid) + hcol_ref[:, 1:2]
    step_c = softplus(raw_c)
    step_r = softplus(raw_r)
    log_c = nn(triangle(span, True), -step_c * jnp.exp(hrow_ref[0:1]), HIGHEST)
    log_r = nn(-step_r * jnp.exp(hcol_ref[:, 0:1]), triangle(span, False), HIGHEST)
    raw_ref[...] = raw_c
    stepc_ref[...] = step_c
    logc_ref[...] = log_c
    stepr_ref[...] = step_r
    logr_ref[...] = log_r

    values = mixed[:, :width]
    write = mixed[:, width : width + STATE]
    read = mixed[:, width + STATE :]
    row = lax.broadcasted_iota(jnp.int32, (span, span), 0)
    col = lax.broadcasted_iota(jnp.int32, (span, span), 1)
    visible = (seg_here == segr_ref[...]) & (row >= col)
    scores = jnp.where(visible, nt(read, write), 0.0)
    lane = lax.broadcasted_iota(jnp.int32, (span, 2 * HEAD_DIM), 1)

    seg_prev = seg_ref[7:8]
    seg_last = seg_ref[span + 7 : span + 8]
    last = log_c[span - 1 : span]
    enter = jnp.where(seg_here == seg_prev, jnp.exp(log_c), 0.0)
    tail = jnp.where(seg_here == seg_last, jnp.exp(last - log_c), 0.0) * step_c
    keep = jnp.where(seg_last == seg_prev, jnp.exp(last), 0.0)
    state = state_ref[...]
    start_ref[0] = state
    values_f = values.astype(F32)
    base = spread(enter, width) * nn(read, state.astype(BF16)) + spread(
        hrow_ref[2:3] + jnp.zeros((8, heads), F32), width
    )[0:1] * values_f
    for pair in range(heads // 2):
        lanes = slice(pair * 2 * HEAD_DIM, (pair + 1) * 2 * HEAD_DIM)
        pieces = []
        for head in (2 * pair, 2 * pair + 1):
            gap = jnp.minimum(log_c[:, head : head + 1] - log_r[head : head + 1], 0.0)
            weights = scores * jnp.exp(gap) * step_r[head : head + 1]
            pieces.append(nn(weights.astype(BF16), values[:, lanes]))
        inner_ref[:, lanes] = base[:, lanes] + jnp.where(lane < HEAD_DIM, pieces[0], pieces[1])
    moved = (spread(tail, width) * values_f).astype(BF16)
    state_ref[...] = spread(keep + jnp.zeros((8, heads), F32), width)[0:1] * state + tn(
        write, moved
    )


def gate_kernel(
    here_ref,
    at_ref,
    hid_ref,
    g2_pieces,
    cot_pieces,
    inner_ref,
    gain_ref,
    wg_ref,
    wout_ref,
    cot_ref,
    gate_ref,
    ng_ref,
    stat_ref,
    sems,
    cot_sems,
):
    step = pl.program_id(0)
    rows = wg_ref.shape[0] // (wout_ref.shape[0] // HEAD_DIM)
    width = wg_ref.shape[1]

    @pl.when(step == 0)
    def _():
        some = rows_of(wout_ref, HEAD_DIM)
        copies = place(
            g2_pieces,
            at_ref,
            sems,
            [
                (0, rows, rows_of(wg_ref, rows)),
                (rows, HEAD_DIM, lambda at: some(at).at[:, 0:width]),
                (rows + HEAD_DIM, HEAD_DIM, lambda at: some(at).at[:, width : 2 * width]),
            ],
        )
        cots = [
            pltpu.make_async_copy(piece, cot_ref.at[here_ref[2] ^ index], cot_sems.at[index])
            for index, piece in enumerate(cot_pieces)
        ]
        for copy in cots:
            copy.start()
        for copy in copies + cots:
            copy.wait()

    gate = nn(hid_ref[...], wg_ref[...]).astype(BF16)
    gate_ref[...] = gate
    gate = gate.astype(F32)
    grad = nt(cot_ref[step], wout_ref[...])
    ng_ref[...] = grad
    gated = inner_ref[...] * (gate * sigmoid(gate))
    squares = jnp.sum(gated * gated, axis=1, keepdims=True)
    crossed = jnp.sum(gated * (grad * gain_ref[...]), axis=1, keepdims=True)
    same = diagonal(gated.shape[0])
    squares = jnp.sum(jnp.where(same, squares, 0.0), axis=0, keepdims=True)
    crossed = jnp.sum(jnp.where(same, crossed, 0.0), axis=0, keepdims=True)
    at = lax.broadcasted_iota(jnp.int32, stat_ref.shape, 0)
    stat_ref[...] = jnp.where(at == 0, squares, crossed)


def norm_back_kernel(
    perm_ref,
    here_ref,
    hid_ref,
    inner_ref,
    gate_ref,
    ng_ref,
    stat_ref,
    gain_ref,
    mixed_ref,
    wout_ref,
    cot_ref,
    bkeep_ref,
    bsend_ref,
    keep_ref,
    send_ref,
    dy_ref,
    dgate_ref,
    sums_ref,
    outacc_ref,
    inacc_ref,
):
    step = pl.program_id(0)
    span, width = inner_ref.shape

    @pl.when(step == 0)
    def _():
        outacc_ref[...] = jnp.zeros_like(outacc_ref)
        inacc_ref[...] = jnp.zeros_like(inacc_ref)
        sums_ref[...] = jnp.zeros_like(sums_ref)

    same = diagonal(span)
    squares = jnp.sum(jnp.where(same, stat_ref[0:1], 0.0), axis=1, keepdims=True)
    cross = jnp.sum(jnp.where(same, stat_ref[1:2], 0.0), axis=1, keepdims=True)
    inv = lax.rsqrt(squares * (1.0 / INNER) + NORM_EPS)
    gate = gate_ref[...].astype(F32)
    sig = sigmoid(gate)
    silu = gate * sig
    inner = inner_ref[...]
    gated = inner * silu
    unit = gated * inv
    normed = (unit * gain_ref[...]).astype(BF16)
    cot = cot_ref[perm_ref[step]]
    block = nn(normed, wout_ref[...]).astype(BF16)

    @pl.when(step < 2)
    def _():
        bsend_ref[0] = block

    @pl.when(step >= 2)
    def _():
        bkeep_ref[0] = block

    outacc_ref[...] += tn(normed, cot)
    grad = ng_ref[...]
    dgated = inv * (grad * gain_ref[...] - unit * (cross * inv * (1.0 / INNER)))
    dy = dgated * silu
    dy_ref[...] = dy
    dgate = (dgated * inner * (sig * (1.0 + gate * (1.0 - sig)))).astype(BF16)
    dgate_ref[...] = dgate
    inacc_ref[...] += tn(hid_ref[...], dgate)
    gain_sum = jnp.sum(grad * unit, axis=0, keepdims=True)
    skip_sum = jnp.sum(dy * mixed_ref[...].astype(F32), axis=0, keepdims=True)
    at = lax.broadcasted_iota(jnp.int32, (8, width), 0)
    sums_ref[...] += jnp.where(at == 0, gain_sum, jnp.where(at == 1, skip_sum, 0.0))

    @pl.when(step == pl.num_programs(0) - 1)
    def _():
        own = here_ref[0]
        rows = inacc_ref.shape[0] // (2 * keep_ref.shape[0])
        part_of(lambda at: inacc_ref[at * rows : (at + 1) * rows], own, keep_ref, send_ref)
        outs = lambda at: outacc_ref[at * HEAD_DIM : (at + 1) * HEAD_DIM]
        part_of(lambda at: outs(at)[:, :width], own, keep_ref, send_ref, rows)
        part_of(lambda at: outs(at)[:, width:], own, keep_ref, send_ref, rows + HEAD_DIM)


def scan_back_kernel(
    perm_ref,
    here_ref,
    hid_ref,
    dy_ref,
    mixed_ref,
    convin_ref,
    convsum_ref,
    raw_ref,
    stepc_ref,
    logc_ref,
    stepr_ref,
    logr_ref,
    start_ref,
    conv_ref,
    hrow_ref,
    segc_ref,
    segr_ref,
    keep_ref,
    send_ref,
    dval_ref,
    dbc_ref,
    dstep_ref,
    convg_ref,
    dtg_ref,
    headg_ref,
    ext_ref,
    seg_ref,
    grad_ref,
    inacc_ref,
    dx_ref,
):
    step = pl.program_id(0)
    chunk = pl.num_programs(0) - 1 - step
    span = hid_ref.shape[0]
    heads = stepc_ref.shape[1]
    width = heads * HEAD_DIM

    @pl.when(step == 0)
    def _():
        ext_ref[span : span + 8] = jnp.zeros((8, width), F32)
        grad_ref[...] = jnp.zeros_like(grad_ref)
        inacc_ref[...] = jnp.zeros_like(inacc_ref)
        convg_ref[...] = jnp.zeros_like(convg_ref)
        dtg_ref[...] = jnp.zeros_like(dtg_ref)
        headg_ref[...] = jnp.zeros_like(headg_ref)

    seg_ref[...] = segc_ref[pl.ds(pl.multiple_of(chunk * span, 8), span + 16), :]
    seg_here = seg_ref[8 : 8 + span]
    seg_prev = seg_ref[7:8]
    seg_last = seg_ref[span + 7 : span + 8]
    mixed = mixed_ref[...]
    values = mixed[:, :width]
    write = mixed[:, width : width + STATE]
    read = mixed[:, width + STATE :]
    values_f = values.astype(F32)
    dy = dy_ref[...]
    dy_low = dy.astype(BF16)
    step_c = stepc_ref[...]
    log_c = logc_ref[...]
    step_r = stepr_ref[...]
    log_r = logr_ref[...]
    last = log_c[span - 1 : span]
    enter = jnp.where(seg_here == seg_prev, jnp.exp(log_c), 0.0)
    tail_raw = jnp.where(seg_here == seg_last, jnp.exp(last - log_c), 0.0)
    tail = tail_raw * step_c
    keep = jnp.where(seg_last == seg_prev, jnp.exp(last), 0.0)
    enter_w = spread(enter, width)
    tail_w = spread(tail, width)
    wide = spread(
        jnp.concatenate([hrow_ref[2:3] + jnp.zeros((8, heads), F32), keep + jnp.zeros((8, heads), F32)], axis=0),
        width,
    )
    skip_w = wide[0:1]
    keep_w = wide[8:9]
    state = start_ref[0]
    state_low = state.astype(BF16)
    later = grad_ref[...]
    later_low = later.astype(BF16)

    row = lax.broadcasted_iota(jnp.int32, (span, span), 0)
    col = lax.broadcasted_iota(jnp.int32, (span, span), 1)
    visible = (seg_here == segr_ref[...]) & (row >= col)
    scores = jnp.where(visible, nt(read, write), 0.0)
    lane = lax.broadcasted_iota(jnp.int32, (span, 2 * HEAD_DIM), 1)
    head_at = lax.broadcasted_iota(jnp.int32, (8, span), 0)
    lane_at = lax.broadcasted_iota(jnp.int32, (span, heads), 1)

    entered = enter_w * dy
    entered_low = entered.astype(BF16)
    inter = enter_w * nn(read, state_low)
    from_later = nn(write, later_low)
    moved_low = (tail_w * values_f).astype(BF16)
    dread = nt(entered_low, state_low)
    dwrite = nt(moved_low, later_low)
    dlog_c = gather_heads(dy * inter, heads)
    tail_dot = gather_heads(values_f * from_later, heads)
    dlog_c = dlog_c - tail_dot * tail
    dstep_c = tail_dot * tail_raw
    carried = gather_heads(jnp.sum(later * state, axis=0, keepdims=True) + jnp.zeros((8, width), F32), heads)[0:1]
    at_last = lax.broadcasted_iota(jnp.int32, (span, heads), 0) == span - 1
    dlog_c = dlog_c + jnp.where(
        at_last, jnp.sum(tail_dot * tail, axis=0, keepdims=True) + keep * carried, 0.0
    )
    grad_ref[...] = keep_w * later + tn(read, entered_low)
    dx_ref[...] = tail_w * from_later + skip_w * dy

    dscores = jnp.zeros((span, span), F32)
    dstep_r = jnp.zeros((8, span), F32)
    for pair in range(heads // 2):
        lanes = slice(pair * 2 * HEAD_DIM, (pair + 1) * 2 * HEAD_DIM)
        dy_pair = dy_low[:, lanes]
        pieces = []
        for head in (2 * pair, 2 * pair + 1):
            mine = lane < HEAD_DIM if head % 2 == 0 else lane >= HEAD_DIM
            gap = jnp.minimum(log_c[:, head : head + 1] - log_r[head : head + 1], 0.0)
            decay = jnp.exp(gap)
            outer = nt(jnp.where(mine, dy_pair, jnp.zeros_like(dy_pair)), values[:, lanes])
            fade = decay * step_r[head : head + 1]
            dscores = dscores + outer * fade
            flow = outer * scores
            base = flow * decay
            dstep_r = dstep_r + jnp.where(head_at == head, jnp.sum(base, axis=0, keepdims=True), 0.0)
            dlog_c = dlog_c + jnp.where(
                lane_at == head, jnp.sum(flow * fade, axis=1, keepdims=True), 0.0
            )
            pieces.append(tn((scores * fade).astype(BF16), dy_pair))
        dx_ref[:, lanes] += jnp.where(lane < HEAD_DIM, pieces[0], pieces[1])
    dscores = jnp.where(visible, dscores, 0.0).astype(BF16)
    dread = dread + nn(dscores, write)
    dwrite = dwrite + tn(dscores, read)
    dbc_ref[:, :STATE] = dwrite.astype(BF16)
    dbc_ref[:, STATE:] = dread.astype(BF16)

    upper = triangle(span, False)
    eye = jnp.where(row == col, 1.0, 0.0).astype(F32)
    dalpha = nn(upper, dlog_c, HIGHEST) - nt(upper, dstep_r * step_r, HIGHEST)[:, :heads]
    dstep = dstep_c + nt(eye, dstep_r, HIGHEST)[:, :heads]
    rate = jnp.exp(hrow_ref[0:1])
    draw = (dstep - rate * dalpha) * sigmoid(raw_ref[...])
    draw_low = draw.astype(BF16)
    dstep_ref[...] = draw_low
    hid = hid_ref[...]
    dtg_ref[...] += tn(draw_low, hid)
    rate_sum = jnp.sum(-dalpha * step_c * rate, axis=0, keepdims=True)
    bias_sum = jnp.sum(draw, axis=0, keepdims=True)
    at = lax.broadcasted_iota(jnp.int32, (8, heads), 0)
    headg_ref[...] += jnp.where(at == 0, rate_sum, jnp.where(at == 1, bias_sum, 0.0))

    ext_ref[0:span] = dx_ref[...] * silu_grad(convsum_ref[...])
    back = jnp.zeros((span, width), F32)
    conv_in = convin_ref[...].astype(F32)
    at = lax.broadcasted_iota(jnp.int32, (8, width), 0)
    sums = jnp.where(at == CONV, jnp.sum(ext_ref[0:span], axis=0, keepdims=True), 0.0)
    for tap in range(CONV):
        ahead = CONV - 1 - tap
        same = seg_ref[8 + ahead : 8 + ahead + span] == seg_here
        term = jnp.where(same, ext_ref[ahead : ahead + span], 0.0)
        back = back + conv_ref[tap : tap + 1] * term
        sums = sums + jnp.where(at == tap, jnp.sum(conv_in * term, axis=0, keepdims=True), 0.0)
    convg_ref[...] += sums
    ext_ref[span : span + 8] = ext_ref[0:8]
    dval = back.astype(BF16)
    dval_ref[...] = dval
    inacc_ref[...] += tn(hid, dval)

    @pl.when(step == pl.num_programs(0) - 1)
    def _():
        rows = inacc_ref.shape[0] // (2 * keep_ref.shape[0])
        part_of(lambda at: inacc_ref[at * rows : (at + 1) * rows], here_ref[0], keep_ref, send_ref)


def hidden_back_kernel(
    perm_ref,
    dgate_ref,
    dval_ref,
    dstep_ref,
    wg_ref,
    wv_ref,
    wdt_ref,
    hid_ref,
    gain_ref,
    keep_ref,
    send_ref,
    gsum_ref,
):
    @pl.when(pl.program_id(0) == 0)
    def _():
        gsum_ref[...] = jnp.zeros_like(gsum_ref)

    total = nt(dgate_ref[...], wg_ref[...]) + nt(dval_ref[...], wv_ref[...])
    total = total + nn(dstep_ref[...], wdt_ref[...])
    step = pl.program_id(0)

    @pl.when(step < 2)
    def _():
        send_ref[0] = total.astype(BF16)

    @pl.when(step >= 2)
    def _():
        keep_ref[0] = total.astype(BF16)

    unit = hid_ref[...].astype(F32) / gain_ref[...]
    gsum_ref[...] += jnp.sum(total * unit, axis=0, keepdims=True) + jnp.zeros(gsum_ref.shape, F32)


def maps_back_kernel(
    here_ref,
    dbc_ref,
    dbcfar_ref,
    convsum_ref,
    convin_ref,
    conv_ref,
    segc_ref,
    hid_ref,
    w1_ref,
    gain_ref,
    convg_ref,
    sums_ref,
    headg_ref,
    dtg_ref,
    gall_ref,
    keep_ref,
    send_ref,
    own_ref,
    ext_ref,
    acc_ref,
    dmap_ref,
    small_ref,
):
    size, width = dmap_ref.shape
    total = dbc_ref[...].astype(F32) + dbcfar_ref[...].astype(F32)
    ext_ref[0:size] = total * silu_grad(convsum_ref[...])
    ext_ref[size : size + 8] = jnp.zeros((8, width), F32)
    back = jnp.zeros((size, width), F32)
    conv_in = convin_ref[...].astype(F32)
    at = lax.broadcasted_iota(jnp.int32, (8, width), 0)
    sums = jnp.where(at == CONV, jnp.sum(ext_ref[0:size], axis=0, keepdims=True), 0.0)
    seg_here = segc_ref[8 : 8 + size]
    for tap in range(CONV):
        ahead = CONV - 1 - tap
        same = segc_ref[8 + ahead : 8 + ahead + size] == seg_here
        term = jnp.where(same, ext_ref[ahead : ahead + size], 0.0)
        back = back + conv_ref[tap : tap + 1] * term
        sums = sums + jnp.where(at == tap, jnp.sum(conv_in * term, axis=0, keepdims=True), 0.0)
    dmap_ref[...] = back.astype(BF16)
    ctx = here_ref[2]
    acc_ref[...] = tn(hid_ref[...], dmap_ref[...])
    span = own_ref.shape[0]
    own = pl.ds(pl.multiple_of(ctx * span, 16), span)
    grad = nt(dmap_ref[own, :], w1_ref[...])
    own_ref[...] = grad
    unit = hid_ref[own, :].astype(F32) / gain_ref[...]
    gain_sum = gall_ref[0:1] + jnp.sum(grad * unit, axis=0, keepdims=True)
    half = small_ref.shape[1]
    heads = headg_ref.shape[1]
    small_ref[...] = jnp.zeros_like(small_ref)
    small_ref[0 : CONV + 1] = convg_ref[0 : CONV + 1]
    small_ref[CONV + 1 : CONV + 3] = sums_ref[0:2]
    small_ref[7:8, 0:heads] = headg_ref[0:1]
    small_ref[7:8, 128 : 128 + heads] = headg_ref[1:2]
    small_ref[8 : 8 + CONV + 1, 0:width] = sums[0 : CONV + 1]
    small_ref[13:14] = gain_sum[:, :half]
    small_ref[14:15] = gain_sum[:, half:]
    small_ref[15:16] = small_ref[7:8] - small_ref[7:8].astype(BF16).astype(F32)
    small_ref[16:24] = dtg_ref[:, :half]
    small_ref[24:32] = dtg_ref[:, half:]
    small = small_ref[...].astype(BF16)
    count = keep_ref.shape[0] // 32 - 1
    block = acc_ref.shape[0] // (2 * count)
    some = block // 4
    keep_ref[0:32] = small
    send_ref[0:32] = small
    for at in range(count):
        start = pl.multiple_of(2 * at * block + ctx * some, 8)
        low = acc_ref[pl.ds(start, some), :].astype(BF16)
        start = pl.multiple_of((2 * at + 1) * block + ctx * some, 8)
        high = acc_ref[pl.ds(start, some), :].astype(BF16)
        keep_ref[32 + 32 * at : 64 + 32 * at, 0:width] = jnp.where(here_ref[0] == 0, low, high)
        send_ref[32 + 32 * at : 64 + 32 * at, 0:width] = jnp.where(here_ref[0] == 0, high, low)


def input_back_kernel(keep_ref, came_ref, far_ref, own_ref, tok_ref, gain_ref, cot_ref, out_ref):
    grad = keep_ref[0].astype(F32) + came_ref[0].astype(F32) + far_ref[...].astype(F32) + own_ref[...]
    tok = tok_ref[...]
    scale = lax.rsqrt(jnp.mean(tok * tok, axis=-1, keepdims=True) + NORM_EPS)
    unit = tok * scale
    scaled = grad * gain_ref[...]
    mean = jnp.mean(scaled * unit, axis=-1, keepdims=True)
    out_ref[...] = cot_ref[...] + scale * (scaled - unit * mean)


def pair_sum_kernel(here_ref, keep_ref, came_ref, out_refs):
    for at, out_ref in enumerate(out_refs):
        index = pl.ds(here_ref[1] ^ at, 1)
        out_ref[...] = (keep_ref[index].astype(F32) + came_ref[index].astype(F32))[0].astype(BF16)


def pair_sum_late_kernel(here_ref, keep_ref, came_ref, mkeep_ref, mcame_ref, out_refs):
    rows, width = keep_ref.shape[1:]
    small = (mkeep_ref[0:32].astype(F32) + mcame_ref[0:32].astype(F32))
    row = lax.broadcasted_iota(jnp.int32, small.shape, 0)
    head = small[7:8] + small[15:16]
    rest = head - head.astype(BF16).astype(F32)
    small = jnp.where(row == 7, head, jnp.where(row == 15, rest, small)).astype(BF16)
    for at, out_ref in enumerate(out_refs):
        block = here_ref[1] ^ at
        index = pl.ds(block, 1)
        out_ref[0:rows] = (keep_ref[index].astype(F32) + came_ref[index].astype(F32))[0].astype(BF16)
        out_ref[rows : rows + 32] = small
        index = pl.ds(pl.multiple_of(32 + 32 * block, 32), 32)
        out_ref[rows + 32 : rows + 64] = (
            mkeep_ref[index].astype(F32) + mcame_ref[index].astype(F32)
        ).astype(BF16)


def sum_kernel(late, part_refs, out_ref):
    terms = [ref[...].astype(F32) for ref in part_refs]
    while len(terms) > 1:
        terms = [terms[at] + terms[at + 1] for at in range(0, len(terms), 2)]
    total = terms[0]
    if late:
        first = out_ref.shape[0] - 64
        row = lax.broadcasted_iota(jnp.int32, total.shape, 0)
        head = total[first + 7 : first + 8] + total[first + 15 : first + 16]
        rest = head - head.astype(BF16).astype(F32)
        total = jnp.where(row == first + 7, head, jnp.where(row == first + 15, rest, total))
    out_ref[...] = total.astype(out_ref.dtype)


def adam_out_kernel(here_ref, weight_ref, first_ref, second_ref, early_refs, *rest):
    new_refs, early_ref = rest[:3], rest[3]
    step = pl.program_id(0)

    @pl.when(step == 0)
    def _():
        for at, ref in enumerate(early_refs):
            early_ref[pl.ds(here_ref[2] ^ at, 1)] = ref[...][None]

    rows = weight_ref.shape[0]
    width = early_ref.shape[2]
    first = early_ref.shape[1] - 2 * rows
    for at in range(2):
        lanes = slice(at * width, (at + 1) * width)
        grad = early_ref[step, first + at * rows : first + (at + 1) * rows].astype(F32)
        news = adam_step(
            weight_ref[:, lanes], first_ref[:, lanes], second_ref[:, lanes], grad, 0.02, WEIGHT_DECAY
        )
        for ref, new in zip(new_refs, news):
            ref[:, lanes] = new


def adam_in_kernel(here_ref, weight_ref, first_ref, second_ref, early_refs, late_refs, *rest):
    new_refs, (early_ref, late_ref) = rest[:3], rest[3:]
    step = pl.program_id(0)
    pieces = len(early_refs)
    rows = weight_ref.shape[0]
    width = early_ref.shape[2]
    block = pieces * HEAD_DIM

    @pl.when(step == 0)
    def _():
        for at in range(pieces):
            owner = pl.ds(here_ref[2] ^ at, 1)
            early_ref[owner] = early_refs[at][...][None]
            late_ref[owner] = late_refs[at][...][None]

    here = pl.ds(pl.multiple_of(step * rows, rows), rows)
    low = lax.broadcasted_iota(jnp.int32, (rows, 2 * HEAD_DIM), 1) < HEAD_DIM

    def update(lanes, grad):
        news = adam_step(
            weight_ref[:, lanes], first_ref[:, lanes], second_ref[:, lanes], grad, 0.03, WEIGHT_DECAY
        )
        for ref, new in zip(new_refs, news):
            ref[:, lanes] = new

    for base, ref in ((0, early_ref), (INNER, late_ref)):
        for pair in range(width // (2 * HEAD_DIM)):
            lanes = slice(pair * 2 * HEAD_DIM, (pair + 1) * 2 * HEAD_DIM)
            for at in range(0, pieces, 2):
                first = ref[at, here, lanes].astype(F32)
                second = ref[at + 1, here, lanes].astype(F32)
                start = base + 2 * pair * block + at * HEAD_DIM
                even = jnp.where(low, first, pltpu.roll(second, HEAD_DIM, 1))
                update(slice(start, start + 2 * HEAD_DIM), even)
                start = start + block
                odd = jnp.where(low, pltpu.roll(first, HEAD_DIM, 1), second)
                update(slice(start, start + 2 * HEAD_DIM), odd)
    first = late_ref.shape[1] - 32
    update(
        slice(2 * INNER, 2 * INNER + 2 * STATE),
        late_ref[step, first : first + 32, 0 : 2 * STATE].astype(F32),
    )


def swap(value, axis, bit):
    count = lax.axis_size(axis)
    return lax.ppermute(value, axis, [(at, at ^ bit) for at in range(count)])


def gather_ctx(value):
    far = swap(value, "ctx", 2)
    return [value, swap(value, "ctx", 1), far, swap(far, "ctx", 1)]


def gather_dp(value):
    count, here = lax.axis_size("dp"), lax.axis_index("dp")
    if count != 8:
        return [lax.all_gather(value, "dp", axis=0)], jnp.zeros((1,), jnp.int32)
    value = value[None]
    pieces = [(value, 0)] + [(swap(value, "dp", bit), bit) for bit in range(2, count, 2)]
    pieces += [(swap(piece, "dp", 1), bit + 1) for piece, bit in pieces]
    return [piece for piece, _ in pieces], here ^ jnp.asarray([bit for _, bit in pieces], jnp.int32)


def spread_dp(parts):
    return [parts[0]] + [swap(part, "dp", 2 * at) for at, part in enumerate(parts) if at]


def fan_ctx(value):
    return [value] + [swap(value, "ctx", bit) for bit in range(1, lax.axis_size("ctx"))]


def adam_step(weight, moment_one, second, gradient, step_rate, decay_rate):
    moment_new = BETA_ONE * moment_one + (1.0 - BETA_ONE) * gradient
    second_new = BETA_TWO * second + (1.0 - BETA_TWO) * gradient * gradient
    first_hat = moment_new / (1.0 - BETA_ONE**STEP)
    second_hat = second_new / (1.0 - BETA_TWO**STEP)
    weight_new = weight - step_rate * (
        first_hat / (jnp.sqrt(second_hat) + ADAM_EPS) + decay_rate * weight
    )
    return (weight_new, moment_new, second_new)


def full(shape):
    return pl.BlockSpec(shape, lambda *_: (0,) * len(shape))


def shape_of(*shape, dtype=F32):
    return jax.ShapeDtypeStruct(shape, dtype)


def shards(
    tokens,
    segment_ids,
    cotangent,
    in_weight,
    dt_weight,
    out_weight,
    conv_params,
    gains,
    head_params,
    in_first,
    in_second,
    dt_first,
    dt_second,
    out_first,
    out_second,
    conv_first,
    conv_second,
    gain_first,
    gain_second,
    head_first,
    head_second,
):
    _, span, model = tokens.shape
    length = segment_ids.shape[1]
    ndp, nctx = lax.axis_size("dp"), lax.axis_size("ctx")
    d, c = lax.axis_index("dp"), lax.axis_index("ctx")
    heads = HEADS // nctx
    width = INNER // nctx
    maps = 2 * STATE
    wide = width + maps
    chunks = nctx
    rows_in = in_weight.shape[0]
    conv_cols = conv_params.shape[1]
    gain_len = gains.shape[0]
    dt_cols = dt_weight.shape[1]
    near = ndp == heads
    high = heads // 2
    block_in = model // heads
    tok = tokens[0]
    bits = jnp.stack([d & 1, d >> 1, c] if near else [0 * d, 0 * d, c]).astype(jnp.int32)
    perm = c ^ jnp.asarray([1, 3, 0, 2], jnp.int32)
    smem = pl.BlockSpec(memory_space=pltpu.SMEM)
    vmem = pl.BlockSpec(memory_space=pltpu.VMEM)
    anywhere = lambda pieces: [pl.BlockSpec(memory_space=pl.ANY)] * len(pieces)

    w1, g2 = pl.pallas_call(
        pack_kernel,
        in_specs=[smem] + [vmem] * 5,
        out_shape=[
            shape_of(rows_in + 16, wide, dtype=BF16),
            shape_of(rows_in + (2 * HEAD_DIM if near else 0), width, dtype=BF16),
        ],
        scratch_shapes=[pltpu.VMEM((16, wide), F32)],
        compiler_params=params(),
        cost_estimate=cost(3),
        name="pack",
    )(bits, in_weight, out_weight, dt_weight, conv_params, gains)
    tok_sent, w1 = lax.optimization_barrier((tok, w1))
    w1, at_rows = gather_dp(w1)
    toks = gather_ctx(tok_sent)
    if near:
        g2 = [lax.all_gather(g2, "dp", axis=0)]
    else:
        wg = lax.all_gather(g2, "dp", axis=0, tiled=True).reshape(heads, block_in, width)
        wout = lax.all_gather(out_weight.astype(BF16), "dp", axis=0, tiled=True)
        wout = lax.dynamic_index_in_dim(wout.reshape(heads, nctx, HEAD_DIM, model), c, 1, False)
        g2 = [jnp.concatenate([wg, wout[:, :, :width], wout[:, :, width:]], axis=1)]
    at_g2 = jnp.zeros((1,), jnp.int32)
    cot_low, w1 = lax.optimization_barrier((cotangent[0].astype(BF16), w1))
    cots = fan_ctx(cot_low)

    ids = segment_ids[0]
    seg_col = jnp.pad(ids, (8, 8), constant_values=-1)[:, None]
    seg_row = segment_ids
    head_mine = lax.dynamic_index_in_dim(head_params.reshape(3, heads, nctx), c, 2, False)
    head_col = head_mine.T

    rows = lambda cols: pl.BlockSpec((span, cols), lambda i, *_: (i, 0))
    row_of = pl.BlockSpec((heads, span), lambda i, *_: (0, i))
    rows_at = lambda cols: pl.BlockSpec((span, cols), lambda i, p, *_: (p[i], 0))
    sent = pl.BlockSpec((1, span, model), lambda i, *_: (jnp.minimum(i, 1), 0, 0))
    kept = pl.BlockSpec((1, span, model), lambda i, *_: (jnp.maximum(i - 2, 0), 0, 0))
    shards_in = sum(piece.shape[0] for piece in w1)

    (
        hid, conv_mine, gain_pre, gain_mine, dt_mine, w1, mixed, conv_in, conv_sum, inner, raw,
        step_c, log_c, step_r, log_r, starts,
    ) = pl.pallas_call(
        scan_forward_kernel,
        grid_spec=pltpu.PrefetchScalarGridSpec(
            num_scalar_prefetch=2,
            grid=(chunks,),
            in_specs=[
                anywhere(toks),
                anywhere(w1),
                full((3, heads)),
                full((heads, 3)),
                full((length + 16, 1)),
                pl.BlockSpec((1, span), lambda i, *_: (0, i)),
            ],
            out_specs=[
                rows(model),
                full((8, wide)),
                full((1, model)),
                full((1, width)),
                full((heads, model)),
                full((model, wide)),
                rows(wide),
                rows(wide),
                rows(wide),
                rows(width),
                rows(heads),
                rows(heads),
                rows(heads),
                row_of,
                row_of,
                pl.BlockSpec((1, STATE, width), lambda i, *_: (i, 0, 0)),
            ],
            scratch_shapes=[
                pltpu.VMEM((span + 8, wide), F32),
                pltpu.VMEM((span + 8, 1), jnp.int32),
                pltpu.VMEM((STATE, width), F32),
                pltpu.VMEM((shards_in, 16, wide), BF16),
                pltpu.VMEM((nctx, span, model), F32),
                pltpu.VMEM((8, INNER + maps), F32),
                pltpu.VMEM((1, model + INNER), F32),
                pltpu.SemaphoreType.DMA((copies_of(w1, 2),)),
                pltpu.SemaphoreType.DMA((nctx,)),
            ],
        ),
        out_shape=[
            shape_of(length, model, dtype=BF16),
            shape_of(8, wide),
            shape_of(1, model),
            shape_of(1, width),
            shape_of(heads, model, dtype=BF16),
            shape_of(model, wide, dtype=BF16),
            shape_of(length, wide, dtype=BF16),
            shape_of(length, wide, dtype=BF16),
            shape_of(length, wide),
            shape_of(length, width),
            shape_of(length, heads),
            shape_of(length, heads),
            shape_of(length, heads),
            shape_of(heads, length),
            shape_of(heads, length),
            shape_of(chunks, STATE, width),
        ],
        compiler_params=params("arbitrary"),
        cost_estimate=cost(18),
        name="scan_forward",
    )(bits, at_rows, toks, w1, head_mine, head_col, seg_col, seg_row)

    wg, wout, cot_all, gate, normed_grad, stats = pl.pallas_call(
        gate_kernel,
        grid_spec=pltpu.PrefetchScalarGridSpec(
            num_scalar_prefetch=2,
            grid=(chunks,),
            in_specs=[rows(model), anywhere(g2), anywhere(cots), rows(width), full((1, width))],
            out_specs=[
                full((model, width)),
                full((width, model)),
                full((nctx, span, model)),
                rows(width),
                rows(width),
                pl.BlockSpec((8, span), lambda i, *_: (0, i)),
            ],
            scratch_shapes=[
                pltpu.SemaphoreType.DMA((copies_of(g2, 3),)),
                pltpu.SemaphoreType.DMA((nctx,)),
            ],
        ),
        out_shape=[
            shape_of(model, width, dtype=BF16),
            shape_of(width, model, dtype=BF16),
            shape_of(nctx, span, model, dtype=BF16),
            shape_of(length, width, dtype=BF16),
            shape_of(length, width),
            shape_of(8, length),
        ],
        compiler_params=params("arbitrary"),
        cost_estimate=cost(12),
        name="gate",
    )(bits, at_g2, hid, g2, cots, inner, gain_mine)
    stats = sum(fan_ctx(stats))

    early_rows = block_in + 2 * HEAD_DIM
    block_keep, block_send, early_keep, early_send, dy, dgate, col_sums = pl.pallas_call(
        norm_back_kernel,
        grid_spec=pltpu.PrefetchScalarGridSpec(
            num_scalar_prefetch=2,
            grid=(chunks,),
            in_specs=[
                rows_at(model),
                rows_at(width),
                rows_at(width),
                rows_at(width),
                pl.BlockSpec((8, span), lambda i, p, *_: (0, p[i])),
                full((1, width)),
                rows_at(width),
                full((width, model)),
                full((nctx, span, model)),
            ],
            out_specs=[
                kept,
                sent,
                full((high, early_rows, width)),
                full((high, early_rows, width)),
                rows_at(width),
                rows_at(width),
                full((8, width)),
            ],
            scratch_shapes=[pltpu.VMEM((width, model), F32), pltpu.VMEM((model, width), F32)],
        ),
        out_shape=[
            shape_of(2, span, model, dtype=BF16),
            shape_of(2, span, model, dtype=BF16),
            shape_of(high, early_rows, width, dtype=BF16),
            shape_of(high, early_rows, width, dtype=BF16),
            shape_of(length, width),
            shape_of(length, width, dtype=BF16),
            shape_of(8, width),
        ],
        compiler_params=params("arbitrary"),
        cost_estimate=cost(13),
        name="norm_back",
    )(perm, bits, hid, inner, gate, normed_grad, stats, gain_mine, mixed, wout, cot_all)
    block_came = swap(block_send, "ctx", 1)
    if near:
        early_came = swap(early_send, "dp", 1)

    back = lambda cols: pl.BlockSpec((span, cols), lambda i, *_: (chunks - 1 - i, 0))
    back_row = pl.BlockSpec((heads, span), lambda i, *_: (0, chunks - 1 - i))
    late_keep, late_send, dval, dbc, dstep, conv_grad, dt_grad, head_grad = pl.pallas_call(
        scan_back_kernel,
        grid_spec=pltpu.PrefetchScalarGridSpec(
            num_scalar_prefetch=2,
            grid=(chunks,),
            in_specs=[
                back(model),
                back(width),
                back(wide),
                back(width),
                back(width),
                back(heads),
                back(heads),
                back(heads),
                back_row,
                back_row,
                pl.BlockSpec((1, STATE, width), lambda i, *_: (chunks - 1 - i, 0, 0)),
                full((8, width)),
                full((3, heads)),
                full((length + 16, 1)),
                pl.BlockSpec((1, span), lambda i, *_: (0, chunks - 1 - i)),
            ],
            out_specs=[
                full((high, block_in, width)),
                full((high, block_in, width)),
                back(width),
                back(maps),
                back(heads),
                full((8, width)),
                full((heads, model)),
                full((8, heads)),
            ],
            scratch_shapes=[
                pltpu.VMEM((span + 8, width), F32),
                pltpu.VMEM((span + 16, 1), jnp.int32),
                pltpu.VMEM((STATE, width), F32),
                pltpu.VMEM((model, width), F32),
                pltpu.VMEM((span, width), F32),
            ],
        ),
        out_shape=[
            shape_of(high, block_in, width, dtype=BF16),
            shape_of(high, block_in, width, dtype=BF16),
            shape_of(length, width, dtype=BF16),
            shape_of(length, maps, dtype=BF16),
            shape_of(length, heads, dtype=BF16),
            shape_of(8, width),
            shape_of(heads, model),
            shape_of(8, heads),
        ],
        compiler_params=params("arbitrary"),
        cost_estimate=cost(21),
        name="scan_back",
    )(
        perm, bits, hid, dy, mixed, conv_in, conv_sum, raw, step_c, log_c, step_r, log_r, starts,
        conv_mine, head_mine, seg_col, seg_row,
    )
    block_far = (block_keep[1].astype(F32) + block_came[1].astype(F32)).astype(BF16)
    dbc_came = swap(dbc, "ctx", 1)
    if near:
        late_came = swap(late_send, "dp", 1)
        early_parts = pl.pallas_call(
            pair_sum_kernel,
            in_specs=[smem, vmem, vmem],
            out_shape=[[shape_of(early_rows, width, dtype=BF16)] * high],
            compiler_params=params(),
            cost_estimate=cost(3),
            name="pair_sum_early",
        )(bits, early_keep, early_came)[0]
        dval, early_parts = lax.optimization_barrier((dval, early_parts))
        early_parts = spread_dp(early_parts)
    dbc = (dbc.astype(F32) + dbc_came.astype(F32)).astype(BF16)
    dbc_far = swap(dbc, "ctx", 2)

    hidden_keep, hidden_send, gain_sum = pl.pallas_call(
        hidden_back_kernel,
        grid_spec=pltpu.PrefetchScalarGridSpec(
            num_scalar_prefetch=1,
            grid=(chunks,),
            in_specs=[
                rows_at(width),
                rows_at(width),
                rows_at(heads),
                full((model, width)),
                full((model, width)),
                full((heads, model)),
                rows_at(model),
                full((1, model)),
            ],
            out_specs=[kept, sent, full((8, model))],
        ),
        out_shape=[
            shape_of(2, span, model, dtype=BF16),
            shape_of(2, span, model, dtype=BF16),
            shape_of(8, model),
        ],
        compiler_params=params("arbitrary"),
        cost_estimate=cost(8),
        name="hidden_back",
    )(perm, dgate, dval, dstep, wg, w1, dt_mine, hid, gain_pre)
    hidden_came = swap(hidden_send, "ctx", 1)
    hidden_far = (hidden_keep[1].astype(F32) + hidden_came[1].astype(F32)).astype(BF16)
    hidden_far = swap(hidden_far, "ctx", 2)

    map_rows = 32 + 32 * high
    map_cols = lambda size: pl.BlockSpec((size, maps), lambda i: (0, width // maps))
    map_keep, map_send, hidden_own = pl.pallas_call(
        maps_back_kernel,
        grid=(1,),
        in_specs=[
            smem,
            full((length, maps)),
            full((length, maps)),
            map_cols(length),
            map_cols(length),
            map_cols(8),
            full((length + 16, 1)),
            full((length, model)),
            map_cols(model),
            full((1, model)),
            full((8, width)),
            full((8, width)),
            full((8, heads)),
            full((heads, model)),
            full((8, model)),
        ],
        out_specs=[full((map_rows, width)), full((map_rows, width)), full((span, model))],
        out_shape=[
            shape_of(map_rows, width, dtype=BF16),
            shape_of(map_rows, width, dtype=BF16),
            shape_of(span, model),
        ],
        scratch_shapes=[
            pltpu.VMEM((length + 8, maps), F32),
            pltpu.VMEM((model, maps), F32),
            pltpu.VMEM((length, maps), BF16),
            pltpu.VMEM((32, width), F32),
        ],
        compiler_params=params("arbitrary"),
        cost_estimate=cost(6),
        name="maps_back",
    )(
        bits,
        dbc,
        dbc_far,
        conv_sum,
        conv_in,
        conv_mine,
        seg_col,
        hid,
        w1,
        gain_pre,
        conv_grad,
        col_sums,
        head_grad,
        dt_grad,
        gain_sum,
    )

    mine = pl.BlockSpec((1, span, model), lambda i: (0, 0, 0))
    input_grad = pl.pallas_call(
        input_back_kernel,
        grid=(1,),
        in_specs=[mine, mine] + [full((span, model))] * 3 + [full((1, model)), full((span, model))],
        out_specs=full((span, model)),
        out_shape=shape_of(span, model),
        compiler_params=params("arbitrary"),
        cost_estimate=cost(4),
        name="input_back",
    )(hidden_keep, hidden_came, hidden_far, hidden_own, tok, gain_pre, cotangent[0])
    block_far = swap(block_far, "ctx", 2)
    block_output = tok + (
        block_keep[0].astype(F32) + block_came[0].astype(F32) + block_far.astype(F32)
    )

    late_rows = block_in + 64
    if near:
        map_came = swap(map_send, "dp", 1)
        late_parts = pl.pallas_call(
            pair_sum_late_kernel,
            in_specs=[smem] + [vmem] * 4,
            out_shape=[[shape_of(late_rows, width, dtype=BF16)] * high],
            compiler_params=params(),
            cost_estimate=cost(2),
        name="pair_sum_late",
        )(bits, late_keep, late_came, map_keep, map_came)[0]
        late_parts = spread_dp(late_parts)
        early, late = [
            pl.pallas_call(
                functools.partial(sum_kernel, name == "late"),
                in_specs=[[vmem] * high],
                out_shape=shape_of(*parts[0].shape, dtype=BF16),
                compiler_params=params(),
                cost_estimate=cost(2),
                name="sum_" + name,
            )(parts)
            for name, parts in (("early", early_parts), ("late", late_parts))
        ]
        early, late = fan_ctx(early), fan_ctx(late)
        row_block = lambda ref_rows, cols: pl.BlockSpec((ref_rows, cols), lambda i, *_: (i, 0))
        in_block = row_block(rows_in // nctx, in_weight.shape[1])
        out_block = row_block(out_weight.shape[0] // nctx, model)
        early_spec = [full((early_rows, width))] * nctx
        early_scratch = pltpu.VMEM((nctx, early_rows, width), BF16)
        out_new = pl.pallas_call(
            adam_out_kernel,
            grid_spec=pltpu.PrefetchScalarGridSpec(
                num_scalar_prefetch=1,
                grid=(nctx,),
                in_specs=[out_block] * 3 + [early_spec],
                out_specs=[out_block] * 3,
                scratch_shapes=[early_scratch],
            ),
            out_shape=[shape_of(*out_weight.shape)] * 3,
            compiler_params=params("arbitrary"),
            cost_estimate=cost(4),
            name="adam_out",
        )(bits, out_weight, out_first, out_second, early)
        in_new = pl.pallas_call(
            adam_in_kernel,
            grid_spec=pltpu.PrefetchScalarGridSpec(
                num_scalar_prefetch=1,
                grid=(nctx,),
                in_specs=[in_block] * 3 + [early_spec, [full((late_rows, width))] * nctx],
                out_specs=[in_block] * 3,
                scratch_shapes=[early_scratch, pltpu.VMEM((nctx, late_rows, width), BF16)],
            ),
            out_shape=[shape_of(*in_weight.shape)] * 3,
            compiler_params=params("arbitrary"),
            cost_estimate=cost(7),
            name="adam_in",
        )(bits, in_weight, in_first, in_second, early, late)
        in_new, out_new = tuple(in_new), tuple(out_new)
        small = jnp.stack([part[block_in : block_in + 32] for part in late])[c ^ jnp.arange(nctx)]
        small = small.astype(F32)
    else:
        blocks = lambda keep, send: jnp.stack([keep, send], axis=1).reshape((heads,) + keep.shape[1:])
        early = blocks(early_keep, early_send).astype(F32)
        late = blocks(late_keep, late_send).astype(F32)
        part = lambda value: value[32:].reshape(high, 32, width)[:, :, :maps]
        map_blocks = blocks(part(map_keep), part(map_send)).astype(F32)

        def total(value):
            return lax.psum_scatter(value, "dp", scatter_dimension=0, tiled=True)

        def spaced(value):
            place_at = (jnp.arange(nctx) == c).astype(F32).reshape((1, nctx, 1, 1))
            value = value[:, None] * place_at
            return lax.psum(total(value.reshape(-1, value.shape[-1])), "ctx")

        def by_head(value):
            value = lax.all_gather(total(value.reshape(model, width)), "ctx", axis=0)
            value = value.reshape(nctx, rows_in, heads, HEAD_DIM)
            return jnp.transpose(value, (1, 2, 0, 3)).reshape(rows_in, INNER)

        in_total = jnp.concatenate(
            [by_head(early[:, :block_in]), by_head(late), spaced(map_blocks)], axis=1
        )
        out_total = spaced(
            jnp.concatenate([early[:, block_in : block_in + HEAD_DIM], early[:, block_in + HEAD_DIM :]], axis=2)
        )
        in_new = adam_step(in_weight, in_first, in_second, in_total, 0.03, WEIGHT_DECAY)
        out_new = adam_step(out_weight, out_first, out_second, out_total, 0.02, WEIGHT_DECAY)
        small = lax.all_gather(lax.psum(map_keep[:32].astype(F32), "dp"), "ctx", axis=0)

    def in_order(value):
        return jnp.swapaxes(value.reshape(nctx, -1, heads, HEAD_DIM), 0, 1).swapaxes(1, 2).reshape(-1, INNER)

    columns = in_order(small[:, : CONV + 2])
    conv_total = jnp.concatenate([columns[: CONV + 1], small[0, 8 : 8 + CONV + 1, :maps]], axis=1)
    conv_total = lax.dynamic_slice_in_dim(conv_total, d * conv_cols, conv_cols, 1)
    dt_total = small[:, 16:32].reshape(nctx, 2, heads, width)
    dt_total = jnp.transpose(dt_total, (2, 0, 1, 3)).reshape(HEADS, model)
    dt_total = lax.dynamic_slice_in_dim(dt_total, d * dt_cols, dt_cols, 1)
    pre_total = jnp.sum(small[:, 13:15], axis=0).reshape(-1)
    gain_total = jnp.concatenate([pre_total, columns[CONV + 1]])
    gain_total = lax.dynamic_slice_in_dim(gain_total, d * gain_len, gain_len, 0)
    head_row = small[:, 7] + small[:, 15]
    head_total = jnp.stack(
        [
            head_row[:, :heads].T.reshape(-1),
            head_row[:, 128 : 128 + heads].T.reshape(-1),
            jnp.sum(small[:, CONV + 2].reshape(nctx, heads, HEAD_DIM), axis=2).T.reshape(-1),
        ]
    )

    dt_new = adam_step(dt_weight, dt_first, dt_second, dt_total, 0.03, WEIGHT_DECAY)
    conv_new = adam_step(conv_params, conv_first, conv_second, conv_total, 0.3, 0.0)
    gain_new = adam_step(gains, gain_first, gain_second, gain_total, 0.5, 0.0)
    head_new = adam_step(head_params, head_first, head_second, head_total, 2.0, 0.0)
    return (block_output[None], input_grad[None]) + in_new + dt_new + out_new + conv_new + gain_new + head_new


def solution(mesh):
    tokens, rows, cols = P("dp", "ctx", None), P("dp", None), P(None, "dp")
    return jax.shard_map(
        shards,
        mesh=mesh,
        in_specs=(tokens, rows, tokens, rows, cols, rows, cols, P("dp"), P())
        + (rows, rows, cols, cols, rows, rows, cols, cols, P("dp"), P("dp"), P(), P()),
        out_specs=(tokens, tokens)
        + (rows,) * 3
        + (cols,) * 3
        + (rows,) * 3
        + (cols,) * 3
        + (P("dp"),) * 3
        + (P(),) * 3,
        check_vma=False,
    )
```

```python
import functools

import jax
import jax.numpy as jnp
from jax import lax
from jax.experimental import pallas as pl
from jax.experimental.pallas import tpu as pltpu
from jax.sharding import PartitionSpec as P

INNER = 2048
HEADS = 32
HEAD_DIM = 64
STATE = 128
CONV = 4
STEP = 10

F32 = jnp.float32
BF16 = jnp.bfloat16
HIGHEST = lax.Precision.HIGHEST
NORM_EPS = 1e-05
BETA_ONE = 0.9
BETA_TWO = 0.95
ADAM_EPS = 1e-08
WEIGHT_DECAY = 0.1
VMEM_LIMIT = 56 * 1024 * 1024


def nn(a, b, precision=None):
    return lax.dot_general(
        a, b, (((1,), (0,)), ((), ())), precision=precision, preferred_element_type=F32
    )


def nt(a, b, precision=None):
    return lax.dot_general(
        a, b, (((1,), (1,)), ((), ())), precision=precision, preferred_element_type=F32
    )


def tn(a, b, precision=None):
    return lax.dot_general(
        a, b, (((0,), (0,)), ((), ())), precision=precision, preferred_element_type=F32
    )


def halves(value):
    high = value.astype(BF16)
    return high, (value - high.astype(F32)).astype(BF16)


def spread(value, width):
    heads = value.shape[1]
    row = lax.broadcasted_iota(jnp.int32, (heads, width), 0)
    col = lax.broadcasted_iota(jnp.int32, (heads, width), 1)
    table = jnp.where(col // HEAD_DIM == row, 1.0, 0.0).astype(BF16)
    high, low = halves(value)
    return nn(high, table) + nn(low, table)


def gather_heads(value, heads):
    width = value.shape[1]
    row = lax.broadcasted_iota(jnp.int32, (width, heads), 0)
    col = lax.broadcasted_iota(jnp.int32, (width, heads), 1)
    table = jnp.where(row // HEAD_DIM == col, 1.0, 0.0).astype(BF16)
    high, low = halves(value)
    return nn(high, table) + nn(low, table)


def softplus(value):
    return jnp.maximum(value, 0.0) + jnp.log1p(jnp.exp(-jnp.abs(value)))


def sigmoid(value):
    return 1.0 / (1.0 + jnp.exp(-value))


def silu_grad(value):
    sig = sigmoid(value)
    return sig * (1.0 + value * (1.0 - sig))


def diagonal(size):
    row = lax.broadcasted_iota(jnp.int32, (size, size), 0)
    return row == lax.broadcasted_iota(jnp.int32, (size, size), 1)


def triangle(size, lower):
    row = lax.broadcasted_iota(jnp.int32, (size, size), 0)
    col = lax.broadcasted_iota(jnp.int32, (size, size), 1)
    keep = row >= col if lower else row <= col
    return jnp.where(keep, 1.0, 0.0).astype(F32)


def params(*semantics):
    return pltpu.CompilerParams(
        dimension_semantics=semantics or None, vmem_limit_bytes=VMEM_LIMIT
    )


def place(pieces, at_ref, stride, sems, targets):
    copies = []
    for index, piece in enumerate(pieces):
        for block in range(piece.shape[0]):
            for first, rows, target in targets:
                copies.append(
                    pltpu.make_async_copy(
                        piece.at[block, first : first + rows],
                        target(at_ref[index] + stride * block),
                        sems.at[len(copies)],
                    )
                )
    for copy in copies:
        copy.start()
    return copies


def copies_of(pieces, targets):
    return sum(piece.shape[0] for piece in pieces) * targets


def rows_of(ref, rows):
    return lambda at: ref.at[pl.ds(pl.multiple_of(at * rows, 16), rows)]


def part_of(block, own_bit, keep_ref, send_ref, first=0):
    for at in range(keep_ref.shape[0]):
        low, high = block(2 * at).astype(BF16), block(2 * at + 1).astype(BF16)
        rows = slice(first, first + low.shape[0])
        keep_ref[at, rows] = jnp.where(own_bit == 0, low, high)
        send_ref[at, rows] = jnp.where(own_bit == 0, high, low)


def pick_heads(ref, base, ctx, heads):
    first = pl.multiple_of(base + (ctx >> 1) * 2 * HEAD_DIM, 2 * HEAD_DIM)
    wide = ref[:, pl.ds(first, 2 * HEAD_DIM)]
    low = lax.broadcasted_iota(jnp.int32, wide.shape, 1) < HEAD_DIM
    odd = (ctx & 1) == 1
    out = []
    for pair in range(heads // 2):
        parts = []
        for head in (2 * pair, 2 * pair + 1):
            first = pl.multiple_of(base + head * 4 * HEAD_DIM + (ctx >> 1) * 2 * HEAD_DIM, 2 * HEAD_DIM)
            parts.append(ref[:, pl.ds(first, 2 * HEAD_DIM)])
        even = jnp.where(low, parts[0], pltpu.roll(parts[1], HEAD_DIM, 1))
        other = jnp.where(low, pltpu.roll(parts[0], HEAD_DIM, 1), parts[1])
        out.append(jnp.where(odd, other, even))
    return out


def pack_kernel(here_ref, win_ref, wout_ref, dt_ref, conv_ref, gain_ref, w1_ref, g2_ref, tmp_ref):
    ctx = here_ref[2]
    rows = win_ref.shape[0]
    heads = HEADS // 4
    width = heads * HEAD_DIM
    copies = range(w1_ref.shape[0])
    for at, part in enumerate(pick_heads(win_ref, INNER, ctx, heads)):
        part = part.astype(BF16)
        for copy in copies:
            w1_ref[copy, 0:rows, at * 128 : (at + 1) * 128] = part
    part = win_ref[:, 2 * INNER :].astype(BF16)
    for copy in copies:
        w1_ref[copy, 0:rows, width:] = part
    tmp_ref[...] = jnp.zeros_like(tmp_ref)
    row = lax.broadcasted_iota(jnp.int32, (heads, HEADS), 0)
    col = lax.broadcasted_iota(jnp.int32, (heads, HEADS), 1)
    table = jnp.where(col == 4 * row + ctx, 1.0, 0.0).astype(BF16)
    tmp_ref[0:heads, 384 : 384 + dt_ref.shape[1]] = nn(table, dt_ref[...].astype(BF16))
    tmp_ref[8 : 8 + CONV + 1, 0 : conv_ref.shape[1]] = conv_ref[...]
    tmp_ref[8 + CONV + 1 : 8 + CONV + 2, 0 : gain_ref.shape[0]] = gain_ref[...].reshape(1, -1)
    for copy in copies:
        w1_ref[copy, rows : rows + 16, :] = tmp_ref[...].astype(BF16)
    for at, part in enumerate(pick_heads(win_ref, 0, ctx, heads)):
        g2_ref[0:rows, at * 128 : (at + 1) * 128] = part.astype(BF16)
    if g2_ref.shape[0] > rows:
        some = wout_ref.shape[0] // 4
        mine = wout_ref[pl.ds(pl.multiple_of(ctx * some, 8), some), :].astype(BF16)
        g2_ref[rows : rows + some] = mine[:, :width]
        g2_ref[rows + some : rows + 2 * some] = mine[:, width:]


def scan_forward_kernel(
    here_ref,
    at_ref,
    tok_pieces,
    w1_pieces,
    hrow_ref,
    hcol_ref,
    segc_ref,
    segr_ref,
    hid_ref,
    conv_ref,
    gpre_ref,
    gmine_ref,
    wdt_ref,
    w1_ref,
    mixed_ref,
    convin_ref,
    convsum_ref,
    inner_ref,
    raw_ref,
    stepc_ref,
    logc_ref,
    stepr_ref,
    logr_ref,
    start_ref,
    ext_ref,
    seg_ref,
    state_ref,
    small_ref,
    tok_ref,
    conv_all,
    gain_all,
    sems,
    tok_sems,
):
    step = pl.program_id(0)
    span, model = hid_ref.shape
    heads = wdt_ref.shape[0]
    width = heads * HEAD_DIM
    shards = small_ref.shape[0]
    rows = model // shards

    @pl.when(step == 0)
    def _():
        copies = place(
            w1_pieces,
            at_ref,
            len(w1_pieces),
            sems,
            [(0, rows, rows_of(w1_ref, rows)), (rows, 16, lambda at: small_ref.at[at])],
        )
        tokens = [
            pltpu.make_async_copy(piece, tok_ref.at[here_ref[2] ^ index], tok_sems.at[index])
            for index, piece in enumerate(tok_pieces)
        ]
        for copy in tokens:
            copy.start()
        ext_ref[0:8] = jnp.zeros((8, ext_ref.shape[1]), F32)
        state_ref[...] = jnp.zeros_like(state_ref)
        conv_all[...] = jnp.zeros_like(conv_all)
        for copy in copies:
            copy.wait()
        conv_cols = conv_all.shape[1] // shards
        gain_len = gain_all.shape[1] // shards
        for shard in range(shards):
            small = small_ref[shard].astype(F32)
            wdt_ref[:, shard * rows : (shard + 1) * rows] = small[0:8, 384 : 384 + rows].astype(BF16)
            conv_all[0 : CONV + 1, shard * conv_cols : (shard + 1) * conv_cols] = small[
                8 : 8 + CONV + 1, :conv_cols
            ]
            gain_all[:, shard * gain_len : (shard + 1) * gain_len] = small[13:14, :gain_len]
        for at, part in enumerate(pick_heads(conv_all, 0, here_ref[2], heads)):
            conv_ref[:, at * 128 : (at + 1) * 128] = part
        conv_ref[:, width:] = conv_all[:, INNER:]
        gpre_ref[...] = gain_all[:, :model]
        for at, part in enumerate(pick_heads(gain_all, model, here_ref[2], heads)):
            gmine_ref[:, at * 128 : (at + 1) * 128] = part
        for copy in tokens:
            copy.wait()

    tok = tok_ref[step]
    scale = lax.rsqrt(jnp.mean(tok * tok, axis=-1, keepdims=True) + NORM_EPS)
    hid = (tok * scale * gpre_ref[...]).astype(BF16)
    hid_ref[...] = hid
    proj = nn(hid, w1_ref[...]).astype(BF16)
    convin_ref[...] = proj
    ext_ref[8 : 8 + span] = proj.astype(F32)
    seg_ref[...] = segc_ref[pl.ds(pl.multiple_of(step * span, 8), span + 8), :]
    seg_here = seg_ref[8 : 8 + span]
    total = conv_ref[CONV : CONV + 1]
    for tap in range(CONV):
        at = 8 - (CONV - 1) + tap
        same = seg_ref[at : at + span] == seg_here
        total = total + conv_ref[tap : tap + 1] * jnp.where(same, ext_ref[at : at + span], 0.0)
    ext_ref[0:8] = ext_ref[span : span + 8]
    convsum_ref[...] = total
    mixed = (total * sigmoid(total)).astype(BF16)
    mixed_ref[...] = mixed

    raw_c = nt(hid, wdt_ref[...]) + hrow_ref[1:2]
    raw_r = nt(wdt_ref[...], hid) + hcol_ref[:, 1:2]
    step_c = softplus(raw_c)
    step_r = softplus(raw_r)
    log_c = nn(triangle(span, True), -step_c * jnp.exp(hrow_ref[0:1]), HIGHEST)
    log_r = nn(-step_r * jnp.exp(hcol_ref[:, 0:1]), triangle(span, False), HIGHEST)
    raw_ref[...] = raw_c
    stepc_ref[...] = step_c
    logc_ref[...] = log_c
    stepr_ref[...] = step_r
    logr_ref[...] = log_r

    values = mixed[:, :width]
    write = mixed[:, width : width + STATE]
    read = mixed[:, width + STATE :]
    row = lax.broadcasted_iota(jnp.int32, (span, span), 0)
    col = lax.broadcasted_iota(jnp.int32, (span, span), 1)
    visible = (seg_here == segr_ref[...]) & (row >= col)
    scores = jnp.where(visible, nt(read, write), 0.0)
    lane = lax.broadcasted_iota(jnp.int32, (span, 2 * HEAD_DIM), 1)

    seg_prev = seg_ref[7:8]
    seg_last = seg_ref[span + 7 : span + 8]
    last = log_c[span - 1 : span]
    enter = jnp.where(seg_here == seg_prev, jnp.exp(log_c), 0.0)
    tail = jnp.where(seg_here == seg_last, jnp.exp(last - log_c), 0.0) * step_c
    keep = jnp.where(seg_last == seg_prev, jnp.exp(last), 0.0)
    state = state_ref[...]
    start_ref[0] = state
    values_f = values.astype(F32)
    base = spread(enter, width) * nn(read, state.astype(BF16)) + spread(
        hrow_ref[2:3] + jnp.zeros((8, heads), F32), width
    )[0:1] * values_f
    for pair in range(heads // 2):
        lanes = slice(pair * 2 * HEAD_DIM, (pair + 1) * 2 * HEAD_DIM)
        pieces = []
        for head in (2 * pair, 2 * pair + 1):
            gap = jnp.minimum(log_c[:, head : head + 1] - log_r[head : head + 1], 0.0)
            weights = scores * jnp.exp(gap) * step_r[head : head + 1]
            pieces.append(nn(weights.astype(BF16), values[:, lanes]))
        inner_ref[:, lanes] = base[:, lanes] + jnp.where(lane < HEAD_DIM, pieces[0], pieces[1])
    moved = (spread(tail, width) * values_f).astype(BF16)
    state_ref[...] = spread(keep + jnp.zeros((8, heads), F32), width)[0:1] * state + tn(
        write, moved
    )


def gate_kernel(
    here_ref,
    at_ref,
    hid_ref,
    g2_pieces,
    cot_pieces,
    inner_ref,
    gain_ref,
    wg_ref,
    wout_ref,
    cot_ref,
    gate_ref,
    ng_ref,
    stat_ref,
    sems,
    cot_sems,
):
    step = pl.program_id(0)
    rows = wg_ref.shape[0] // (wout_ref.shape[0] // HEAD_DIM)
    width = wg_ref.shape[1]

    @pl.when(step == 0)
    def _():
        some = rows_of(wout_ref, HEAD_DIM)
        copies = place(
            g2_pieces,
            at_ref,
            len(g2_pieces),
            sems,
            [
                (0, rows, rows_of(wg_ref, rows)),
                (rows, HEAD_DIM, lambda at: some(at).at[:, 0:width]),
                (rows + HEAD_DIM, HEAD_DIM, lambda at: some(at).at[:, width : 2 * width]),
            ],
        )
        cots = [
            pltpu.make_async_copy(piece, cot_ref.at[here_ref[2] ^ index], cot_sems.at[index])
            for index, piece in enumerate(cot_pieces)
        ]
        for copy in cots:
            copy.start()
        for copy in copies + cots:
            copy.wait()

    gate = nn(hid_ref[...], wg_ref[...]).astype(BF16)
    gate_ref[...] = gate
    gate = gate.astype(F32)
    grad = nt(cot_ref[step], wout_ref[...])
    ng_ref[...] = grad
    gated = inner_ref[...] * (gate * sigmoid(gate))
    squares = jnp.sum(gated * gated, axis=1, keepdims=True)
    crossed = jnp.sum(gated * (grad * gain_ref[...]), axis=1, keepdims=True)
    same = diagonal(gated.shape[0])
    squares = jnp.sum(jnp.where(same, squares, 0.0), axis=0, keepdims=True)
    crossed = jnp.sum(jnp.where(same, crossed, 0.0), axis=0, keepdims=True)
    at = lax.broadcasted_iota(jnp.int32, stat_ref.shape, 0)
    stat_ref[...] = jnp.where(at == 0, squares, crossed)


def norm_back_kernel(
    perm_ref,
    here_ref,
    hid_ref,
    inner_ref,
    gate_ref,
    ng_ref,
    stat_ref,
    gain_ref,
    mixed_ref,
    wout_ref,
    cot_ref,
    bkeep_ref,
    bsend_ref,
    keep_ref,
    send_ref,
    dy_ref,
    dgate_ref,
    sums_ref,
    outacc_ref,
    inacc_ref,
):
    step = pl.program_id(0)
    span, width = inner_ref.shape

    @pl.when(step == 0)
    def _():
        outacc_ref[...] = jnp.zeros_like(outacc_ref)
        inacc_ref[...] = jnp.zeros_like(inacc_ref)
        sums_ref[...] = jnp.zeros_like(sums_ref)

    same = diagonal(span)
    squares = jnp.sum(jnp.where(same, stat_ref[0:1], 0.0), axis=1, keepdims=True)
    cross = jnp.sum(jnp.where(same, stat_ref[1:2], 0.0), axis=1, keepdims=True)
    inv = lax.rsqrt(squares * (1.0 / INNER) + NORM_EPS)
    gate = gate_ref[...].astype(F32)
    sig = sigmoid(gate)
    silu = gate * sig
    inner = inner_ref[...]
    gated = inner * silu
    unit = gated * inv
    normed = (unit * gain_ref[...]).astype(BF16)
    cot = cot_ref[perm_ref[step]]
    block = nn(normed, wout_ref[...]).astype(BF16)

    @pl.when(step < 2)
    def _():
        bsend_ref[0] = block

    @pl.when(step >= 2)
    def _():
        bkeep_ref[0] = block

    outacc_ref[...] += tn(normed, cot)
    grad = ng_ref[...]
    dgated = inv * (grad * gain_ref[...] - unit * (cross * inv * (1.0 / INNER)))
    dy = dgated * silu
    dy_ref[...] = dy
    dgate = (dgated * inner * (sig * (1.0 + gate * (1.0 - sig)))).astype(BF16)
    dgate_ref[...] = dgate
    inacc_ref[...] += tn(hid_ref[...], dgate)
    gain_sum = jnp.sum(grad * unit, axis=0, keepdims=True)
    skip_sum = jnp.sum(dy * mixed_ref[...].astype(F32), axis=0, keepdims=True)
    at = lax.broadcasted_iota(jnp.int32, (8, width), 0)
    sums_ref[...] += jnp.where(at == 0, gain_sum, jnp.where(at == 1, skip_sum, 0.0))

    @pl.when(step == pl.num_programs(0) - 1)
    def _():
        own = here_ref[0]
        rows = inacc_ref.shape[0] // (2 * keep_ref.shape[0])
        part_of(lambda at: inacc_ref[at * rows : (at + 1) * rows], own, keep_ref, send_ref)
        outs = lambda at: outacc_ref[at * HEAD_DIM : (at + 1) * HEAD_DIM]
        part_of(lambda at: outs(at)[:, :width], own, keep_ref, send_ref, rows)
        part_of(lambda at: outs(at)[:, width:], own, keep_ref, send_ref, rows + HEAD_DIM)


def scan_back_kernel(
    perm_ref,
    here_ref,
    hid_ref,
    dy_ref,
    mixed_ref,
    convin_ref,
    convsum_ref,
    raw_ref,
    stepc_ref,
    logc_ref,
    stepr_ref,
    logr_ref,
    start_ref,
    conv_ref,
    hrow_ref,
    segc_ref,
    segr_ref,
    keep_ref,
    send_ref,
    dval_ref,
    dbc_ref,
    dstep_ref,
    convg_ref,
    dtg_ref,
    headg_ref,
    ext_ref,
    seg_ref,
    grad_ref,
    inacc_ref,
    dx_ref,
):
    step = pl.program_id(0)
    chunk = pl.num_programs(0) - 1 - step
    span = hid_ref.shape[0]
    heads = stepc_ref.shape[1]
    width = heads * HEAD_DIM

    @pl.when(step == 0)
    def _():
        ext_ref[span : span + 8] = jnp.zeros((8, width), F32)
        grad_ref[...] = jnp.zeros_like(grad_ref)
        inacc_ref[...] = jnp.zeros_like(inacc_ref)
        convg_ref[...] = jnp.zeros_like(convg_ref)
        dtg_ref[...] = jnp.zeros_like(dtg_ref)
        headg_ref[...] = jnp.zeros_like(headg_ref)

    seg_ref[...] = segc_ref[pl.ds(pl.multiple_of(chunk * span, 8), span + 16), :]
    seg_here = seg_ref[8 : 8 + span]
    seg_prev = seg_ref[7:8]
    seg_last = seg_ref[span + 7 : span + 8]
    mixed = mixed_ref[...]
    values = mixed[:, :width]
    write = mixed[:, width : width + STATE]
    read = mixed[:, width + STATE :]
    values_f = values.astype(F32)
    dy = dy_ref[...]
    dy_low = dy.astype(BF16)
    step_c = stepc_ref[...]
    log_c = logc_ref[...]
    step_r = stepr_ref[...]
    log_r = logr_ref[...]
    last = log_c[span - 1 : span]
    enter = jnp.where(seg_here == seg_prev, jnp.exp(log_c), 0.0)
    tail_raw = jnp.where(seg_here == seg_last, jnp.exp(last - log_c), 0.0)
    tail = tail_raw * step_c
    keep = jnp.where(seg_last == seg_prev, jnp.exp(last), 0.0)
    enter_w = spread(enter, width)
    tail_w = spread(tail, width)
    wide = spread(
        jnp.concatenate([hrow_ref[2:3] + jnp.zeros((8, heads), F32), keep + jnp.zeros((8, heads), F32)], axis=0),
        width,
    )
    skip_w = wide[0:1]
    keep_w = wide[8:9]
    state = start_ref[0]
    state_low = state.astype(BF16)
    later = grad_ref[...]
    later_low = later.astype(BF16)

    row = lax.broadcasted_iota(jnp.int32, (span, span), 0)
    col = lax.broadcasted_iota(jnp.int32, (span, span), 1)
    visible = (seg_here == segr_ref[...]) & (row >= col)
    scores = jnp.where(visible, nt(read, write), 0.0)
    lane = lax.broadcasted_iota(jnp.int32, (span, 2 * HEAD_DIM), 1)
    head_at = lax.broadcasted_iota(jnp.int32, (8, span), 0)
    lane_at = lax.broadcasted_iota(jnp.int32, (span, heads), 1)

    entered = enter_w * dy
    entered_low = entered.astype(BF16)
    inter = enter_w * nn(read, state_low)
    from_later = nn(write, later_low)
    moved_low = (tail_w * values_f).astype(BF16)
    dread = nt(entered_low, state_low)
    dwrite = nt(moved_low, later_low)
    dlog_c = gather_heads(dy * inter, heads)
    tail_dot = gather_heads(values_f * from_later, heads)
    dlog_c = dlog_c - tail_dot * tail
    dstep_c = tail_dot * tail_raw
    carried = gather_heads(jnp.sum(later * state, axis=0, keepdims=True) + jnp.zeros((8, width), F32), heads)[0:1]
    at_last = lax.broadcasted_iota(jnp.int32, (span, heads), 0) == span - 1
    dlog_c = dlog_c + jnp.where(
        at_last, jnp.sum(tail_dot * tail, axis=0, keepdims=True) + keep * carried, 0.0
    )
    grad_ref[...] = keep_w * later + tn(read, entered_low)
    dx_ref[...] = tail_w * from_later + skip_w * dy

    dscores = jnp.zeros((span, span), F32)
    dstep_r = jnp.zeros((8, span), F32)
    for pair in range(heads // 2):
        lanes = slice(pair * 2 * HEAD_DIM, (pair + 1) * 2 * HEAD_DIM)
        dy_pair = dy_low[:, lanes]
        pieces = []
        for head in (2 * pair, 2 * pair + 1):
            mine = lane < HEAD_DIM if head % 2 == 0 else lane >= HEAD_DIM
            gap = jnp.minimum(log_c[:, head : head + 1] - log_r[head : head + 1], 0.0)
            decay = jnp.exp(gap)
            outer = nt(jnp.where(mine, dy_pair, jnp.zeros_like(dy_pair)), values[:, lanes])
            fade = decay * step_r[head : head + 1]
            dscores = dscores + outer * fade
            flow = outer * scores
            base = flow * decay
            dstep_r = dstep_r + jnp.where(head_at == head, jnp.sum(base, axis=0, keepdims=True), 0.0)
            dlog_c = dlog_c + jnp.where(
                lane_at == head, jnp.sum(flow * fade, axis=1, keepdims=True), 0.0
            )
            pieces.append(tn((scores * fade).astype(BF16), dy_pair))
        dx_ref[:, lanes] += jnp.where(lane < HEAD_DIM, pieces[0], pieces[1])
    dscores = jnp.where(visible, dscores, 0.0).astype(BF16)
    dread = dread + nn(dscores, write)
    dwrite = dwrite + tn(dscores, read)
    dbc_ref[:, :STATE] = dwrite.astype(BF16)
    dbc_ref[:, STATE:] = dread.astype(BF16)

    upper = triangle(span, False)
    eye = jnp.where(row == col, 1.0, 0.0).astype(F32)
    dalpha = nn(upper, dlog_c, HIGHEST) - nt(upper, dstep_r * step_r, HIGHEST)[:, :heads]
    dstep = dstep_c + nt(eye, dstep_r, HIGHEST)[:, :heads]
    rate = jnp.exp(hrow_ref[0:1])
    draw = (dstep - rate * dalpha) * sigmoid(raw_ref[...])
    draw_low = draw.astype(BF16)
    dstep_ref[...] = draw_low
    hid = hid_ref[...]
    dtg_ref[...] += tn(draw_low, hid)
    rate_sum = jnp.sum(-dalpha * step_c * rate, axis=0, keepdims=True)
    bias_sum = jnp.sum(draw, axis=0, keepdims=True)
    at = lax.broadcasted_iota(jnp.int32, (8, heads), 0)
    headg_ref[...] += jnp.where(at == 0, rate_sum, jnp.where(at == 1, bias_sum, 0.0))

    ext_ref[0:span] = dx_ref[...] * silu_grad(convsum_ref[...])
    back = jnp.zeros((span, width), F32)
    conv_in = convin_ref[...].astype(F32)
    at = lax.broadcasted_iota(jnp.int32, (8, width), 0)
    sums = jnp.where(at == CONV, jnp.sum(ext_ref[0:span], axis=0, keepdims=True), 0.0)
    for tap in range(CONV):
        ahead = CONV - 1 - tap
        same = seg_ref[8 + ahead : 8 + ahead + span] == seg_here
        term = jnp.where(same, ext_ref[ahead : ahead + span], 0.0)
        back = back + conv_ref[tap : tap + 1] * term
        sums = sums + jnp.where(at == tap, jnp.sum(conv_in * term, axis=0, keepdims=True), 0.0)
    convg_ref[...] += sums
    ext_ref[span : span + 8] = ext_ref[0:8]
    dval = back.astype(BF16)
    dval_ref[...] = dval
    inacc_ref[...] += tn(hid, dval)

    @pl.when(step == pl.num_programs(0) - 1)
    def _():
        rows = inacc_ref.shape[0] // (2 * keep_ref.shape[0])
        part_of(lambda at: inacc_ref[at * rows : (at + 1) * rows], here_ref[0], keep_ref, send_ref)


def hidden_back_kernel(
    perm_ref,
    dgate_ref,
    dval_ref,
    dstep_ref,
    wg_ref,
    wv_ref,
    wdt_ref,
    hid_ref,
    gain_ref,
    keep_ref,
    send_ref,
    gsum_ref,
):
    @pl.when(pl.program_id(0) == 0)
    def _():
        gsum_ref[...] = jnp.zeros_like(gsum_ref)

    total = nt(dgate_ref[...], wg_ref[...]) + nt(dval_ref[...], wv_ref[...])
    total = total + nn(dstep_ref[...], wdt_ref[...])
    step = pl.program_id(0)

    @pl.when(step < 2)
    def _():
        send_ref[0] = total.astype(BF16)

    @pl.when(step >= 2)
    def _():
        keep_ref[0] = total.astype(BF16)

    unit = hid_ref[...].astype(F32) / gain_ref[...]
    gsum_ref[...] += jnp.sum(total * unit, axis=0, keepdims=True) + jnp.zeros(gsum_ref.shape, F32)


def maps_back_kernel(
    here_ref,
    dbc_ref,
    dbcfar_ref,
    convsum_ref,
    convin_ref,
    conv_ref,
    segc_ref,
    hid_ref,
    w1_ref,
    gain_ref,
    convg_ref,
    sums_ref,
    headg_ref,
    dtg_ref,
    gall_ref,
    keep_ref,
    send_ref,
    own_ref,
    ext_ref,
    acc_ref,
    dmap_ref,
    small_ref,
):
    size, width = dmap_ref.shape
    total = dbc_ref[...].astype(F32) + dbcfar_ref[...].astype(F32)
    ext_ref[0:size] = total * silu_grad(convsum_ref[...])
    ext_ref[size : size + 8] = jnp.zeros((8, width), F32)
    back = jnp.zeros((size, width), F32)
    conv_in = convin_ref[...].astype(F32)
    at = lax.broadcasted_iota(jnp.int32, (8, width), 0)
    sums = jnp.where(at == CONV, jnp.sum(ext_ref[0:size], axis=0, keepdims=True), 0.0)
    seg_here = segc_ref[8 : 8 + size]
    for tap in range(CONV):
        ahead = CONV - 1 - tap
        same = segc_ref[8 + ahead : 8 + ahead + size] == seg_here
        term = jnp.where(same, ext_ref[ahead : ahead + size], 0.0)
        back = back + conv_ref[tap : tap + 1] * term
        sums = sums + jnp.where(at == tap, jnp.sum(conv_in * term, axis=0, keepdims=True), 0.0)
    dmap_ref[...] = back.astype(BF16)
    ctx = here_ref[2]
    acc_ref[...] = tn(hid_ref[...], dmap_ref[...])
    span = own_ref.shape[0]
    own = pl.ds(pl.multiple_of(ctx * span, 16), span)
    grad = nt(dmap_ref[own, :], w1_ref[...])
    own_ref[...] = grad
    unit = hid_ref[own, :].astype(F32) / gain_ref[...]
    gain_sum = gall_ref[0:1] + jnp.sum(grad * unit, axis=0, keepdims=True)
    half = small_ref.shape[1]
    heads = headg_ref.shape[1]
    small_ref[...] = jnp.zeros_like(small_ref)
    small_ref[0 : CONV + 1] = convg_ref[0 : CONV + 1]
    small_ref[CONV + 1 : CONV + 3] = sums_ref[0:2]
    small_ref[7:8, 0:heads] = headg_ref[0:1]
    small_ref[7:8, 128 : 128 + heads] = headg_ref[1:2]
    small_ref[8 : 8 + CONV + 1, 0:width] = sums[0 : CONV + 1]
    small_ref[13:14] = gain_sum[:, :half]
    small_ref[14:15] = gain_sum[:, half:]
    small_ref[15:16] = small_ref[7:8] - small_ref[7:8].astype(BF16).astype(F32)
    small_ref[16:24] = dtg_ref[:, :half]
    small_ref[24:32] = dtg_ref[:, half:]
    small = small_ref[...].astype(BF16)
    count = keep_ref.shape[0] // 32 - 1
    block = acc_ref.shape[0] // (2 * count)
    some = block // 4
    keep_ref[0:32] = small
    send_ref[0:32] = small
    for at in range(count):
        start = pl.multiple_of(2 * at * block + ctx * some, 8)
        low = acc_ref[pl.ds(start, some), :].astype(BF16)
        start = pl.multiple_of((2 * at + 1) * block + ctx * some, 8)
        high = acc_ref[pl.ds(start, some), :].astype(BF16)
        keep_ref[32 + 32 * at : 64 + 32 * at, 0:width] = jnp.where(here_ref[0] == 0, low, high)
        send_ref[32 + 32 * at : 64 + 32 * at, 0:width] = jnp.where(here_ref[0] == 0, high, low)


def input_back_kernel(keep_ref, came_ref, far_ref, own_ref, tok_ref, gain_ref, cot_ref, out_ref):
    grad = keep_ref[0].astype(F32) + came_ref[0].astype(F32) + far_ref[...].astype(F32) + own_ref[...]
    tok = tok_ref[...]
    scale = lax.rsqrt(jnp.mean(tok * tok, axis=-1, keepdims=True) + NORM_EPS)
    unit = tok * scale
    scaled = grad * gain_ref[...]
    mean = jnp.mean(scaled * unit, axis=-1, keepdims=True)
    out_ref[...] = cot_ref[...] + scale * (scaled - unit * mean)


def pair_sum_kernel(keep_ref, came_ref, out_ref):
    out_ref[...] = (keep_ref[...].astype(F32) + came_ref[...].astype(F32)).astype(BF16)


def with_rest(value, first):
    row = lax.broadcasted_iota(jnp.int32, value.shape, 0)
    head = value[first + 7 : first + 8] + value[first + 15 : first + 16]
    rest = head - head.astype(BF16).astype(F32)
    return jnp.where(row == first + 7, head, jnp.where(row == first + 15, rest, value))


def pair_sum_late_kernel(keep_ref, came_ref, mkeep_ref, mcame_ref, out_ref):
    count, rows, width = keep_ref.shape
    small = with_rest(mkeep_ref[0:32].astype(F32) + mcame_ref[0:32].astype(F32), 0).astype(BF16)
    for block in range(count):
        out_ref[block, 0:rows] = (keep_ref[block].astype(F32) + came_ref[block].astype(F32)).astype(BF16)
        out_ref[block, rows : rows + 32] = small
        at = slice(32 + 32 * block, 64 + 32 * block)
        out_ref[block, rows + 32 : rows + 64] = (
            mkeep_ref[at].astype(F32) + mcame_ref[at].astype(F32)
        ).astype(BF16)


def sum_late_kernel(parts_ref, out_ref):
    total = parts_ref[0].astype(F32)
    for at in range(1, parts_ref.shape[0]):
        total = total + parts_ref[at].astype(F32)
    out_ref[...] = with_rest(total, out_ref.shape[0] - 64).astype(BF16)


def adam_out_kernel(here_ref, weight_ref, first_ref, second_ref, early_refs, *rest):
    new_refs, early_ref = rest[:3], rest[3]
    step = pl.program_id(0)

    @pl.when(step == 0)
    def _():
        for at, ref in enumerate(early_refs):
            early_ref[pl.ds(here_ref[2] ^ at, 1)] = ref[...][None]

    rows = weight_ref.shape[0]
    width = early_ref.shape[2]
    first = early_ref.shape[1] - 2 * rows
    for at in range(2):
        lanes = slice(at * width, (at + 1) * width)
        grad = early_ref[step, first + at * rows : first + (at + 1) * rows].astype(F32)
        news = adam_step(
            weight_ref[:, lanes], first_ref[:, lanes], second_ref[:, lanes], grad, 0.02, WEIGHT_DECAY
        )
        for ref, new in zip(new_refs, news):
            ref[:, lanes] = new


def adam_in_kernel(here_ref, weight_ref, first_ref, second_ref, early_refs, late_refs, *rest):
    new_refs, (early_ref, late_ref) = rest[:3], rest[3:]
    step = pl.program_id(0)
    pieces = len(early_refs)
    rows = weight_ref.shape[0]
    width = early_ref.shape[2]
    block = pieces * HEAD_DIM

    @pl.when(step == 0)
    def _():
        for at in range(pieces):
            owner = pl.ds(here_ref[2] ^ at, 1)
            early_ref[owner] = early_refs[at][...][None]
            late_ref[owner] = late_refs[at][...][None]

    here = pl.ds(pl.multiple_of(step * rows, rows), rows)
    low = lax.broadcasted_iota(jnp.int32, (rows, 2 * HEAD_DIM), 1) < HEAD_DIM

    def update(lanes, grad):
        news = adam_step(
            weight_ref[:, lanes], first_ref[:, lanes], second_ref[:, lanes], grad, 0.03, WEIGHT_DECAY
        )
        for ref, new in zip(new_refs, news):
            ref[:, lanes] = new

    for base, ref in ((0, early_ref), (INNER, late_ref)):
        for pair in range(width // (2 * HEAD_DIM)):
            lanes = slice(pair * 2 * HEAD_DIM, (pair + 1) * 2 * HEAD_DIM)
            for at in range(0, pieces, 2):
                first = ref[at, here, lanes].astype(F32)
                second = ref[at + 1, here, lanes].astype(F32)
                start = base + 2 * pair * block + at * HEAD_DIM
                even = jnp.where(low, first, pltpu.roll(second, HEAD_DIM, 1))
                update(slice(start, start + 2 * HEAD_DIM), even)
                start = start + block
                odd = jnp.where(low, pltpu.roll(first, HEAD_DIM, 1), second)
                update(slice(start, start + 2 * HEAD_DIM), odd)
    first = late_ref.shape[1] - 32
    update(
        slice(2 * INNER, 2 * INNER + 2 * STATE),
        late_ref[step, first : first + 32, 0 : 2 * STATE].astype(F32),
    )


def swap(value, axis, bit):
    count = lax.axis_size(axis)
    return lax.ppermute(value, axis, [(at, at ^ bit) for at in range(count)])


def gather_ctx(value):
    far = swap(value, "ctx", 2)
    return [value, swap(value, "ctx", 1), far, swap(far, "ctx", 1)]


def high_all_to_all(value):
    count = lax.axis_size("dp")
    groups = [list(range(low, count, 2)) for low in range(2)]
    return lax.all_to_all(value, "dp", 0, 0, axis_index_groups=groups)


def fan_ctx(value):
    return [value] + [swap(value, "ctx", bit) for bit in range(1, lax.axis_size("ctx"))]


def adam_step(weight, moment_one, second, gradient, step_rate, decay_rate):
    moment_new = BETA_ONE * moment_one + (1.0 - BETA_ONE) * gradient
    second_new = BETA_TWO * second + (1.0 - BETA_TWO) * gradient * gradient
    first_hat = moment_new / (1.0 - BETA_ONE**STEP)
    second_hat = second_new / (1.0 - BETA_TWO**STEP)
    weight_new = weight - step_rate * (
        first_hat / (jnp.sqrt(second_hat) + ADAM_EPS) + decay_rate * weight
    )
    return (weight_new, moment_new, second_new)


def full(shape):
    return pl.BlockSpec(shape, lambda *_: (0,) * len(shape))


def shape_of(*shape, dtype=F32):
    return jax.ShapeDtypeStruct(shape, dtype)


def shards(
    tokens,
    segment_ids,
    cotangent,
    in_weight,
    dt_weight,
    out_weight,
    conv_params,
    gains,
    head_params,
    in_first,
    in_second,
    dt_first,
    dt_second,
    out_first,
    out_second,
    conv_first,
    conv_second,
    gain_first,
    gain_second,
    head_first,
    head_second,
):
    _, span, model = tokens.shape
    length = segment_ids.shape[1]
    ndp, nctx = lax.axis_size("dp"), lax.axis_size("ctx")
    d, c = lax.axis_index("dp"), lax.axis_index("ctx")
    heads = HEADS // nctx
    width = INNER // nctx
    maps = 2 * STATE
    wide = width + maps
    chunks = nctx
    rows_in = in_weight.shape[0]
    conv_cols = conv_params.shape[1]
    gain_len = gains.shape[0]
    dt_cols = dt_weight.shape[1]
    near = ndp == heads
    high = heads // 2
    block_in = model // heads
    tok = tokens[0]
    bits = jnp.stack([d & 1, d >> 1, c] if near else [0 * d, 0 * d, c]).astype(jnp.int32)
    perm = c ^ jnp.asarray([1, 3, 0, 2], jnp.int32)
    smem = pl.BlockSpec(memory_space=pltpu.SMEM)
    vmem = pl.BlockSpec(memory_space=pltpu.VMEM)
    anywhere = lambda pieces: [pl.BlockSpec(memory_space=pl.ANY)] * len(pieces)

    w1, g2 = pl.pallas_call(
        pack_kernel,
        in_specs=[smem] + [vmem] * 5,
        out_shape=[
            shape_of(high if near else 1, rows_in + 16, wide, dtype=BF16),
            shape_of(rows_in + (2 * HEAD_DIM if near else 0), width, dtype=BF16),
        ],
        scratch_shapes=[pltpu.VMEM((16, wide), F32)],
        compiler_params=params(),
        name="pack",
    )(bits, in_weight, out_weight, dt_weight, conv_params, gains)
    tok_sent, w1 = lax.optimization_barrier((tok, w1))
    tok_far = swap(tok_sent, "ctx", 2)
    if near:
        w1 = high_all_to_all(w1)
        w1, tok_far, tok_sent = lax.optimization_barrier((w1, tok_far, tok_sent))
        w1 = [w1, swap(w1, "dp", 1)]
        at_rows = jnp.stack([d & 1, 1 - (d & 1)]).astype(jnp.int32)
    else:
        w1 = [lax.all_gather(w1[0], "dp", axis=0)]
        at_rows = jnp.zeros((1,), jnp.int32)
    toks = [tok, swap(tok_sent, "ctx", 1), tok_far, swap(tok_far, "ctx", 1)]
    if near:
        g2 = [lax.all_gather(g2, "dp", axis=0)]
    else:
        wg = lax.all_gather(g2, "dp", axis=0, tiled=True).reshape(heads, block_in, width)
        wout = lax.all_gather(out_weight.astype(BF16), "dp", axis=0, tiled=True)
        wout = lax.dynamic_index_in_dim(wout.reshape(heads, nctx, HEAD_DIM, model), c, 1, False)
        g2 = [jnp.concatenate([wg, wout[:, :, :width], wout[:, :, width:]], axis=1)]
    at_g2 = jnp.zeros((1,), jnp.int32)
    cot_low, w1 = lax.optimization_barrier((cotangent[0].astype(BF16), w1))
    cots = gather_ctx(cot_low)

    ids = segment_ids[0]
    seg_col = jnp.pad(ids, (8, 8), constant_values=-1)[:, None]
    seg_row = segment_ids
    head_mine = lax.dynamic_index_in_dim(head_params.reshape(3, heads, nctx), c, 2, False)
    head_col = head_mine.T

    rows = lambda cols: pl.BlockSpec((span, cols), lambda i, *_: (i, 0))
    row_of = pl.BlockSpec((heads, span), lambda i, *_: (0, i))
    rows_at = lambda cols: pl.BlockSpec((span, cols), lambda i, p, *_: (p[i], 0))
    sent = pl.BlockSpec((1, span, model), lambda i, *_: (jnp.minimum(i, 1), 0, 0))
    kept = pl.BlockSpec((1, span, model), lambda i, *_: (jnp.maximum(i - 2, 0), 0, 0))
    shards_in = sum(piece.shape[0] for piece in w1)

    (
        hid, conv_mine, gain_pre, gain_mine, dt_mine, w1, mixed, conv_in, conv_sum, inner, raw,
        step_c, log_c, step_r, log_r, starts,
    ) = pl.pallas_call(
        scan_forward_kernel,
        grid_spec=pltpu.PrefetchScalarGridSpec(
            num_scalar_prefetch=2,
            grid=(chunks,),
            in_specs=[
                anywhere(toks),
                anywhere(w1),
                full((3, heads)),
                full((heads, 3)),
                full((length + 16, 1)),
                pl.BlockSpec((1, span), lambda i, *_: (0, i)),
            ],
            out_specs=[
                rows(model),
                full((8, wide)),
                full((1, model)),
                full((1, width)),
                full((heads, model)),
                full((model, wide)),
                rows(wide),
                rows(wide),
                rows(wide),
                rows(width),
                rows(heads),
                rows(heads),
                rows(heads),
                row_of,
                row_of,
                pl.BlockSpec((1, STATE, width), lambda i, *_: (i, 0, 0)),
            ],
            scratch_shapes=[
                pltpu.VMEM((span + 8, wide), F32),
                pltpu.VMEM((span + 8, 1), jnp.int32),
                pltpu.VMEM((STATE, width), F32),
                pltpu.VMEM((shards_in, 16, wide), BF16),
                pltpu.VMEM((nctx, span, model), F32),
                pltpu.VMEM((8, INNER + maps), F32),
                pltpu.VMEM((1, model + INNER), F32),
                pltpu.SemaphoreType.DMA((copies_of(w1, 2),)),
                pltpu.SemaphoreType.DMA((nctx,)),
            ],
        ),
        out_shape=[
            shape_of(length, model, dtype=BF16),
            shape_of(8, wide),
            shape_of(1, model),
            shape_of(1, width),
            shape_of(heads, model, dtype=BF16),
            shape_of(model, wide, dtype=BF16),
            shape_of(length, wide, dtype=BF16),
            shape_of(length, wide, dtype=BF16),
            shape_of(length, wide),
            shape_of(length, width),
            shape_of(length, heads),
            shape_of(length, heads),
            shape_of(length, heads),
            shape_of(heads, length),
            shape_of(heads, length),
            shape_of(chunks, STATE, width),
        ],
        compiler_params=params("arbitrary"),
        name="scan_forward",
    )(bits, at_rows, toks, w1, head_mine, head_col, seg_col, seg_row)

    wg, wout, cot_all, gate, normed_grad, stats = pl.pallas_call(
        gate_kernel,
        grid_spec=pltpu.PrefetchScalarGridSpec(
            num_scalar_prefetch=2,
            grid=(chunks,),
            in_specs=[rows(model), anywhere(g2), anywhere(cots), rows(width), full((1, width))],
            out_specs=[
                full((model, width)),
                full((width, model)),
                full((nctx, span, model)),
                rows(width),
                rows(width),
                pl.BlockSpec((8, span), lambda i, *_: (0, i)),
            ],
            scratch_shapes=[
                pltpu.SemaphoreType.DMA((copies_of(g2, 3),)),
                pltpu.SemaphoreType.DMA((nctx,)),
            ],
        ),
        out_shape=[
            shape_of(model, width, dtype=BF16),
            shape_of(width, model, dtype=BF16),
            shape_of(nctx, span, model, dtype=BF16),
            shape_of(length, width, dtype=BF16),
            shape_of(length, width),
            shape_of(8, length),
        ],
        compiler_params=params("arbitrary"),
        name="gate",
    )(bits, at_g2, hid, g2, cots, inner, gain_mine)
    stats = sum(fan_ctx(stats))

    early_rows = block_in + 2 * HEAD_DIM
    block_keep, block_send, early_keep, early_send, dy, dgate, col_sums = pl.pallas_call(
        norm_back_kernel,
        grid_spec=pltpu.PrefetchScalarGridSpec(
            num_scalar_prefetch=2,
            grid=(chunks,),
            in_specs=[
                rows_at(model),
                rows_at(width),
                rows_at(width),
                rows_at(width),
                pl.BlockSpec((8, span), lambda i, p, *_: (0, p[i])),
                full((1, width)),
                rows_at(width),
                full((width, model)),
                full((nctx, span, model)),
            ],
            out_specs=[
                kept,
                sent,
                full((high, early_rows, width)),
                full((high, early_rows, width)),
                rows_at(width),
                rows_at(width),
                full((8, width)),
            ],
            scratch_shapes=[pltpu.VMEM((width, model), F32), pltpu.VMEM((model, width), F32)],
        ),
        out_shape=[
            shape_of(2, span, model, dtype=BF16),
            shape_of(2, span, model, dtype=BF16),
            shape_of(high, early_rows, width, dtype=BF16),
            shape_of(high, early_rows, width, dtype=BF16),
            shape_of(length, width),
            shape_of(length, width, dtype=BF16),
            shape_of(8, width),
        ],
        compiler_params=params("arbitrary"),
        name="norm_back",
    )(perm, bits, hid, inner, gate, normed_grad, stats, gain_mine, mixed, wout, cot_all)
    block_came = swap(block_send, "ctx", 1)
    if near:
        early_came = swap(early_send, "dp", 1)

    back = lambda cols: pl.BlockSpec((span, cols), lambda i, *_: (chunks - 1 - i, 0))
    back_row = pl.BlockSpec((heads, span), lambda i, *_: (0, chunks - 1 - i))
    late_keep, late_send, dval, dbc, dstep, conv_grad, dt_grad, head_grad = pl.pallas_call(
        scan_back_kernel,
        grid_spec=pltpu.PrefetchScalarGridSpec(
            num_scalar_prefetch=2,
            grid=(chunks,),
            in_specs=[
                back(model),
                back(width),
                back(wide),
                back(width),
                back(width),
                back(heads),
                back(heads),
                back(heads),
                back_row,
                back_row,
                pl.BlockSpec((1, STATE, width), lambda i, *_: (chunks - 1 - i, 0, 0)),
                full((8, width)),
                full((3, heads)),
                full((length + 16, 1)),
                pl.BlockSpec((1, span), lambda i, *_: (0, chunks - 1 - i)),
            ],
            out_specs=[
                full((high, block_in, width)),
                full((high, block_in, width)),
                back(width),
                back(maps),
                back(heads),
                full((8, width)),
                full((heads, model)),
                full((8, heads)),
            ],
            scratch_shapes=[
                pltpu.VMEM((span + 8, width), F32),
                pltpu.VMEM((span + 16, 1), jnp.int32),
                pltpu.VMEM((STATE, width), F32),
                pltpu.VMEM((model, width), F32),
                pltpu.VMEM((span, width), F32),
            ],
        ),
        out_shape=[
            shape_of(high, block_in, width, dtype=BF16),
            shape_of(high, block_in, width, dtype=BF16),
            shape_of(length, width, dtype=BF16),
            shape_of(length, maps, dtype=BF16),
            shape_of(length, heads, dtype=BF16),
            shape_of(8, width),
            shape_of(heads, model),
            shape_of(8, heads),
        ],
        compiler_params=params("arbitrary"),
        name="scan_back",
    )(
        perm, bits, hid, dy, mixed, conv_in, conv_sum, raw, step_c, log_c, step_r, log_r, starts,
        conv_mine, head_mine, seg_col, seg_row,
    )
    dbc_came = swap(dbc, "ctx", 1)
    if near:
        late_came = swap(late_send, "dp", 1)
        early_parts = pl.pallas_call(
            pair_sum_kernel,
            grid=(high,),
            in_specs=[pl.BlockSpec((1, early_rows, width), lambda i: (i, 0, 0))] * 2,
            out_specs=pl.BlockSpec((1, early_rows, width), lambda i: (i, 0, 0)),
            out_shape=shape_of(high, early_rows, width, dtype=BF16),
            compiler_params=params("arbitrary"),
            name="pair_sum_early",
        )(early_keep, early_came)
        dval, early_parts = lax.optimization_barrier((dval, early_parts))
        early_parts = high_all_to_all(early_parts)
    dbc = (dbc.astype(F32) + dbc_came.astype(F32)).astype(BF16)
    dbc_far = swap(dbc, "ctx", 2)

    hidden_keep, hidden_send, gain_sum = pl.pallas_call(
        hidden_back_kernel,
        grid_spec=pltpu.PrefetchScalarGridSpec(
            num_scalar_prefetch=1,
            grid=(chunks,),
            in_specs=[
                rows_at(width),
                rows_at(width),
                rows_at(heads),
                full((model, width)),
                full((model, width)),
                full((heads, model)),
                rows_at(model),
                full((1, model)),
            ],
            out_specs=[kept, sent, full((8, model))],
        ),
        out_shape=[
            shape_of(2, span, model, dtype=BF16),
            shape_of(2, span, model, dtype=BF16),
            shape_of(8, model),
        ],
        compiler_params=params("arbitrary"),
        name="hidden_back",
    )(perm, dgate, dval, dstep, wg, w1, dt_mine, hid, gain_pre)
    hidden_came = swap(hidden_send, "ctx", 1)
    map_rows = 32 + 32 * high
    map_cols = lambda size: pl.BlockSpec((size, maps), lambda i: (0, width // maps))
    map_keep, map_send, hidden_own = pl.pallas_call(
        maps_back_kernel,
        grid=(1,),
        in_specs=[
            smem,
            full((length, maps)),
            full((length, maps)),
            map_cols(length),
            map_cols(length),
            map_cols(8),
            full((length + 16, 1)),
            full((length, model)),
            map_cols(model),
            full((1, model)),
            full((8, width)),
            full((8, width)),
            full((8, heads)),
            full((heads, model)),
            full((8, model)),
        ],
        out_specs=[full((map_rows, width)), full((map_rows, width)), full((span, model))],
        out_shape=[
            shape_of(map_rows, width, dtype=BF16),
            shape_of(map_rows, width, dtype=BF16),
            shape_of(span, model),
        ],
        scratch_shapes=[
            pltpu.VMEM((length + 8, maps), F32),
            pltpu.VMEM((model, maps), F32),
            pltpu.VMEM((length, maps), BF16),
            pltpu.VMEM((32, width), F32),
        ],
        compiler_params=params("arbitrary"),
        name="maps_back",
    )(
        bits,
        dbc,
        dbc_far,
        conv_sum,
        conv_in,
        conv_mine,
        seg_col,
        hid,
        w1,
        gain_pre,
        conv_grad,
        col_sums,
        head_grad,
        dt_grad,
        gain_sum,
    )

    map_send, hidden_came, block_came = lax.optimization_barrier((map_send, hidden_came, block_came))
    hidden_far = (hidden_keep[1].astype(F32) + hidden_came[1].astype(F32)).astype(BF16)
    hidden_far = swap(hidden_far, "ctx", 2)
    block_far = (block_keep[1].astype(F32) + block_came[1].astype(F32)).astype(BF16)
    mine = pl.BlockSpec((1, span, model), lambda i: (0, 0, 0))
    input_grad = pl.pallas_call(
        input_back_kernel,
        grid=(1,),
        in_specs=[mine, mine] + [full((span, model))] * 3 + [full((1, model)), full((span, model))],
        out_specs=full((span, model)),
        out_shape=shape_of(span, model),
        compiler_params=params("arbitrary"),
        name="input_back",
    )(hidden_keep, hidden_came, hidden_far, hidden_own, tok, gain_pre, cotangent[0])
    block_far = swap(block_far, "ctx", 2)
    block_output = tok + (
        block_keep[0].astype(F32) + block_came[0].astype(F32) + block_far.astype(F32)
    )

    late_rows = block_in + 64
    if near:
        map_came = swap(map_send, "dp", 1)
        late_parts = pl.pallas_call(
            pair_sum_late_kernel,
            out_shape=shape_of(high, late_rows, width, dtype=BF16),
            compiler_params=params(),
            name="pair_sum_late",
        )(late_keep, late_came, map_keep, map_came)
        late_parts = high_all_to_all(late_parts)
        late_parts, input_grad, block_output = lax.optimization_barrier(
            (late_parts, input_grad, block_output)
        )
        early = jnp.sum(early_parts.astype(F32), axis=0).astype(BF16)
        late = pl.pallas_call(
            sum_late_kernel,
            out_shape=shape_of(late_rows, width, dtype=BF16),
            compiler_params=params(),
            name="sum_late",
        )(late_parts)
        early, late = fan_ctx(early), fan_ctx(late)
        row_block = lambda ref_rows, cols: pl.BlockSpec((ref_rows, cols), lambda i, *_: (i, 0))
        in_block = row_block(rows_in // nctx, in_weight.shape[1])
        out_block = row_block(out_weight.shape[0] // nctx, model)
        early_spec = [full((early_rows, width))] * nctx
        early_scratch = pltpu.VMEM((nctx, early_rows, width), BF16)
        out_new = pl.pallas_call(
            adam_out_kernel,
            grid_spec=pltpu.PrefetchScalarGridSpec(
                num_scalar_prefetch=1,
                grid=(nctx,),
                in_specs=[out_block] * 3 + [early_spec],
                out_specs=[out_block] * 3,
                scratch_shapes=[early_scratch],
            ),
            out_shape=[shape_of(*out_weight.shape)] * 3,
            compiler_params=params("arbitrary"),
            name="adam_out",
        )(bits, out_weight, out_first, out_second, early)
        in_new = pl.pallas_call(
            adam_in_kernel,
            grid_spec=pltpu.PrefetchScalarGridSpec(
                num_scalar_prefetch=1,
                grid=(nctx,),
                in_specs=[in_block] * 3 + [early_spec, [full((late_rows, width))] * nctx],
                out_specs=[in_block] * 3,
                scratch_shapes=[early_scratch, pltpu.VMEM((nctx, late_rows, width), BF16)],
            ),
            out_shape=[shape_of(*in_weight.shape)] * 3,
            compiler_params=params("arbitrary"),
            name="adam_in",
        )(bits, in_weight, in_first, in_second, early, late)
        in_new, out_new = tuple(in_new), tuple(out_new)
        small = jnp.stack([part[block_in : block_in + 32] for part in late])[c ^ jnp.arange(nctx)]
        small = small.astype(F32)
    else:
        blocks = lambda keep, send: jnp.stack([keep, send], axis=1).reshape((heads,) + keep.shape[1:])
        early = blocks(early_keep, early_send).astype(F32)
        late = blocks(late_keep, late_send).astype(F32)
        part = lambda value: value[32:].reshape(high, 32, width)[:, :, :maps]
        map_blocks = blocks(part(map_keep), part(map_send)).astype(F32)

        def total(value):
            return lax.psum_scatter(value, "dp", scatter_dimension=0, tiled=True)

        def spaced(value):
            place_at = (jnp.arange(nctx) == c).astype(F32).reshape((1, nctx, 1, 1))
            value = value[:, None] * place_at
            return lax.psum(total(value.reshape(-1, value.shape[-1])), "ctx")

        def by_head(value):
            value = lax.all_gather(total(value.reshape(model, width)), "ctx", axis=0)
            value = value.reshape(nctx, rows_in, heads, HEAD_DIM)
            return jnp.transpose(value, (1, 2, 0, 3)).reshape(rows_in, INNER)

        in_total = jnp.concatenate(
            [by_head(early[:, :block_in]), by_head(late), spaced(map_blocks)], axis=1
        )
        out_total = spaced(
            jnp.concatenate([early[:, block_in : block_in + HEAD_DIM], early[:, block_in + HEAD_DIM :]], axis=2)
        )
        in_new = adam_step(in_weight, in_first, in_second, in_total, 0.03, WEIGHT_DECAY)
        out_new = adam_step(out_weight, out_first, out_second, out_total, 0.02, WEIGHT_DECAY)
        small = lax.all_gather(lax.psum(map_keep[:32].astype(F32), "dp"), "ctx", axis=0)

    def in_order(value):
        return jnp.swapaxes(value.reshape(nctx, -1, heads, HEAD_DIM), 0, 1).swapaxes(1, 2).reshape(-1, INNER)

    columns = in_order(small[:, : CONV + 2])
    conv_total = jnp.concatenate([columns[: CONV + 1], small[0, 8 : 8 + CONV + 1, :maps]], axis=1)
    conv_total = lax.dynamic_slice_in_dim(conv_total, d * conv_cols, conv_cols, 1)
    dt_total = small[:, 16:32].reshape(nctx, 2, heads, width)
    dt_total = jnp.transpose(dt_total, (2, 0, 1, 3)).reshape(HEADS, model)
    dt_total = lax.dynamic_slice_in_dim(dt_total, d * dt_cols, dt_cols, 1)
    pre_total = jnp.sum(small[:, 13:15], axis=0).reshape(-1)
    gain_total = jnp.concatenate([pre_total, columns[CONV + 1]])
    gain_total = lax.dynamic_slice_in_dim(gain_total, d * gain_len, gain_len, 0)
    head_row = small[:, 7] + small[:, 15]
    head_total = jnp.stack(
        [
            head_row[:, :heads].T.reshape(-1),
            head_row[:, 128 : 128 + heads].T.reshape(-1),
            jnp.sum(small[:, CONV + 2].reshape(nctx, heads, HEAD_DIM), axis=2).T.reshape(-1),
        ]
    )

    dt_new = adam_step(dt_weight, dt_first, dt_second, dt_total, 0.03, WEIGHT_DECAY)
    conv_new = adam_step(conv_params, conv_first, conv_second, conv_total, 0.3, 0.0)
    gain_new = adam_step(gains, gain_first, gain_second, gain_total, 0.5, 0.0)
    head_new = adam_step(head_params, head_first, head_second, head_total, 2.0, 0.0)
    return (block_output[None], input_grad[None]) + in_new + dt_new + out_new + conv_new + gain_new + head_new


def solution(mesh):
    tokens, rows, cols = P("dp", "ctx", None), P("dp", None), P(None, "dp")
    return jax.shard_map(
        shards,
        mesh=mesh,
        in_specs=(tokens, rows, tokens, rows, cols, rows, cols, P("dp"), P())
        + (rows, rows, cols, cols, rows, rows, cols, cols, P("dp"), P("dp"), P(), P()),
        out_specs=(tokens, tokens)
        + (rows,) * 3
        + (cols,) * 3
        + (rows,) * 3
        + (cols,) * 3
        + (P("dp"),) * 3
        + (P(),) * 3,
        check_vma=False,
    )
```

```python
import functools

import jax
import jax.numpy as jnp
from jax import lax
from jax.experimental import pallas as pl
from jax.experimental.pallas import tpu as pltpu
from jax.sharding import PartitionSpec as P

INNER = 2048
HEADS = 32
HEAD_DIM = 64
STATE = 128
CONV = 4
STEP = 10

F32 = jnp.float32
BF16 = jnp.bfloat16
HIGHEST = lax.Precision.HIGHEST
NORM_EPS = 1e-05
BETA_ONE = 0.9
BETA_TWO = 0.95
ADAM_EPS = 1e-08
WEIGHT_DECAY = 0.1
VMEM_LIMIT = 56 * 1024 * 1024


def nn(a, b, precision=None):
    return lax.dot_general(
        a, b, (((1,), (0,)), ((), ())), precision=precision, preferred_element_type=F32
    )


def nt(a, b, precision=None):
    return lax.dot_general(
        a, b, (((1,), (1,)), ((), ())), precision=precision, preferred_element_type=F32
    )


def tn(a, b, precision=None):
    return lax.dot_general(
        a, b, (((0,), (0,)), ((), ())), precision=precision, preferred_element_type=F32
    )


def halves(value):
    high = value.astype(BF16)
    return high, (value - high.astype(F32)).astype(BF16)


def spread(value, width):
    heads = value.shape[1]
    row = lax.broadcasted_iota(jnp.int32, (heads, width), 0)
    col = lax.broadcasted_iota(jnp.int32, (heads, width), 1)
    table = jnp.where(col // HEAD_DIM == row, 1.0, 0.0).astype(BF16)
    high, low = halves(value)
    return nn(high, table) + nn(low, table)


def gather_heads(value, heads):
    width = value.shape[1]
    row = lax.broadcasted_iota(jnp.int32, (width, heads), 0)
    col = lax.broadcasted_iota(jnp.int32, (width, heads), 1)
    table = jnp.where(row // HEAD_DIM == col, 1.0, 0.0).astype(BF16)
    high, low = halves(value)
    return nn(high, table) + nn(low, table)


def softplus(value):
    return jnp.maximum(value, 0.0) + jnp.log1p(jnp.exp(-jnp.abs(value)))


def sigmoid(value):
    return 1.0 / (1.0 + jnp.exp(-value))


def silu_grad(value):
    sig = sigmoid(value)
    return sig * (1.0 + value * (1.0 - sig))


def diagonal(size):
    row = lax.broadcasted_iota(jnp.int32, (size, size), 0)
    return row == lax.broadcasted_iota(jnp.int32, (size, size), 1)


def triangle(size, lower):
    row = lax.broadcasted_iota(jnp.int32, (size, size), 0)
    col = lax.broadcasted_iota(jnp.int32, (size, size), 1)
    keep = row >= col if lower else row <= col
    return jnp.where(keep, 1.0, 0.0).astype(F32)


def params(*semantics):
    return pltpu.CompilerParams(
        dimension_semantics=semantics or None, vmem_limit_bytes=VMEM_LIMIT
    )


def place(pieces, at_ref, stride, sems, targets):
    copies = []
    for index, piece in enumerate(pieces):
        for block in range(piece.shape[0]):
            for first, rows, target in targets:
                copies.append(
                    pltpu.make_async_copy(
                        piece.at[block, first : first + rows],
                        target(at_ref[index] + stride * block),
                        sems.at[len(copies)],
                    )
                )
    for copy in copies:
        copy.start()
    return copies


def copies_of(pieces, targets):
    return sum(piece.shape[0] for piece in pieces) * targets


def rows_of(ref, rows):
    return lambda at: ref.at[pl.ds(pl.multiple_of(at * rows, 16), rows)]


def part_of(block, own_bit, keep_ref, send_ref, first=0):
    for at in range(keep_ref.shape[0]):
        low, high = block(2 * at).astype(BF16), block(2 * at + 1).astype(BF16)
        rows = slice(first, first + low.shape[0])
        keep_ref[at, rows] = jnp.where(own_bit == 0, low, high)
        send_ref[at, rows] = jnp.where(own_bit == 0, high, low)


def pick_heads(ref, base, ctx, heads):
    first = pl.multiple_of(base + (ctx >> 1) * 2 * HEAD_DIM, 2 * HEAD_DIM)
    wide = ref[:, pl.ds(first, 2 * HEAD_DIM)]
    low = lax.broadcasted_iota(jnp.int32, wide.shape, 1) < HEAD_DIM
    odd = (ctx & 1) == 1
    out = []
    for pair in range(heads // 2):
        parts = []
        for head in (2 * pair, 2 * pair + 1):
            first = pl.multiple_of(base + head * 4 * HEAD_DIM + (ctx >> 1) * 2 * HEAD_DIM, 2 * HEAD_DIM)
            parts.append(ref[:, pl.ds(first, 2 * HEAD_DIM)])
        even = jnp.where(low, parts[0], pltpu.roll(parts[1], HEAD_DIM, 1))
        other = jnp.where(low, pltpu.roll(parts[0], HEAD_DIM, 1), parts[1])
        out.append(jnp.where(odd, other, even))
    return out


def pack_kernel(here_ref, win_ref, wout_ref, dt_ref, conv_ref, gain_ref, w1_ref, g2_ref, tmp_ref):
    ctx = here_ref[2]
    rows = win_ref.shape[0]
    heads = HEADS // 4
    width = heads * HEAD_DIM
    copies = range(w1_ref.shape[0])
    for at, part in enumerate(pick_heads(win_ref, INNER, ctx, heads)):
        part = part.astype(BF16)
        for copy in copies:
            w1_ref[copy, 0:rows, at * 128 : (at + 1) * 128] = part
    part = win_ref[:, 2 * INNER :].astype(BF16)
    for copy in copies:
        w1_ref[copy, 0:rows, width:] = part
    tmp_ref[...] = jnp.zeros_like(tmp_ref)
    row = lax.broadcasted_iota(jnp.int32, (heads, HEADS), 0)
    col = lax.broadcasted_iota(jnp.int32, (heads, HEADS), 1)
    table = jnp.where(col == 4 * row + ctx, 1.0, 0.0).astype(BF16)
    tmp_ref[0:heads, 384 : 384 + dt_ref.shape[1]] = nn(table, dt_ref[...].astype(BF16))
    tmp_ref[8 : 8 + CONV + 1, 0 : conv_ref.shape[1]] = conv_ref[...]
    tmp_ref[8 + CONV + 1 : 8 + CONV + 2, 0 : gain_ref.shape[0]] = gain_ref[...].reshape(1, -1)
    for copy in copies:
        w1_ref[copy, rows : rows + 16, :] = tmp_ref[...].astype(BF16)
    copies = range(g2_ref.shape[0])
    for at, part in enumerate(pick_heads(win_ref, 0, ctx, heads)):
        part = part.astype(BF16)
        for copy in copies:
            g2_ref[copy, 0:rows, at * 128 : (at + 1) * 128] = part
    if g2_ref.shape[1] > rows:
        some = wout_ref.shape[0] // 4
        mine = wout_ref[pl.ds(pl.multiple_of(ctx * some, 8), some), :].astype(BF16)
        for copy in copies:
            g2_ref[copy, rows : rows + some] = mine[:, :width]
            g2_ref[copy, rows + some : rows + 2 * some] = mine[:, width:]


def scan_forward_kernel(
    here_ref,
    at_ref,
    tok_pieces,
    w1_pieces,
    hrow_ref,
    hcol_ref,
    segc_ref,
    segr_ref,
    hid_ref,
    conv_ref,
    gpre_ref,
    gmine_ref,
    wdt_ref,
    w1_ref,
    mixed_ref,
    convin_ref,
    convsum_ref,
    inner_ref,
    raw_ref,
    stepc_ref,
    logc_ref,
    stepr_ref,
    logr_ref,
    start_ref,
    ext_ref,
    seg_ref,
    state_ref,
    small_ref,
    tok_ref,
    conv_all,
    gain_all,
    sems,
    tok_sems,
):
    step = pl.program_id(0)
    span, model = hid_ref.shape
    heads = wdt_ref.shape[0]
    width = heads * HEAD_DIM
    shards = small_ref.shape[0]
    rows = model // shards

    @pl.when(step == 0)
    def _():
        copies = place(
            w1_pieces,
            at_ref,
            len(w1_pieces),
            sems,
            [(0, rows, rows_of(w1_ref, rows)), (rows, 16, lambda at: small_ref.at[at])],
        )
        tokens = [
            pltpu.make_async_copy(piece, tok_ref.at[here_ref[2] ^ index], tok_sems.at[index])
            for index, piece in enumerate(tok_pieces)
        ]
        for copy in tokens:
            copy.start()
        ext_ref[0:8] = jnp.zeros((8, ext_ref.shape[1]), F32)
        state_ref[...] = jnp.zeros_like(state_ref)
        conv_all[...] = jnp.zeros_like(conv_all)
        for copy in copies:
            copy.wait()
        conv_cols = conv_all.shape[1] // shards
        gain_len = gain_all.shape[1] // shards
        for shard in range(shards):
            small = small_ref[shard].astype(F32)
            wdt_ref[:, shard * rows : (shard + 1) * rows] = small[0:8, 384 : 384 + rows].astype(BF16)
            conv_all[0 : CONV + 1, shard * conv_cols : (shard + 1) * conv_cols] = small[
                8 : 8 + CONV + 1, :conv_cols
            ]
            gain_all[:, shard * gain_len : (shard + 1) * gain_len] = small[13:14, :gain_len]
        for at, part in enumerate(pick_heads(conv_all, 0, here_ref[2], heads)):
            conv_ref[:, at * 128 : (at + 1) * 128] = part
        conv_ref[:, width:] = conv_all[:, INNER:]
        gpre_ref[...] = gain_all[:, :model]
        for at, part in enumerate(pick_heads(gain_all, model, here_ref[2], heads)):
            gmine_ref[:, at * 128 : (at + 1) * 128] = part
        for copy in tokens:
            copy.wait()

    tok = tok_ref[step]
    scale = lax.rsqrt(jnp.mean(tok * tok, axis=-1, keepdims=True) + NORM_EPS)
    hid = (tok * scale * gpre_ref[...]).astype(BF16)
    hid_ref[...] = hid
    proj = nn(hid, w1_ref[...]).astype(BF16)
    convin_ref[...] = proj
    ext_ref[8 : 8 + span] = proj.astype(F32)
    seg_ref[...] = segc_ref[pl.ds(pl.multiple_of(step * span, 8), span + 8), :]
    seg_here = seg_ref[8 : 8 + span]
    total = conv_ref[CONV : CONV + 1]
    for tap in range(CONV):
        at = 8 - (CONV - 1) + tap
        same = seg_ref[at : at + span] == seg_here
        total = total + conv_ref[tap : tap + 1] * jnp.where(same, ext_ref[at : at + span], 0.0)
    ext_ref[0:8] = ext_ref[span : span + 8]
    convsum_ref[...] = total
    mixed = (total * sigmoid(total)).astype(BF16)
    mixed_ref[...] = mixed

    raw_c = nt(hid, wdt_ref[...]) + hrow_ref[1:2]
    raw_r = nt(wdt_ref[...], hid) + hcol_ref[:, 1:2]
    step_c = softplus(raw_c)
    step_r = softplus(raw_r)
    log_c = nn(triangle(span, True), -step_c * jnp.exp(hrow_ref[0:1]), HIGHEST)
    log_r = nn(-step_r * jnp.exp(hcol_ref[:, 0:1]), triangle(span, False), HIGHEST)
    raw_ref[...] = raw_c
    stepc_ref[...] = step_c
    logc_ref[...] = log_c
    stepr_ref[...] = step_r
    logr_ref[...] = log_r

    values = mixed[:, :width]
    write = mixed[:, width : width + STATE]
    read = mixed[:, width + STATE :]
    row = lax.broadcasted_iota(jnp.int32, (span, span), 0)
    col = lax.broadcasted_iota(jnp.int32, (span, span), 1)
    visible = (seg_here == segr_ref[...]) & (row >= col)
    scores = jnp.where(visible, nt(read, write), 0.0)
    lane = lax.broadcasted_iota(jnp.int32, (span, 2 * HEAD_DIM), 1)

    seg_prev = seg_ref[7:8]
    seg_last = seg_ref[span + 7 : span + 8]
    last = log_c[span - 1 : span]
    enter = jnp.where(seg_here == seg_prev, jnp.exp(log_c), 0.0)
    tail = jnp.where(seg_here == seg_last, jnp.exp(last - log_c), 0.0) * step_c
    keep = jnp.where(seg_last == seg_prev, jnp.exp(last), 0.0)
    state = state_ref[...]
    start_ref[0] = state
    values_f = values.astype(F32)
    base = spread(enter, width) * nn(read, state.astype(BF16)) + spread(
        hrow_ref[2:3] + jnp.zeros((8, heads), F32), width
    )[0:1] * values_f
    for pair in range(heads // 2):
        lanes = slice(pair * 2 * HEAD_DIM, (pair + 1) * 2 * HEAD_DIM)
        pieces = []
        for head in (2 * pair, 2 * pair + 1):
            gap = jnp.minimum(log_c[:, head : head + 1] - log_r[head : head + 1], 0.0)
            weights = scores * jnp.exp(gap) * step_r[head : head + 1]
            pieces.append(nn(weights.astype(BF16), values[:, lanes]))
        inner_ref[:, lanes] = base[:, lanes] + jnp.where(lane < HEAD_DIM, pieces[0], pieces[1])
    moved = (spread(tail, width) * values_f).astype(BF16)
    state_ref[...] = spread(keep + jnp.zeros((8, heads), F32), width)[0:1] * state + tn(
        write, moved
    )


def gate_kernel(
    here_ref,
    at_ref,
    hid_ref,
    g2_pieces,
    cot_pieces,
    inner_ref,
    gain_ref,
    wg_ref,
    wout_ref,
    cot_ref,
    gate_ref,
    ng_ref,
    stat_ref,
    sems,
    cot_sems,
):
    step = pl.program_id(0)
    rows = wg_ref.shape[0] // (wout_ref.shape[0] // HEAD_DIM)
    width = wg_ref.shape[1]

    @pl.when(step == 0)
    def _():
        some = rows_of(wout_ref, HEAD_DIM)
        copies = place(
            g2_pieces,
            at_ref,
            len(g2_pieces),
            sems,
            [
                (0, rows, rows_of(wg_ref, rows)),
                (rows, HEAD_DIM, lambda at: some(at).at[:, 0:width]),
                (rows + HEAD_DIM, HEAD_DIM, lambda at: some(at).at[:, width : 2 * width]),
            ],
        )
        cots = [
            pltpu.make_async_copy(piece, cot_ref.at[here_ref[2] ^ index], cot_sems.at[index])
            for index, piece in enumerate(cot_pieces)
        ]
        for copy in cots:
            copy.start()
        for copy in copies + cots:
            copy.wait()

    gate = nn(hid_ref[...], wg_ref[...]).astype(BF16)
    gate_ref[...] = gate
    gate = gate.astype(F32)
    grad = nt(cot_ref[step], wout_ref[...])
    ng_ref[...] = grad
    gated = inner_ref[...] * (gate * sigmoid(gate))
    squares = jnp.sum(gated * gated, axis=1, keepdims=True)
    crossed = jnp.sum(gated * (grad * gain_ref[...]), axis=1, keepdims=True)
    same = diagonal(gated.shape[0])
    squares = jnp.sum(jnp.where(same, squares, 0.0), axis=0, keepdims=True)
    crossed = jnp.sum(jnp.where(same, crossed, 0.0), axis=0, keepdims=True)
    at = lax.broadcasted_iota(jnp.int32, stat_ref.shape, 0)
    stat_ref[...] = jnp.where(at == 0, squares, crossed)


def norm_back_kernel(
    perm_ref,
    here_ref,
    hid_ref,
    inner_ref,
    gate_ref,
    ng_ref,
    stat_ref,
    gain_ref,
    mixed_ref,
    wout_ref,
    cot_ref,
    bkeep_ref,
    bsend_ref,
    keep_ref,
    send_ref,
    dy_ref,
    dgate_ref,
    sums_ref,
    outacc_ref,
    inacc_ref,
):
    step = pl.program_id(0)
    span, width = inner_ref.shape

    @pl.when(step == 0)
    def _():
        outacc_ref[...] = jnp.zeros_like(outacc_ref)
        inacc_ref[...] = jnp.zeros_like(inacc_ref)
        sums_ref[...] = jnp.zeros_like(sums_ref)

    same = diagonal(span)
    squares = jnp.sum(jnp.where(same, stat_ref[0:1], 0.0), axis=1, keepdims=True)
    cross = jnp.sum(jnp.where(same, stat_ref[1:2], 0.0), axis=1, keepdims=True)
    inv = lax.rsqrt(squares * (1.0 / INNER) + NORM_EPS)
    gate = gate_ref[...].astype(F32)
    sig = sigmoid(gate)
    silu = gate * sig
    inner = inner_ref[...]
    gated = inner * silu
    unit = gated * inv
    normed = (unit * gain_ref[...]).astype(BF16)
    cot = cot_ref[perm_ref[step]]
    block = nn(normed, wout_ref[...]).astype(BF16)

    @pl.when(step < 2)
    def _():
        bsend_ref[0] = block

    @pl.when(step >= 2)
    def _():
        bkeep_ref[0] = block

    outacc_ref[...] += tn(normed, cot)
    grad = ng_ref[...]
    dgated = inv * (grad * gain_ref[...] - unit * (cross * inv * (1.0 / INNER)))
    dy = dgated * silu
    dy_ref[...] = dy
    dgate = (dgated * inner * (sig * (1.0 + gate * (1.0 - sig)))).astype(BF16)
    dgate_ref[...] = dgate
    inacc_ref[...] += tn(hid_ref[...], dgate)
    gain_sum = jnp.sum(grad * unit, axis=0, keepdims=True)
    skip_sum = jnp.sum(dy * mixed_ref[...].astype(F32), axis=0, keepdims=True)
    at = lax.broadcasted_iota(jnp.int32, (8, width), 0)
    sums_ref[...] += jnp.where(at == 0, gain_sum, jnp.where(at == 1, skip_sum, 0.0))

    @pl.when(step == pl.num_programs(0) - 1)
    def _():
        own = here_ref[0]
        rows = inacc_ref.shape[0] // (2 * keep_ref.shape[0])
        part_of(lambda at: inacc_ref[at * rows : (at + 1) * rows], own, keep_ref, send_ref)
        outs = lambda at: outacc_ref[at * HEAD_DIM : (at + 1) * HEAD_DIM]
        part_of(lambda at: outs(at)[:, :width], own, keep_ref, send_ref, rows)
        part_of(lambda at: outs(at)[:, width:], own, keep_ref, send_ref, rows + HEAD_DIM)


def scan_back_kernel(
    perm_ref,
    here_ref,
    hid_ref,
    dy_ref,
    mixed_ref,
    convin_ref,
    convsum_ref,
    raw_ref,
    stepc_ref,
    logc_ref,
    stepr_ref,
    logr_ref,
    start_ref,
    conv_ref,
    hrow_ref,
    segc_ref,
    segr_ref,
    keep_ref,
    send_ref,
    dval_ref,
    dbc_ref,
    dstep_ref,
    convg_ref,
    dtg_ref,
    headg_ref,
    ext_ref,
    seg_ref,
    grad_ref,
    inacc_ref,
    dx_ref,
):
    step = pl.program_id(0)
    chunk = pl.num_programs(0) - 1 - step
    span = hid_ref.shape[0]
    heads = stepc_ref.shape[1]
    width = heads * HEAD_DIM

    @pl.when(step == 0)
    def _():
        ext_ref[span : span + 8] = jnp.zeros((8, width), F32)
        grad_ref[...] = jnp.zeros_like(grad_ref)
        inacc_ref[...] = jnp.zeros_like(inacc_ref)
        convg_ref[...] = jnp.zeros_like(convg_ref)
        dtg_ref[...] = jnp.zeros_like(dtg_ref)
        headg_ref[...] = jnp.zeros_like(headg_ref)

    seg_ref[...] = segc_ref[pl.ds(pl.multiple_of(chunk * span, 8), span + 16), :]
    seg_here = seg_ref[8 : 8 + span]
    seg_prev = seg_ref[7:8]
    seg_last = seg_ref[span + 7 : span + 8]
    mixed = mixed_ref[...]
    values = mixed[:, :width]
    write = mixed[:, width : width + STATE]
    read = mixed[:, width + STATE :]
    values_f = values.astype(F32)
    dy = dy_ref[...]
    dy_low = dy.astype(BF16)
    step_c = stepc_ref[...]
    log_c = logc_ref[...]
    step_r = stepr_ref[...]
    log_r = logr_ref[...]
    last = log_c[span - 1 : span]
    enter = jnp.where(seg_here == seg_prev, jnp.exp(log_c), 0.0)
    tail_raw = jnp.where(seg_here == seg_last, jnp.exp(last - log_c), 0.0)
    tail = tail_raw * step_c
    keep = jnp.where(seg_last == seg_prev, jnp.exp(last), 0.0)
    enter_w = spread(enter, width)
    tail_w = spread(tail, width)
    wide = spread(
        jnp.concatenate([hrow_ref[2:3] + jnp.zeros((8, heads), F32), keep + jnp.zeros((8, heads), F32)], axis=0),
        width,
    )
    skip_w = wide[0:1]
    keep_w = wide[8:9]
    state = start_ref[0]
    state_low = state.astype(BF16)
    later = grad_ref[...]
    later_low = later.astype(BF16)

    row = lax.broadcasted_iota(jnp.int32, (span, span), 0)
    col = lax.broadcasted_iota(jnp.int32, (span, span), 1)
    visible = (seg_here == segr_ref[...]) & (row >= col)
    scores = jnp.where(visible, nt(read, write), 0.0)
    lane = lax.broadcasted_iota(jnp.int32, (span, 2 * HEAD_DIM), 1)
    head_at = lax.broadcasted_iota(jnp.int32, (8, span), 0)
    lane_at = lax.broadcasted_iota(jnp.int32, (span, heads), 1)

    entered = enter_w * dy
    entered_low = entered.astype(BF16)
    inter = enter_w * nn(read, state_low)
    from_later = nn(write, later_low)
    moved_low = (tail_w * values_f).astype(BF16)
    dread = nt(entered_low, state_low)
    dwrite = nt(moved_low, later_low)
    dlog_c = gather_heads(dy * inter, heads)
    tail_dot = gather_heads(values_f * from_later, heads)
    dlog_c = dlog_c - tail_dot * tail
    dstep_c = tail_dot * tail_raw
    carried = gather_heads(jnp.sum(later * state, axis=0, keepdims=True) + jnp.zeros((8, width), F32), heads)[0:1]
    at_last = lax.broadcasted_iota(jnp.int32, (span, heads), 0) == span - 1
    dlog_c = dlog_c + jnp.where(
        at_last, jnp.sum(tail_dot * tail, axis=0, keepdims=True) + keep * carried, 0.0
    )
    grad_ref[...] = keep_w * later + tn(read, entered_low)
    dx_ref[...] = tail_w * from_later + skip_w * dy

    dscores = jnp.zeros((span, span), F32)
    dstep_r = jnp.zeros((8, span), F32)
    for pair in range(heads // 2):
        lanes = slice(pair * 2 * HEAD_DIM, (pair + 1) * 2 * HEAD_DIM)
        dy_pair = dy_low[:, lanes]
        pieces = []
        for head in (2 * pair, 2 * pair + 1):
            mine = lane < HEAD_DIM if head % 2 == 0 else lane >= HEAD_DIM
            gap = jnp.minimum(log_c[:, head : head + 1] - log_r[head : head + 1], 0.0)
            decay = jnp.exp(gap)
            outer = nt(jnp.where(mine, dy_pair, jnp.zeros_like(dy_pair)), values[:, lanes])
            fade = decay * step_r[head : head + 1]
            dscores = dscores + outer * fade
            flow = outer * scores
            base = flow * decay
            dstep_r = dstep_r + jnp.where(head_at == head, jnp.sum(base, axis=0, keepdims=True), 0.0)
            dlog_c = dlog_c + jnp.where(
                lane_at == head, jnp.sum(flow * fade, axis=1, keepdims=True), 0.0
            )
            pieces.append(tn((scores * fade).astype(BF16), dy_pair))
        dx_ref[:, lanes] += jnp.where(lane < HEAD_DIM, pieces[0], pieces[1])
    dscores = jnp.where(visible, dscores, 0.0).astype(BF16)
    dread = dread + nn(dscores, write)
    dwrite = dwrite + tn(dscores, read)
    dbc_ref[:, :STATE] = dwrite.astype(BF16)
    dbc_ref[:, STATE:] = dread.astype(BF16)

    upper = triangle(span, False)
    eye = jnp.where(row == col, 1.0, 0.0).astype(F32)
    dalpha = nn(upper, dlog_c, HIGHEST) - nt(upper, dstep_r * step_r, HIGHEST)[:, :heads]
    dstep = dstep_c + nt(eye, dstep_r, HIGHEST)[:, :heads]
    rate = jnp.exp(hrow_ref[0:1])
    draw = (dstep - rate * dalpha) * sigmoid(raw_ref[...])
    draw_low = draw.astype(BF16)
    dstep_ref[...] = draw_low
    hid = hid_ref[...]
    dtg_ref[...] += tn(draw_low, hid)
    rate_sum = jnp.sum(-dalpha * step_c * rate, axis=0, keepdims=True)
    bias_sum = jnp.sum(draw, axis=0, keepdims=True)
    at = lax.broadcasted_iota(jnp.int32, (8, heads), 0)
    headg_ref[...] += jnp.where(at == 0, rate_sum, jnp.where(at == 1, bias_sum, 0.0))

    ext_ref[0:span] = dx_ref[...] * silu_grad(convsum_ref[...])
    back = jnp.zeros((span, width), F32)
    conv_in = convin_ref[...].astype(F32)
    at = lax.broadcasted_iota(jnp.int32, (8, width), 0)
    sums = jnp.where(at == CONV, jnp.sum(ext_ref[0:span], axis=0, keepdims=True), 0.0)
    for tap in range(CONV):
        ahead = CONV - 1 - tap
        same = seg_ref[8 + ahead : 8 + ahead + span] == seg_here
        term = jnp.where(same, ext_ref[ahead : ahead + span], 0.0)
        back = back + conv_ref[tap : tap + 1] * term
        sums = sums + jnp.where(at == tap, jnp.sum(conv_in * term, axis=0, keepdims=True), 0.0)
    convg_ref[...] += sums
    ext_ref[span : span + 8] = ext_ref[0:8]
    dval = back.astype(BF16)
    dval_ref[...] = dval
    inacc_ref[...] += tn(hid, dval)

    @pl.when(step == pl.num_programs(0) - 1)
    def _():
        rows = inacc_ref.shape[0] // (2 * keep_ref.shape[0])
        part_of(lambda at: inacc_ref[at * rows : (at + 1) * rows], here_ref[0], keep_ref, send_ref)


def hidden_back_kernel(
    perm_ref,
    dgate_ref,
    dval_ref,
    dstep_ref,
    wg_ref,
    wv_ref,
    wdt_ref,
    hid_ref,
    gain_ref,
    keep_ref,
    send_ref,
    gsum_ref,
):
    @pl.when(pl.program_id(0) == 0)
    def _():
        gsum_ref[...] = jnp.zeros_like(gsum_ref)

    total = nt(dgate_ref[...], wg_ref[...]) + nt(dval_ref[...], wv_ref[...])
    total = total + nn(dstep_ref[...], wdt_ref[...])
    step = pl.program_id(0)

    @pl.when(step < 2)
    def _():
        send_ref[0] = total.astype(BF16)

    @pl.when(step >= 2)
    def _():
        keep_ref[0] = total.astype(BF16)

    unit = hid_ref[...].astype(F32) / gain_ref[...]
    gsum_ref[...] += jnp.sum(total * unit, axis=0, keepdims=True) + jnp.zeros(gsum_ref.shape, F32)


def maps_back_kernel(
    here_ref,
    dbc_ref,
    dbcfar_ref,
    convsum_ref,
    convin_ref,
    conv_ref,
    segc_ref,
    hid_ref,
    w1_ref,
    gain_ref,
    convg_ref,
    sums_ref,
    headg_ref,
    dtg_ref,
    gall_ref,
    keep_ref,
    send_ref,
    own_ref,
    ext_ref,
    acc_ref,
    dmap_ref,
    small_ref,
):
    size, width = dmap_ref.shape
    total = dbc_ref[...].astype(F32) + dbcfar_ref[...].astype(F32)
    ext_ref[0:size] = total * silu_grad(convsum_ref[...])
    ext_ref[size : size + 8] = jnp.zeros((8, width), F32)
    back = jnp.zeros((size, width), F32)
    conv_in = convin_ref[...].astype(F32)
    at = lax.broadcasted_iota(jnp.int32, (8, width), 0)
    sums = jnp.where(at == CONV, jnp.sum(ext_ref[0:size], axis=0, keepdims=True), 0.0)
    seg_here = segc_ref[8 : 8 + size]
    for tap in range(CONV):
        ahead = CONV - 1 - tap
        same = segc_ref[8 + ahead : 8 + ahead + size] == seg_here
        term = jnp.where(same, ext_ref[ahead : ahead + size], 0.0)
        back = back + conv_ref[tap : tap + 1] * term
        sums = sums + jnp.where(at == tap, jnp.sum(conv_in * term, axis=0, keepdims=True), 0.0)
    dmap_ref[...] = back.astype(BF16)
    ctx = here_ref[2]
    acc_ref[...] = tn(hid_ref[...], dmap_ref[...])
    span = own_ref.shape[0]
    own = pl.ds(pl.multiple_of(ctx * span, 16), span)
    grad = nt(dmap_ref[own, :], w1_ref[...])
    own_ref[...] = grad
    unit = hid_ref[own, :].astype(F32) / gain_ref[...]
    gain_sum = gall_ref[0:1] + jnp.sum(grad * unit, axis=0, keepdims=True)
    half = small_ref.shape[1]
    heads = headg_ref.shape[1]
    small_ref[...] = jnp.zeros_like(small_ref)
    small_ref[0 : CONV + 1] = convg_ref[0 : CONV + 1]
    small_ref[CONV + 1 : CONV + 3] = sums_ref[0:2]
    small_ref[7:8, 0:heads] = headg_ref[0:1]
    small_ref[7:8, 128 : 128 + heads] = headg_ref[1:2]
    small_ref[8 : 8 + CONV + 1, 0:width] = sums[0 : CONV + 1]
    small_ref[13:14] = gain_sum[:, :half]
    small_ref[14:15] = gain_sum[:, half:]
    small_ref[15:16] = small_ref[7:8] - small_ref[7:8].astype(BF16).astype(F32)
    small_ref[16:24] = dtg_ref[:, :half]
    small_ref[24:32] = dtg_ref[:, half:]
    small = small_ref[...].astype(BF16)
    count = keep_ref.shape[0] // 32 - 1
    block = acc_ref.shape[0] // (2 * count)
    some = block // 4
    keep_ref[0:32] = small
    send_ref[0:32] = small
    for at in range(count):
        start = pl.multiple_of(2 * at * block + ctx * some, 8)
        low = acc_ref[pl.ds(start, some), :].astype(BF16)
        start = pl.multiple_of((2 * at + 1) * block + ctx * some, 8)
        high = acc_ref[pl.ds(start, some), :].astype(BF16)
        keep_ref[32 + 32 * at : 64 + 32 * at, 0:width] = jnp.where(here_ref[0] == 0, low, high)
        send_ref[32 + 32 * at : 64 + 32 * at, 0:width] = jnp.where(here_ref[0] == 0, high, low)


def input_back_kernel(keep_ref, came_ref, far_ref, own_ref, tok_ref, gain_ref, cot_ref, out_ref):
    grad = keep_ref[0].astype(F32) + came_ref[0].astype(F32) + far_ref[...].astype(F32) + own_ref[...]
    tok = tok_ref[...]
    scale = lax.rsqrt(jnp.mean(tok * tok, axis=-1, keepdims=True) + NORM_EPS)
    unit = tok * scale
    scaled = grad * gain_ref[...]
    mean = jnp.mean(scaled * unit, axis=-1, keepdims=True)
    out_ref[...] = cot_ref[...] + scale * (scaled - unit * mean)


def pair_sum_kernel(keep_ref, came_ref, out_ref):
    out_ref[...] = (keep_ref[...].astype(F32) + came_ref[...].astype(F32)).astype(BF16)


def with_rest(value, first):
    row = lax.broadcasted_iota(jnp.int32, value.shape, 0)
    head = value[first + 7 : first + 8] + value[first + 15 : first + 16]
    rest = head - head.astype(BF16).astype(F32)
    return jnp.where(row == first + 7, head, jnp.where(row == first + 15, rest, value))


def pair_sum_late_kernel(keep_ref, came_ref, mkeep_ref, mcame_ref, out_ref):
    count, rows, width = keep_ref.shape
    small = with_rest(mkeep_ref[0:32].astype(F32) + mcame_ref[0:32].astype(F32), 0).astype(BF16)
    for block in range(count):
        out_ref[block, 0:rows] = (keep_ref[block].astype(F32) + came_ref[block].astype(F32)).astype(BF16)
        out_ref[block, rows : rows + 32] = small
        at = slice(32 + 32 * block, 64 + 32 * block)
        out_ref[block, rows + 32 : rows + 64] = (
            mkeep_ref[at].astype(F32) + mcame_ref[at].astype(F32)
        ).astype(BF16)


def sum_late_kernel(parts_ref, out_ref):
    total = parts_ref[0].astype(F32)
    for at in range(1, parts_ref.shape[0]):
        total = total + parts_ref[at].astype(F32)
    out_ref[...] = with_rest(total, out_ref.shape[0] - 64).astype(BF16)


def adam_out_kernel(here_ref, weight_ref, first_ref, second_ref, early_refs, *rest):
    new_refs, early_ref = rest[:3], rest[3]
    step = pl.program_id(0)

    @pl.when(step == 0)
    def _():
        by_owner(early_refs, here_ref[2], early_ref)

    rows = weight_ref.shape[0]
    width = early_ref.shape[2]
    first = early_ref.shape[1] - 2 * rows
    for at in range(2):
        lanes = slice(at * width, (at + 1) * width)
        grad = early_ref[step, first + at * rows : first + (at + 1) * rows].astype(F32)
        news = adam_step(
            weight_ref[:, lanes], first_ref[:, lanes], second_ref[:, lanes], grad, 0.02, WEIGHT_DECAY
        )
        for ref, new in zip(new_refs, news):
            ref[:, lanes] = new


def by_owner(refs, ctx, natural_ref):
    for at, ref in enumerate(refs):
        natural_ref[pl.ds(ctx ^ at, 1)] = ref[...][None]


def mixed_columns(ref, pair, odd):
    lanes = slice(pair * 2 * HEAD_DIM, (pair + 1) * 2 * HEAD_DIM)
    out = []
    for at in range(0, ref.shape[0], 2):
        first = ref[at, :, lanes].astype(F32)
        second = ref[at + 1, :, lanes].astype(F32)
        low = lax.broadcasted_iota(jnp.int32, first.shape, 1) < HEAD_DIM
        if odd:
            out.append(jnp.where(low, pltpu.roll(first, HEAD_DIM, 1), second))
        else:
            out.append(jnp.where(low, first, pltpu.roll(second, HEAD_DIM, 1)))
    return out


def adam_in_kernel(count, tail, here_ref, weight_ref, first_ref, second_ref, part_refs, *rest):
    new_refs, (rows_ref, all_ref) = rest[-5:-2], rest[-2:]
    step = pl.program_id(0)
    rows = weight_ref.shape[0]

    @pl.when(step == 0)
    def _():
        by_owner(part_refs, here_ref[2], all_ref)
        rows_ref[...] = all_ref[:, 0:rows, :]

    def update(lanes, grad):
        news = adam_step(
            weight_ref[:, lanes], first_ref[:, lanes], second_ref[:, lanes], grad, 0.03, WEIGHT_DECAY
        )
        for ref, new in zip(new_refs, news):
            ref[:, lanes] = new

    for head in range(count):

        @pl.when(step == head)
        def _():
            for at, grad in enumerate(mixed_columns(rows_ref, head // 2, head % 2)):
                update(slice(at * 2 * HEAD_DIM, (at + 1) * 2 * HEAD_DIM), grad)

    if tail:

        @pl.when(step == count)
        def _():
            some = rows // all_ref.shape[0]
            first = all_ref.shape[1] - 32
            for at in range(all_ref.shape[0]):
                grad = all_ref[at, first : first + some, 0 : 2 * STATE].astype(F32)
                here = slice(at * some, (at + 1) * some)
                news = adam_step(
                    weight_ref[here], first_ref[here], second_ref[here], grad, 0.03, WEIGHT_DECAY
                )
                for ref, new in zip(new_refs, news):
                    ref[here] = new


def swap(value, axis, bit):
    count = lax.axis_size(axis)
    return lax.ppermute(value, axis, [(at, at ^ bit) for at in range(count)])


def gather_ctx(value):
    far = swap(value, "ctx", 2)
    return [value, swap(value, "ctx", 1), far, swap(far, "ctx", 1)]


def high_all_to_all(value):
    count = lax.axis_size("dp")
    groups = [list(range(low, count, 2)) for low in range(2)]
    return lax.all_to_all(value, "dp", 0, 0, axis_index_groups=groups)


def fan_ctx(value):
    return [value] + [swap(value, "ctx", bit) for bit in range(1, lax.axis_size("ctx"))]


def adam_step(weight, moment_one, second, gradient, step_rate, decay_rate):
    moment_new = BETA_ONE * moment_one + (1.0 - BETA_ONE) * gradient
    second_new = BETA_TWO * second + (1.0 - BETA_TWO) * gradient * gradient
    first_hat = moment_new / (1.0 - BETA_ONE**STEP)
    second_hat = second_new / (1.0 - BETA_TWO**STEP)
    weight_new = weight - step_rate * (
        first_hat / (jnp.sqrt(second_hat) + ADAM_EPS) + decay_rate * weight
    )
    return (weight_new, moment_new, second_new)


def full(shape):
    return pl.BlockSpec(shape, lambda *_: (0,) * len(shape))


def shape_of(*shape, dtype=F32):
    return jax.ShapeDtypeStruct(shape, dtype)


def shards(
    tokens,
    segment_ids,
    cotangent,
    in_weight,
    dt_weight,
    out_weight,
    conv_params,
    gains,
    head_params,
    in_first,
    in_second,
    dt_first,
    dt_second,
    out_first,
    out_second,
    conv_first,
    conv_second,
    gain_first,
    gain_second,
    head_first,
    head_second,
):
    _, span, model = tokens.shape
    length = segment_ids.shape[1]
    ndp, nctx = lax.axis_size("dp"), lax.axis_size("ctx")
    d, c = lax.axis_index("dp"), lax.axis_index("ctx")
    heads = HEADS // nctx
    width = INNER // nctx
    maps = 2 * STATE
    wide = width + maps
    chunks = nctx
    rows_in = in_weight.shape[0]
    conv_cols = conv_params.shape[1]
    gain_len = gains.shape[0]
    dt_cols = dt_weight.shape[1]
    near = ndp == heads
    high = heads // 2
    block_in = model // heads
    tok = tokens[0]
    bits = jnp.stack([d & 1, d >> 1, c] if near else [0 * d, 0 * d, c]).astype(jnp.int32)
    perm = c ^ jnp.asarray([1, 3, 0, 2], jnp.int32)
    perm_far = c ^ jnp.asarray([2, 3, 0, 1], jnp.int32)
    smem = pl.BlockSpec(memory_space=pltpu.SMEM)
    vmem = pl.BlockSpec(memory_space=pltpu.VMEM)
    anywhere = lambda pieces: [pl.BlockSpec(memory_space=pl.ANY)] * len(pieces)

    w1, g2 = pl.pallas_call(
        pack_kernel,
        in_specs=[smem] + [vmem] * 5,
        out_shape=[
            shape_of(high if near else 1, rows_in + 16, wide, dtype=BF16),
            shape_of(high if near else 1, rows_in + (2 * HEAD_DIM if near else 0), width, dtype=BF16),
        ],
        scratch_shapes=[pltpu.VMEM((16, wide), F32)],
        compiler_params=params(),
        name="pack",
    )(bits, in_weight, out_weight, dt_weight, conv_params, gains)
    cot_low = cotangent[0].astype(BF16)
    if near:
        tok_sent, w1 = lax.optimization_barrier((tok, w1))
        tok_far = swap(tok_sent, "ctx", 2)
        w1 = high_all_to_all(w1)
        w1, tok_far, tok_sent, g2, cot_low = lax.optimization_barrier((w1, tok_far, tok_sent, g2, cot_low))
        w1_came = swap(w1, "dp", 1)
        toks = [tok, swap(tok_sent, "ctx", 1), tok_far, swap(tok_far, "ctx", 1)]
        g2 = high_all_to_all(g2)
        cot_far = swap(cot_low, "ctx", 2)
        w1, w1_came, toks, g2, cot_far, cot_low = lax.optimization_barrier(
            (w1, w1_came, toks, g2, cot_far, cot_low)
        )
        w1 = [w1, w1_came]
        g2 = [g2, swap(g2, "dp", 1)]
        cots = [cot_low, swap(cot_low, "ctx", 1), cot_far, swap(cot_far, "ctx", 1)]
        at_rows = at_g2 = jnp.stack([d & 1, 1 - (d & 1)]).astype(jnp.int32)
    else:
        w1 = [lax.all_gather(w1[0], "dp", axis=0)]
        toks = gather_ctx(tok)
        cots = gather_ctx(cot_low)
        wg = lax.all_gather(g2[0], "dp", axis=0, tiled=True).reshape(heads, block_in, width)
        wout = lax.all_gather(out_weight.astype(BF16), "dp", axis=0, tiled=True)
        wout = lax.dynamic_index_in_dim(wout.reshape(heads, nctx, HEAD_DIM, model), c, 1, False)
        g2 = [jnp.concatenate([wg, wout[:, :, :width], wout[:, :, width:]], axis=1)]
        at_rows = at_g2 = jnp.zeros((1,), jnp.int32)

    ids = segment_ids[0]
    seg_col = jnp.pad(ids, (8, 8), constant_values=-1)[:, None]
    seg_row = segment_ids
    head_mine = lax.dynamic_index_in_dim(head_params.reshape(3, heads, nctx), c, 2, False)
    head_col = head_mine.T

    rows = lambda cols: pl.BlockSpec((span, cols), lambda i, *_: (i, 0))
    row_of = pl.BlockSpec((heads, span), lambda i, *_: (0, i))
    rows_at = lambda cols: pl.BlockSpec((span, cols), lambda i, p, *_: (p[i], 0))
    sent = pl.BlockSpec((1, span, model), lambda i, *_: (jnp.minimum(i, 1), 0, 0))
    kept = pl.BlockSpec((1, span, model), lambda i, *_: (jnp.maximum(i - 2, 0), 0, 0))
    shards_in = sum(piece.shape[0] for piece in w1)

    (
        hid, conv_mine, gain_pre, gain_mine, dt_mine, w1, mixed, conv_in, conv_sum, inner, raw,
        step_c, log_c, step_r, log_r, starts,
    ) = pl.pallas_call(
        scan_forward_kernel,
        grid_spec=pltpu.PrefetchScalarGridSpec(
            num_scalar_prefetch=2,
            grid=(chunks,),
            in_specs=[
                anywhere(toks),
                anywhere(w1),
                full((3, heads)),
                full((heads, 3)),
                full((length + 16, 1)),
                pl.BlockSpec((1, span), lambda i, *_: (0, i)),
            ],
            out_specs=[
                rows(model),
                full((8, wide)),
                full((1, model)),
                full((1, width)),
                full((heads, model)),
                full((model, wide)),
                rows(wide),
                rows(wide),
                rows(wide),
                rows(width),
                rows(heads),
                rows(heads),
                rows(heads),
                row_of,
                row_of,
                pl.BlockSpec((1, STATE, width), lambda i, *_: (i, 0, 0)),
            ],
            scratch_shapes=[
                pltpu.VMEM((span + 8, wide), F32),
                pltpu.VMEM((span + 8, 1), jnp.int32),
                pltpu.VMEM((STATE, width), F32),
                pltpu.VMEM((shards_in, 16, wide), BF16),
                pltpu.VMEM((nctx, span, model), F32),
                pltpu.VMEM((8, INNER + maps), F32),
                pltpu.VMEM((1, model + INNER), F32),
                pltpu.SemaphoreType.DMA((copies_of(w1, 2),)),
                pltpu.SemaphoreType.DMA((nctx,)),
            ],
        ),
        out_shape=[
            shape_of(length, model, dtype=BF16),
            shape_of(8, wide),
            shape_of(1, model),
            shape_of(1, width),
            shape_of(heads, model, dtype=BF16),
            shape_of(model, wide, dtype=BF16),
            shape_of(length, wide, dtype=BF16),
            shape_of(length, wide, dtype=BF16),
            shape_of(length, wide),
            shape_of(length, width),
            shape_of(length, heads),
            shape_of(length, heads),
            shape_of(length, heads),
            shape_of(heads, length),
            shape_of(heads, length),
            shape_of(chunks, STATE, width),
        ],
        compiler_params=params("arbitrary"),
        name="scan_forward",
    )(bits, at_rows, toks, w1, head_mine, head_col, seg_col, seg_row)

    wg, wout, cot_all, gate, normed_grad, stats = pl.pallas_call(
        gate_kernel,
        grid_spec=pltpu.PrefetchScalarGridSpec(
            num_scalar_prefetch=2,
            grid=(chunks,),
            in_specs=[rows(model), anywhere(g2), anywhere(cots), rows(width), full((1, width))],
            out_specs=[
                full((model, width)),
                full((width, model)),
                full((nctx, span, model)),
                rows(width),
                rows(width),
                pl.BlockSpec((8, span), lambda i, *_: (0, i)),
            ],
            scratch_shapes=[
                pltpu.SemaphoreType.DMA((copies_of(g2, 3),)),
                pltpu.SemaphoreType.DMA((nctx,)),
            ],
        ),
        out_shape=[
            shape_of(model, width, dtype=BF16),
            shape_of(width, model, dtype=BF16),
            shape_of(nctx, span, model, dtype=BF16),
            shape_of(length, width, dtype=BF16),
            shape_of(length, width),
            shape_of(8, length),
        ],
        compiler_params=params("arbitrary"),
        name="gate",
    )(bits, at_g2, hid, g2, cots, inner, gain_mine)
    stats = sum(fan_ctx(stats))

    early_rows = block_in + 2 * HEAD_DIM
    block_keep, block_send, early_keep, early_send, dy, dgate, col_sums = pl.pallas_call(
        norm_back_kernel,
        grid_spec=pltpu.PrefetchScalarGridSpec(
            num_scalar_prefetch=2,
            grid=(chunks,),
            in_specs=[
                rows_at(model),
                rows_at(width),
                rows_at(width),
                rows_at(width),
                pl.BlockSpec((8, span), lambda i, p, *_: (0, p[i])),
                full((1, width)),
                rows_at(width),
                full((width, model)),
                full((nctx, span, model)),
            ],
            out_specs=[
                kept,
                sent,
                full((high, early_rows, width)),
                full((high, early_rows, width)),
                rows_at(width),
                rows_at(width),
                full((8, width)),
            ],
            scratch_shapes=[pltpu.VMEM((width, model), F32), pltpu.VMEM((model, width), F32)],
        ),
        out_shape=[
            shape_of(2, span, model, dtype=BF16),
            shape_of(2, span, model, dtype=BF16),
            shape_of(high, early_rows, width, dtype=BF16),
            shape_of(high, early_rows, width, dtype=BF16),
            shape_of(length, width),
            shape_of(length, width, dtype=BF16),
            shape_of(8, width),
        ],
        compiler_params=params("arbitrary"),
        name="norm_back",
    )(perm_far, bits, hid, inner, gate, normed_grad, stats, gain_mine, mixed, wout, cot_all)
    block_came = swap(block_send, "ctx", 2)
    if near:
        early_came = swap(early_send, "dp", 1)

    back = lambda cols: pl.BlockSpec((span, cols), lambda i, *_: (chunks - 1 - i, 0))
    back_row = pl.BlockSpec((heads, span), lambda i, *_: (0, chunks - 1 - i))
    late_keep, late_send, dval, dbc, dstep, conv_grad, dt_grad, head_grad = pl.pallas_call(
        scan_back_kernel,
        grid_spec=pltpu.PrefetchScalarGridSpec(
            num_scalar_prefetch=2,
            grid=(chunks,),
            in_specs=[
                back(model),
                back(width),
                back(wide),
                back(width),
                back(width),
                back(heads),
                back(heads),
                back(heads),
                back_row,
                back_row,
                pl.BlockSpec((1, STATE, width), lambda i, *_: (chunks - 1 - i, 0, 0)),
                full((8, width)),
                full((3, heads)),
                full((length + 16, 1)),
                pl.BlockSpec((1, span), lambda i, *_: (0, chunks - 1 - i)),
            ],
            out_specs=[
                full((high, block_in, width)),
                full((high, block_in, width)),
                back(width),
                back(maps),
                back(heads),
                full((8, width)),
                full((heads, model)),
                full((8, heads)),
            ],
            scratch_shapes=[
                pltpu.VMEM((span + 8, width), F32),
                pltpu.VMEM((span + 16, 1), jnp.int32),
                pltpu.VMEM((STATE, width), F32),
                pltpu.VMEM((model, width), F32),
                pltpu.VMEM((span, width), F32),
            ],
        ),
        out_shape=[
            shape_of(high, block_in, width, dtype=BF16),
            shape_of(high, block_in, width, dtype=BF16),
            shape_of(length, width, dtype=BF16),
            shape_of(length, maps, dtype=BF16),
            shape_of(length, heads, dtype=BF16),
            shape_of(8, width),
            shape_of(heads, model),
            shape_of(8, heads),
        ],
        compiler_params=params("arbitrary"),
        name="scan_back",
    )(
        perm, bits, hid, dy, mixed, conv_in, conv_sum, raw, step_c, log_c, step_r, log_r, starts,
        conv_mine, head_mine, seg_col, seg_row,
    )
    dbc_came = swap(dbc, "ctx", 1)
    if near:
        late_came = swap(late_send, "dp", 1)
        early_parts = pl.pallas_call(
            pair_sum_kernel,
            out_shape=shape_of(high, early_rows, width, dtype=BF16),
            compiler_params=params(),
            name="pair_sum_early",
        )(early_keep, early_came)
        early_parts = high_all_to_all(early_parts)
    dbc = (dbc.astype(F32) + dbc_came.astype(F32)).astype(BF16)
    dval, dbc = lax.optimization_barrier((dval, dbc))
    dbc_far = swap(dbc, "ctx", 2)

    hidden_keep, hidden_send, gain_sum = pl.pallas_call(
        hidden_back_kernel,
        grid_spec=pltpu.PrefetchScalarGridSpec(
            num_scalar_prefetch=1,
            grid=(chunks,),
            in_specs=[
                rows_at(width),
                rows_at(width),
                rows_at(heads),
                full((model, width)),
                full((model, width)),
                full((heads, model)),
                rows_at(model),
                full((1, model)),
            ],
            out_specs=[kept, sent, full((8, model))],
        ),
        out_shape=[
            shape_of(2, span, model, dtype=BF16),
            shape_of(2, span, model, dtype=BF16),
            shape_of(8, model),
        ],
        compiler_params=params("arbitrary"),
        name="hidden_back",
    )(perm, dgate, dval, dstep, wg, w1, dt_mine, hid, gain_pre)
    hidden_came = swap(hidden_send, "ctx", 1)
    map_rows = 32 + 32 * high
    map_cols = lambda size: pl.BlockSpec((size, maps), lambda i: (0, width // maps))
    map_keep, map_send, hidden_own = pl.pallas_call(
        maps_back_kernel,
        grid=(1,),
        in_specs=[
            smem,
            full((length, maps)),
            full((length, maps)),
            map_cols(length),
            map_cols(length),
            map_cols(8),
            full((length + 16, 1)),
            full((length, model)),
            map_cols(model),
            full((1, model)),
            full((8, width)),
            full((8, width)),
            full((8, heads)),
            full((heads, model)),
            full((8, model)),
        ],
        out_specs=[full((map_rows, width)), full((map_rows, width)), full((span, model))],
        out_shape=[
            shape_of(map_rows, width, dtype=BF16),
            shape_of(map_rows, width, dtype=BF16),
            shape_of(span, model),
        ],
        scratch_shapes=[
            pltpu.VMEM((length + 8, maps), F32),
            pltpu.VMEM((model, maps), F32),
            pltpu.VMEM((length, maps), BF16),
            pltpu.VMEM((32, width), F32),
        ],
        compiler_params=params("arbitrary"),
        name="maps_back",
    )(
        bits,
        dbc,
        dbc_far,
        conv_sum,
        conv_in,
        conv_mine,
        seg_col,
        hid,
        w1,
        gain_pre,
        conv_grad,
        col_sums,
        head_grad,
        dt_grad,
        gain_sum,
    )

    map_send, hidden_came, block_came = lax.optimization_barrier((map_send, hidden_came, block_came))
    hidden_far = (hidden_keep[1].astype(F32) + hidden_came[1].astype(F32)).astype(BF16)
    hidden_far = swap(hidden_far, "ctx", 2)
    block_near = (block_keep[1].astype(F32) + block_came[1].astype(F32)).astype(BF16)
    block_near = swap(block_near, "ctx", 1)
    mine = pl.BlockSpec((1, span, model), lambda i: (0, 0, 0))
    input_grad = pl.pallas_call(
        input_back_kernel,
        grid=(1,),
        in_specs=[mine, mine] + [full((span, model))] * 3 + [full((1, model)), full((span, model))],
        out_specs=full((span, model)),
        out_shape=shape_of(span, model),
        compiler_params=params("arbitrary"),
        name="input_back",
    )(hidden_keep, hidden_came, hidden_far, hidden_own, tok, gain_pre, cotangent[0])
    block_output = tok + (
        block_keep[0].astype(F32) + block_came[0].astype(F32) + block_near.astype(F32)
    )

    late_rows = block_in + 64
    if near:
        map_came = swap(map_send, "dp", 1)
        late_parts = pl.pallas_call(
            pair_sum_late_kernel,
            out_shape=shape_of(high, late_rows, width, dtype=BF16),
            compiler_params=params(),
            name="pair_sum_late",
        )(late_keep, late_came, map_keep, map_came)
        late_parts = high_all_to_all(late_parts)
        late_parts, input_grad, block_output = lax.optimization_barrier(
            (late_parts, input_grad, block_output)
        )
        early = jnp.sum(early_parts.astype(F32), axis=0).astype(BF16)
        late = pl.pallas_call(
            sum_late_kernel,
            out_shape=shape_of(late_rows, width, dtype=BF16),
            compiler_params=params(),
            name="sum_late",
        )(late_parts)
        early, late = gather_ctx(early), fan_ctx(late)
        row_block = lambda ref_rows, cols: pl.BlockSpec((ref_rows, cols), lambda i, *_: (i, 0))
        out_block = row_block(out_weight.shape[0] // nctx, model)
        early_spec = [full((early_rows, width))] * nctx
        early_scratch = pltpu.VMEM((nctx, early_rows, width), BF16)
        out_new = pl.pallas_call(
            adam_out_kernel,
            grid_spec=pltpu.PrefetchScalarGridSpec(
                num_scalar_prefetch=1,
                grid=(nctx,),
                in_specs=[out_block] * 3 + [early_spec],
                out_specs=[out_block] * 3,
                scratch_shapes=[early_scratch],
            ),
            out_shape=[shape_of(*out_weight.shape)] * 3,
            compiler_params=params("arbitrary"),
            name="adam_out",
        )(bits, out_weight, out_first, out_second, early)

        def adam_in(first_block, steps, tail, parts, part_rows, done, name):
            part = pl.BlockSpec((rows_in, nctx * HEAD_DIM), lambda i, *_: (0, first_block + i))
            return pl.pallas_call(
                functools.partial(adam_in_kernel, heads, tail),
                grid_spec=pltpu.PrefetchScalarGridSpec(
                    num_scalar_prefetch=1,
                    grid=(steps,),
                    in_specs=[part] * 3 + [[full((part_rows, width))] * nctx] + anywhere(done),
                    out_specs=[part] * 3,
                    scratch_shapes=[
                        pltpu.VMEM((nctx, rows_in, width), BF16),
                        pltpu.VMEM((nctx, part_rows, width), BF16),
                    ],
                ),
                out_shape=[shape_of(*in_weight.shape)] * 3,
                input_output_aliases={4 + nctx + at: at for at in range(len(done))},
                compiler_params=params("arbitrary"),
                name=name,
            )(bits, in_weight, in_first, in_second, parts, *done)

        in_new = adam_in(0, heads, False, early, early_rows, [], "adam_gate")
        late, in_new = lax.optimization_barrier((late, in_new))
        in_new = adam_in(heads, heads + 1, True, late, late_rows, in_new, "adam_rest")
        in_new, out_new = tuple(in_new), tuple(out_new)
        small = jnp.stack([part[block_in : block_in + 32] for part in late])[c ^ jnp.arange(nctx)]
        small = small.astype(F32)
    else:
        blocks = lambda keep, send: jnp.stack([keep, send], axis=1).reshape((heads,) + keep.shape[1:])
        early = blocks(early_keep, early_send).astype(F32)
        late = blocks(late_keep, late_send).astype(F32)
        part = lambda value: value[32:].reshape(high, 32, width)[:, :, :maps]
        map_blocks = blocks(part(map_keep), part(map_send)).astype(F32)

        def total(value):
            return lax.psum_scatter(value, "dp", scatter_dimension=0, tiled=True)

        def spaced(value):
            place_at = (jnp.arange(nctx) == c).astype(F32).reshape((1, nctx, 1, 1))
            value = value[:, None] * place_at
            return lax.psum(total(value.reshape(-1, value.shape[-1])), "ctx")

        def by_head(value):
            value = lax.all_gather(total(value.reshape(model, width)), "ctx", axis=0)
            value = value.reshape(nctx, rows_in, heads, HEAD_DIM)
            return jnp.transpose(value, (1, 2, 0, 3)).reshape(rows_in, INNER)

        in_total = jnp.concatenate(
            [by_head(early[:, :block_in]), by_head(late), spaced(map_blocks)], axis=1
        )
        out_total = spaced(
            jnp.concatenate([early[:, block_in : block_in + HEAD_DIM], early[:, block_in + HEAD_DIM :]], axis=2)
        )
        in_new = adam_step(in_weight, in_first, in_second, in_total, 0.03, WEIGHT_DECAY)
        out_new = adam_step(out_weight, out_first, out_second, out_total, 0.02, WEIGHT_DECAY)
        small = lax.all_gather(lax.psum(map_keep[:32].astype(F32), "dp"), "ctx", axis=0)

    def in_order(value):
        return jnp.swapaxes(value.reshape(nctx, -1, heads, HEAD_DIM), 0, 1).swapaxes(1, 2).reshape(-1, INNER)

    columns = in_order(small[:, : CONV + 2])
    conv_total = jnp.concatenate([columns[: CONV + 1], small[0, 8 : 8 + CONV + 1, :maps]], axis=1)
    conv_total = lax.dynamic_slice_in_dim(conv_total, d * conv_cols, conv_cols, 1)
    dt_total = small[:, 16:32].reshape(nctx, 2, heads, width)
    dt_total = jnp.transpose(dt_total, (2, 0, 1, 3)).reshape(HEADS, model)
    dt_total = lax.dynamic_slice_in_dim(dt_total, d * dt_cols, dt_cols, 1)
    pre_total = jnp.sum(small[:, 13:15], axis=0).reshape(-1)
    gain_total = jnp.concatenate([pre_total, columns[CONV + 1]])
    gain_total = lax.dynamic_slice_in_dim(gain_total, d * gain_len, gain_len, 0)
    head_row = small[:, 7] + small[:, 15]
    head_total = jnp.stack(
        [
            head_row[:, :heads].T.reshape(-1),
            head_row[:, 128 : 128 + heads].T.reshape(-1),
            jnp.sum(small[:, CONV + 2].reshape(nctx, heads, HEAD_DIM), axis=2).T.reshape(-1),
        ]
    )

    dt_new = adam_step(dt_weight, dt_first, dt_second, dt_total, 0.03, WEIGHT_DECAY)
    conv_new = adam_step(conv_params, conv_first, conv_second, conv_total, 0.3, 0.0)
    gain_new = adam_step(gains, gain_first, gain_second, gain_total, 0.5, 0.0)
    head_new = adam_step(head_params, head_first, head_second, head_total, 2.0, 0.0)
    return (block_output[None], input_grad[None]) + in_new + dt_new + out_new + conv_new + gain_new + head_new


def solution(mesh):
    tokens, rows, cols = P("dp", "ctx", None), P("dp", None), P(None, "dp")
    return jax.shard_map(
        shards,
        mesh=mesh,
        in_specs=(tokens, rows, tokens, rows, cols, rows, cols, P("dp"), P())
        + (rows, rows, cols, cols, rows, rows, cols, cols, P("dp"), P("dp"), P(), P()),
        out_specs=(tokens, tokens)
        + (rows,) * 3
        + (cols,) * 3
        + (rows,) * 3
        + (cols,) * 3
        + (P("dp"),) * 3
        + (P(),) * 3,
        check_vma=False,
    )
```

```python
import functools

import jax
import jax.numpy as jnp
from jax import lax
from jax.experimental import pallas as pl
from jax.experimental.pallas import tpu as pltpu
from jax.sharding import PartitionSpec as P

INNER = 2048
HEADS = 32
HEAD_DIM = 64
STATE = 128
CONV = 4
STEP = 10

F32 = jnp.float32
BF16 = jnp.bfloat16
HIGHEST = lax.Precision.HIGHEST
NORM_EPS = 1e-05
BETA_ONE = 0.9
BETA_TWO = 0.95
ADAM_EPS = 1e-08
WEIGHT_DECAY = 0.1
VMEM_LIMIT = 56 * 1024 * 1024


def nn(a, b, precision=None):
    return lax.dot_general(
        a, b, (((1,), (0,)), ((), ())), precision=precision, preferred_element_type=F32
    )


def nt(a, b, precision=None):
    return lax.dot_general(
        a, b, (((1,), (1,)), ((), ())), precision=precision, preferred_element_type=F32
    )


def tn(a, b, precision=None):
    return lax.dot_general(
        a, b, (((0,), (0,)), ((), ())), precision=precision, preferred_element_type=F32
    )


def halves(value):
    high = value.astype(BF16)
    return high, (value - high.astype(F32)).astype(BF16)


def spread(value, width):
    heads = value.shape[1]
    row = lax.broadcasted_iota(jnp.int32, (heads, width), 0)
    col = lax.broadcasted_iota(jnp.int32, (heads, width), 1)
    table = jnp.where(col // HEAD_DIM == row, 1.0, 0.0).astype(BF16)
    high, low = halves(value)
    return nn(high, table) + nn(low, table)


def gather_heads(value, heads):
    width = value.shape[1]
    row = lax.broadcasted_iota(jnp.int32, (width, heads), 0)
    col = lax.broadcasted_iota(jnp.int32, (width, heads), 1)
    table = jnp.where(row // HEAD_DIM == col, 1.0, 0.0).astype(BF16)
    high, low = halves(value)
    return nn(high, table) + nn(low, table)


def softplus(value):
    return jnp.maximum(value, 0.0) + jnp.log1p(jnp.exp(-jnp.abs(value)))


def sigmoid(value):
    return 1.0 / (1.0 + jnp.exp(-value))


def silu_grad(value):
    sig = sigmoid(value)
    return sig * (1.0 + value * (1.0 - sig))


def diagonal(size):
    row = lax.broadcasted_iota(jnp.int32, (size, size), 0)
    return row == lax.broadcasted_iota(jnp.int32, (size, size), 1)


def triangle(size, lower):
    row = lax.broadcasted_iota(jnp.int32, (size, size), 0)
    col = lax.broadcasted_iota(jnp.int32, (size, size), 1)
    keep = row >= col if lower else row <= col
    return jnp.where(keep, 1.0, 0.0).astype(F32)


def params(*semantics):
    return pltpu.CompilerParams(
        dimension_semantics=semantics or None, vmem_limit_bytes=VMEM_LIMIT
    )


def place(pieces, at_ref, stride, sems, targets):
    copies = []
    for index, piece in enumerate(pieces):
        for block in range(piece.shape[0]):
            for first, rows, target in targets:
                copies.append(
                    pltpu.make_async_copy(
                        piece.at[block, first : first + rows],
                        target(at_ref[index] + stride * block),
                        sems.at[len(copies)],
                    )
                )
    for copy in copies:
        copy.start()
    return copies


def copies_of(pieces, targets):
    return sum(piece.shape[0] for piece in pieces) * targets


def rows_of(ref, rows):
    return lambda at: ref.at[pl.ds(pl.multiple_of(at * rows, 16), rows)]


def part_of(block, own_bit, keep_ref, send_ref, first=0):
    for at in range(keep_ref.shape[0]):
        low, high = block(2 * at).astype(BF16), block(2 * at + 1).astype(BF16)
        rows = slice(first, first + low.shape[0])
        keep_ref[at, rows] = jnp.where(own_bit == 0, low, high)
        send_ref[at, rows] = jnp.where(own_bit == 0, high, low)


def pick_heads(ref, base, ctx, heads):
    first = pl.multiple_of(base + (ctx >> 1) * 2 * HEAD_DIM, 2 * HEAD_DIM)
    wide = ref[:, pl.ds(first, 2 * HEAD_DIM)]
    low = lax.broadcasted_iota(jnp.int32, wide.shape, 1) < HEAD_DIM
    odd = (ctx & 1) == 1
    out = []
    for pair in range(heads // 2):
        parts = []
        for head in (2 * pair, 2 * pair + 1):
            first = pl.multiple_of(base + head * 4 * HEAD_DIM + (ctx >> 1) * 2 * HEAD_DIM, 2 * HEAD_DIM)
            parts.append(ref[:, pl.ds(first, 2 * HEAD_DIM)])
        even = jnp.where(low, parts[0], pltpu.roll(parts[1], HEAD_DIM, 1))
        other = jnp.where(low, pltpu.roll(parts[0], HEAD_DIM, 1), parts[1])
        out.append(jnp.where(odd, other, even))
    return out


def pack_kernel(here_ref, win_ref, wout_ref, dt_ref, conv_ref, gain_ref, w1_ref, g2_ref, tmp_ref):
    ctx = here_ref[2]
    rows = win_ref.shape[0]
    heads = HEADS // 4
    width = heads * HEAD_DIM
    copies = range(w1_ref.shape[0])
    for at, part in enumerate(pick_heads(win_ref, INNER, ctx, heads)):
        part = part.astype(BF16)
        for copy in copies:
            w1_ref[copy, 0:rows, at * 128 : (at + 1) * 128] = part
    part = win_ref[:, 2 * INNER :].astype(BF16)
    for copy in copies:
        w1_ref[copy, 0:rows, width:] = part
    tmp_ref[...] = jnp.zeros_like(tmp_ref)
    row = lax.broadcasted_iota(jnp.int32, (heads, HEADS), 0)
    col = lax.broadcasted_iota(jnp.int32, (heads, HEADS), 1)
    table = jnp.where(col == 4 * row + ctx, 1.0, 0.0).astype(BF16)
    tmp_ref[0:heads, 384 : 384 + dt_ref.shape[1]] = nn(table, dt_ref[...].astype(BF16))
    tmp_ref[8 : 8 + CONV + 1, 0 : conv_ref.shape[1]] = conv_ref[...]
    tmp_ref[8 + CONV + 1 : 8 + CONV + 2, 0 : gain_ref.shape[0]] = gain_ref[...].reshape(1, -1)
    for copy in copies:
        w1_ref[copy, rows : rows + 16, :] = tmp_ref[...].astype(BF16)
    copies = range(g2_ref.shape[0])
    for at, part in enumerate(pick_heads(win_ref, 0, ctx, heads)):
        part = part.astype(BF16)
        for copy in copies:
            g2_ref[copy, 0:rows, at * 128 : (at + 1) * 128] = part
    if g2_ref.shape[1] > rows:
        some = wout_ref.shape[0] // 4
        mine = wout_ref[pl.ds(pl.multiple_of(ctx * some, 8), some), :].astype(BF16)
        for copy in copies:
            g2_ref[copy, rows : rows + some] = mine[:, :width]
            g2_ref[copy, rows + some : rows + 2 * some] = mine[:, width:]


def scan_forward_kernel(
    here_ref,
    at_ref,
    tok_pieces,
    w1_pieces,
    hrow_ref,
    hcol_ref,
    segc_ref,
    segr_ref,
    hid_ref,
    conv_ref,
    gpre_ref,
    gmine_ref,
    wdt_ref,
    w1_ref,
    mixed_ref,
    convin_ref,
    convsum_ref,
    inner_ref,
    raw_ref,
    stepc_ref,
    logc_ref,
    stepr_ref,
    logr_ref,
    start_ref,
    ext_ref,
    seg_ref,
    state_ref,
    small_ref,
    tok_ref,
    conv_all,
    gain_all,
    sems,
    tok_sems,
):
    step = pl.program_id(0)
    span, model = hid_ref.shape
    heads = wdt_ref.shape[0]
    width = heads * HEAD_DIM
    shards = small_ref.shape[0]
    rows = model // shards

    @pl.when(step == 0)
    def _():
        copies = place(
            w1_pieces,
            at_ref,
            len(w1_pieces),
            sems,
            [(0, rows, rows_of(w1_ref, rows)), (rows, 16, lambda at: small_ref.at[at])],
        )
        tokens = [
            pltpu.make_async_copy(piece, tok_ref.at[here_ref[2] ^ index], tok_sems.at[index])
            for index, piece in enumerate(tok_pieces)
        ]
        for copy in tokens:
            copy.start()
        ext_ref[0:8] = jnp.zeros((8, ext_ref.shape[1]), F32)
        state_ref[...] = jnp.zeros_like(state_ref)
        conv_all[...] = jnp.zeros_like(conv_all)
        for copy in copies:
            copy.wait()
        conv_cols = conv_all.shape[1] // shards
        gain_len = gain_all.shape[1] // shards
        for shard in range(shards):
            small = small_ref[shard].astype(F32)
            wdt_ref[:, shard * rows : (shard + 1) * rows] = small[0:8, 384 : 384 + rows].astype(BF16)
            conv_all[0 : CONV + 1, shard * conv_cols : (shard + 1) * conv_cols] = small[
                8 : 8 + CONV + 1, :conv_cols
            ]
            gain_all[:, shard * gain_len : (shard + 1) * gain_len] = small[13:14, :gain_len]
        for at, part in enumerate(pick_heads(conv_all, 0, here_ref[2], heads)):
            conv_ref[:, at * 128 : (at + 1) * 128] = part
        conv_ref[:, width:] = conv_all[:, INNER:]
        gpre_ref[...] = gain_all[:, :model]
        for at, part in enumerate(pick_heads(gain_all, model, here_ref[2], heads)):
            gmine_ref[:, at * 128 : (at + 1) * 128] = part
        for copy in tokens:
            copy.wait()

    tok = tok_ref[step]
    scale = lax.rsqrt(jnp.mean(tok * tok, axis=-1, keepdims=True) + NORM_EPS)
    hid = (tok * scale * gpre_ref[...]).astype(BF16)
    hid_ref[...] = hid
    proj = nn(hid, w1_ref[...]).astype(BF16)
    convin_ref[...] = proj
    ext_ref[8 : 8 + span] = proj.astype(F32)
    seg_ref[...] = segc_ref[pl.ds(pl.multiple_of(step * span, 8), span + 8), :]
    seg_here = seg_ref[8 : 8 + span]
    total = conv_ref[CONV : CONV + 1]
    for tap in range(CONV):
        at = 8 - (CONV - 1) + tap
        same = seg_ref[at : at + span] == seg_here
        total = total + conv_ref[tap : tap + 1] * jnp.where(same, ext_ref[at : at + span], 0.0)
    ext_ref[0:8] = ext_ref[span : span + 8]
    convsum_ref[...] = total
    mixed = (total * sigmoid(total)).astype(BF16)
    mixed_ref[...] = mixed

    raw_c = nt(hid, wdt_ref[...]) + hrow_ref[1:2]
    raw_r = nt(wdt_ref[...], hid) + hcol_ref[:, 1:2]
    step_c = softplus(raw_c)
    step_r = softplus(raw_r)
    log_c = nn(triangle(span, True), -step_c * jnp.exp(hrow_ref[0:1]), HIGHEST)
    log_r = nn(-step_r * jnp.exp(hcol_ref[:, 0:1]), triangle(span, False), HIGHEST)
    raw_ref[...] = raw_c
    stepc_ref[...] = step_c
    logc_ref[...] = log_c
    stepr_ref[...] = step_r
    logr_ref[...] = log_r

    values = mixed[:, :width]
    write = mixed[:, width : width + STATE]
    read = mixed[:, width + STATE :]
    row = lax.broadcasted_iota(jnp.int32, (span, span), 0)
    col = lax.broadcasted_iota(jnp.int32, (span, span), 1)
    visible = (seg_here == segr_ref[...]) & (row >= col)
    scores = jnp.where(visible, nt(read, write), 0.0)
    lane = lax.broadcasted_iota(jnp.int32, (span, 2 * HEAD_DIM), 1)

    seg_prev = seg_ref[7:8]
    seg_last = seg_ref[span + 7 : span + 8]
    last = log_c[span - 1 : span]
    enter = jnp.where(seg_here == seg_prev, jnp.exp(log_c), 0.0)
    tail = jnp.where(seg_here == seg_last, jnp.exp(last - log_c), 0.0) * step_c
    keep = jnp.where(seg_last == seg_prev, jnp.exp(last), 0.0)
    state = state_ref[...]
    start_ref[0] = state
    values_f = values.astype(F32)
    base = spread(enter, width) * nn(read, state.astype(BF16)) + spread(
        hrow_ref[2:3] + jnp.zeros((8, heads), F32), width
    )[0:1] * values_f
    for pair in range(heads // 2):
        lanes = slice(pair * 2 * HEAD_DIM, (pair + 1) * 2 * HEAD_DIM)
        pieces = []
        for head in (2 * pair, 2 * pair + 1):
            gap = jnp.minimum(log_c[:, head : head + 1] - log_r[head : head + 1], 0.0)
            weights = scores * jnp.exp(gap) * step_r[head : head + 1]
            pieces.append(nn(weights.astype(BF16), values[:, lanes]))
        inner_ref[:, lanes] = base[:, lanes] + jnp.where(lane < HEAD_DIM, pieces[0], pieces[1])
    moved = (spread(tail, width) * values_f).astype(BF16)
    state_ref[...] = spread(keep + jnp.zeros((8, heads), F32), width)[0:1] * state + tn(
        write, moved
    )


def gate_kernel(
    here_ref,
    at_ref,
    hid_ref,
    g2_pieces,
    cot_pieces,
    inner_ref,
    gain_ref,
    wg_ref,
    wout_ref,
    cot_ref,
    gate_ref,
    ng_ref,
    stat_ref,
    sems,
    cot_sems,
):
    step = pl.program_id(0)
    rows = wg_ref.shape[0] // (wout_ref.shape[0] // HEAD_DIM)
    width = wg_ref.shape[1]

    @pl.when(step == 0)
    def _():
        some = rows_of(wout_ref, HEAD_DIM)
        copies = place(
            g2_pieces,
            at_ref,
            len(g2_pieces),
            sems,
            [
                (0, rows, rows_of(wg_ref, rows)),
                (rows, HEAD_DIM, lambda at: some(at).at[:, 0:width]),
                (rows + HEAD_DIM, HEAD_DIM, lambda at: some(at).at[:, width : 2 * width]),
            ],
        )
        cots = [
            pltpu.make_async_copy(piece, cot_ref.at[here_ref[2] ^ index], cot_sems.at[index])
            for index, piece in enumerate(cot_pieces)
        ]
        for copy in cots:
            copy.start()
        for copy in copies + cots:
            copy.wait()

    gate = nn(hid_ref[...], wg_ref[...]).astype(BF16)
    gate_ref[...] = gate
    gate = gate.astype(F32)
    grad = nt(cot_ref[step], wout_ref[...])
    ng_ref[...] = grad
    gated = inner_ref[...] * (gate * sigmoid(gate))
    squares = jnp.sum(gated * gated, axis=1, keepdims=True)
    crossed = jnp.sum(gated * (grad * gain_ref[...]), axis=1, keepdims=True)
    same = diagonal(gated.shape[0])
    squares = jnp.sum(jnp.where(same, squares, 0.0), axis=0, keepdims=True)
    crossed = jnp.sum(jnp.where(same, crossed, 0.0), axis=0, keepdims=True)
    at = lax.broadcasted_iota(jnp.int32, stat_ref.shape, 0)
    stat_ref[...] = jnp.where(at == 0, squares, crossed)


def norm_back_kernel(
    perm_ref,
    here_ref,
    hid_ref,
    inner_ref,
    gate_ref,
    ng_ref,
    stat_ref,
    gain_ref,
    mixed_ref,
    wout_ref,
    cot_ref,
    block_refs,
    keep_ref,
    send_ref,
    dy_ref,
    dgate_ref,
    sums_ref,
    outacc_ref,
    inacc_ref,
):
    step = pl.program_id(0)
    span, width = inner_ref.shape

    @pl.when(step == 0)
    def _():
        outacc_ref[...] = jnp.zeros_like(outacc_ref)
        inacc_ref[...] = jnp.zeros_like(inacc_ref)
        sums_ref[...] = jnp.zeros_like(sums_ref)

    same = diagonal(span)
    squares = jnp.sum(jnp.where(same, stat_ref[0:1], 0.0), axis=1, keepdims=True)
    cross = jnp.sum(jnp.where(same, stat_ref[1:2], 0.0), axis=1, keepdims=True)
    inv = lax.rsqrt(squares * (1.0 / INNER) + NORM_EPS)
    gate = gate_ref[...].astype(F32)
    sig = sigmoid(gate)
    silu = gate * sig
    inner = inner_ref[...]
    gated = inner * silu
    unit = gated * inv
    normed = (unit * gain_ref[...]).astype(BF16)
    cot = cot_ref[perm_ref[step]]
    block = nn(normed, wout_ref[...]).astype(BF16)

    for at, block_ref in enumerate(block_refs):

        @pl.when(step == at)
        def _():
            block_ref[...] = block

    outacc_ref[...] += tn(normed, cot)
    grad = ng_ref[...]
    dgated = inv * (grad * gain_ref[...] - unit * (cross * inv * (1.0 / INNER)))
    dy = dgated * silu
    dy_ref[...] = dy
    dgate = (dgated * inner * (sig * (1.0 + gate * (1.0 - sig)))).astype(BF16)
    dgate_ref[...] = dgate
    inacc_ref[...] += tn(hid_ref[...], dgate)
    gain_sum = jnp.sum(grad * unit, axis=0, keepdims=True)
    skip_sum = jnp.sum(dy * mixed_ref[...].astype(F32), axis=0, keepdims=True)
    at = lax.broadcasted_iota(jnp.int32, (8, width), 0)
    sums_ref[...] += jnp.where(at == 0, gain_sum, jnp.where(at == 1, skip_sum, 0.0))

    @pl.when(step == pl.num_programs(0) - 1)
    def _():
        own = here_ref[0]
        rows = inacc_ref.shape[0] // (2 * keep_ref.shape[0])
        part_of(lambda at: inacc_ref[at * rows : (at + 1) * rows], own, keep_ref, send_ref)
        outs = lambda at: outacc_ref[at * HEAD_DIM : (at + 1) * HEAD_DIM]
        part_of(lambda at: outs(at)[:, :width], own, keep_ref, send_ref, rows)
        part_of(lambda at: outs(at)[:, width:], own, keep_ref, send_ref, rows + HEAD_DIM)


def scan_back_kernel(
    perm_ref,
    here_ref,
    hid_ref,
    dy_ref,
    mixed_ref,
    convin_ref,
    convsum_ref,
    raw_ref,
    stepc_ref,
    logc_ref,
    stepr_ref,
    logr_ref,
    start_ref,
    conv_ref,
    hrow_ref,
    segc_ref,
    segr_ref,
    keep_ref,
    send_ref,
    dval_ref,
    dbc_ref,
    dstep_ref,
    convg_ref,
    dtg_ref,
    headg_ref,
    ext_ref,
    seg_ref,
    grad_ref,
    inacc_ref,
    dx_ref,
):
    step = pl.program_id(0)
    chunk = pl.num_programs(0) - 1 - step
    span = hid_ref.shape[0]
    heads = stepc_ref.shape[1]
    width = heads * HEAD_DIM

    @pl.when(step == 0)
    def _():
        ext_ref[span : span + 8] = jnp.zeros((8, width), F32)
        grad_ref[...] = jnp.zeros_like(grad_ref)
        inacc_ref[...] = jnp.zeros_like(inacc_ref)
        convg_ref[...] = jnp.zeros_like(convg_ref)
        dtg_ref[...] = jnp.zeros_like(dtg_ref)
        headg_ref[...] = jnp.zeros_like(headg_ref)

    seg_ref[...] = segc_ref[pl.ds(pl.multiple_of(chunk * span, 8), span + 16), :]
    seg_here = seg_ref[8 : 8 + span]
    seg_prev = seg_ref[7:8]
    seg_last = seg_ref[span + 7 : span + 8]
    mixed = mixed_ref[...]
    values = mixed[:, :width]
    write = mixed[:, width : width + STATE]
    read = mixed[:, width + STATE :]
    values_f = values.astype(F32)
    dy = dy_ref[...]
    dy_low = dy.astype(BF16)
    step_c = stepc_ref[...]
    log_c = logc_ref[...]
    step_r = stepr_ref[...]
    log_r = logr_ref[...]
    last = log_c[span - 1 : span]
    enter = jnp.where(seg_here == seg_prev, jnp.exp(log_c), 0.0)
    tail_raw = jnp.where(seg_here == seg_last, jnp.exp(last - log_c), 0.0)
    tail = tail_raw * step_c
    keep = jnp.where(seg_last == seg_prev, jnp.exp(last), 0.0)
    enter_w = spread(enter, width)
    tail_w = spread(tail, width)
    wide = spread(
        jnp.concatenate([hrow_ref[2:3] + jnp.zeros((8, heads), F32), keep + jnp.zeros((8, heads), F32)], axis=0),
        width,
    )
    skip_w = wide[0:1]
    keep_w = wide[8:9]
    state = start_ref[0]
    state_low = state.astype(BF16)
    later = grad_ref[...]
    later_low = later.astype(BF16)

    row = lax.broadcasted_iota(jnp.int32, (span, span), 0)
    col = lax.broadcasted_iota(jnp.int32, (span, span), 1)
    visible = (seg_here == segr_ref[...]) & (row >= col)
    scores = jnp.where(visible, nt(read, write), 0.0)
    lane = lax.broadcasted_iota(jnp.int32, (span, 2 * HEAD_DIM), 1)
    head_at = lax.broadcasted_iota(jnp.int32, (8, span), 0)
    lane_at = lax.broadcasted_iota(jnp.int32, (span, heads), 1)

    entered = enter_w * dy
    entered_low = entered.astype(BF16)
    inter = enter_w * nn(read, state_low)
    from_later = nn(write, later_low)
    moved_low = (tail_w * values_f).astype(BF16)
    dread = nt(entered_low, state_low)
    dwrite = nt(moved_low, later_low)
    dlog_c = gather_heads(dy * inter, heads)
    tail_dot = gather_heads(values_f * from_later, heads)
    dlog_c = dlog_c - tail_dot * tail
    dstep_c = tail_dot * tail_raw
    carried = gather_heads(jnp.sum(later * state, axis=0, keepdims=True) + jnp.zeros((8, width), F32), heads)[0:1]
    at_last = lax.broadcasted_iota(jnp.int32, (span, heads), 0) == span - 1
    dlog_c = dlog_c + jnp.where(
        at_last, jnp.sum(tail_dot * tail, axis=0, keepdims=True) + keep * carried, 0.0
    )
    grad_ref[...] = keep_w * later + tn(read, entered_low)
    dx_ref[...] = tail_w * from_later + skip_w * dy

    dscores = jnp.zeros((span, span), F32)
    dstep_r = jnp.zeros((8, span), F32)
    for pair in range(heads // 2):
        lanes = slice(pair * 2 * HEAD_DIM, (pair + 1) * 2 * HEAD_DIM)
        dy_pair = dy_low[:, lanes]
        pieces = []
        for head in (2 * pair, 2 * pair + 1):
            mine = lane < HEAD_DIM if head % 2 == 0 else lane >= HEAD_DIM
            gap = jnp.minimum(log_c[:, head : head + 1] - log_r[head : head + 1], 0.0)
            decay = jnp.exp(gap)
            outer = nt(jnp.where(mine, dy_pair, jnp.zeros_like(dy_pair)), values[:, lanes])
            fade = decay * step_r[head : head + 1]
            dscores = dscores + outer * fade
            flow = outer * scores
            base = flow * decay
            dstep_r = dstep_r + jnp.where(head_at == head, jnp.sum(base, axis=0, keepdims=True), 0.0)
            dlog_c = dlog_c + jnp.where(
                lane_at == head, jnp.sum(flow * fade, axis=1, keepdims=True), 0.0
            )
            pieces.append(tn((scores * fade).astype(BF16), dy_pair))
        dx_ref[:, lanes] += jnp.where(lane < HEAD_DIM, pieces[0], pieces[1])
    dscores = jnp.where(visible, dscores, 0.0).astype(BF16)
    dread = dread + nn(dscores, write)
    dwrite = dwrite + tn(dscores, read)
    dbc_ref[:, :STATE] = dwrite.astype(BF16)
    dbc_ref[:, STATE:] = dread.astype(BF16)

    upper = triangle(span, False)
    eye = jnp.where(row == col, 1.0, 0.0).astype(F32)
    dalpha = nn(upper, dlog_c, HIGHEST) - nt(upper, dstep_r * step_r, HIGHEST)[:, :heads]
    dstep = dstep_c + nt(eye, dstep_r, HIGHEST)[:, :heads]
    rate = jnp.exp(hrow_ref[0:1])
    draw = (dstep - rate * dalpha) * sigmoid(raw_ref[...])
    draw_low = draw.astype(BF16)
    dstep_ref[...] = draw_low
    hid = hid_ref[...]
    dtg_ref[...] += tn(draw_low, hid)
    rate_sum = jnp.sum(-dalpha * step_c * rate, axis=0, keepdims=True)
    bias_sum = jnp.sum(draw, axis=0, keepdims=True)
    at = lax.broadcasted_iota(jnp.int32, (8, heads), 0)
    headg_ref[...] += jnp.where(at == 0, rate_sum, jnp.where(at == 1, bias_sum, 0.0))

    ext_ref[0:span] = dx_ref[...] * silu_grad(convsum_ref[...])
    back = jnp.zeros((span, width), F32)
    conv_in = convin_ref[...].astype(F32)
    at = lax.broadcasted_iota(jnp.int32, (8, width), 0)
    sums = jnp.where(at == CONV, jnp.sum(ext_ref[0:span], axis=0, keepdims=True), 0.0)
    for tap in range(CONV):
        ahead = CONV - 1 - tap
        same = seg_ref[8 + ahead : 8 + ahead + span] == seg_here
        term = jnp.where(same, ext_ref[ahead : ahead + span], 0.0)
        back = back + conv_ref[tap : tap + 1] * term
        sums = sums + jnp.where(at == tap, jnp.sum(conv_in * term, axis=0, keepdims=True), 0.0)
    convg_ref[...] += sums
    ext_ref[span : span + 8] = ext_ref[0:8]
    dval = back.astype(BF16)
    dval_ref[...] = dval
    inacc_ref[...] += tn(hid, dval)

    @pl.when(step == pl.num_programs(0) - 1)
    def _():
        rows = inacc_ref.shape[0] // (2 * keep_ref.shape[0])
        part_of(lambda at: inacc_ref[at * rows : (at + 1) * rows], here_ref[0], keep_ref, send_ref)


def hidden_back_kernel(
    perm_ref,
    dgate_ref,
    dval_ref,
    dstep_ref,
    wg_ref,
    wv_ref,
    wdt_ref,
    hid_ref,
    gain_ref,
    out_refs,
    gsum_ref,
):
    @pl.when(pl.program_id(0) == 0)
    def _():
        gsum_ref[...] = jnp.zeros_like(gsum_ref)

    total = nt(dgate_ref[...], wg_ref[...]) + nt(dval_ref[...], wv_ref[...])
    total = total + nn(dstep_ref[...], wdt_ref[...])
    step = pl.program_id(0)

    for at, out_ref in enumerate(out_refs):

        @pl.when(step == at)
        def _():
            out_ref[...] = total.astype(BF16)

    unit = hid_ref[...].astype(F32) / gain_ref[...]
    gsum_ref[...] += jnp.sum(total * unit, axis=0, keepdims=True) + jnp.zeros(gsum_ref.shape, F32)


def maps_back_kernel(
    here_ref,
    dbc_ref,
    dbcfar_ref,
    convsum_ref,
    convin_ref,
    conv_ref,
    segc_ref,
    hid_ref,
    w1_ref,
    gain_ref,
    convg_ref,
    sums_ref,
    headg_ref,
    dtg_ref,
    gall_ref,
    keep_ref,
    send_ref,
    own_ref,
    ext_ref,
    acc_ref,
    dmap_ref,
    small_ref,
):
    size, width = dmap_ref.shape
    total = dbc_ref[...].astype(F32) + dbcfar_ref[...].astype(F32)
    ext_ref[0:size] = total * silu_grad(convsum_ref[...])
    ext_ref[size : size + 8] = jnp.zeros((8, width), F32)
    back = jnp.zeros((size, width), F32)
    conv_in = convin_ref[...].astype(F32)
    at = lax.broadcasted_iota(jnp.int32, (8, width), 0)
    sums = jnp.where(at == CONV, jnp.sum(ext_ref[0:size], axis=0, keepdims=True), 0.0)
    seg_here = segc_ref[8 : 8 + size]
    for tap in range(CONV):
        ahead = CONV - 1 - tap
        same = segc_ref[8 + ahead : 8 + ahead + size] == seg_here
        term = jnp.where(same, ext_ref[ahead : ahead + size], 0.0)
        back = back + conv_ref[tap : tap + 1] * term
        sums = sums + jnp.where(at == tap, jnp.sum(conv_in * term, axis=0, keepdims=True), 0.0)
    dmap_ref[...] = back.astype(BF16)
    ctx = here_ref[2]
    acc_ref[...] = tn(hid_ref[...], dmap_ref[...])
    span = own_ref.shape[0]
    own = pl.ds(pl.multiple_of(ctx * span, 16), span)
    grad = nt(dmap_ref[own, :], w1_ref[...])
    own_ref[...] = grad
    unit = hid_ref[own, :].astype(F32) / gain_ref[...]
    gain_sum = gall_ref[0:1] + jnp.sum(grad * unit, axis=0, keepdims=True)
    half = small_ref.shape[1]
    heads = headg_ref.shape[1]
    small_ref[...] = jnp.zeros_like(small_ref)
    small_ref[0 : CONV + 1] = convg_ref[0 : CONV + 1]
    small_ref[CONV + 1 : CONV + 3] = sums_ref[0:2]
    small_ref[7:8, 0:heads] = headg_ref[0:1]
    small_ref[7:8, 128 : 128 + heads] = headg_ref[1:2]
    small_ref[8 : 8 + CONV + 1, 0:width] = sums[0 : CONV + 1]
    small_ref[13:14] = gain_sum[:, :half]
    small_ref[14:15] = gain_sum[:, half:]
    small_ref[15:16] = small_ref[7:8] - small_ref[7:8].astype(BF16).astype(F32)
    small_ref[16:24] = dtg_ref[:, :half]
    small_ref[24:32] = dtg_ref[:, half:]
    small = small_ref[...].astype(BF16)
    count = keep_ref.shape[0] // 32 - 1
    block = acc_ref.shape[0] // (2 * count)
    some = block // 4
    keep_ref[0:32] = small
    send_ref[0:32] = small
    for at in range(count):
        start = pl.multiple_of(2 * at * block + ctx * some, 8)
        low = acc_ref[pl.ds(start, some), :].astype(BF16)
        start = pl.multiple_of((2 * at + 1) * block + ctx * some, 8)
        high = acc_ref[pl.ds(start, some), :].astype(BF16)
        keep_ref[32 + 32 * at : 64 + 32 * at, 0:width] = jnp.where(here_ref[0] == 0, low, high)
        send_ref[32 + 32 * at : 64 + 32 * at, 0:width] = jnp.where(here_ref[0] == 0, high, low)


def input_back_kernel(part_refs, own_ref, tok_ref, gain_ref, cot_ref, out_ref):
    grad = own_ref[...]
    for ref in part_refs:
        grad = grad + ref[...].astype(F32)
    tok = tok_ref[...]
    scale = lax.rsqrt(jnp.mean(tok * tok, axis=-1, keepdims=True) + NORM_EPS)
    unit = tok * scale
    scaled = grad * gain_ref[...]
    mean = jnp.mean(scaled * unit, axis=-1, keepdims=True)
    out_ref[...] = cot_ref[...] + scale * (scaled - unit * mean)


def with_rest(value, first):
    row = lax.broadcasted_iota(jnp.int32, value.shape, 0)
    head = value[first + 7 : first + 8] + value[first + 15 : first + 16]
    rest = head - head.astype(BF16).astype(F32)
    return jnp.where(row == first + 7, head, jnp.where(row == first + 15, rest, value))


def pair_sum_late_kernel(keep_ref, came_ref, mkeep_ref, mcame_ref, out_ref):
    count, rows, width = keep_ref.shape
    small = with_rest(mkeep_ref[0:32].astype(F32) + mcame_ref[0:32].astype(F32), 0).astype(BF16)
    for block in range(count):
        out_ref[block, 0:rows] = (keep_ref[block].astype(F32) + came_ref[block].astype(F32)).astype(BF16)
        out_ref[block, rows : rows + 32] = small
        at = slice(32 + 32 * block, 64 + 32 * block)
        out_ref[block, rows + 32 : rows + 64] = (
            mkeep_ref[at].astype(F32) + mcame_ref[at].astype(F32)
        ).astype(BF16)


def sum_late_kernel(parts_ref, out_ref):
    total = parts_ref[0].astype(F32)
    for at in range(1, parts_ref.shape[0]):
        total = total + parts_ref[at].astype(F32)
    out_ref[...] = with_rest(total, out_ref.shape[0] - 64).astype(BF16)


def adam_out_kernel(here_ref, weight_ref, first_ref, second_ref, early_refs, *rest):
    new_refs, early_ref = rest[:3], rest[3]
    step = pl.program_id(0)

    @pl.when(step == 0)
    def _():
        by_owner(early_refs, here_ref[2], early_ref)

    rows = weight_ref.shape[0]
    width = early_ref.shape[2]
    first = early_ref.shape[1] - 2 * rows
    for at in range(2):
        lanes = slice(at * width, (at + 1) * width)
        grad = early_ref[step, first + at * rows : first + (at + 1) * rows].astype(F32)
        news = adam_step(
            weight_ref[:, lanes], first_ref[:, lanes], second_ref[:, lanes], grad, 0.02, WEIGHT_DECAY
        )
        for ref, new in zip(new_refs, news):
            ref[:, lanes] = new


def by_owner(refs, ctx, natural_ref):
    for at, ref in enumerate(refs):
        natural_ref[pl.ds(ctx ^ at, 1)] = ref[...][None]


def adam_in_kernel(here_ref, weight_ref, first_ref, second_ref, early_refs, late_refs, *rest):
    new_refs, (early_ref, late_ref) = rest[:3], rest[3:]
    step = pl.program_id(0)
    pieces = len(early_refs)
    rows = weight_ref.shape[0]
    width = early_ref.shape[2]
    block = pieces * HEAD_DIM

    @pl.when(step == 0)
    def _():
        by_owner(early_refs, here_ref[2], early_ref)
        by_owner(late_refs, here_ref[2], late_ref)

    here = pl.ds(pl.multiple_of(step * rows, rows), rows)
    low = lax.broadcasted_iota(jnp.int32, (rows, 2 * HEAD_DIM), 1) < HEAD_DIM

    def update(lanes, grad):
        news = adam_step(
            weight_ref[:, lanes], first_ref[:, lanes], second_ref[:, lanes], grad, 0.03, WEIGHT_DECAY
        )
        for ref, new in zip(new_refs, news):
            ref[:, lanes] = new

    for base, ref in ((0, early_ref), (INNER, late_ref)):
        for pair in range(width // (2 * HEAD_DIM)):
            lanes = slice(pair * 2 * HEAD_DIM, (pair + 1) * 2 * HEAD_DIM)
            for at in range(0, pieces, 2):
                first = ref[at, here, lanes].astype(F32)
                second = ref[at + 1, here, lanes].astype(F32)
                start = base + 2 * pair * block + at * HEAD_DIM
                even = jnp.where(low, first, pltpu.roll(second, HEAD_DIM, 1))
                update(slice(start, start + 2 * HEAD_DIM), even)
                start = start + block
                odd = jnp.where(low, pltpu.roll(first, HEAD_DIM, 1), second)
                update(slice(start, start + 2 * HEAD_DIM), odd)
    some = 32 // rows
    first = pl.multiple_of(late_ref.shape[1] - 32 + (step % some) * rows, rows)
    grad = late_ref[step // some, pl.ds(first, rows), 0 : 2 * STATE].astype(F32)
    update(slice(2 * INNER, 2 * INNER + 2 * STATE), grad)


def swap(value, axis, bit):
    count = lax.axis_size(axis)
    return lax.ppermute(value, axis, [(at, at ^ bit) for at in range(count)])


def gather_ctx(value):
    far = swap(value, "ctx", 2)
    return [value, swap(value, "ctx", 1), far, swap(far, "ctx", 1)]


def high_all_to_all(value):
    count = lax.axis_size("dp")
    groups = [list(range(low, count, 2)) for low in range(2)]
    return lax.all_to_all(value, "dp", 0, 0, axis_index_groups=groups)


def from_owners(parts):
    count = len(parts)
    return [swap(parts[bit - 1], "ctx", bit) for bit in range(1, count)] + [parts[-1]]


def fan_ctx(value):
    return [value] + [swap(value, "ctx", bit) for bit in range(1, lax.axis_size("ctx"))]


def adam_step(weight, moment_one, second, gradient, step_rate, decay_rate):
    moment_new = BETA_ONE * moment_one + (1.0 - BETA_ONE) * gradient
    second_new = BETA_TWO * second + (1.0 - BETA_TWO) * gradient * gradient
    first_hat = moment_new / (1.0 - BETA_ONE**STEP)
    second_hat = second_new / (1.0 - BETA_TWO**STEP)
    weight_new = weight - step_rate * (
        first_hat / (jnp.sqrt(second_hat) + ADAM_EPS) + decay_rate * weight
    )
    return (weight_new, moment_new, second_new)


def full(shape):
    return pl.BlockSpec(shape, lambda *_: (0,) * len(shape))


def shape_of(*shape, dtype=F32):
    return jax.ShapeDtypeStruct(shape, dtype)


def shards(
    tokens,
    segment_ids,
    cotangent,
    in_weight,
    dt_weight,
    out_weight,
    conv_params,
    gains,
    head_params,
    in_first,
    in_second,
    dt_first,
    dt_second,
    out_first,
    out_second,
    conv_first,
    conv_second,
    gain_first,
    gain_second,
    head_first,
    head_second,
):
    _, span, model = tokens.shape
    length = segment_ids.shape[1]
    ndp, nctx = lax.axis_size("dp"), lax.axis_size("ctx")
    d, c = lax.axis_index("dp"), lax.axis_index("ctx")
    heads = HEADS // nctx
    width = INNER // nctx
    maps = 2 * STATE
    wide = width + maps
    chunks = nctx
    rows_in = in_weight.shape[0]
    conv_cols = conv_params.shape[1]
    gain_len = gains.shape[0]
    dt_cols = dt_weight.shape[1]
    near = ndp == heads
    high = heads // 2
    block_in = model // heads
    tok = tokens[0]
    bits = jnp.stack([d & 1, d >> 1, c] if near else [0 * d, 0 * d, c]).astype(jnp.int32)
    perm = c ^ jnp.asarray([1, 2, 3, 0], jnp.int32)
    smem = pl.BlockSpec(memory_space=pltpu.SMEM)
    vmem = pl.BlockSpec(memory_space=pltpu.VMEM)
    anywhere = lambda pieces: [pl.BlockSpec(memory_space=pl.ANY)] * len(pieces)

    w1, g2 = pl.pallas_call(
        pack_kernel,
        in_specs=[smem] + [vmem] * 5,
        out_shape=[
            shape_of(high if near else 1, rows_in + 16, wide, dtype=BF16),
            shape_of(high if near else 1, rows_in + (2 * HEAD_DIM if near else 0), width, dtype=BF16),
        ],
        scratch_shapes=[pltpu.VMEM((16, wide), F32)],
        compiler_params=params(),
        name="pack",
    )(bits, in_weight, out_weight, dt_weight, conv_params, gains)
    cot_low = cotangent[0].astype(BF16)
    if near:
        tok_far = swap(tok, "ctx", 2)
        w1 = high_all_to_all(w1)
        w1, tok_far, tok_sent, g2, cot_low = lax.optimization_barrier((w1, tok_far, tok, g2, cot_low))
        w1_came = swap(w1, "dp", 1)
        toks = [tok, swap(tok_sent, "ctx", 1), tok_far, swap(tok_far, "ctx", 1)]
        g2 = high_all_to_all(g2)
        cot_far = swap(cot_low, "ctx", 2)
        w1, w1_came, toks, g2, cot_far, cot_low = lax.optimization_barrier(
            (w1, w1_came, toks, g2, cot_far, cot_low)
        )
        w1 = [w1, w1_came]
        g2 = [g2, swap(g2, "dp", 1)]
        cots = [cot_low, swap(cot_low, "ctx", 1), cot_far, swap(cot_far, "ctx", 1)]
        at_rows = at_g2 = jnp.stack([d & 1, 1 - (d & 1)]).astype(jnp.int32)
    else:
        w1 = [lax.all_gather(w1[0], "dp", axis=0)]
        toks = gather_ctx(tok)
        cots = gather_ctx(cot_low)
        wg = lax.all_gather(g2[0], "dp", axis=0, tiled=True).reshape(heads, block_in, width)
        wout = lax.all_gather(out_weight.astype(BF16), "dp", axis=0, tiled=True)
        wout = lax.dynamic_index_in_dim(wout.reshape(heads, nctx, HEAD_DIM, model), c, 1, False)
        g2 = [jnp.concatenate([wg, wout[:, :, :width], wout[:, :, width:]], axis=1)]
        at_rows = at_g2 = jnp.zeros((1,), jnp.int32)

    ids = segment_ids[0]
    seg_col = jnp.pad(ids, (8, 8), constant_values=-1)[:, None]
    seg_row = segment_ids
    head_mine = lax.dynamic_index_in_dim(head_params.reshape(3, heads, nctx), c, 2, False)
    head_col = head_mine.T

    rows = lambda cols: pl.BlockSpec((span, cols), lambda i, *_: (i, 0))
    row_of = pl.BlockSpec((heads, span), lambda i, *_: (0, i))
    rows_at = lambda cols: pl.BlockSpec((span, cols), lambda i, p, *_: (p[i], 0))
    whole = full((span, model))
    shards_in = sum(piece.shape[0] for piece in w1)

    (
        hid, conv_mine, gain_pre, gain_mine, dt_mine, w1, mixed, conv_in, conv_sum, inner, raw,
        step_c, log_c, step_r, log_r, starts,
    ) = pl.pallas_call(
        scan_forward_kernel,
        grid_spec=pltpu.PrefetchScalarGridSpec(
            num_scalar_prefetch=2,
            grid=(chunks,),
            in_specs=[
                anywhere(toks),
                anywhere(w1),
                full((3, heads)),
                full((heads, 3)),
                full((length + 16, 1)),
                pl.BlockSpec((1, span), lambda i, *_: (0, i)),
            ],
            out_specs=[
                rows(model),
                full((8, wide)),
                full((1, model)),
                full((1, width)),
                full((heads, model)),
                full((model, wide)),
                rows(wide),
                rows(wide),
                rows(wide),
                rows(width),
                rows(heads),
                rows(heads),
                rows(heads),
                row_of,
                row_of,
                pl.BlockSpec((1, STATE, width), lambda i, *_: (i, 0, 0)),
            ],
            scratch_shapes=[
                pltpu.VMEM((span + 8, wide), F32),
                pltpu.VMEM((span + 8, 1), jnp.int32),
                pltpu.VMEM((STATE, width), F32),
                pltpu.VMEM((shards_in, 16, wide), BF16),
                pltpu.VMEM((nctx, span, model), F32),
                pltpu.VMEM((8, INNER + maps), F32),
                pltpu.VMEM((1, model + INNER), F32),
                pltpu.SemaphoreType.DMA((copies_of(w1, 2),)),
                pltpu.SemaphoreType.DMA((nctx,)),
            ],
        ),
        out_shape=[
            shape_of(length, model, dtype=BF16),
            shape_of(8, wide),
            shape_of(1, model),
            shape_of(1, width),
            shape_of(heads, model, dtype=BF16),
            shape_of(model, wide, dtype=BF16),
            shape_of(length, wide, dtype=BF16),
            shape_of(length, wide, dtype=BF16),
            shape_of(length, wide),
            shape_of(length, width),
            shape_of(length, heads),
            shape_of(length, heads),
            shape_of(length, heads),
            shape_of(heads, length),
            shape_of(heads, length),
            shape_of(chunks, STATE, width),
        ],
        compiler_params=params("arbitrary"),
        name="scan_forward",
    )(bits, at_rows, toks, w1, head_mine, head_col, seg_col, seg_row)

    wg, wout, cot_all, gate, normed_grad, stats = pl.pallas_call(
        gate_kernel,
        grid_spec=pltpu.PrefetchScalarGridSpec(
            num_scalar_prefetch=2,
            grid=(chunks,),
            in_specs=[rows(model), anywhere(g2), anywhere(cots), rows(width), full((1, width))],
            out_specs=[
                full((model, width)),
                full((width, model)),
                full((nctx, span, model)),
                rows(width),
                rows(width),
                pl.BlockSpec((8, span), lambda i, *_: (0, i)),
            ],
            scratch_shapes=[
                pltpu.SemaphoreType.DMA((copies_of(g2, 3),)),
                pltpu.SemaphoreType.DMA((nctx,)),
            ],
        ),
        out_shape=[
            shape_of(model, width, dtype=BF16),
            shape_of(width, model, dtype=BF16),
            shape_of(nctx, span, model, dtype=BF16),
            shape_of(length, width, dtype=BF16),
            shape_of(length, width),
            shape_of(8, length),
        ],
        compiler_params=params("arbitrary"),
        name="gate",
    )(bits, at_g2, hid, g2, cots, inner, gain_mine)
    stats = sum(fan_ctx(stats))

    early_rows = block_in + 2 * HEAD_DIM
    blocks_out, early_keep, early_send, dy, dgate, col_sums = pl.pallas_call(
        norm_back_kernel,
        grid_spec=pltpu.PrefetchScalarGridSpec(
            num_scalar_prefetch=2,
            grid=(chunks,),
            in_specs=[
                rows_at(model),
                rows_at(width),
                rows_at(width),
                rows_at(width),
                pl.BlockSpec((8, span), lambda i, p, *_: (0, p[i])),
                full((1, width)),
                rows_at(width),
                full((width, model)),
                full((nctx, span, model)),
            ],
            out_specs=[
                [whole] * nctx,
                full((high, early_rows, width)),
                full((high, early_rows, width)),
                rows_at(width),
                rows_at(width),
                full((8, width)),
            ],
            scratch_shapes=[pltpu.VMEM((width, model), F32), pltpu.VMEM((model, width), F32)],
        ),
        out_shape=[
            [shape_of(span, model, dtype=BF16)] * nctx,
            shape_of(high, early_rows, width, dtype=BF16),
            shape_of(high, early_rows, width, dtype=BF16),
            shape_of(length, width),
            shape_of(length, width, dtype=BF16),
            shape_of(8, width),
        ],
        compiler_params=params("arbitrary"),
        name="norm_back",
    )(perm, bits, hid, inner, gate, normed_grad, stats, gain_mine, mixed, wout, cot_all)
    blocks_out = from_owners(blocks_out)
    if near:
        early_came = swap(early_send, "dp", 1)

    back = lambda cols: pl.BlockSpec((span, cols), lambda i, *_: (chunks - 1 - i, 0))
    back_row = pl.BlockSpec((heads, span), lambda i, *_: (0, chunks - 1 - i))
    late_keep, late_send, dval, dbc, dstep, conv_grad, dt_grad, head_grad = pl.pallas_call(
        scan_back_kernel,
        grid_spec=pltpu.PrefetchScalarGridSpec(
            num_scalar_prefetch=2,
            grid=(chunks,),
            in_specs=[
                back(model),
                back(width),
                back(wide),
                back(width),
                back(width),
                back(heads),
                back(heads),
                back(heads),
                back_row,
                back_row,
                pl.BlockSpec((1, STATE, width), lambda i, *_: (chunks - 1 - i, 0, 0)),
                full((8, width)),
                full((3, heads)),
                full((length + 16, 1)),
                pl.BlockSpec((1, span), lambda i, *_: (0, chunks - 1 - i)),
            ],
            out_specs=[
                full((high, block_in, width)),
                full((high, block_in, width)),
                back(width),
                back(maps),
                back(heads),
                full((8, width)),
                full((heads, model)),
                full((8, heads)),
            ],
            scratch_shapes=[
                pltpu.VMEM((span + 8, width), F32),
                pltpu.VMEM((span + 16, 1), jnp.int32),
                pltpu.VMEM((STATE, width), F32),
                pltpu.VMEM((model, width), F32),
                pltpu.VMEM((span, width), F32),
            ],
        ),
        out_shape=[
            shape_of(high, block_in, width, dtype=BF16),
            shape_of(high, block_in, width, dtype=BF16),
            shape_of(length, width, dtype=BF16),
            shape_of(length, maps, dtype=BF16),
            shape_of(length, heads, dtype=BF16),
            shape_of(8, width),
            shape_of(heads, model),
            shape_of(8, heads),
        ],
        compiler_params=params("arbitrary"),
        name="scan_back",
    )(
        perm, bits, hid, dy, mixed, conv_in, conv_sum, raw, step_c, log_c, step_r, log_r, starts,
        conv_mine, head_mine, seg_col, seg_row,
    )
    dbc_came = swap(dbc, "ctx", 1)
    if near:
        late_came = swap(late_send, "dp", 1)
        early_came, blocks_out, dval = lax.optimization_barrier((early_came, blocks_out, dval))
        early_parts = (early_keep.astype(F32) + early_came.astype(F32)).astype(BF16)
        early_parts = high_all_to_all(early_parts)
    dbc = (dbc.astype(F32) + dbc_came.astype(F32)).astype(BF16)
    dval, dbc = lax.optimization_barrier((dval, dbc))
    dbc_far = swap(dbc, "ctx", 2)
    if near:
        dbc_far, late_came = lax.optimization_barrier((dbc_far, late_came))

    hidden_out, gain_sum = pl.pallas_call(
        hidden_back_kernel,
        grid_spec=pltpu.PrefetchScalarGridSpec(
            num_scalar_prefetch=1,
            grid=(chunks,),
            in_specs=[
                rows_at(width),
                rows_at(width),
                rows_at(heads),
                full((model, width)),
                full((model, width)),
                full((heads, model)),
                rows_at(model),
                full((1, model)),
            ],
            out_specs=[[whole] * nctx, full((8, model))],
        ),
        out_shape=[
            [shape_of(span, model, dtype=BF16)] * nctx,
            shape_of(8, model),
        ],
        compiler_params=params("arbitrary"),
        name="hidden_back",
    )(perm, dgate, dval, dstep, wg, w1, dt_mine, hid, gain_pre)
    hidden_out = from_owners(hidden_out)
    map_rows = 32 + 32 * high
    map_cols = lambda size: pl.BlockSpec((size, maps), lambda i: (0, width // maps))
    map_keep, map_send, hidden_own = pl.pallas_call(
        maps_back_kernel,
        grid=(1,),
        in_specs=[
            smem,
            full((length, maps)),
            full((length, maps)),
            map_cols(length),
            map_cols(length),
            map_cols(8),
            full((length + 16, 1)),
            full((length, model)),
            map_cols(model),
            full((1, model)),
            full((8, width)),
            full((8, width)),
            full((8, heads)),
            full((heads, model)),
            full((8, model)),
        ],
        out_specs=[full((map_rows, width)), full((map_rows, width)), full((span, model))],
        out_shape=[
            shape_of(map_rows, width, dtype=BF16),
            shape_of(map_rows, width, dtype=BF16),
            shape_of(span, model),
        ],
        scratch_shapes=[
            pltpu.VMEM((length + 8, maps), F32),
            pltpu.VMEM((model, maps), F32),
            pltpu.VMEM((length, maps), BF16),
            pltpu.VMEM((32, width), F32),
        ],
        compiler_params=params("arbitrary"),
        name="maps_back",
    )(
        bits,
        dbc,
        dbc_far,
        conv_sum,
        conv_in,
        conv_mine,
        seg_col,
        hid,
        w1,
        gain_pre,
        conv_grad,
        col_sums,
        head_grad,
        dt_grad,
        gain_sum,
    )

    input_grad = pl.pallas_call(
        input_back_kernel,
        in_specs=[[vmem] * nctx] + [vmem] * 4,
        out_shape=shape_of(span, model),
        compiler_params=params(),
        name="input_back",
    )(hidden_out, hidden_own, tok, gain_pre, cotangent[0])
    block_output = tok + sum(part.astype(F32) for part in blocks_out)

    late_rows = block_in + 64
    if near:
        map_came = swap(map_send, "dp", 1)
        late_parts = pl.pallas_call(
            pair_sum_late_kernel,
            out_shape=shape_of(high, late_rows, width, dtype=BF16),
            compiler_params=params(),
            name="pair_sum_late",
        )(late_keep, late_came, map_keep, map_came)
        late_parts = high_all_to_all(late_parts)
        early = jnp.sum(early_parts.astype(F32), axis=0).astype(BF16)
        early = gather_ctx(early)
        row_block = lambda ref_rows, cols: pl.BlockSpec((ref_rows, cols), lambda i, *_: (i, 0))
        out_block = row_block(out_weight.shape[0] // nctx, model)
        early_spec = [full((early_rows, width))] * nctx
        early_scratch = pltpu.VMEM((nctx, early_rows, width), BF16)
        out_new = pl.pallas_call(
            adam_out_kernel,
            grid_spec=pltpu.PrefetchScalarGridSpec(
                num_scalar_prefetch=1,
                grid=(nctx,),
                in_specs=[out_block] * 3 + [early_spec],
                out_specs=[out_block] * 3,
                scratch_shapes=[early_scratch],
            ),
            out_shape=[shape_of(*out_weight.shape)] * 3,
            compiler_params=params("arbitrary"),
            name="adam_out",
        )(bits, out_weight, out_first, out_second, early)

        late_parts, block_output, out_new = lax.optimization_barrier((late_parts, block_output, out_new))
        late = pl.pallas_call(
            sum_late_kernel,
            out_shape=shape_of(late_rows, width, dtype=BF16),
            compiler_params=params(),
            name="sum_late",
        )(late_parts)
        late = fan_ctx(late)
        in_block = row_block(16, in_weight.shape[1])
        in_new = pl.pallas_call(
            adam_in_kernel,
            grid_spec=pltpu.PrefetchScalarGridSpec(
                num_scalar_prefetch=1,
                grid=(rows_in // 16,),
                in_specs=[in_block] * 3 + [early_spec, [full((late_rows, width))] * nctx],
                out_specs=[in_block] * 3,
                scratch_shapes=[early_scratch, pltpu.VMEM((nctx, late_rows, width), BF16)],
            ),
            out_shape=[shape_of(*in_weight.shape)] * 3,
            compiler_params=params("arbitrary"),
            name="adam_in",
        )(bits, in_weight, in_first, in_second, early, late)
        in_new, out_new = tuple(in_new), tuple(out_new)
        small = jnp.stack([part[block_in : block_in + 32] for part in late])[c ^ jnp.arange(nctx)]
        small = small.astype(F32)
    else:
        blocks = lambda keep, send: jnp.stack([keep, send], axis=1).reshape((heads,) + keep.shape[1:])
        early = blocks(early_keep, early_send).astype(F32)
        late = blocks(late_keep, late_send).astype(F32)
        part = lambda value: value[32:].reshape(high, 32, width)[:, :, :maps]
        map_blocks = blocks(part(map_keep), part(map_send)).astype(F32)

        def total(value):
            return lax.psum_scatter(value, "dp", scatter_dimension=0, tiled=True)

        def spaced(value):
            place_at = (jnp.arange(nctx) == c).astype(F32).reshape((1, nctx, 1, 1))
            value = value[:, None] * place_at
            return lax.psum(total(value.reshape(-1, value.shape[-1])), "ctx")

        def by_head(value):
            value = lax.all_gather(total(value.reshape(model, width)), "ctx", axis=0)
            value = value.reshape(nctx, rows_in, heads, HEAD_DIM)
            return jnp.transpose(value, (1, 2, 0, 3)).reshape(rows_in, INNER)

        in_total = jnp.concatenate(
            [by_head(early[:, :block_in]), by_head(late), spaced(map_blocks)], axis=1
        )
        out_total = spaced(
            jnp.concatenate([early[:, block_in : block_in + HEAD_DIM], early[:, block_in + HEAD_DIM :]], axis=2)
        )
        in_new = adam_step(in_weight, in_first, in_second, in_total, 0.03, WEIGHT_DECAY)
        out_new = adam_step(out_weight, out_first, out_second, out_total, 0.02, WEIGHT_DECAY)
        small = lax.all_gather(lax.psum(map_keep[:32].astype(F32), "dp"), "ctx", axis=0)

    def in_order(value):
        return jnp.swapaxes(value.reshape(nctx, -1, heads, HEAD_DIM), 0, 1).swapaxes(1, 2).reshape(-1, INNER)

    columns = in_order(small[:, : CONV + 2])
    conv_total = jnp.concatenate([columns[: CONV + 1], small[0, 8 : 8 + CONV + 1, :maps]], axis=1)
    conv_total = lax.dynamic_slice_in_dim(conv_total, d * conv_cols, conv_cols, 1)
    dt_total = small[:, 16:32].reshape(nctx, 2, heads, width)
    dt_total = jnp.transpose(dt_total, (2, 0, 1, 3)).reshape(HEADS, model)
    dt_total = lax.dynamic_slice_in_dim(dt_total, d * dt_cols, dt_cols, 1)
    pre_total = jnp.sum(small[:, 13:15], axis=0).reshape(-1)
    gain_total = jnp.concatenate([pre_total, columns[CONV + 1]])
    gain_total = lax.dynamic_slice_in_dim(gain_total, d * gain_len, gain_len, 0)
    head_row = small[:, 7] + small[:, 15]
    head_total = jnp.stack(
        [
            head_row[:, :heads].T.reshape(-1),
            head_row[:, 128 : 128 + heads].T.reshape(-1),
            jnp.sum(small[:, CONV + 2].reshape(nctx, heads, HEAD_DIM), axis=2).T.reshape(-1),
        ]
    )

    dt_new = adam_step(dt_weight, dt_first, dt_second, dt_total, 0.03, WEIGHT_DECAY)
    conv_new = adam_step(conv_params, conv_first, conv_second, conv_total, 0.3, 0.0)
    gain_new = adam_step(gains, gain_first, gain_second, gain_total, 0.5, 0.0)
    head_new = adam_step(head_params, head_first, head_second, head_total, 2.0, 0.0)
    return (block_output[None], input_grad[None]) + in_new + dt_new + out_new + conv_new + gain_new + head_new


def solution(mesh):
    tokens, rows, cols = P("dp", "ctx", None), P("dp", None), P(None, "dp")
    return jax.shard_map(
        shards,
        mesh=mesh,
        in_specs=(tokens, rows, tokens, rows, cols, rows, cols, P("dp"), P())
        + (rows, rows, cols, cols, rows, rows, cols, cols, P("dp"), P("dp"), P(), P()),
        out_specs=(tokens, tokens)
        + (rows,) * 3
        + (cols,) * 3
        + (rows,) * 3
        + (cols,) * 3
        + (P("dp"),) * 3
        + (P(),) * 3,
        check_vma=False,
    )
```

```python
import functools

import jax
import jax.numpy as jnp
from jax import lax
from jax.experimental import pallas as pl
from jax.experimental.pallas import tpu as pltpu
from jax.sharding import PartitionSpec as P

INNER = 2048
HEADS = 32
HEAD_DIM = 64
STATE = 128
CONV = 4
STEP = 10
SPAN = 128

F32 = jnp.float32
BF16 = jnp.bfloat16
HIGHEST = lax.Precision.HIGHEST
NORM_EPS = 1e-05
BETA_ONE = 0.9
BETA_TWO = 0.95
ADAM_EPS = 1e-08
WEIGHT_DECAY = 0.1
VMEM_LIMIT = 56 * 1024 * 1024


def nn(a, b, precision=None):
    return lax.dot_general(
        a, b, (((1,), (0,)), ((), ())), precision=precision, preferred_element_type=F32
    )


def nt(a, b, precision=None):
    return lax.dot_general(
        a, b, (((1,), (1,)), ((), ())), precision=precision, preferred_element_type=F32
    )


def tn(a, b, precision=None):
    return lax.dot_general(
        a, b, (((0,), (0,)), ((), ())), precision=precision, preferred_element_type=F32
    )


def halves(value):
    high = value.astype(BF16)
    return high, (value - high.astype(F32)).astype(BF16)


def spread(value, width):
    heads = value.shape[1]
    row = lax.broadcasted_iota(jnp.int32, (heads, width), 0)
    col = lax.broadcasted_iota(jnp.int32, (heads, width), 1)
    table = jnp.where(col // HEAD_DIM == row, 1.0, 0.0).astype(BF16)
    high, low = halves(value)
    return nn(high, table) + nn(low, table)


def gather_heads(value, heads):
    width = value.shape[1]
    row = lax.broadcasted_iota(jnp.int32, (width, heads), 0)
    col = lax.broadcasted_iota(jnp.int32, (width, heads), 1)
    table = jnp.where(row // HEAD_DIM == col, 1.0, 0.0).astype(BF16)
    high, low = halves(value)
    return nn(high, table) + nn(low, table)


def softplus(value):
    return jnp.maximum(value, 0.0) + jnp.log1p(jnp.exp(-jnp.abs(value)))


def sigmoid(value):
    return 1.0 / (1.0 + jnp.exp(-value))


def silu_grad(value):
    sig = sigmoid(value)
    return sig * (1.0 + value * (1.0 - sig))


def diagonal(size):
    row = lax.broadcasted_iota(jnp.int32, (size, size), 0)
    return row == lax.broadcasted_iota(jnp.int32, (size, size), 1)


def triangle(size, lower):
    row = lax.broadcasted_iota(jnp.int32, (size, size), 0)
    col = lax.broadcasted_iota(jnp.int32, (size, size), 1)
    keep = (row >= col if lower else row <= col) & (row // SPAN == col // SPAN)
    return jnp.where(keep, 1.0, 0.0).astype(F32)


def params(*semantics):
    return pltpu.CompilerParams(
        dimension_semantics=semantics or None, vmem_limit_bytes=VMEM_LIMIT
    )


def place(pieces, at_ref, stride, sems, targets):
    copies = []
    for index, piece in enumerate(pieces):
        for block in range(piece.shape[0]):
            for first, rows, target in targets:
                copies.append(
                    pltpu.make_async_copy(
                        piece.at[block, first : first + rows],
                        target(at_ref[index] + stride * block),
                        sems.at[len(copies)],
                    )
                )
    for copy in copies:
        copy.start()
    return copies


def copies_of(pieces, targets):
    return sum(piece.shape[0] for piece in pieces) * targets


def rows_of(ref, rows):
    return lambda at: ref.at[pl.ds(pl.multiple_of(at * rows, 16), rows)]


def part_of(block, own_bit, keep_ref, send_ref, first=0):
    for at in range(keep_ref.shape[0]):
        low, high = block(2 * at).astype(BF16), block(2 * at + 1).astype(BF16)
        rows = slice(first, first + low.shape[0])
        keep_ref[at, rows] = jnp.where(own_bit == 0, low, high)
        send_ref[at, rows] = jnp.where(own_bit == 0, high, low)


def pick_heads(ref, base, ctx, heads):
    first = pl.multiple_of(base + (ctx >> 1) * 2 * HEAD_DIM, 2 * HEAD_DIM)
    wide = ref[:, pl.ds(first, 2 * HEAD_DIM)]
    low = lax.broadcasted_iota(jnp.int32, wide.shape, 1) < HEAD_DIM
    odd = (ctx & 1) == 1
    out = []
    for pair in range(heads // 2):
        parts = []
        for head in (2 * pair, 2 * pair + 1):
            first = pl.multiple_of(base + head * 4 * HEAD_DIM + (ctx >> 1) * 2 * HEAD_DIM, 2 * HEAD_DIM)
            parts.append(ref[:, pl.ds(first, 2 * HEAD_DIM)])
        even = jnp.where(low, parts[0], pltpu.roll(parts[1], HEAD_DIM, 1))
        other = jnp.where(low, pltpu.roll(parts[0], HEAD_DIM, 1), parts[1])
        out.append(jnp.where(odd, other, even))
    return out


def pack_kernel(here_ref, win_ref, wout_ref, dt_ref, conv_ref, gain_ref, w1_ref, g2_ref, tmp_ref):
    ctx = here_ref[2]
    rows = win_ref.shape[0]
    heads = HEADS // 4
    width = heads * HEAD_DIM
    copies = range(w1_ref.shape[0])
    for at, part in enumerate(pick_heads(win_ref, INNER, ctx, heads)):
        part = part.astype(BF16)
        for copy in copies:
            w1_ref[copy, 0:rows, at * 128 : (at + 1) * 128] = part
    part = win_ref[:, 2 * INNER :].astype(BF16)
    for copy in copies:
        w1_ref[copy, 0:rows, width:] = part
    tmp_ref[...] = jnp.zeros_like(tmp_ref)
    row = lax.broadcasted_iota(jnp.int32, (heads, HEADS), 0)
    col = lax.broadcasted_iota(jnp.int32, (heads, HEADS), 1)
    table = jnp.where(col == 4 * row + ctx, 1.0, 0.0).astype(BF16)
    tmp_ref[0:heads, 384 : 384 + dt_ref.shape[1]] = nn(table, dt_ref[...].astype(BF16))
    tmp_ref[8 : 8 + CONV + 1, 0 : conv_ref.shape[1]] = conv_ref[...]
    tmp_ref[8 + CONV + 1 : 8 + CONV + 2, 0 : gain_ref.shape[0]] = gain_ref[...].reshape(1, -1)
    for copy in copies:
        w1_ref[copy, rows : rows + 16, :] = tmp_ref[...].astype(BF16)
    copies = range(g2_ref.shape[0])
    for at, part in enumerate(pick_heads(win_ref, 0, ctx, heads)):
        part = part.astype(BF16)
        for copy in copies:
            g2_ref[copy, 0:rows, at * 128 : (at + 1) * 128] = part
    if g2_ref.shape[1] > rows:
        some = wout_ref.shape[0] // 4
        mine = wout_ref[pl.ds(pl.multiple_of(ctx * some, 8), some), :].astype(BF16)
        for copy in copies:
            g2_ref[copy, rows : rows + some] = mine[:, :width]
            g2_ref[copy, rows + some : rows + 2 * some] = mine[:, width:]


def scan_forward_kernel(
    here_ref,
    at_ref,
    tok_pieces,
    w1_pieces,
    hrow_ref,
    hcol_ref,
    segc_ref,
    segr_ref,
    hid_ref,
    conv_ref,
    gpre_ref,
    gmine_ref,
    wdt_ref,
    w1_ref,
    mixed_ref,
    convin_ref,
    convsum_ref,
    inner_ref,
    raw_ref,
    stepc_ref,
    logc_ref,
    stepr_ref,
    logr_ref,
    start_ref,
    ext_ref,
    seg_ref,
    state_ref,
    small_ref,
    tok_ref,
    conv_all,
    gain_all,
    sems,
    tok_sems,
):
    step = pl.program_id(0)
    span, model = hid_ref.shape
    heads = wdt_ref.shape[0]
    width = heads * HEAD_DIM
    shards = small_ref.shape[0]
    rows = model // shards

    @pl.when(step == 0)
    def _():
        copies = place(
            w1_pieces,
            at_ref,
            len(w1_pieces),
            sems,
            [(0, rows, rows_of(w1_ref, rows)), (rows, 16, lambda at: small_ref.at[at])],
        )
        tokens = [
            pltpu.make_async_copy(piece, tok_ref.at[here_ref[2] ^ index], tok_sems.at[index])
            for index, piece in enumerate(tok_pieces)
        ]
        for copy in tokens:
            copy.start()
        ext_ref[0:8] = jnp.zeros((8, ext_ref.shape[1]), F32)
        state_ref[...] = jnp.zeros_like(state_ref)
        conv_all[...] = jnp.zeros_like(conv_all)
        for copy in copies:
            copy.wait()
        conv_cols = conv_all.shape[1] // shards
        gain_len = gain_all.shape[1] // shards
        for shard in range(shards):
            small = small_ref[shard].astype(F32)
            wdt_ref[:, shard * rows : (shard + 1) * rows] = small[0:8, 384 : 384 + rows].astype(BF16)
            conv_all[0 : CONV + 1, shard * conv_cols : (shard + 1) * conv_cols] = small[
                8 : 8 + CONV + 1, :conv_cols
            ]
            gain_all[:, shard * gain_len : (shard + 1) * gain_len] = small[13:14, :gain_len]
        for at, part in enumerate(pick_heads(conv_all, 0, here_ref[2], heads)):
            conv_ref[:, at * 128 : (at + 1) * 128] = part
        conv_ref[:, width:] = conv_all[:, INNER:]
        gpre_ref[...] = gain_all[:, :model]
        for at, part in enumerate(pick_heads(gain_all, model, here_ref[2], heads)):
            gmine_ref[:, at * 128 : (at + 1) * 128] = part
        for copy in tokens:
            copy.wait()

    tok = tok_ref[step]
    scale = lax.rsqrt(jnp.mean(tok * tok, axis=-1, keepdims=True) + NORM_EPS)
    hid = (tok * scale * gpre_ref[...]).astype(BF16)
    hid_ref[...] = hid
    proj = nn(hid, w1_ref[...]).astype(BF16)
    convin_ref[...] = proj
    ext_ref[8 : 8 + span] = proj.astype(F32)
    seg_ref[...] = segc_ref[pl.ds(pl.multiple_of(step * span, 8), span + 8), :]
    seg_here = seg_ref[8 : 8 + span]
    total = conv_ref[CONV : CONV + 1]
    for tap in range(CONV):
        at = 8 - (CONV - 1) + tap
        same = seg_ref[at : at + span] == seg_here
        total = total + conv_ref[tap : tap + 1] * jnp.where(same, ext_ref[at : at + span], 0.0)
    ext_ref[0:8] = ext_ref[span : span + 8]
    convsum_ref[...] = total
    mixed = (total * sigmoid(total)).astype(BF16)
    mixed_ref[...] = mixed

    raw_c = nt(hid, wdt_ref[...]) + hrow_ref[1:2]
    raw_r = nt(wdt_ref[...], hid) + hcol_ref[:, 1:2]
    step_c = softplus(raw_c)
    step_r = softplus(raw_r)
    log_c = nn(triangle(span, True), -step_c * jnp.exp(hrow_ref[0:1]), HIGHEST)
    log_r = nn(-step_r * jnp.exp(hcol_ref[:, 0:1]), triangle(span, False), HIGHEST)
    raw_ref[...] = raw_c
    stepc_ref[...] = step_c
    logc_ref[...] = log_c
    stepr_ref[...] = step_r
    logr_ref[...] = log_r

    low = lax.broadcasted_iota(jnp.int32, (SPAN, 2 * HEAD_DIM), 1) < HEAD_DIM
    earlier = lax.broadcasted_iota(jnp.int32, (SPAN, SPAN), 0) >= lax.broadcasted_iota(
        jnp.int32, (SPAN, SPAN), 1
    )
    skip_w = spread(hrow_ref[2:3] + jnp.zeros((8, heads), F32), width)[0:1]
    state = state_ref[...]
    for block in range(span // SPAN):
        here = slice(block * SPAN, (block + 1) * SPAN)
        values = mixed[here, :width]
        write = mixed[here, width : width + STATE]
        read = mixed[here, width + STATE :]
        seg = seg_here[here]
        log = log_c[here]
        log_row = log_r[:, here]
        step_row = step_r[:, here]
        scores = jnp.where((seg == segr_ref[:, here]) & earlier, nt(read, write), 0.0)
        seg_prev = seg_ref[7 + block * SPAN : 8 + block * SPAN]
        seg_last = seg_ref[7 + (block + 1) * SPAN : 8 + (block + 1) * SPAN]
        last = log[SPAN - 1 : SPAN]
        enter = jnp.where(seg == seg_prev, jnp.exp(log), 0.0)
        tail = jnp.where(seg == seg_last, jnp.exp(last - log), 0.0) * step_c[here]
        keep = jnp.where(seg_last == seg_prev, jnp.exp(last), 0.0)
        start_ref[block] = state
        values_f = values.astype(F32)
        base = spread(enter, width) * nn(read, state.astype(BF16)) + skip_w * values_f
        for pair in range(heads // 2):
            lanes = slice(pair * 2 * HEAD_DIM, (pair + 1) * 2 * HEAD_DIM)
            pieces = []
            for head in (2 * pair, 2 * pair + 1):
                gap = jnp.minimum(log[:, head : head + 1] - log_row[head : head + 1], 0.0)
                weights = scores * jnp.exp(gap) * step_row[head : head + 1]
                pieces.append(nn(weights.astype(BF16), values[:, lanes]))
            inner_ref[here, lanes] = base[:, lanes] + jnp.where(low, pieces[0], pieces[1])
        moved = (spread(tail, width) * values_f).astype(BF16)
        keep_w = spread(keep + jnp.zeros((8, heads), F32), width)[0:1]
        state = keep_w * state + tn(write, moved)
    state_ref[...] = state


def gate_kernel(
    here_ref,
    at_ref,
    hid_ref,
    g2_pieces,
    cot_pieces,
    inner_ref,
    gain_ref,
    wg_ref,
    wout_ref,
    cot_ref,
    gate_ref,
    ng_ref,
    stat_ref,
    turned_ref,
    sems,
    cot_sems,
):
    step = pl.program_id(0)
    rows = wg_ref.shape[0] // (wout_ref.shape[0] // HEAD_DIM)
    width = wg_ref.shape[1]

    @pl.when(step == 0)
    def _():
        some = rows_of(wout_ref, HEAD_DIM)
        copies = place(
            g2_pieces,
            at_ref,
            len(g2_pieces),
            sems,
            [
                (0, rows, rows_of(wg_ref, rows)),
                (rows, HEAD_DIM, lambda at: some(at).at[:, 0:width]),
                (rows + HEAD_DIM, HEAD_DIM, lambda at: some(at).at[:, width : 2 * width]),
            ],
        )
        cots = [
            pltpu.make_async_copy(piece, cot_ref.at[here_ref[2] ^ index], cot_sems.at[index])
            for index, piece in enumerate(cot_pieces)
        ]
        for copy in cots:
            copy.start()
        for copy in copies + cots:
            copy.wait()
        turned_ref[...] = wout_ref[...].T

    gate = nn(hid_ref[...], wg_ref[...]).astype(BF16)
    gate_ref[...] = gate
    gate = gate.astype(F32)
    grad = nn(cot_ref[step], turned_ref[...])
    ng_ref[...] = grad
    gated = inner_ref[...] * (gate * sigmoid(gate))
    squares = jnp.sum(gated * gated, axis=1, keepdims=True)
    crossed = jnp.sum(gated * (grad * gain_ref[...]), axis=1, keepdims=True)
    same = diagonal(gated.shape[0])
    squares = jnp.sum(jnp.where(same, squares, 0.0), axis=0, keepdims=True)
    crossed = jnp.sum(jnp.where(same, crossed, 0.0), axis=0, keepdims=True)
    at = lax.broadcasted_iota(jnp.int32, stat_ref.shape, 0)
    stat_ref[...] = jnp.where(at == 0, squares, crossed)


def norm_back_kernel(
    perm_ref,
    here_ref,
    hid_ref,
    inner_ref,
    gate_ref,
    ng_ref,
    stat_ref,
    gain_ref,
    mixed_ref,
    wout_ref,
    cot_ref,
    block_refs,
    keep_ref,
    send_ref,
    dy_ref,
    dgate_ref,
    sums_ref,
    outacc_ref,
    inacc_ref,
):
    step = pl.program_id(0)
    span, width = inner_ref.shape

    @pl.when(step == 0)
    def _():
        outacc_ref[...] = jnp.zeros_like(outacc_ref)
        inacc_ref[...] = jnp.zeros_like(inacc_ref)
        sums_ref[...] = jnp.zeros_like(sums_ref)

    same = diagonal(span)
    squares = jnp.sum(jnp.where(same, stat_ref[0:1], 0.0), axis=1, keepdims=True)
    cross = jnp.sum(jnp.where(same, stat_ref[1:2], 0.0), axis=1, keepdims=True)
    inv = lax.rsqrt(squares * (1.0 / INNER) + NORM_EPS)
    gate = gate_ref[...].astype(F32)
    sig = sigmoid(gate)
    silu = gate * sig
    inner = inner_ref[...]
    gated = inner * silu
    unit = gated * inv
    normed = (unit * gain_ref[...]).astype(BF16)
    cot = cot_ref[perm_ref[step]]
    block = nn(normed, wout_ref[...]).astype(BF16)

    for at, block_ref in enumerate(block_refs):

        @pl.when(step == at)
        def _():
            block_ref[...] = block

    outacc_ref[...] += tn(normed, cot)
    grad = ng_ref[...]
    dgated = inv * (grad * gain_ref[...] - unit * (cross * inv * (1.0 / INNER)))
    dy = dgated * silu
    dy_ref[...] = dy
    dgate = (dgated * inner * (sig * (1.0 + gate * (1.0 - sig)))).astype(BF16)
    dgate_ref[...] = dgate
    inacc_ref[...] += tn(hid_ref[...], dgate)
    gain_sum = jnp.sum(grad * unit, axis=0, keepdims=True)
    skip_sum = jnp.sum(dy * mixed_ref[...].astype(F32), axis=0, keepdims=True)
    at = lax.broadcasted_iota(jnp.int32, (8, width), 0)
    sums_ref[...] += jnp.where(at == 0, gain_sum, jnp.where(at == 1, skip_sum, 0.0))

    @pl.when(step == pl.num_programs(0) - 1)
    def _():
        own = here_ref[0]
        rows = inacc_ref.shape[0] // (2 * keep_ref.shape[0])
        part_of(lambda at: inacc_ref[at * rows : (at + 1) * rows], own, keep_ref, send_ref)
        outs = lambda at: outacc_ref[at * HEAD_DIM : (at + 1) * HEAD_DIM]
        part_of(lambda at: outs(at)[:, :width], own, keep_ref, send_ref, rows)
        part_of(lambda at: outs(at)[:, width:], own, keep_ref, send_ref, rows + HEAD_DIM)


def scan_back_kernel(
    perm_ref,
    here_ref,
    hid_ref,
    dy_ref,
    mixed_ref,
    convin_ref,
    convsum_ref,
    raw_ref,
    stepc_ref,
    logc_ref,
    stepr_ref,
    logr_ref,
    start_ref,
    conv_ref,
    hrow_ref,
    segc_ref,
    segr_ref,
    keep_ref,
    send_ref,
    dval_ref,
    dbc_ref,
    dstep_ref,
    convg_ref,
    dtg_ref,
    headg_ref,
    ext_ref,
    seg_ref,
    grad_ref,
    inacc_ref,
    dx_ref,
):
    step = pl.program_id(0)
    chunk = pl.num_programs(0) - 1 - step
    span = hid_ref.shape[0]
    heads = stepc_ref.shape[1]
    width = heads * HEAD_DIM

    @pl.when(step == 0)
    def _():
        ext_ref[span : span + 8] = jnp.zeros((8, width), F32)
        grad_ref[...] = jnp.zeros_like(grad_ref)
        inacc_ref[...] = jnp.zeros_like(inacc_ref)
        convg_ref[...] = jnp.zeros_like(convg_ref)
        dtg_ref[...] = jnp.zeros_like(dtg_ref)
        headg_ref[...] = jnp.zeros_like(headg_ref)

    seg_ref[...] = segc_ref[pl.ds(pl.multiple_of(chunk * span, 8), span + 16), :]
    seg_here = seg_ref[8 : 8 + span]
    low = lax.broadcasted_iota(jnp.int32, (SPAN, 2 * HEAD_DIM), 1) < HEAD_DIM
    earlier = lax.broadcasted_iota(jnp.int32, (SPAN, SPAN), 0) >= lax.broadcasted_iota(
        jnp.int32, (SPAN, SPAN), 1
    )
    head_at = lax.broadcasted_iota(jnp.int32, (heads, SPAN), 0)
    lane_at = lax.broadcasted_iota(jnp.int32, (SPAN, heads), 1)
    at_last = lax.broadcasted_iota(jnp.int32, (SPAN, heads), 0) == SPAN - 1
    skip_w = spread(hrow_ref[2:3] + jnp.zeros((8, heads), F32), width)[0:1]
    step_c = stepc_ref[...]
    step_r = stepr_ref[...]
    later = grad_ref[...]
    count = span // SPAN
    dlogs, dsteps_c, dsteps_r = [None] * count, [None] * count, [None] * count
    for block in reversed(range(count)):
        here = slice(block * SPAN, (block + 1) * SPAN)
        values = mixed_ref[here, :width]
        write = mixed_ref[here, width : width + STATE]
        read = mixed_ref[here, width + STATE :]
        values_f = values.astype(F32)
        seg = seg_here[here]
        seg_prev = seg_ref[7 + block * SPAN : 8 + block * SPAN]
        seg_last = seg_ref[7 + (block + 1) * SPAN : 8 + (block + 1) * SPAN]
        dy = dy_ref[here]
        dy_low = dy.astype(BF16)
        log = logc_ref[here]
        log_row = logr_ref[:, here]
        step_row = step_r[:, here]
        last = log[SPAN - 1 : SPAN]
        enter = jnp.where(seg == seg_prev, jnp.exp(log), 0.0)
        tail_raw = jnp.where(seg == seg_last, jnp.exp(last - log), 0.0)
        tail = tail_raw * step_c[here]
        keep = jnp.where(seg_last == seg_prev, jnp.exp(last), 0.0)
        enter_w = spread(enter, width)
        tail_w = spread(tail, width)
        keep_w = spread(keep + jnp.zeros((8, heads), F32), width)[0:1]
        state = start_ref[block]
        state_low = state.astype(BF16)
        later_low = later.astype(BF16)

        entered_low = (enter_w * dy).astype(BF16)
        inter = enter_w * nn(read, state_low)
        from_later = nn(write, later_low)
        moved_low = (tail_w * values_f).astype(BF16)
        dread = nt(entered_low, state_low)
        dwrite = nt(moved_low, later_low)
        tail_dot = gather_heads(values_f * from_later, heads)
        dlog = gather_heads(dy * inter, heads) - tail_dot * tail
        dsteps_c[block] = tail_dot * tail_raw
        carried = jnp.sum(later * state, axis=0, keepdims=True) + jnp.zeros((8, width), F32)
        carried = gather_heads(carried, heads)[0:1]
        dlog = dlog + jnp.where(
            at_last, jnp.sum(tail_dot * tail, axis=0, keepdims=True) + keep * carried, 0.0
        )
        later = keep_w * later + tn(read, entered_low)
        direct = tail_w * from_later + skip_w * dy

        visible = (seg == segr_ref[:, here]) & earlier
        scores = jnp.where(visible, nt(read, write), 0.0)
        dscores = jnp.zeros((SPAN, SPAN), F32)
        dstep = jnp.zeros((heads, SPAN), F32)
        for pair in range(heads // 2):
            lanes = slice(pair * 2 * HEAD_DIM, (pair + 1) * 2 * HEAD_DIM)
            dy_pair = dy_low[:, lanes]
            pieces = []
            for head in (2 * pair, 2 * pair + 1):
                mine = low if head % 2 == 0 else ~low
                gap = jnp.minimum(log[:, head : head + 1] - log_row[head : head + 1], 0.0)
                decay = jnp.exp(gap)
                outer = nt(jnp.where(mine, dy_pair, jnp.zeros_like(dy_pair)), values[:, lanes])
                fade = decay * step_row[head : head + 1]
                dscores = dscores + outer * fade
                weights = scores * fade
                flow = outer * scores
                dstep = dstep + jnp.where(
                    head_at == head, jnp.sum(flow * decay, axis=0, keepdims=True), 0.0
                )
                dlog = dlog + jnp.where(
                    lane_at == head, jnp.sum(outer * weights, axis=1, keepdims=True), 0.0
                )
                pieces.append(tn(weights.astype(BF16), dy_pair))
            dx_ref[here, lanes] = direct[:, lanes] + jnp.where(low, pieces[0], pieces[1])
        dscores = jnp.where(visible, dscores, 0.0).astype(BF16)
        dbc_ref[here, :STATE] = (dwrite + tn(dscores, read)).astype(BF16)
        dbc_ref[here, STATE:] = (dread + nn(dscores, write)).astype(BF16)
        dlogs[block], dsteps_r[block] = dlog, dstep
    grad_ref[...] = later
    dlog_c = jnp.concatenate(dlogs, axis=0)
    dstep_c = jnp.concatenate(dsteps_c, axis=0)
    dstep_r = jnp.concatenate(dsteps_r, axis=1)

    upper = triangle(span, False)
    eye = jnp.where(diagonal(span), 1.0, 0.0).astype(F32)
    dalpha = nn(upper, dlog_c, HIGHEST) - nt(upper, dstep_r * step_r, HIGHEST)
    dstep = dstep_c + nt(eye, dstep_r, HIGHEST)
    rate = jnp.exp(hrow_ref[0:1])
    draw = (dstep - rate * dalpha) * sigmoid(raw_ref[...])
    draw_low = draw.astype(BF16)
    dstep_ref[...] = draw_low
    hid = hid_ref[...]
    dtg_ref[...] += tn(draw_low, hid)
    rate_sum = jnp.sum(-dalpha * step_c * rate, axis=0, keepdims=True)
    bias_sum = jnp.sum(draw, axis=0, keepdims=True)
    at = lax.broadcasted_iota(jnp.int32, (8, heads), 0)
    headg_ref[...] += jnp.where(at == 0, rate_sum, jnp.where(at == 1, bias_sum, 0.0))

    ext_ref[0:span] = dx_ref[...] * silu_grad(convsum_ref[...])
    back = jnp.zeros((span, width), F32)
    conv_in = convin_ref[...].astype(F32)
    at = lax.broadcasted_iota(jnp.int32, (8, width), 0)
    sums = jnp.where(at == CONV, jnp.sum(ext_ref[0:span], axis=0, keepdims=True), 0.0)
    for tap in range(CONV):
        ahead = CONV - 1 - tap
        same = seg_ref[8 + ahead : 8 + ahead + span] == seg_here
        term = jnp.where(same, ext_ref[ahead : ahead + span], 0.0)
        back = back + conv_ref[tap : tap + 1] * term
        sums = sums + jnp.where(at == tap, jnp.sum(conv_in * term, axis=0, keepdims=True), 0.0)
    convg_ref[...] += sums
    ext_ref[span : span + 8] = ext_ref[0:8]
    dval = back.astype(BF16)
    dval_ref[...] = dval
    inacc_ref[...] += tn(hid, dval)

    @pl.when(step == pl.num_programs(0) - 1)
    def _():
        rows = inacc_ref.shape[0] // (2 * keep_ref.shape[0])
        part_of(lambda at: inacc_ref[at * rows : (at + 1) * rows], here_ref[0], keep_ref, send_ref)


def hidden_back_kernel(
    perm_ref,
    dgate_ref,
    dval_ref,
    dstep_ref,
    wg_ref,
    wv_ref,
    wdt_ref,
    hid_ref,
    gain_ref,
    out_refs,
    gsum_ref,
    turned_ref,
):
    width = wg_ref.shape[1]

    @pl.when(pl.program_id(0) == 0)
    def _():
        gsum_ref[...] = jnp.zeros_like(gsum_ref)
        turned_ref[0:width] = wg_ref[...].T
        turned_ref[width:] = wv_ref[...].T

    total = nn(dgate_ref[...], turned_ref[0:width]) + nn(dval_ref[...], turned_ref[width:])
    total = total + nn(dstep_ref[...], wdt_ref[...])
    step = pl.program_id(0)

    for at, out_ref in enumerate(out_refs):

        @pl.when(step == at)
        def _():
            out_ref[...] = total.astype(BF16)

    unit = hid_ref[...].astype(F32) / gain_ref[...]
    gsum_ref[...] += jnp.sum(total * unit, axis=0, keepdims=True) + jnp.zeros(gsum_ref.shape, F32)


def maps_back_kernel(
    here_ref,
    dbc_ref,
    dbcfar_ref,
    convsum_ref,
    convin_ref,
    conv_ref,
    segc_ref,
    hid_ref,
    w1_ref,
    gain_ref,
    convg_ref,
    sums_ref,
    headg_ref,
    dtg_ref,
    gall_ref,
    keep_ref,
    send_ref,
    own_ref,
    ext_ref,
    acc_ref,
    dmap_ref,
    small_ref,
):
    size, width = dmap_ref.shape
    total = dbc_ref[...].astype(F32) + dbcfar_ref[...].astype(F32)
    ext_ref[0:size] = total * silu_grad(convsum_ref[...])
    ext_ref[size : size + 8] = jnp.zeros((8, width), F32)
    back = jnp.zeros((size, width), F32)
    conv_in = convin_ref[...].astype(F32)
    at = lax.broadcasted_iota(jnp.int32, (8, width), 0)
    sums = jnp.where(at == CONV, jnp.sum(ext_ref[0:size], axis=0, keepdims=True), 0.0)
    seg_here = segc_ref[8 : 8 + size]
    for tap in range(CONV):
        ahead = CONV - 1 - tap
        same = segc_ref[8 + ahead : 8 + ahead + size] == seg_here
        term = jnp.where(same, ext_ref[ahead : ahead + size], 0.0)
        back = back + conv_ref[tap : tap + 1] * term
        sums = sums + jnp.where(at == tap, jnp.sum(conv_in * term, axis=0, keepdims=True), 0.0)
    dmap_ref[...] = back.astype(BF16)
    ctx = here_ref[2]
    acc_ref[...] = tn(hid_ref[...], dmap_ref[...])
    span = own_ref.shape[0]
    own = pl.ds(pl.multiple_of(ctx * span, 16), span)
    grad = nt(dmap_ref[own, :], w1_ref[...])
    own_ref[...] = grad
    unit = hid_ref[own, :].astype(F32) / gain_ref[...]
    gain_sum = gall_ref[0:1] + jnp.sum(grad * unit, axis=0, keepdims=True)
    half = small_ref.shape[1]
    heads = headg_ref.shape[1]
    small_ref[...] = jnp.zeros_like(small_ref)
    small_ref[0 : CONV + 1] = convg_ref[0 : CONV + 1]
    small_ref[CONV + 1 : CONV + 3] = sums_ref[0:2]
    small_ref[7:8, 0:heads] = headg_ref[0:1]
    small_ref[7:8, 128 : 128 + heads] = headg_ref[1:2]
    small_ref[8 : 8 + CONV + 1, 0:width] = sums[0 : CONV + 1]
    small_ref[13:14] = gain_sum[:, :half]
    small_ref[14:15] = gain_sum[:, half:]
    small_ref[15:16] = small_ref[7:8] - small_ref[7:8].astype(BF16).astype(F32)
    small_ref[16:24] = dtg_ref[:, :half]
    small_ref[24:32] = dtg_ref[:, half:]
    small = small_ref[...].astype(BF16)
    count = keep_ref.shape[0] // 32 - 1
    block = acc_ref.shape[0] // (2 * count)
    some = block // 4
    keep_ref[0:32] = small
    send_ref[0:32] = small
    for at in range(count):
        start = pl.multiple_of(2 * at * block + ctx * some, 8)
        low = acc_ref[pl.ds(start, some), :].astype(BF16)
        start = pl.multiple_of((2 * at + 1) * block + ctx * some, 8)
        high = acc_ref[pl.ds(start, some), :].astype(BF16)
        keep_ref[32 + 32 * at : 64 + 32 * at, 0:width] = jnp.where(here_ref[0] == 0, low, high)
        send_ref[32 + 32 * at : 64 + 32 * at, 0:width] = jnp.where(here_ref[0] == 0, high, low)


def input_back_kernel(part_refs, own_ref, tok_ref, gain_ref, cot_ref, out_ref):
    grad = own_ref[...]
    for ref in part_refs:
        grad = grad + ref[...].astype(F32)
    tok = tok_ref[...]
    scale = lax.rsqrt(jnp.mean(tok * tok, axis=-1, keepdims=True) + NORM_EPS)
    unit = tok * scale
    scaled = grad * gain_ref[...]
    mean = jnp.mean(scaled * unit, axis=-1, keepdims=True)
    out_ref[...] = cot_ref[...] + scale * (scaled - unit * mean)


def with_rest(value, first):
    row = lax.broadcasted_iota(jnp.int32, value.shape, 0)
    head = value[first + 7 : first + 8] + value[first + 15 : first + 16]
    rest = head - head.astype(BF16).astype(F32)
    return jnp.where(row == first + 7, head, jnp.where(row == first + 15, rest, value))


def pair_sum_late_kernel(keep_ref, came_ref, mkeep_ref, mcame_ref, out_ref):
    count, rows, width = keep_ref.shape
    small = with_rest(mkeep_ref[0:32].astype(F32) + mcame_ref[0:32].astype(F32), 0).astype(BF16)
    for block in range(count):
        out_ref[block, 0:rows] = (keep_ref[block].astype(F32) + came_ref[block].astype(F32)).astype(BF16)
        out_ref[block, rows : rows + 32] = small
        at = slice(32 + 32 * block, 64 + 32 * block)
        out_ref[block, rows + 32 : rows + 64] = (
            mkeep_ref[at].astype(F32) + mcame_ref[at].astype(F32)
        ).astype(BF16)


def sum_late_kernel(parts_ref, out_ref):
    total = parts_ref[0].astype(F32)
    for at in range(1, parts_ref.shape[0]):
        total = total + parts_ref[at].astype(F32)
    out_ref[...] = with_rest(total, out_ref.shape[0] - 64).astype(BF16)


def adam_out_kernel(here_ref, weight_ref, first_ref, second_ref, early_refs, *rest):
    new_refs, early_ref = rest[:3], rest[3]
    step = pl.program_id(0)

    @pl.when(step == 0)
    def _():
        by_owner(early_refs, here_ref[2], early_ref)

    rows = weight_ref.shape[0]
    width = early_ref.shape[2]
    first = early_ref.shape[1] - 2 * rows
    for at in range(2):
        lanes = slice(at * width, (at + 1) * width)
        grad = early_ref[step, first + at * rows : first + (at + 1) * rows].astype(F32)
        news = adam_step(
            weight_ref[:, lanes], first_ref[:, lanes], second_ref[:, lanes], grad, 0.02, WEIGHT_DECAY
        )
        for ref, new in zip(new_refs, news):
            ref[:, lanes] = new


def by_owner(refs, ctx, natural_ref):
    for at, ref in enumerate(refs):
        natural_ref[pl.ds(ctx ^ at, 1)] = ref[...][None]


def adam_in_kernel(here_ref, weight_ref, first_ref, second_ref, early_refs, late_refs, *rest):
    new_refs, (early_ref, late_ref) = rest[:3], rest[3:]
    step = pl.program_id(0)
    pieces = len(early_refs)
    rows = weight_ref.shape[0]
    width = early_ref.shape[2]
    block = pieces * HEAD_DIM

    @pl.when(step == 0)
    def _():
        by_owner(early_refs, here_ref[2], early_ref)
        by_owner(late_refs, here_ref[2], late_ref)

    here = pl.ds(pl.multiple_of(step * rows, rows), rows)
    low = lax.broadcasted_iota(jnp.int32, (rows, 2 * HEAD_DIM), 1) < HEAD_DIM

    def update(lanes, grad):
        news = adam_step(
            weight_ref[:, lanes], first_ref[:, lanes], second_ref[:, lanes], grad, 0.03, WEIGHT_DECAY
        )
        for ref, new in zip(new_refs, news):
            ref[:, lanes] = new

    for base, ref in ((0, early_ref), (INNER, late_ref)):
        for pair in range(width // (2 * HEAD_DIM)):
            lanes = slice(pair * 2 * HEAD_DIM, (pair + 1) * 2 * HEAD_DIM)
            for at in range(0, pieces, 2):
                first = ref[at, here, lanes].astype(F32)
                second = ref[at + 1, here, lanes].astype(F32)
                start = base + 2 * pair * block + at * HEAD_DIM
                even = jnp.where(low, first, pltpu.roll(second, HEAD_DIM, 1))
                update(slice(start, start + 2 * HEAD_DIM), even)
                start = start + block
                odd = jnp.where(low, pltpu.roll(first, HEAD_DIM, 1), second)
                update(slice(start, start + 2 * HEAD_DIM), odd)
    some = 32 // rows
    first = pl.multiple_of(late_ref.shape[1] - 32 + (step % some) * rows, rows)
    grad = late_ref[step // some, pl.ds(first, rows), 0 : 2 * STATE].astype(F32)
    update(slice(2 * INNER, 2 * INNER + 2 * STATE), grad)


def swap(value, axis, bit):
    count = lax.axis_size(axis)
    return lax.ppermute(value, axis, [(at, at ^ bit) for at in range(count)])


def gather_ctx(value):
    far = swap(value, "ctx", 2)
    return [value, swap(value, "ctx", 1), far, swap(far, "ctx", 1)]


def high_all_to_all(value):
    count = lax.axis_size("dp")
    groups = [list(range(low, count, 2)) for low in range(2)]
    return lax.all_to_all(value, "dp", 0, 0, axis_index_groups=groups)


def from_owners(parts):
    count = len(parts)
    return [swap(parts[bit - 1], "ctx", bit) for bit in range(1, count)] + [parts[-1]]


def fan_ctx(value):
    return [value] + [swap(value, "ctx", bit) for bit in range(1, lax.axis_size("ctx"))]


def adam_step(weight, moment_one, second, gradient, step_rate, decay_rate):
    moment_new = BETA_ONE * moment_one + (1.0 - BETA_ONE) * gradient
    second_new = BETA_TWO * second + (1.0 - BETA_TWO) * gradient * gradient
    first_hat = moment_new / (1.0 - BETA_ONE**STEP)
    second_hat = second_new / (1.0 - BETA_TWO**STEP)
    weight_new = weight - step_rate * (
        first_hat / (jnp.sqrt(second_hat) + ADAM_EPS) + decay_rate * weight
    )
    return (weight_new, moment_new, second_new)


def full(shape):
    return pl.BlockSpec(shape, lambda *_: (0,) * len(shape))


def shape_of(*shape, dtype=F32):
    return jax.ShapeDtypeStruct(shape, dtype)


def shards(
    tokens,
    segment_ids,
    cotangent,
    in_weight,
    dt_weight,
    out_weight,
    conv_params,
    gains,
    head_params,
    in_first,
    in_second,
    dt_first,
    dt_second,
    out_first,
    out_second,
    conv_first,
    conv_second,
    gain_first,
    gain_second,
    head_first,
    head_second,
):
    _, span, model = tokens.shape
    length = segment_ids.shape[1]
    ndp, nctx = lax.axis_size("dp"), lax.axis_size("ctx")
    d, c = lax.axis_index("dp"), lax.axis_index("ctx")
    heads = HEADS // nctx
    width = INNER // nctx
    maps = 2 * STATE
    wide = width + maps
    chunks = nctx
    rows_in = in_weight.shape[0]
    conv_cols = conv_params.shape[1]
    gain_len = gains.shape[0]
    dt_cols = dt_weight.shape[1]
    near = ndp == heads
    high = heads // 2
    block_in = model // heads
    tok = tokens[0]
    bits = jnp.stack([d & 1, d >> 1, c] if near else [0 * d, 0 * d, c]).astype(jnp.int32)
    perm = c ^ jnp.asarray([1, 2, 3, 0], jnp.int32)
    smem = pl.BlockSpec(memory_space=pltpu.SMEM)
    vmem = pl.BlockSpec(memory_space=pltpu.VMEM)
    anywhere = lambda pieces: [pl.BlockSpec(memory_space=pl.ANY)] * len(pieces)

    w1, g2 = pl.pallas_call(
        pack_kernel,
        in_specs=[smem] + [vmem] * 5,
        out_shape=[
            shape_of(high if near else 1, rows_in + 16, wide, dtype=BF16),
            shape_of(high if near else 1, rows_in + (2 * HEAD_DIM if near else 0), width, dtype=BF16),
        ],
        scratch_shapes=[pltpu.VMEM((16, wide), F32)],
        compiler_params=params(),
        name="pack",
    )(bits, in_weight, out_weight, dt_weight, conv_params, gains)
    cot_low = cotangent[0].astype(BF16)
    if near:
        tok_far = swap(tok, "ctx", 2)
        tok_core = swap(tok, "ctx", 1)
        w1 = high_all_to_all(w1)
        w1, g2, cot_low = lax.optimization_barrier((w1, g2, cot_low))
        w1_came = swap(w1, "dp", 1)
        g2 = high_all_to_all(g2)
        cot_far = swap(cot_low, "ctx", 2)
        w1, w1_came, tok_far = lax.optimization_barrier((w1, w1_came, tok_far))
        toks = [tok, tok_core, tok_far, swap(tok_far, "ctx", 1)]
        w1, w1_came, toks, g2, cot_far, cot_low = lax.optimization_barrier(
            (w1, w1_came, toks, g2, cot_far, cot_low)
        )
        w1 = [w1, w1_came]
        g2 = [g2, swap(g2, "dp", 1)]
        cots = [cot_low, swap(cot_low, "ctx", 1), cot_far, swap(cot_far, "ctx", 1)]
        at_rows = at_g2 = jnp.stack([d & 1, 1 - (d & 1)]).astype(jnp.int32)
    else:
        w1 = [lax.all_gather(w1[0], "dp", axis=0)]
        toks = gather_ctx(tok)
        cots = gather_ctx(cot_low)
        wg = lax.all_gather(g2[0], "dp", axis=0, tiled=True).reshape(heads, block_in, width)
        wout = lax.all_gather(out_weight.astype(BF16), "dp", axis=0, tiled=True)
        wout = lax.dynamic_index_in_dim(wout.reshape(heads, nctx, HEAD_DIM, model), c, 1, False)
        g2 = [jnp.concatenate([wg, wout[:, :, :width], wout[:, :, width:]], axis=1)]
        at_rows = at_g2 = jnp.zeros((1,), jnp.int32)

    ids = segment_ids[0]
    seg_col = jnp.pad(ids, (8, 8), constant_values=-1)[:, None]
    seg_row = segment_ids
    head_mine = lax.dynamic_index_in_dim(head_params.reshape(3, heads, nctx), c, 2, False)
    head_col = head_mine.T

    rows = lambda cols: pl.BlockSpec((span, cols), lambda i, *_: (i, 0))
    row_of = pl.BlockSpec((heads, span), lambda i, *_: (0, i))
    rows_at = lambda cols: pl.BlockSpec((span, cols), lambda i, p, *_: (p[i], 0))
    whole = full((span, model))
    shards_in = sum(piece.shape[0] for piece in w1)

    (
        hid, conv_mine, gain_pre, gain_mine, dt_mine, w1, mixed, conv_in, conv_sum, inner, raw,
        step_c, log_c, step_r, log_r, starts,
    ) = pl.pallas_call(
        scan_forward_kernel,
        grid_spec=pltpu.PrefetchScalarGridSpec(
            num_scalar_prefetch=2,
            grid=(chunks,),
            in_specs=[
                anywhere(toks),
                anywhere(w1),
                full((3, heads)),
                full((heads, 3)),
                full((length + 16, 1)),
                pl.BlockSpec((1, span), lambda i, *_: (0, i)),
            ],
            out_specs=[
                rows(model),
                full((8, wide)),
                full((1, model)),
                full((1, width)),
                full((heads, model)),
                full((model, wide)),
                rows(wide),
                rows(wide),
                rows(wide),
                rows(width),
                rows(heads),
                rows(heads),
                rows(heads),
                row_of,
                row_of,
                pl.BlockSpec((span // SPAN, STATE, width), lambda i, *_: (i, 0, 0)),
            ],
            scratch_shapes=[
                pltpu.VMEM((span + 8, wide), F32),
                pltpu.VMEM((span + 8, 1), jnp.int32),
                pltpu.VMEM((STATE, width), F32),
                pltpu.VMEM((shards_in, 16, wide), BF16),
                pltpu.VMEM((nctx, span, model), F32),
                pltpu.VMEM((8, INNER + maps), F32),
                pltpu.VMEM((1, model + INNER), F32),
                pltpu.SemaphoreType.DMA((copies_of(w1, 2),)),
                pltpu.SemaphoreType.DMA((nctx,)),
            ],
        ),
        out_shape=[
            shape_of(length, model, dtype=BF16),
            shape_of(8, wide),
            shape_of(1, model),
            shape_of(1, width),
            shape_of(heads, model, dtype=BF16),
            shape_of(model, wide, dtype=BF16),
            shape_of(length, wide, dtype=BF16),
            shape_of(length, wide, dtype=BF16),
            shape_of(length, wide),
            shape_of(length, width),
            shape_of(length, heads),
            shape_of(length, heads),
            shape_of(length, heads),
            shape_of(heads, length),
            shape_of(heads, length),
            shape_of(length // SPAN, STATE, width),
        ],
        compiler_params=params("arbitrary"),
        name="scan_forward",
    )(bits, at_rows, toks, w1, head_mine, head_col, seg_col, seg_row)

    wg, wout, cot_all, gate, normed_grad, stats = pl.pallas_call(
        gate_kernel,
        grid_spec=pltpu.PrefetchScalarGridSpec(
            num_scalar_prefetch=2,
            grid=(chunks,),
            in_specs=[rows(model), anywhere(g2), anywhere(cots), rows(width), full((1, width))],
            out_specs=[
                full((model, width)),
                full((width, model)),
                full((nctx, span, model)),
                rows(width),
                rows(width),
                pl.BlockSpec((8, span), lambda i, *_: (0, i)),
            ],
            scratch_shapes=[
                pltpu.VMEM((model, width), BF16),
                pltpu.SemaphoreType.DMA((copies_of(g2, 3),)),
                pltpu.SemaphoreType.DMA((nctx,)),
            ],
        ),
        out_shape=[
            shape_of(model, width, dtype=BF16),
            shape_of(width, model, dtype=BF16),
            shape_of(nctx, span, model, dtype=BF16),
            shape_of(length, width, dtype=BF16),
            shape_of(length, width),
            shape_of(8, length),
        ],
        compiler_params=params("arbitrary"),
        name="gate",
    )(bits, at_g2, hid, g2, cots, inner, gain_mine)
    stats = sum(fan_ctx(stats))

    early_rows = block_in + 2 * HEAD_DIM
    blocks_out, early_keep, early_send, dy, dgate, col_sums = pl.pallas_call(
        norm_back_kernel,
        grid_spec=pltpu.PrefetchScalarGridSpec(
            num_scalar_prefetch=2,
            grid=(chunks,),
            in_specs=[
                rows_at(model),
                rows_at(width),
                rows_at(width),
                rows_at(width),
                pl.BlockSpec((8, span), lambda i, p, *_: (0, p[i])),
                full((1, width)),
                rows_at(width),
                full((width, model)),
                full((nctx, span, model)),
            ],
            out_specs=[
                [whole] * nctx,
                full((high, early_rows, width)),
                full((high, early_rows, width)),
                rows_at(width),
                rows_at(width),
                full((8, width)),
            ],
            scratch_shapes=[pltpu.VMEM((width, model), F32), pltpu.VMEM((model, width), F32)],
        ),
        out_shape=[
            [shape_of(span, model, dtype=BF16)] * nctx,
            shape_of(high, early_rows, width, dtype=BF16),
            shape_of(high, early_rows, width, dtype=BF16),
            shape_of(length, width),
            shape_of(length, width, dtype=BF16),
            shape_of(8, width),
        ],
        compiler_params=params("arbitrary"),
        name="norm_back",
    )(perm, bits, hid, inner, gate, normed_grad, stats, gain_mine, mixed, wout, cot_all)
    blocks_out = from_owners(blocks_out)
    if near:
        early_came = swap(early_send, "dp", 1)

    back = lambda cols: pl.BlockSpec((span, cols), lambda i, *_: (chunks - 1 - i, 0))
    back_row = pl.BlockSpec((heads, span), lambda i, *_: (0, chunks - 1 - i))
    late_keep, late_send, dval, dbc, dstep, conv_grad, dt_grad, head_grad = pl.pallas_call(
        scan_back_kernel,
        grid_spec=pltpu.PrefetchScalarGridSpec(
            num_scalar_prefetch=2,
            grid=(chunks,),
            in_specs=[
                back(model),
                back(width),
                back(wide),
                back(width),
                back(width),
                back(heads),
                back(heads),
                back(heads),
                back_row,
                back_row,
                pl.BlockSpec((span // SPAN, STATE, width), lambda i, *_: (chunks - 1 - i, 0, 0)),
                full((8, width)),
                full((3, heads)),
                full((length + 16, 1)),
                pl.BlockSpec((1, span), lambda i, *_: (0, chunks - 1 - i)),
            ],
            out_specs=[
                full((high, block_in, width)),
                full((high, block_in, width)),
                back(width),
                back(maps),
                back(heads),
                full((8, width)),
                full((heads, model)),
                full((8, heads)),
            ],
            scratch_shapes=[
                pltpu.VMEM((span + 8, width), F32),
                pltpu.VMEM((span + 16, 1), jnp.int32),
                pltpu.VMEM((STATE, width), F32),
                pltpu.VMEM((model, width), F32),
                pltpu.VMEM((span, width), F32),
            ],
        ),
        out_shape=[
            shape_of(high, block_in, width, dtype=BF16),
            shape_of(high, block_in, width, dtype=BF16),
            shape_of(length, width, dtype=BF16),
            shape_of(length, maps, dtype=BF16),
            shape_of(length, heads, dtype=BF16),
            shape_of(8, width),
            shape_of(heads, model),
            shape_of(8, heads),
        ],
        compiler_params=params("arbitrary"),
        name="scan_back",
    )(
        perm, bits, hid, dy, mixed, conv_in, conv_sum, raw, step_c, log_c, step_r, log_r, starts,
        conv_mine, head_mine, seg_col, seg_row,
    )
    dbc_came = swap(dbc, "ctx", 1)
    if near:
        late_came = swap(late_send, "dp", 1)
        early_came, blocks_out, dval = lax.optimization_barrier((early_came, blocks_out, dval))
    dbc = (dbc.astype(F32) + dbc_came.astype(F32)).astype(BF16)
    if near:
        early_came, dbc = lax.optimization_barrier((early_came, dbc))
        early_parts = (early_keep.astype(F32) + early_came.astype(F32)).astype(BF16)
    dbc_far = swap(dbc, "ctx", 2)
    if near:
        dval, early_parts = lax.optimization_barrier((dval, early_parts))
        early_parts = high_all_to_all(early_parts)
        dbc_far, late_came = lax.optimization_barrier((dbc_far, late_came))

    hidden_out, gain_sum = pl.pallas_call(
        hidden_back_kernel,
        grid_spec=pltpu.PrefetchScalarGridSpec(
            num_scalar_prefetch=1,
            grid=(chunks,),
            in_specs=[
                rows_at(width),
                rows_at(width),
                rows_at(heads),
                full((model, width)),
                full((model, width)),
                full((heads, model)),
                rows_at(model),
                full((1, model)),
            ],
            out_specs=[[whole] * nctx, full((8, model))],
            scratch_shapes=[pltpu.VMEM((2 * width, model), BF16)],
        ),
        out_shape=[
            [shape_of(span, model, dtype=BF16)] * nctx,
            shape_of(8, model),
        ],
        compiler_params=params("arbitrary"),
        name="hidden_back",
    )(perm, dgate, dval, dstep, wg, w1, dt_mine, hid, gain_pre)
    hidden_out = from_owners(hidden_out)
    map_rows = 32 + 32 * high
    map_cols = lambda size: pl.BlockSpec((size, maps), lambda i: (0, width // maps))
    map_keep, map_send, hidden_own = pl.pallas_call(
        maps_back_kernel,
        grid=(1,),
        in_specs=[
            smem,
            full((length, maps)),
            full((length, maps)),
            map_cols(length),
            map_cols(length),
            map_cols(8),
            full((length + 16, 1)),
            full((length, model)),
            map_cols(model),
            full((1, model)),
            full((8, width)),
            full((8, width)),
            full((8, heads)),
            full((heads, model)),
            full((8, model)),
        ],
        out_specs=[full((map_rows, width)), full((map_rows, width)), full((span, model))],
        out_shape=[
            shape_of(map_rows, width, dtype=BF16),
            shape_of(map_rows, width, dtype=BF16),
            shape_of(span, model),
        ],
        scratch_shapes=[
            pltpu.VMEM((length + 8, maps), F32),
            pltpu.VMEM((model, maps), F32),
            pltpu.VMEM((length, maps), BF16),
            pltpu.VMEM((32, width), F32),
        ],
        compiler_params=params("arbitrary"),
        name="maps_back",
    )(
        bits,
        dbc,
        dbc_far,
        conv_sum,
        conv_in,
        conv_mine,
        seg_col,
        hid,
        w1,
        gain_pre,
        conv_grad,
        col_sums,
        head_grad,
        dt_grad,
        gain_sum,
    )

    block_output = tok + sum(part.astype(F32) for part in blocks_out)

    input_part = lambda parts, own: pl.pallas_call(
        input_back_kernel,
        in_specs=[[vmem] * nctx] + [vmem] * 4,
        out_shape=shape_of(span, model),
        compiler_params=params(),
        name="input_back",
    )(parts, own, tok, gain_pre, cotangent[0])

    late_rows = block_in + 64
    if near:
        map_came = swap(map_send, "dp", 1)
        late_parts = pl.pallas_call(
            pair_sum_late_kernel,
            out_shape=shape_of(high, late_rows, width, dtype=BF16),
            compiler_params=params(),
            name="pair_sum_late",
        )(late_keep, late_came, map_keep, map_came)
        late_parts = high_all_to_all(late_parts)
        early = jnp.sum(early_parts.astype(F32), axis=0).astype(BF16)
        early = gather_ctx(early)
        row_block = lambda ref_rows, cols: pl.BlockSpec((ref_rows, cols), lambda i, *_: (i, 0))
        out_block = row_block(out_weight.shape[0] // nctx, model)
        early_spec = [full((early_rows, width))] * nctx
        early_scratch = pltpu.VMEM((nctx, early_rows, width), BF16)
        out_new = pl.pallas_call(
            adam_out_kernel,
            grid_spec=pltpu.PrefetchScalarGridSpec(
                num_scalar_prefetch=1,
                grid=(nctx,),
                in_specs=[out_block] * 3 + [early_spec],
                out_specs=[out_block] * 3,
                scratch_shapes=[early_scratch],
            ),
            out_shape=[shape_of(*out_weight.shape)] * 3,
            compiler_params=params("arbitrary"),
            name="adam_out",
        )(bits, out_weight, out_first, out_second, early)

        late_parts, block_output, out_new = lax.optimization_barrier((late_parts, block_output, out_new))
        late = pl.pallas_call(
            sum_late_kernel,
            out_shape=shape_of(late_rows, width, dtype=BF16),
            compiler_params=params(),
            name="sum_late",
        )(late_parts)
        late, hidden_out = lax.optimization_barrier((late, hidden_out))
        late = fan_ctx(late)
        input_grad = input_part(hidden_out, hidden_own)
        late, input_grad = lax.optimization_barrier((late, input_grad))
        in_block = row_block(32, in_weight.shape[1])
        in_new = pl.pallas_call(
            adam_in_kernel,
            grid_spec=pltpu.PrefetchScalarGridSpec(
                num_scalar_prefetch=1,
                grid=(rows_in // 32,),
                in_specs=[in_block] * 3 + [early_spec, [full((late_rows, width))] * nctx],
                out_specs=[in_block] * 3,
                scratch_shapes=[early_scratch, pltpu.VMEM((nctx, late_rows, width), BF16)],
            ),
            out_shape=[shape_of(*in_weight.shape)] * 3,
            compiler_params=params("arbitrary"),
            name="adam_in",
        )(bits, in_weight, in_first, in_second, early, late)
        in_new, out_new = tuple(in_new), tuple(out_new)
        small = jnp.stack([part[block_in : block_in + 32] for part in late])[c ^ jnp.arange(nctx)]
        small = small.astype(F32)
    else:
        input_grad = input_part(hidden_out, hidden_own)
        blocks = lambda keep, send: jnp.stack([keep, send], axis=1).reshape((heads,) + keep.shape[1:])
        early = blocks(early_keep, early_send).astype(F32)
        late = blocks(late_keep, late_send).astype(F32)
        part = lambda value: value[32:].reshape(high, 32, width)[:, :, :maps]
        map_blocks = blocks(part(map_keep), part(map_send)).astype(F32)

        def total(value):
            return lax.psum_scatter(value, "dp", scatter_dimension=0, tiled=True)

        def spaced(value):
            place_at = (jnp.arange(nctx) == c).astype(F32).reshape((1, nctx, 1, 1))
            value = value[:, None] * place_at
            return lax.psum(total(value.reshape(-1, value.shape[-1])), "ctx")

        def by_head(value):
            value = lax.all_gather(total(value.reshape(model, width)), "ctx", axis=0)
            value = value.reshape(nctx, rows_in, heads, HEAD_DIM)
            return jnp.transpose(value, (1, 2, 0, 3)).reshape(rows_in, INNER)

        in_total = jnp.concatenate(
            [by_head(early[:, :block_in]), by_head(late), spaced(map_blocks)], axis=1
        )
        out_total = spaced(
            jnp.concatenate([early[:, block_in : block_in + HEAD_DIM], early[:, block_in + HEAD_DIM :]], axis=2)
        )
        in_new = adam_step(in_weight, in_first, in_second, in_total, 0.03, WEIGHT_DECAY)
        out_new = adam_step(out_weight, out_first, out_second, out_total, 0.02, WEIGHT_DECAY)
        small = lax.all_gather(lax.psum(map_keep[:32].astype(F32), "dp"), "ctx", axis=0)

    def in_order(value):
        return jnp.swapaxes(value.reshape(nctx, -1, heads, HEAD_DIM), 0, 1).swapaxes(1, 2).reshape(-1, INNER)

    columns = in_order(small[:, : CONV + 2])
    conv_total = jnp.concatenate([columns[: CONV + 1], small[0, 8 : 8 + CONV + 1, :maps]], axis=1)
    conv_total = lax.dynamic_slice_in_dim(conv_total, d * conv_cols, conv_cols, 1)
    dt_total = small[:, 16:32].reshape(nctx, 2, heads, width)
    dt_total = jnp.transpose(dt_total, (2, 0, 1, 3)).reshape(HEADS, model)
    dt_total = lax.dynamic_slice_in_dim(dt_total, d * dt_cols, dt_cols, 1)
    pre_total = jnp.sum(small[:, 13:15], axis=0).reshape(-1)
    gain_total = jnp.concatenate([pre_total, columns[CONV + 1]])
    gain_total = lax.dynamic_slice_in_dim(gain_total, d * gain_len, gain_len, 0)
    head_row = small[:, 7] + small[:, 15]
    head_total = jnp.stack(
        [
            head_row[:, :heads].T.reshape(-1),
            head_row[:, 128 : 128 + heads].T.reshape(-1),
            jnp.sum(small[:, CONV + 2].reshape(nctx, heads, HEAD_DIM), axis=2).T.reshape(-1),
        ]
    )

    dt_new = adam_step(dt_weight, dt_first, dt_second, dt_total, 0.03, WEIGHT_DECAY)
    conv_new = adam_step(conv_params, conv_first, conv_second, conv_total, 0.3, 0.0)
    gain_new = adam_step(gains, gain_first, gain_second, gain_total, 0.5, 0.0)
    head_new = adam_step(head_params, head_first, head_second, head_total, 2.0, 0.0)
    return (block_output[None], input_grad[None]) + in_new + dt_new + out_new + conv_new + gain_new + head_new


def solution(mesh):
    tokens, rows, cols = P("dp", "ctx", None), P("dp", None), P(None, "dp")
    return jax.shard_map(
        shards,
        mesh=mesh,
        in_specs=(tokens, rows, tokens, rows, cols, rows, cols, P("dp"), P())
        + (rows, rows, cols, cols, rows, rows, cols, cols, P("dp"), P("dp"), P(), P()),
        out_specs=(tokens, tokens)
        + (rows,) * 3
        + (cols,) * 3
        + (rows,) * 3
        + (cols,) * 3
        + (P("dp"),) * 3
        + (P(),) * 3,
        check_vma=False,
    )
```

```python
import functools

import jax
import jax.numpy as jnp
from jax import lax
from jax.experimental import pallas as pl
from jax.experimental.pallas import tpu as pltpu
from jax.sharding import PartitionSpec as P

INNER = 2048
HEADS = 32
HEAD_DIM = 64
STATE = 128
CONV = 4
STEP = 10
SPAN = 128

F32 = jnp.float32
BF16 = jnp.bfloat16
HIGHEST = lax.Precision.HIGHEST
NORM_EPS = 1e-05
BETA_ONE = 0.9
BETA_TWO = 0.95
ADAM_EPS = 1e-08
WEIGHT_DECAY = 0.1
VMEM_LIMIT = 56 * 1024 * 1024


def nn(a, b, precision=None):
    return lax.dot_general(
        a, b, (((1,), (0,)), ((), ())), precision=precision, preferred_element_type=F32
    )


def nt(a, b, precision=None):
    return lax.dot_general(
        a, b, (((1,), (1,)), ((), ())), precision=precision, preferred_element_type=F32
    )


def tn(a, b, precision=None):
    return lax.dot_general(
        a, b, (((0,), (0,)), ((), ())), precision=precision, preferred_element_type=F32
    )


def halves(value):
    high = value.astype(BF16)
    return high, (value - high.astype(F32)).astype(BF16)


def spread(value, width):
    heads = value.shape[1]
    row = lax.broadcasted_iota(jnp.int32, (heads, width), 0)
    col = lax.broadcasted_iota(jnp.int32, (heads, width), 1)
    table = jnp.where(col // HEAD_DIM == row, 1.0, 0.0).astype(BF16)
    high, low = halves(value)
    return nn(high, table) + nn(low, table)


def gather_heads(value, heads):
    width = value.shape[1]
    row = lax.broadcasted_iota(jnp.int32, (width, heads), 0)
    col = lax.broadcasted_iota(jnp.int32, (width, heads), 1)
    table = jnp.where(row // HEAD_DIM == col, 1.0, 0.0).astype(BF16)
    high, low = halves(value)
    return nn(high, table) + nn(low, table)


def softplus(value):
    return jnp.maximum(value, 0.0) + jnp.log1p(jnp.exp(-jnp.abs(value)))


def sigmoid(value):
    return 1.0 / (1.0 + jnp.exp(-value))


def silu_grad(value):
    sig = sigmoid(value)
    return sig * (1.0 + value * (1.0 - sig))


def diagonal(size):
    row = lax.broadcasted_iota(jnp.int32, (size, size), 0)
    return row == lax.broadcasted_iota(jnp.int32, (size, size), 1)


def triangle(size, lower):
    row = lax.broadcasted_iota(jnp.int32, (size, size), 0)
    col = lax.broadcasted_iota(jnp.int32, (size, size), 1)
    keep = (row >= col if lower else row <= col) & (row // SPAN == col // SPAN)
    return jnp.where(keep, 1.0, 0.0).astype(F32)


def params(*semantics):
    return pltpu.CompilerParams(
        dimension_semantics=semantics or None, vmem_limit_bytes=VMEM_LIMIT
    )


def place(pieces, at_ref, stride, sems, targets):
    copies = []
    for index, piece in enumerate(pieces):
        for block in range(piece.shape[0]):
            for first, rows, target in targets:
                copies.append(
                    pltpu.make_async_copy(
                        piece.at[block, first : first + rows],
                        target(at_ref[index] + stride * block),
                        sems.at[len(copies)],
                    )
                )
    for copy in copies:
        copy.start()
    return copies


def copies_of(pieces, targets):
    return sum(piece.shape[0] for piece in pieces) * targets


def rows_of(ref, rows):
    return lambda at: ref.at[pl.ds(pl.multiple_of(at * rows, 16), rows)]


def part_of(block, own_bit, keep_ref, send_ref, first=0):
    for at in range(keep_ref.shape[0]):
        low, high = block(2 * at).astype(BF16), block(2 * at + 1).astype(BF16)
        rows = slice(first, first + low.shape[0])
        keep_ref[at, rows] = jnp.where(own_bit == 0, low, high)
        send_ref[at, rows] = jnp.where(own_bit == 0, high, low)


def pick_heads(ref, base, ctx, heads):
    first = pl.multiple_of(base + (ctx >> 1) * 2 * HEAD_DIM, 2 * HEAD_DIM)
    wide = ref[:, pl.ds(first, 2 * HEAD_DIM)]
    low = lax.broadcasted_iota(jnp.int32, wide.shape, 1) < HEAD_DIM
    odd = (ctx & 1) == 1
    out = []
    for pair in range(heads // 2):
        parts = []
        for head in (2 * pair, 2 * pair + 1):
            first = pl.multiple_of(base + head * 4 * HEAD_DIM + (ctx >> 1) * 2 * HEAD_DIM, 2 * HEAD_DIM)
            parts.append(ref[:, pl.ds(first, 2 * HEAD_DIM)])
        even = jnp.where(low, parts[0], pltpu.roll(parts[1], HEAD_DIM, 1))
        other = jnp.where(low, pltpu.roll(parts[0], HEAD_DIM, 1), parts[1])
        out.append(jnp.where(odd, other, even))
    return out


def conv_back(size, width, grad, convsum_ref, convin_ref, conv_ref, ext_ref, seg, out_ref):
    sums = [[jnp.zeros((1, 128), F32)] * (CONV + 1) for _ in range(0, width, 128)]
    for first in range(0, size, 64):
        here = slice(first, first + 64)
        for strip, lane in enumerate(range(0, width, 128)):
            lanes = slice(lane, lane + 128)
            value = grad(here, lanes) * silu_grad(convsum_ref[here, lanes])
            ext_ref[here, lanes] = value
            sums[strip][CONV] = sums[strip][CONV] + jnp.sum(value, axis=0, keepdims=True)
    for first in range(0, size, 64):
        here = slice(first, first + 64)
        ids = seg(first, 64)
        same = [
            jnp.broadcast_to(seg(first + CONV - 1 - tap, 64) == ids, (64, 128)) for tap in range(CONV - 1)
        ]
        for strip, lane in enumerate(range(0, width, 128)):
            lanes = slice(lane, lane + 128)
            conv_in = convin_ref[here, lanes].astype(F32)
            back = jnp.zeros((64, 128), F32)
            for tap in range(CONV):
                at = first + CONV - 1 - tap
                term = ext_ref[at : at + 64, lanes]
                if tap < CONV - 1:
                    term = jnp.where(same[tap], term, 0.0)
                back = back + conv_ref[tap : tap + 1, lanes] * term
                sums[strip][tap] = sums[strip][tap] + jnp.sum(conv_in * term, axis=0, keepdims=True)
            out_ref[here, lanes] = back.astype(BF16)
    row = lax.broadcasted_iota(jnp.int32, (8, 128), 0)
    out = []
    for strip in sums:
        total = jnp.zeros((8, 128), F32)
        for at, value in enumerate(strip):
            total = jnp.where(row == at, value, total)
        out.append(total)
    return jnp.concatenate(out, axis=1)


def pack_kernel(here_ref, win_ref, wout_ref, dt_ref, conv_ref, gain_ref, w1_ref, g2_ref, tmp_ref):
    ctx = here_ref[2]
    rows = win_ref.shape[0]
    heads = HEADS // 4
    width = heads * HEAD_DIM
    copies = range(w1_ref.shape[0])
    for at, part in enumerate(pick_heads(win_ref, INNER, ctx, heads)):
        part = part.astype(BF16)
        for copy in copies:
            w1_ref[copy, 0:rows, at * 128 : (at + 1) * 128] = part
    part = win_ref[:, 2 * INNER :].astype(BF16)
    for copy in copies:
        w1_ref[copy, 0:rows, width:] = part
    tmp_ref[...] = jnp.zeros_like(tmp_ref)
    row = lax.broadcasted_iota(jnp.int32, (heads, HEADS), 0)
    col = lax.broadcasted_iota(jnp.int32, (heads, HEADS), 1)
    table = jnp.where(col == 4 * row + ctx, 1.0, 0.0).astype(BF16)
    tmp_ref[0:heads, 384 : 384 + dt_ref.shape[1]] = nn(table, dt_ref[...].astype(BF16))
    tmp_ref[8 : 8 + CONV + 1, 0 : conv_ref.shape[1]] = conv_ref[...]
    tmp_ref[8 + CONV + 1 : 8 + CONV + 2, 0 : gain_ref.shape[0]] = gain_ref[...].reshape(1, -1)
    for copy in copies:
        w1_ref[copy, rows : rows + 16, :] = tmp_ref[...].astype(BF16)
    copies = range(g2_ref.shape[0])
    for at, part in enumerate(pick_heads(win_ref, 0, ctx, heads)):
        part = part.astype(BF16)
        for copy in copies:
            g2_ref[copy, 0:rows, at * 128 : (at + 1) * 128] = part
    if g2_ref.shape[1] > rows:
        some = wout_ref.shape[0] // 4
        mine = wout_ref[pl.ds(pl.multiple_of(ctx * some, 8), some), :].astype(BF16)
        for copy in copies:
            g2_ref[copy, rows : rows + some] = mine[:, :width]
            g2_ref[copy, rows + some : rows + 2 * some] = mine[:, width:]


def scan_forward_kernel(
    here_ref,
    at_ref,
    tok_pieces,
    w1_pieces,
    hrow_ref,
    hcol_ref,
    segc_ref,
    segr_ref,
    hid_ref,
    conv_ref,
    gpre_ref,
    gmine_ref,
    wdt_ref,
    w1_ref,
    mixed_ref,
    convin_ref,
    convsum_ref,
    inner_ref,
    raw_ref,
    stepc_ref,
    logc_ref,
    stepr_ref,
    logr_ref,
    start_ref,
    ext_ref,
    seg_ref,
    state_ref,
    small_ref,
    tok_ref,
    conv_all,
    gain_all,
    sems,
    tok_sems,
):
    step = pl.program_id(0)
    span, model = hid_ref.shape
    heads = wdt_ref.shape[0]
    width = heads * HEAD_DIM
    shards = small_ref.shape[0]
    rows = model // shards

    @pl.when(step == 0)
    def _():
        copies = place(
            w1_pieces,
            at_ref,
            len(w1_pieces),
            sems,
            [(0, rows, rows_of(w1_ref, rows)), (rows, 16, lambda at: small_ref.at[at])],
        )
        tokens = [
            pltpu.make_async_copy(piece, tok_ref.at[here_ref[2] ^ index], tok_sems.at[index])
            for index, piece in enumerate(tok_pieces)
        ]
        for copy in tokens:
            copy.start()
        ext_ref[0:8] = jnp.zeros((8, ext_ref.shape[1]), F32)
        state_ref[...] = jnp.zeros_like(state_ref)
        conv_all[...] = jnp.zeros_like(conv_all)
        for copy in copies:
            copy.wait()
        conv_cols = conv_all.shape[1] // shards
        gain_len = gain_all.shape[1] // shards
        for shard in range(shards):
            small = small_ref[shard].astype(F32)
            wdt_ref[:, shard * rows : (shard + 1) * rows] = small[0:8, 384 : 384 + rows].astype(BF16)
            conv_all[0 : CONV + 1, shard * conv_cols : (shard + 1) * conv_cols] = small[
                8 : 8 + CONV + 1, :conv_cols
            ]
            gain_all[:, shard * gain_len : (shard + 1) * gain_len] = small[13:14, :gain_len]
        for at, part in enumerate(pick_heads(conv_all, 0, here_ref[2], heads)):
            conv_ref[:, at * 128 : (at + 1) * 128] = part
        conv_ref[:, width:] = conv_all[:, INNER:]
        gpre_ref[...] = gain_all[:, :model]
        for at, part in enumerate(pick_heads(gain_all, model, here_ref[2], heads)):
            gmine_ref[:, at * 128 : (at + 1) * 128] = part
        for copy in tokens:
            copy.wait()

    for first in range(0, span, 32):
        tok = tok_ref[step, first : first + 32]
        scale = lax.rsqrt(jnp.mean(tok * tok, axis=-1, keepdims=True) + NORM_EPS)
        hid_ref[first : first + 32] = (tok * scale * gpre_ref[...]).astype(BF16)
    hid = hid_ref[...]
    proj = nn(hid, w1_ref[...]).astype(BF16)
    convin_ref[...] = proj
    ext_ref[8 : 8 + span] = proj.astype(F32)
    seg_ref[...] = segc_ref[pl.ds(pl.multiple_of(step * span, 8), span + 8), :]
    seg_here = seg_ref[8 : 8 + span]
    for first in range(0, span, 64):
        here = seg_ref[8 + first : 72 + first]
        starts = [8 - (CONV - 1) + tap + first for tap in range(CONV)]
        same = [jnp.broadcast_to(seg_ref[at : at + 64] == here, (64, 128)) for at in starts[:-1]]
        for lane in range(0, convin_ref.shape[1], 128):
            lanes = slice(lane, lane + 128)
            total = conv_ref[CONV : CONV + 1, lanes]
            for tap, at in enumerate(starts):
                term = ext_ref[at : at + 64, lanes]
                if tap < CONV - 1:
                    term = jnp.where(same[tap], term, 0.0)
                total = total + conv_ref[tap : tap + 1, lanes] * term
            convsum_ref[first : first + 64, lanes] = total
            mixed_ref[first : first + 64, lanes] = (total * sigmoid(total)).astype(BF16)
    ext_ref[0:8] = ext_ref[span : span + 8]

    raw_c = nt(hid, wdt_ref[...]) + hrow_ref[1:2]
    raw_r = nt(wdt_ref[...], hid) + hcol_ref[:, 1:2]
    step_c = softplus(raw_c)
    step_r = softplus(raw_r)
    log_c = nn(triangle(span, True), -step_c * jnp.exp(hrow_ref[0:1]), HIGHEST)
    log_r = nn(-step_r * jnp.exp(hcol_ref[:, 0:1]), triangle(span, False), HIGHEST)
    raw_ref[...] = raw_c
    stepc_ref[...] = step_c
    logc_ref[...] = log_c
    stepr_ref[...] = step_r
    logr_ref[...] = log_r

    low = lax.broadcasted_iota(jnp.int32, (SPAN, 2 * HEAD_DIM), 1) < HEAD_DIM
    earlier = lax.broadcasted_iota(jnp.int32, (SPAN, SPAN), 0) >= lax.broadcasted_iota(
        jnp.int32, (SPAN, SPAN), 1
    )
    skip_w = spread(hrow_ref[2:3] + jnp.zeros((8, heads), F32), width)[0:1]
    state = state_ref[...]
    for block in range(span // SPAN):
        here = slice(block * SPAN, (block + 1) * SPAN)
        values = mixed_ref[here, :width]
        write = mixed_ref[here, width : width + STATE]
        read = mixed_ref[here, width + STATE :]
        seg = seg_here[here]
        log = log_c[here]
        log_row = log_r[:, here]
        step_row = step_r[:, here]
        scores = jnp.where((seg == segr_ref[:, here]) & earlier, nt(read, write), 0.0)
        seg_prev = seg_ref[7 + block * SPAN : 8 + block * SPAN]
        seg_last = seg_ref[7 + (block + 1) * SPAN : 8 + (block + 1) * SPAN]
        last = log[SPAN - 1 : SPAN]
        enter = jnp.where(seg == seg_prev, jnp.exp(log), 0.0)
        tail = jnp.where(seg == seg_last, jnp.exp(last - log), 0.0) * step_c[here]
        keep = jnp.where(seg_last == seg_prev, jnp.exp(last), 0.0)
        start_ref[block] = state
        values_f = values.astype(F32)
        enter_w = spread(enter, width)
        inter = nn(read, state.astype(BF16))
        for pair in range(heads // 2):
            lanes = slice(pair * 2 * HEAD_DIM, (pair + 1) * 2 * HEAD_DIM)
            pieces = []
            for head in (2 * pair, 2 * pair + 1):
                gap = jnp.minimum(log[:, head : head + 1] - log_row[head : head + 1], 0.0)
                weights = scores * jnp.exp(gap) * step_row[head : head + 1]
                pieces.append(nn(weights.astype(BF16), values[:, lanes]))
            base = enter_w[:, lanes] * inter[:, lanes] + skip_w[:, lanes] * values_f[:, lanes]
            inner_ref[here, lanes] = base + jnp.where(low, pieces[0], pieces[1])
        moved = (spread(tail, width) * values_f).astype(BF16)
        keep_w = spread(keep + jnp.zeros((8, heads), F32), width)[0:1]
        state = keep_w * state + tn(write, moved)
    state_ref[...] = state


def gate_kernel(
    here_ref,
    at_ref,
    hid_ref,
    g2_pieces,
    cot_pieces,
    inner_ref,
    gain_ref,
    wg_ref,
    wout_ref,
    cot_ref,
    gate_ref,
    ng_ref,
    stat_ref,
    turned_ref,
    sems,
    cot_sems,
):
    step = pl.program_id(0)
    rows = wg_ref.shape[0] // (wout_ref.shape[0] // HEAD_DIM)
    width = wg_ref.shape[1]

    @pl.when(step == 0)
    def _():
        some = rows_of(wout_ref, HEAD_DIM)
        copies = place(
            g2_pieces,
            at_ref,
            len(g2_pieces),
            sems,
            [
                (0, rows, rows_of(wg_ref, rows)),
                (rows, HEAD_DIM, lambda at: some(at).at[:, 0:width]),
                (rows + HEAD_DIM, HEAD_DIM, lambda at: some(at).at[:, width : 2 * width]),
            ],
        )
        cots = [
            pltpu.make_async_copy(piece, cot_ref.at[here_ref[2] ^ index], cot_sems.at[index])
            for index, piece in enumerate(cot_pieces)
        ]
        for copy in cots:
            copy.start()
        for copy in copies + cots:
            copy.wait()
        turned_ref[...] = wout_ref[...].T

    gate_ref[...] = nn(hid_ref[...], wg_ref[...]).astype(BF16)
    ng_ref[...] = nn(cot_ref[step], turned_ref[...])
    span = gate_ref.shape[0]
    squares, crossed = [], []
    for first in range(0, span, 32):
        here = slice(first, first + 32)
        gate = gate_ref[here].astype(F32)
        gated = inner_ref[here] * (gate * sigmoid(gate))
        squares.append(jnp.sum(gated * gated, axis=1, keepdims=True))
        crossed.append(jnp.sum(gated * (ng_ref[here] * gain_ref[...]), axis=1, keepdims=True))
    squares = jnp.concatenate(squares, axis=0)
    crossed = jnp.concatenate(crossed, axis=0)
    same = diagonal(span)
    squares = jnp.sum(jnp.where(same, squares, 0.0), axis=0, keepdims=True)
    crossed = jnp.sum(jnp.where(same, crossed, 0.0), axis=0, keepdims=True)
    at = lax.broadcasted_iota(jnp.int32, stat_ref.shape, 0)
    stat_ref[...] = jnp.where(at == 0, squares, crossed)


def norm_back_kernel(
    perm_ref,
    here_ref,
    hid_ref,
    inner_ref,
    gate_ref,
    ng_ref,
    stat_ref,
    gain_ref,
    mixed_ref,
    wout_ref,
    cot_ref,
    block_refs,
    keep_ref,
    send_ref,
    dy_ref,
    dgate_ref,
    sums_ref,
    outacc_ref,
    inacc_ref,
    normed_ref,
):
    step = pl.program_id(0)
    span, width = inner_ref.shape

    @pl.when(step == 0)
    def _():
        outacc_ref[...] = jnp.zeros_like(outacc_ref)
        inacc_ref[...] = jnp.zeros_like(inacc_ref)
        sums_ref[...] = jnp.zeros_like(sums_ref)

    same = diagonal(span)
    squares = jnp.sum(jnp.where(same, stat_ref[0:1], 0.0), axis=1, keepdims=True)
    cross = jnp.sum(jnp.where(same, stat_ref[1:2], 0.0), axis=1, keepdims=True)
    inv = lax.rsqrt(squares * (1.0 / INNER) + NORM_EPS)
    gain_sum = jnp.zeros((1, width), F32)
    skip_sum = jnp.zeros((1, width), F32)
    for first in range(0, span, 32):
        here = slice(first, first + 32)
        gate = gate_ref[here].astype(F32)
        sig = sigmoid(gate)
        silu = gate * sig
        inner = inner_ref[here]
        scale = inv[here]
        unit = inner * silu * scale
        normed_ref[here] = (unit * gain_ref[...]).astype(BF16)
        grad = ng_ref[here]
        dgated = scale * (grad * gain_ref[...] - unit * (cross[here] * scale * (1.0 / INNER)))
        dy = dgated * silu
        dy_ref[here] = dy
        dgate_ref[here] = (dgated * inner * (sig * (1.0 + gate * (1.0 - sig)))).astype(BF16)
        gain_sum = gain_sum + jnp.sum(grad * unit, axis=0, keepdims=True)
        skip_sum = skip_sum + jnp.sum(dy * mixed_ref[here].astype(F32), axis=0, keepdims=True)
    normed = normed_ref[...]
    cot = cot_ref[perm_ref[step]]
    block = nn(normed, wout_ref[...]).astype(BF16)

    for at, block_ref in enumerate(block_refs):

        @pl.when(step == at)
        def _():
            block_ref[...] = block

    outacc_ref[...] += tn(normed, cot)
    inacc_ref[...] += tn(hid_ref[...], dgate_ref[...])
    at = lax.broadcasted_iota(jnp.int32, (8, width), 0)
    sums_ref[...] += jnp.where(at == 0, gain_sum, jnp.where(at == 1, skip_sum, 0.0))

    @pl.when(step == pl.num_programs(0) - 1)
    def _():
        own = here_ref[0]
        rows = inacc_ref.shape[0] // (2 * keep_ref.shape[0])
        part_of(lambda at: inacc_ref[at * rows : (at + 1) * rows], own, keep_ref, send_ref)
        outs = lambda at: outacc_ref[at * HEAD_DIM : (at + 1) * HEAD_DIM]
        part_of(lambda at: outs(at)[:, :width], own, keep_ref, send_ref, rows)
        part_of(lambda at: outs(at)[:, width:], own, keep_ref, send_ref, rows + HEAD_DIM)


def scan_back_kernel(
    perm_ref,
    here_ref,
    hid_ref,
    dy_ref,
    mixed_ref,
    convin_ref,
    convsum_ref,
    raw_ref,
    stepc_ref,
    logc_ref,
    stepr_ref,
    logr_ref,
    start_ref,
    conv_ref,
    hrow_ref,
    segc_ref,
    segr_ref,
    keep_ref,
    send_ref,
    dval_ref,
    dbc_ref,
    dstep_ref,
    convg_ref,
    dtg_ref,
    headg_ref,
    ext_ref,
    seg_ref,
    grad_ref,
    inacc_ref,
    dx_ref,
):
    step = pl.program_id(0)
    chunk = pl.num_programs(0) - 1 - step
    span = hid_ref.shape[0]
    heads = stepc_ref.shape[1]
    width = heads * HEAD_DIM

    @pl.when(step == 0)
    def _():
        ext_ref[span : span + 8] = jnp.zeros((8, width), F32)
        grad_ref[...] = jnp.zeros_like(grad_ref)
        inacc_ref[...] = jnp.zeros_like(inacc_ref)
        convg_ref[...] = jnp.zeros_like(convg_ref)
        dtg_ref[...] = jnp.zeros_like(dtg_ref)
        headg_ref[...] = jnp.zeros_like(headg_ref)

    seg_ref[...] = segc_ref[pl.ds(pl.multiple_of(chunk * span, 8), span + 16), :]
    seg_here = seg_ref[8 : 8 + span]
    low = lax.broadcasted_iota(jnp.int32, (SPAN, 2 * HEAD_DIM), 1) < HEAD_DIM
    earlier = lax.broadcasted_iota(jnp.int32, (SPAN, SPAN), 0) >= lax.broadcasted_iota(
        jnp.int32, (SPAN, SPAN), 1
    )
    head_at = lax.broadcasted_iota(jnp.int32, (heads, SPAN), 0)
    lane_at = lax.broadcasted_iota(jnp.int32, (SPAN, heads), 1)
    at_last = lax.broadcasted_iota(jnp.int32, (SPAN, heads), 0) == SPAN - 1
    skip_w = spread(hrow_ref[2:3] + jnp.zeros((8, heads), F32), width)[0:1]
    step_c = stepc_ref[...]
    step_r = stepr_ref[...]
    later = grad_ref[...]
    count = span // SPAN
    dlogs, dsteps_c, dsteps_r = [None] * count, [None] * count, [None] * count
    for block in reversed(range(count)):
        here = slice(block * SPAN, (block + 1) * SPAN)
        values = mixed_ref[here, :width]
        write = mixed_ref[here, width : width + STATE]
        read = mixed_ref[here, width + STATE :]
        values_f = values.astype(F32)
        seg = seg_here[here]
        seg_prev = seg_ref[7 + block * SPAN : 8 + block * SPAN]
        seg_last = seg_ref[7 + (block + 1) * SPAN : 8 + (block + 1) * SPAN]
        dy = dy_ref[here]
        dy_low = dy.astype(BF16)
        log = logc_ref[here]
        log_row = logr_ref[:, here]
        step_row = step_r[:, here]
        last = log[SPAN - 1 : SPAN]
        enter = jnp.where(seg == seg_prev, jnp.exp(log), 0.0)
        tail_raw = jnp.where(seg == seg_last, jnp.exp(last - log), 0.0)
        tail = tail_raw * step_c[here]
        keep = jnp.where(seg_last == seg_prev, jnp.exp(last), 0.0)
        enter_w = spread(enter, width)
        tail_w = spread(tail, width)
        keep_w = spread(keep + jnp.zeros((8, heads), F32), width)[0:1]
        state = start_ref[block]
        state_low = state.astype(BF16)
        later_low = later.astype(BF16)

        entered_low = (enter_w * dy).astype(BF16)
        inter = enter_w * nn(read, state_low)
        from_later = nn(write, later_low)
        moved_low = (tail_w * values_f).astype(BF16)
        dread = nt(entered_low, state_low)
        dwrite = nt(moved_low, later_low)
        tail_dot = gather_heads(values_f * from_later, heads)
        dlog = gather_heads(dy * inter, heads) - tail_dot * tail
        dsteps_c[block] = tail_dot * tail_raw
        carried = jnp.sum(later * state, axis=0, keepdims=True) + jnp.zeros((8, width), F32)
        carried = gather_heads(carried, heads)[0:1]
        dlog = dlog + jnp.where(
            at_last, jnp.sum(tail_dot * tail, axis=0, keepdims=True) + keep * carried, 0.0
        )
        later = keep_w * later + tn(read, entered_low)
        direct = tail_w * from_later + skip_w * dy

        visible = (seg == segr_ref[:, here]) & earlier
        scores = jnp.where(visible, nt(read, write), 0.0)
        dscores = jnp.zeros((SPAN, SPAN), F32)
        dstep = jnp.zeros((heads, SPAN), F32)
        for pair in range(heads // 2):
            lanes = slice(pair * 2 * HEAD_DIM, (pair + 1) * 2 * HEAD_DIM)
            dy_pair = dy_low[:, lanes]
            pieces = []
            for head in (2 * pair, 2 * pair + 1):
                mine = low if head % 2 == 0 else ~low
                gap = jnp.minimum(log[:, head : head + 1] - log_row[head : head + 1], 0.0)
                decay = jnp.exp(gap)
                outer = nt(jnp.where(mine, dy_pair, jnp.zeros_like(dy_pair)), values[:, lanes])
                fade = decay * step_row[head : head + 1]
                dscores = dscores + outer * fade
                weights = scores * fade
                flow = outer * scores
                dstep = dstep + jnp.where(
                    head_at == head, jnp.sum(flow * decay, axis=0, keepdims=True), 0.0
                )
                dlog = dlog + jnp.where(
                    lane_at == head, jnp.sum(outer * weights, axis=1, keepdims=True), 0.0
                )
                pieces.append(tn(weights.astype(BF16), dy_pair))
            dx_ref[here, lanes] = direct[:, lanes] + jnp.where(low, pieces[0], pieces[1])
        dscores = jnp.where(visible, dscores, 0.0).astype(BF16)
        dbc_ref[here, :STATE] = (dwrite + tn(dscores, read)).astype(BF16)
        dbc_ref[here, STATE:] = (dread + nn(dscores, write)).astype(BF16)
        dlogs[block], dsteps_r[block] = dlog, dstep
    grad_ref[...] = later
    dlog_c = jnp.concatenate(dlogs, axis=0)
    dstep_c = jnp.concatenate(dsteps_c, axis=0)
    dstep_r = jnp.concatenate(dsteps_r, axis=1)

    upper = triangle(span, False)
    eye = jnp.where(diagonal(span), 1.0, 0.0).astype(F32)
    dalpha = nn(upper, dlog_c, HIGHEST) - nt(upper, dstep_r * step_r, HIGHEST)
    dstep = dstep_c + nt(eye, dstep_r, HIGHEST)
    rate = jnp.exp(hrow_ref[0:1])
    draw = (dstep - rate * dalpha) * sigmoid(raw_ref[...])
    draw_low = draw.astype(BF16)
    dstep_ref[...] = draw_low
    hid = hid_ref[...]
    dtg_ref[...] += tn(draw_low, hid)
    rate_sum = jnp.sum(-dalpha * step_c * rate, axis=0, keepdims=True)
    bias_sum = jnp.sum(draw, axis=0, keepdims=True)
    at = lax.broadcasted_iota(jnp.int32, (8, heads), 0)
    headg_ref[...] += jnp.where(at == 0, rate_sum, jnp.where(at == 1, bias_sum, 0.0))

    convg_ref[...] += conv_back(
        span,
        width,
        lambda here, lanes: dx_ref[here, lanes],
        convsum_ref,
        convin_ref,
        conv_ref,
        ext_ref,
        lambda first, count: seg_ref[8 + first : 8 + first + count],
        dval_ref,
    )
    ext_ref[span : span + 8] = ext_ref[0:8]
    inacc_ref[...] += tn(hid, dval_ref[...])

    @pl.when(step == pl.num_programs(0) - 1)
    def _():
        rows = inacc_ref.shape[0] // (2 * keep_ref.shape[0])
        part_of(lambda at: inacc_ref[at * rows : (at + 1) * rows], here_ref[0], keep_ref, send_ref)


def hidden_back_kernel(
    perm_ref,
    dgate_ref,
    dval_ref,
    dstep_ref,
    wg_ref,
    wv_ref,
    wdt_ref,
    hid_ref,
    gain_ref,
    out_refs,
    gsum_ref,
    turned_ref,
):
    width = wg_ref.shape[1]

    @pl.when(pl.program_id(0) == 0)
    def _():
        gsum_ref[...] = jnp.zeros_like(gsum_ref)
        turned_ref[0:width] = wg_ref[...].T
        turned_ref[width:] = wv_ref[...].T

    total = nn(dgate_ref[...], turned_ref[0:width]) + nn(dval_ref[...], turned_ref[width:])
    total = total + nn(dstep_ref[...], wdt_ref[...])
    step = pl.program_id(0)

    for at, out_ref in enumerate(out_refs):

        @pl.when(step == at)
        def _():
            out_ref[...] = total.astype(BF16)

    gain_sum = jnp.zeros(gain_ref.shape, F32)
    for first in range(0, total.shape[0], 32):
        here = slice(first, first + 32)
        gain_sum = gain_sum + jnp.sum(total[here] * hid_ref[here].astype(F32), axis=0, keepdims=True)
    gsum_ref[...] += gain_sum / gain_ref[...] + jnp.zeros(gsum_ref.shape, F32)


def maps_back_kernel(
    here_ref,
    dbc_ref,
    dbcfar_ref,
    convsum_ref,
    convin_ref,
    conv_ref,
    segc_ref,
    hid_ref,
    w1_ref,
    gain_ref,
    convg_ref,
    sums_ref,
    headg_ref,
    dtg_ref,
    gall_ref,
    keep_ref,
    send_ref,
    own_ref,
    ext_ref,
    acc_ref,
    dmap_ref,
    small_ref,
):
    size, width = dmap_ref.shape
    ext_ref[size : size + 8] = jnp.zeros((8, width), F32)
    sums = conv_back(
        size,
        width,
        lambda here, lanes: dbc_ref[here, lanes].astype(F32) + dbcfar_ref[here, lanes].astype(F32),
        convsum_ref,
        convin_ref,
        conv_ref,
        ext_ref,
        lambda first, count: segc_ref[8 + first : 8 + first + count],
        dmap_ref,
    )
    ctx = here_ref[2]
    acc_ref[...] = tn(hid_ref[...], dmap_ref[...])
    span = own_ref.shape[0]
    own = pl.ds(pl.multiple_of(ctx * span, 16), span)
    grad = nt(dmap_ref[own, :], w1_ref[...])
    own_ref[...] = grad
    unit = hid_ref[own, :].astype(F32) / gain_ref[...]
    gain_sum = gall_ref[0:1] + jnp.sum(grad * unit, axis=0, keepdims=True)
    half = small_ref.shape[1]
    heads = headg_ref.shape[1]
    small_ref[...] = jnp.zeros_like(small_ref)
    small_ref[0 : CONV + 1] = convg_ref[0 : CONV + 1]
    small_ref[CONV + 1 : CONV + 3] = sums_ref[0:2]
    small_ref[7:8, 0:heads] = headg_ref[0:1]
    small_ref[7:8, 128 : 128 + heads] = headg_ref[1:2]
    small_ref[8 : 8 + CONV + 1, 0:width] = sums[0 : CONV + 1]
    small_ref[13:14] = gain_sum[:, :half]
    small_ref[14:15] = gain_sum[:, half:]
    small_ref[15:16] = small_ref[7:8] - small_ref[7:8].astype(BF16).astype(F32)
    small_ref[16:24] = dtg_ref[:, :half]
    small_ref[24:32] = dtg_ref[:, half:]
    small = small_ref[...].astype(BF16)
    count = keep_ref.shape[0] // 32 - 1
    block = acc_ref.shape[0] // (2 * count)
    some = block // 4
    keep_ref[0:32] = small
    send_ref[0:32] = small
    for at in range(count):
        start = pl.multiple_of(2 * at * block + ctx * some, 8)
        low = acc_ref[pl.ds(start, some), :].astype(BF16)
        start = pl.multiple_of((2 * at + 1) * block + ctx * some, 8)
        high = acc_ref[pl.ds(start, some), :].astype(BF16)
        keep_ref[32 + 32 * at : 64 + 32 * at, 0:width] = jnp.where(here_ref[0] == 0, low, high)
        send_ref[32 + 32 * at : 64 + 32 * at, 0:width] = jnp.where(here_ref[0] == 0, high, low)


def input_back_kernel(part_refs, own_ref, tok_ref, gain_ref, cot_ref, out_ref):
    for first in range(0, out_ref.shape[0], 32):
        here = slice(first, first + 32)
        grad = own_ref[here]
        for ref in part_refs:
            grad = grad + ref[here].astype(F32)
        tok = tok_ref[here]
        scale = lax.rsqrt(jnp.mean(tok * tok, axis=-1, keepdims=True) + NORM_EPS)
        unit = tok * scale
        scaled = grad * gain_ref[...]
        mean = jnp.mean(scaled * unit, axis=-1, keepdims=True)
        out_ref[here] = cot_ref[here] + scale * (scaled - unit * mean)


def with_rest(value, first):
    row = lax.broadcasted_iota(jnp.int32, value.shape, 0)
    head = value[first + 7 : first + 8] + value[first + 15 : first + 16]
    rest = head - head.astype(BF16).astype(F32)
    return jnp.where(row == first + 7, head, jnp.where(row == first + 15, rest, value))


def pair_sum_late_kernel(keep_ref, came_ref, mkeep_ref, mcame_ref, out_ref):
    count, rows, width = keep_ref.shape
    small = with_rest(mkeep_ref[0:32].astype(F32) + mcame_ref[0:32].astype(F32), 0).astype(BF16)
    for block in range(count):
        out_ref[block, 0:rows] = (keep_ref[block].astype(F32) + came_ref[block].astype(F32)).astype(BF16)
        out_ref[block, rows : rows + 32] = small
        at = slice(32 + 32 * block, 64 + 32 * block)
        out_ref[block, rows + 32 : rows + 64] = (
            mkeep_ref[at].astype(F32) + mcame_ref[at].astype(F32)
        ).astype(BF16)


def sum_late_kernel(parts_ref, out_ref):
    total = parts_ref[0].astype(F32)
    for at in range(1, parts_ref.shape[0]):
        total = total + parts_ref[at].astype(F32)
    out_ref[...] = with_rest(total, out_ref.shape[0] - 64).astype(BF16)


def adam_out_kernel(here_ref, weight_ref, first_ref, second_ref, early_refs, *rest):
    new_refs, early_ref = rest[:3], rest[3]
    step = pl.program_id(0)

    @pl.when(step == 0)
    def _():
        by_owner(early_refs, here_ref[2], early_ref)

    rows = weight_ref.shape[0]
    width = early_ref.shape[2]
    first = early_ref.shape[1] - 2 * rows
    for at in range(2):
        lanes = slice(at * width, (at + 1) * width)
        grad = early_ref[step, first + at * rows : first + (at + 1) * rows].astype(F32)
        news = adam_step(
            weight_ref[:, lanes], first_ref[:, lanes], second_ref[:, lanes], grad, 0.02, WEIGHT_DECAY
        )
        for ref, new in zip(new_refs, news):
            ref[:, lanes] = new


def by_owner(refs, ctx, natural_ref):
    for at, ref in enumerate(refs):
        natural_ref[pl.ds(ctx ^ at, 1)] = ref[...][None]


def adam_in_kernel(here_ref, weight_ref, first_ref, second_ref, early_refs, late_refs, *rest):
    new_refs, (early_ref, late_ref) = rest[:3], rest[3:]
    step = pl.program_id(0)
    pieces = len(early_refs)
    rows = weight_ref.shape[0]
    width = early_ref.shape[2]
    block = pieces * HEAD_DIM

    @pl.when(step == 0)
    def _():
        by_owner(early_refs, here_ref[2], early_ref)
        by_owner(late_refs, here_ref[2], late_ref)

    here = pl.ds(pl.multiple_of(step * rows, rows), rows)
    low = lax.broadcasted_iota(jnp.int32, (rows, 2 * HEAD_DIM), 1) < HEAD_DIM

    def update(lanes, grad):
        news = adam_step(
            weight_ref[:, lanes], first_ref[:, lanes], second_ref[:, lanes], grad, 0.03, WEIGHT_DECAY
        )
        for ref, new in zip(new_refs, news):
            ref[:, lanes] = new

    for base, ref in ((0, early_ref), (INNER, late_ref)):
        for pair in range(width // (2 * HEAD_DIM)):
            lanes = slice(pair * 2 * HEAD_DIM, (pair + 1) * 2 * HEAD_DIM)
            for at in range(0, pieces, 2):
                first = ref[at, here, lanes].astype(F32)
                second = ref[at + 1, here, lanes].astype(F32)
                start = base + 2 * pair * block + at * HEAD_DIM
                even = jnp.where(low, first, pltpu.roll(second, HEAD_DIM, 1))
                update(slice(start, start + 2 * HEAD_DIM), even)
                start = start + block
                odd = jnp.where(low, pltpu.roll(first, HEAD_DIM, 1), second)
                update(slice(start, start + 2 * HEAD_DIM), odd)
    some = 32 // rows
    first = pl.multiple_of(late_ref.shape[1] - 32 + (step % some) * rows, rows)
    grad = late_ref[step // some, pl.ds(first, rows), 0 : 2 * STATE].astype(F32)
    update(slice(2 * INNER, 2 * INNER + 2 * STATE), grad)


def swap(value, axis, bit):
    count = lax.axis_size(axis)
    return lax.ppermute(value, axis, [(at, at ^ bit) for at in range(count)])


def gather_ctx(value):
    far = swap(value, "ctx", 2)
    return [value, swap(value, "ctx", 1), far, swap(far, "ctx", 1)]


def high_all_to_all(value):
    count = lax.axis_size("dp")
    groups = [list(range(low, count, 2)) for low in range(2)]
    return lax.all_to_all(value, "dp", 0, 0, axis_index_groups=groups)


def from_owners(parts):
    count = len(parts)
    return [swap(parts[bit - 1], "ctx", bit) for bit in range(1, count)] + [parts[-1]]


def fan_ctx(value):
    return [value] + [swap(value, "ctx", bit) for bit in range(1, lax.axis_size("ctx"))]


def adam_step(weight, moment_one, second, gradient, step_rate, decay_rate):
    moment_new = BETA_ONE * moment_one + (1.0 - BETA_ONE) * gradient
    second_new = BETA_TWO * second + (1.0 - BETA_TWO) * gradient * gradient
    first_hat = moment_new / (1.0 - BETA_ONE**STEP)
    second_hat = second_new / (1.0 - BETA_TWO**STEP)
    weight_new = weight - step_rate * (
        first_hat / (jnp.sqrt(second_hat) + ADAM_EPS) + decay_rate * weight
    )
    return (weight_new, moment_new, second_new)


def full(shape):
    return pl.BlockSpec(shape, lambda *_: (0,) * len(shape))


def shape_of(*shape, dtype=F32):
    return jax.ShapeDtypeStruct(shape, dtype)


def shards(
    tokens,
    segment_ids,
    cotangent,
    in_weight,
    dt_weight,
    out_weight,
    conv_params,
    gains,
    head_params,
    in_first,
    in_second,
    dt_first,
    dt_second,
    out_first,
    out_second,
    conv_first,
    conv_second,
    gain_first,
    gain_second,
    head_first,
    head_second,
):
    _, span, model = tokens.shape
    length = segment_ids.shape[1]
    ndp, nctx = lax.axis_size("dp"), lax.axis_size("ctx")
    d, c = lax.axis_index("dp"), lax.axis_index("ctx")
    heads = HEADS // nctx
    width = INNER // nctx
    maps = 2 * STATE
    wide = width + maps
    chunks = nctx
    rows_in = in_weight.shape[0]
    conv_cols = conv_params.shape[1]
    gain_len = gains.shape[0]
    dt_cols = dt_weight.shape[1]
    near = ndp == heads
    high = heads // 2
    block_in = model // heads
    tok = tokens[0]
    bits = jnp.stack([d & 1, d >> 1, c] if near else [0 * d, 0 * d, c]).astype(jnp.int32)
    perm = c ^ jnp.asarray([1, 2, 3, 0], jnp.int32)
    smem = pl.BlockSpec(memory_space=pltpu.SMEM)
    vmem = pl.BlockSpec(memory_space=pltpu.VMEM)
    anywhere = lambda pieces: [pl.BlockSpec(memory_space=pl.ANY)] * len(pieces)

    w1, g2 = pl.pallas_call(
        pack_kernel,
        in_specs=[smem] + [vmem] * 5,
        out_shape=[
            shape_of(high if near else 1, rows_in + 16, wide, dtype=BF16),
            shape_of(high if near else 1, rows_in + (2 * HEAD_DIM if near else 0), width, dtype=BF16),
        ],
        scratch_shapes=[pltpu.VMEM((16, wide), F32)],
        compiler_params=params(),
        name="pack",
    )(bits, in_weight, out_weight, dt_weight, conv_params, gains)
    cot_low = cotangent[0].astype(BF16)
    if near:
        tok_far = swap(tok, "ctx", 2)
        tok_core = swap(tok, "ctx", 1)
        w1 = high_all_to_all(w1)
        w1, g2, cot_low = lax.optimization_barrier((w1, g2, cot_low))
        w1_came = swap(w1, "dp", 1)
        g2 = high_all_to_all(g2)
        w1, w1_came, tok_far = lax.optimization_barrier((w1, w1_came, tok_far))
        toks = [tok, tok_core, tok_far, swap(tok_far, "ctx", 1)]
        w1, w1_came, toks, g2, cot_low = lax.optimization_barrier((w1, w1_came, toks, g2, cot_low))
        w1 = [w1, w1_came]
        g2 = [g2, swap(g2, "dp", 1)]
        cots = fan_ctx(cot_low)
        at_rows = at_g2 = jnp.stack([d & 1, 1 - (d & 1)]).astype(jnp.int32)
    else:
        w1 = [lax.all_gather(w1[0], "dp", axis=0)]
        toks = gather_ctx(tok)
        cots = gather_ctx(cot_low)
        wg = lax.all_gather(g2[0], "dp", axis=0, tiled=True).reshape(heads, block_in, width)
        wout = lax.all_gather(out_weight.astype(BF16), "dp", axis=0, tiled=True)
        wout = lax.dynamic_index_in_dim(wout.reshape(heads, nctx, HEAD_DIM, model), c, 1, False)
        g2 = [jnp.concatenate([wg, wout[:, :, :width], wout[:, :, width:]], axis=1)]
        at_rows = at_g2 = jnp.zeros((1,), jnp.int32)

    ids = segment_ids[0]
    seg_col = jnp.pad(ids, (8, 8), constant_values=-1)[:, None]
    seg_row = segment_ids
    head_mine = lax.dynamic_index_in_dim(head_params.reshape(3, heads, nctx), c, 2, False)
    head_col = head_mine.T

    rows = lambda cols: pl.BlockSpec((span, cols), lambda i, *_: (i, 0))
    row_of = pl.BlockSpec((heads, span), lambda i, *_: (0, i))
    rows_at = lambda cols: pl.BlockSpec((span, cols), lambda i, p, *_: (p[i], 0))
    whole = full((span, model))
    shards_in = sum(piece.shape[0] for piece in w1)

    (
        hid, conv_mine, gain_pre, gain_mine, dt_mine, w1, mixed, conv_in, conv_sum, inner, raw,
        step_c, log_c, step_r, log_r, starts,
    ) = pl.pallas_call(
        scan_forward_kernel,
        grid_spec=pltpu.PrefetchScalarGridSpec(
            num_scalar_prefetch=2,
            grid=(chunks,),
            in_specs=[
                anywhere(toks),
                anywhere(w1),
                full((3, heads)),
                full((heads, 3)),
                full((length + 16, 1)),
                pl.BlockSpec((1, span), lambda i, *_: (0, i)),
            ],
            out_specs=[
                rows(model),
                full((8, wide)),
                full((1, model)),
                full((1, width)),
                full((heads, model)),
                full((model, wide)),
                rows(wide),
                rows(wide),
                rows(wide),
                rows(width),
                rows(heads),
                rows(heads),
                rows(heads),
                row_of,
                row_of,
                pl.BlockSpec((span // SPAN, STATE, width), lambda i, *_: (i, 0, 0)),
            ],
            scratch_shapes=[
                pltpu.VMEM((span + 8, wide), F32),
                pltpu.VMEM((span + 8, 1), jnp.int32),
                pltpu.VMEM((STATE, width), F32),
                pltpu.VMEM((shards_in, 16, wide), BF16),
                pltpu.VMEM((nctx, span, model), F32),
                pltpu.VMEM((8, INNER + maps), F32),
                pltpu.VMEM((1, model + INNER), F32),
                pltpu.SemaphoreType.DMA((copies_of(w1, 2),)),
                pltpu.SemaphoreType.DMA((nctx,)),
            ],
        ),
        out_shape=[
            shape_of(length, model, dtype=BF16),
            shape_of(8, wide),
            shape_of(1, model),
            shape_of(1, width),
            shape_of(heads, model, dtype=BF16),
            shape_of(model, wide, dtype=BF16),
            shape_of(length, wide, dtype=BF16),
            shape_of(length, wide, dtype=BF16),
            shape_of(length, wide),
            shape_of(length, width),
            shape_of(length, heads),
            shape_of(length, heads),
            shape_of(length, heads),
            shape_of(heads, length),
            shape_of(heads, length),
            shape_of(length // SPAN, STATE, width),
        ],
        compiler_params=params("arbitrary"),
        name="scan_forward",
    )(bits, at_rows, toks, w1, head_mine, head_col, seg_col, seg_row)

    wg, wout, cot_all, gate, normed_grad, stats = pl.pallas_call(
        gate_kernel,
        grid_spec=pltpu.PrefetchScalarGridSpec(
            num_scalar_prefetch=2,
            grid=(chunks,),
            in_specs=[rows(model), anywhere(g2), anywhere(cots), rows(width), full((1, width))],
            out_specs=[
                full((model, width)),
                full((width, model)),
                full((nctx, span, model)),
                rows(width),
                rows(width),
                pl.BlockSpec((8, span), lambda i, *_: (0, i)),
            ],
            scratch_shapes=[
                pltpu.VMEM((model, width), BF16),
                pltpu.SemaphoreType.DMA((copies_of(g2, 3),)),
                pltpu.SemaphoreType.DMA((nctx,)),
            ],
        ),
        out_shape=[
            shape_of(model, width, dtype=BF16),
            shape_of(width, model, dtype=BF16),
            shape_of(nctx, span, model, dtype=BF16),
            shape_of(length, width, dtype=BF16),
            shape_of(length, width),
            shape_of(8, length),
        ],
        compiler_params=params("arbitrary"),
        name="gate",
    )(bits, at_g2, hid, g2, cots, inner, gain_mine)
    stats = sum(fan_ctx(stats))

    early_rows = block_in + 2 * HEAD_DIM
    blocks_out, early_keep, early_send, dy, dgate, col_sums = pl.pallas_call(
        norm_back_kernel,
        grid_spec=pltpu.PrefetchScalarGridSpec(
            num_scalar_prefetch=2,
            grid=(chunks,),
            in_specs=[
                rows_at(model),
                rows_at(width),
                rows_at(width),
                rows_at(width),
                pl.BlockSpec((8, span), lambda i, p, *_: (0, p[i])),
                full((1, width)),
                rows_at(width),
                full((width, model)),
                full((nctx, span, model)),
            ],
            out_specs=[
                [whole] * nctx,
                full((high, early_rows, width)),
                full((high, early_rows, width)),
                rows_at(width),
                rows_at(width),
                full((8, width)),
            ],
            scratch_shapes=[
                pltpu.VMEM((width, model), F32),
                pltpu.VMEM((model, width), F32),
                pltpu.VMEM((span, width), BF16),
            ],
        ),
        out_shape=[
            [shape_of(span, model, dtype=BF16)] * nctx,
            shape_of(high, early_rows, width, dtype=BF16),
            shape_of(high, early_rows, width, dtype=BF16),
            shape_of(length, width),
            shape_of(length, width, dtype=BF16),
            shape_of(8, width),
        ],
        compiler_params=params("arbitrary"),
        name="norm_back",
    )(perm, bits, hid, inner, gate, normed_grad, stats, gain_mine, mixed, wout, cot_all)
    blocks_out = from_owners(blocks_out)
    if near:
        early_came = swap(early_send, "dp", 1)

    back = lambda cols: pl.BlockSpec((span, cols), lambda i, *_: (chunks - 1 - i, 0))
    back_row = pl.BlockSpec((heads, span), lambda i, *_: (0, chunks - 1 - i))
    late_keep, late_send, dval, dbc, dstep, conv_grad, dt_grad, head_grad = pl.pallas_call(
        scan_back_kernel,
        grid_spec=pltpu.PrefetchScalarGridSpec(
            num_scalar_prefetch=2,
            grid=(chunks,),
            in_specs=[
                back(model),
                back(width),
                back(wide),
                back(width),
                back(width),
                back(heads),
                back(heads),
                back(heads),
                back_row,
                back_row,
                pl.BlockSpec((span // SPAN, STATE, width), lambda i, *_: (chunks - 1 - i, 0, 0)),
                full((8, width)),
                full((3, heads)),
                full((length + 16, 1)),
                pl.BlockSpec((1, span), lambda i, *_: (0, chunks - 1 - i)),
            ],
            out_specs=[
                full((high, block_in, width)),
                full((high, block_in, width)),
                back(width),
                back(maps),
                back(heads),
                full((8, width)),
                full((heads, model)),
                full((8, heads)),
            ],
            scratch_shapes=[
                pltpu.VMEM((span + 8, width), F32),
                pltpu.VMEM((span + 16, 1), jnp.int32),
                pltpu.VMEM((STATE, width), F32),
                pltpu.VMEM((model, width), F32),
                pltpu.VMEM((span, width), F32),
            ],
        ),
        out_shape=[
            shape_of(high, block_in, width, dtype=BF16),
            shape_of(high, block_in, width, dtype=BF16),
            shape_of(length, width, dtype=BF16),
            shape_of(length, maps, dtype=BF16),
            shape_of(length, heads, dtype=BF16),
            shape_of(8, width),
            shape_of(heads, model),
            shape_of(8, heads),
        ],
        compiler_params=params("arbitrary"),
        name="scan_back",
    )(
        perm, bits, hid, dy, mixed, conv_in, conv_sum, raw, step_c, log_c, step_r, log_r, starts,
        conv_mine, head_mine, seg_col, seg_row,
    )
    dbc_came = swap(dbc, "ctx", 1)
    if near:
        late_came = swap(late_send, "dp", 1)
        early_came, blocks_out, dval = lax.optimization_barrier((early_came, blocks_out, dval))
        early_parts = (early_keep.astype(F32) + early_came.astype(F32)).astype(BF16)
        early_parts = high_all_to_all(early_parts)
    dbc = (dbc.astype(F32) + dbc_came.astype(F32)).astype(BF16)
    dval, dbc = lax.optimization_barrier((dval, dbc))
    dbc_far = swap(dbc, "ctx", 2)
    if near:
        dbc_far, late_came = lax.optimization_barrier((dbc_far, late_came))

    hidden_out, gain_sum = pl.pallas_call(
        hidden_back_kernel,
        grid_spec=pltpu.PrefetchScalarGridSpec(
            num_scalar_prefetch=1,
            grid=(chunks,),
            in_specs=[
                rows_at(width),
                rows_at(width),
                rows_at(heads),
                full((model, width)),
                full((model, width)),
                full((heads, model)),
                rows_at(model),
                full((1, model)),
            ],
            out_specs=[[whole] * nctx, full((8, model))],
            scratch_shapes=[pltpu.VMEM((2 * width, model), BF16)],
        ),
        out_shape=[
            [shape_of(span, model, dtype=BF16)] * nctx,
            shape_of(8, model),
        ],
        compiler_params=params("arbitrary"),
        name="hidden_back",
    )(perm, dgate, dval, dstep, wg, w1, dt_mine, hid, gain_pre)
    hidden_out = from_owners(hidden_out)
    map_rows = 32 + 32 * high
    map_cols = lambda size: pl.BlockSpec((size, maps), lambda i: (0, width // maps))
    map_keep, map_send, hidden_own = pl.pallas_call(
        maps_back_kernel,
        grid=(1,),
        in_specs=[
            smem,
            full((length, maps)),
            full((length, maps)),
            map_cols(length),
            map_cols(length),
            map_cols(8),
            full((length + 16, 1)),
            full((length, model)),
            map_cols(model),
            full((1, model)),
            full((8, width)),
            full((8, width)),
            full((8, heads)),
            full((heads, model)),
            full((8, model)),
        ],
        out_specs=[full((map_rows, width)), full((map_rows, width)), full((span, model))],
        out_shape=[
            shape_of(map_rows, width, dtype=BF16),
            shape_of(map_rows, width, dtype=BF16),
            shape_of(span, model),
        ],
        scratch_shapes=[
            pltpu.VMEM((length + 8, maps), F32),
            pltpu.VMEM((model, maps), F32),
            pltpu.VMEM((length, maps), BF16),
            pltpu.VMEM((32, width), F32),
        ],
        compiler_params=params("arbitrary"),
        name="maps_back",
    )(
        bits,
        dbc,
        dbc_far,
        conv_sum,
        conv_in,
        conv_mine,
        seg_col,
        hid,
        w1,
        gain_pre,
        conv_grad,
        col_sums,
        head_grad,
        dt_grad,
        gain_sum,
    )

    block_output = tok + sum(part.astype(F32) for part in blocks_out)

    input_part = lambda parts, own: pl.pallas_call(
        input_back_kernel,
        in_specs=[[vmem] * nctx] + [vmem] * 4,
        out_shape=shape_of(span, model),
        compiler_params=params(),
        name="input_back",
    )(parts, own, tok, gain_pre, cotangent[0])

    late_rows = block_in + 64
    if near:
        map_came = swap(map_send, "dp", 1)
        late_parts = pl.pallas_call(
            pair_sum_late_kernel,
            out_shape=shape_of(high, late_rows, width, dtype=BF16),
            compiler_params=params(),
            name="pair_sum_late",
        )(late_keep, late_came, map_keep, map_came)
        late_parts = high_all_to_all(late_parts)
        early = jnp.sum(early_parts.astype(F32), axis=0).astype(BF16)
        early = gather_ctx(early)
        row_block = lambda ref_rows, cols: pl.BlockSpec((ref_rows, cols), lambda i, *_: (i, 0))
        out_block = row_block(out_weight.shape[0] // nctx, model)
        early_spec = [full((early_rows, width))] * nctx
        early_scratch = pltpu.VMEM((nctx, early_rows, width), BF16)
        out_new = pl.pallas_call(
            adam_out_kernel,
            grid_spec=pltpu.PrefetchScalarGridSpec(
                num_scalar_prefetch=1,
                grid=(nctx,),
                in_specs=[out_block] * 3 + [early_spec],
                out_specs=[out_block] * 3,
                scratch_shapes=[early_scratch],
            ),
            out_shape=[shape_of(*out_weight.shape)] * 3,
            compiler_params=params("arbitrary"),
            name="adam_out",
        )(bits, out_weight, out_first, out_second, early)

        late_parts, block_output, out_new = lax.optimization_barrier((late_parts, block_output, out_new))
        late = pl.pallas_call(
            sum_late_kernel,
            out_shape=shape_of(late_rows, width, dtype=BF16),
            compiler_params=params(),
            name="sum_late",
        )(late_parts)
        late = fan_ctx(late)
        input_grad = input_part(hidden_out, hidden_own)
        late, input_grad = lax.optimization_barrier((late, input_grad))
        in_block = row_block(32, in_weight.shape[1])
        in_new = pl.pallas_call(
            adam_in_kernel,
            grid_spec=pltpu.PrefetchScalarGridSpec(
                num_scalar_prefetch=1,
                grid=(rows_in // 32,),
                in_specs=[in_block] * 3 + [early_spec, [full((late_rows, width))] * nctx],
                out_specs=[in_block] * 3,
                scratch_shapes=[early_scratch, pltpu.VMEM((nctx, late_rows, width), BF16)],
            ),
            out_shape=[shape_of(*in_weight.shape)] * 3,
            compiler_params=params("arbitrary"),
            name="adam_in",
        )(bits, in_weight, in_first, in_second, early, late)
        in_new, out_new = tuple(in_new), tuple(out_new)
        small = jnp.stack([part[block_in : block_in + 32] for part in late])[c ^ jnp.arange(nctx)]
        small = small.astype(F32)
    else:
        input_grad = input_part(hidden_out, hidden_own)
        blocks = lambda keep, send: jnp.stack([keep, send], axis=1).reshape((heads,) + keep.shape[1:])
        early = blocks(early_keep, early_send).astype(F32)
        late = blocks(late_keep, late_send).astype(F32)
        part = lambda value: value[32:].reshape(high, 32, width)[:, :, :maps]
        map_blocks = blocks(part(map_keep), part(map_send)).astype(F32)

        def total(value):
            return lax.psum_scatter(value, "dp", scatter_dimension=0, tiled=True)

        def spaced(value):
            place_at = (jnp.arange(nctx) == c).astype(F32).reshape((1, nctx, 1, 1))
            value = value[:, None] * place_at
            return lax.psum(total(value.reshape(-1, value.shape[-1])), "ctx")

        def by_head(value):
            value = lax.all_gather(total(value.reshape(model, width)), "ctx", axis=0)
            value = value.reshape(nctx, rows_in, heads, HEAD_DIM)
            return jnp.transpose(value, (1, 2, 0, 3)).reshape(rows_in, INNER)

        in_total = jnp.concatenate(
            [by_head(early[:, :block_in]), by_head(late), spaced(map_blocks)], axis=1
        )
        out_total = spaced(
            jnp.concatenate([early[:, block_in : block_in + HEAD_DIM], early[:, block_in + HEAD_DIM :]], axis=2)
        )
        in_new = adam_step(in_weight, in_first, in_second, in_total, 0.03, WEIGHT_DECAY)
        out_new = adam_step(out_weight, out_first, out_second, out_total, 0.02, WEIGHT_DECAY)
        small = lax.all_gather(lax.psum(map_keep[:32].astype(F32), "dp"), "ctx", axis=0)

    def in_order(value):
        return jnp.swapaxes(value.reshape(nctx, -1, heads, HEAD_DIM), 0, 1).swapaxes(1, 2).reshape(-1, INNER)

    columns = in_order(small[:, : CONV + 2])
    conv_total = jnp.concatenate([columns[: CONV + 1], small[0, 8 : 8 + CONV + 1, :maps]], axis=1)
    conv_total = lax.dynamic_slice_in_dim(conv_total, d * conv_cols, conv_cols, 1)
    dt_total = small[:, 16:32].reshape(nctx, 2, heads, width)
    dt_total = jnp.transpose(dt_total, (2, 0, 1, 3)).reshape(HEADS, model)
    dt_total = lax.dynamic_slice_in_dim(dt_total, d * dt_cols, dt_cols, 1)
    pre_total = jnp.sum(small[:, 13:15], axis=0).reshape(-1)
    gain_total = jnp.concatenate([pre_total, columns[CONV + 1]])
    gain_total = lax.dynamic_slice_in_dim(gain_total, d * gain_len, gain_len, 0)
    head_row = small[:, 7] + small[:, 15]
    head_total = jnp.stack(
        [
            head_row[:, :heads].T.reshape(-1),
            head_row[:, 128 : 128 + heads].T.reshape(-1),
            jnp.sum(small[:, CONV + 2].reshape(nctx, heads, HEAD_DIM), axis=2).T.reshape(-1),
        ]
    )

    dt_new = adam_step(dt_weight, dt_first, dt_second, dt_total, 0.03, WEIGHT_DECAY)
    conv_new = adam_step(conv_params, conv_first, conv_second, conv_total, 0.3, 0.0)
    gain_new = adam_step(gains, gain_first, gain_second, gain_total, 0.5, 0.0)
    head_new = adam_step(head_params, head_first, head_second, head_total, 2.0, 0.0)
    return (block_output[None], input_grad[None]) + in_new + dt_new + out_new + conv_new + gain_new + head_new


def solution(mesh):
    tokens, rows, cols = P("dp", "ctx", None), P("dp", None), P(None, "dp")
    return jax.shard_map(
        shards,
        mesh=mesh,
        in_specs=(tokens, rows, tokens, rows, cols, rows, cols, P("dp"), P())
        + (rows, rows, cols, cols, rows, rows, cols, cols, P("dp"), P("dp"), P(), P()),
        out_specs=(tokens, tokens)
        + (rows,) * 3
        + (cols,) * 3
        + (rows,) * 3
        + (cols,) * 3
        + (P("dp"),) * 3
        + (P(),) * 3,
        check_vma=False,
    )
```

```python
import functools

import jax
import jax.numpy as jnp
from jax import lax
from jax.experimental import pallas as pl
from jax.experimental.pallas import tpu as pltpu
from jax.sharding import PartitionSpec as P

INNER = 2048
HEADS = 32
HEAD_DIM = 64
STATE = 128
CONV = 4
STEP = 10
SPAN = 128

F32 = jnp.float32
BF16 = jnp.bfloat16
HIGHEST = lax.Precision.HIGHEST
NORM_EPS = 1e-05
BETA_ONE = 0.9
BETA_TWO = 0.95
ADAM_EPS = 1e-08
WEIGHT_DECAY = 0.1
VMEM_LIMIT = 56 * 1024 * 1024


def nn(a, b, precision=None):
    return lax.dot_general(
        a, b, (((1,), (0,)), ((), ())), precision=precision, preferred_element_type=F32
    )


def nt(a, b, precision=None):
    return lax.dot_general(
        a, b, (((1,), (1,)), ((), ())), precision=precision, preferred_element_type=F32
    )


def tn(a, b, precision=None):
    return lax.dot_general(
        a, b, (((0,), (0,)), ((), ())), precision=precision, preferred_element_type=F32
    )


def halves(value):
    high = value.astype(BF16)
    return high, (value - high.astype(F32)).astype(BF16)


def spread(value, width):
    heads = value.shape[1]
    row = lax.broadcasted_iota(jnp.int32, (heads, width), 0)
    col = lax.broadcasted_iota(jnp.int32, (heads, width), 1)
    table = jnp.where(col // HEAD_DIM == row, 1.0, 0.0).astype(BF16)
    high, low = halves(value)
    return nn(high, table) + nn(low, table)


def gather_heads(value, heads):
    width = value.shape[1]
    row = lax.broadcasted_iota(jnp.int32, (width, heads), 0)
    col = lax.broadcasted_iota(jnp.int32, (width, heads), 1)
    table = jnp.where(row // HEAD_DIM == col, 1.0, 0.0).astype(BF16)
    high, low = halves(value)
    return nn(high, table) + nn(low, table)


def softplus(value):
    return jnp.maximum(value, 0.0) + jnp.log1p(jnp.exp(-jnp.abs(value)))


def sigmoid(value):
    return 1.0 / (1.0 + jnp.exp(-value))


def silu_grad(value):
    sig = sigmoid(value)
    return sig * (1.0 + value * (1.0 - sig))


def diagonal(size):
    row = lax.broadcasted_iota(jnp.int32, (size, size), 0)
    return row == lax.broadcasted_iota(jnp.int32, (size, size), 1)


def triangle(size, lower):
    row = lax.broadcasted_iota(jnp.int32, (size, size), 0)
    col = lax.broadcasted_iota(jnp.int32, (size, size), 1)
    keep = (row >= col if lower else row <= col) & (row // SPAN == col // SPAN)
    return jnp.where(keep, 1.0, 0.0).astype(F32)


def params(*semantics):
    return pltpu.CompilerParams(
        dimension_semantics=semantics or None, vmem_limit_bytes=VMEM_LIMIT
    )


def place(pieces, at_ref, stride, sems, targets):
    copies = []
    for index, piece in enumerate(pieces):
        for block in range(piece.shape[0]):
            for first, rows, target in targets:
                copies.append(
                    pltpu.make_async_copy(
                        piece.at[block, first : first + rows],
                        target(at_ref[index] + stride * block),
                        sems.at[len(copies)],
                    )
                )
    for copy in copies:
        copy.start()
    return copies


def copies_of(pieces, targets):
    return sum(piece.shape[0] for piece in pieces) * targets


def rows_of(ref, rows):
    return lambda at: ref.at[pl.ds(pl.multiple_of(at * rows, 16), rows)]


def part_of(block, own_bit, keep_ref, send_ref, first=0):
    for at in range(keep_ref.shape[0]):
        low, high = block(2 * at).astype(BF16), block(2 * at + 1).astype(BF16)
        rows = slice(first, first + low.shape[0])
        keep_ref[at, rows] = jnp.where(own_bit == 0, low, high)
        send_ref[at, rows] = jnp.where(own_bit == 0, high, low)


def pick_heads(ref, base, ctx, heads):
    first = pl.multiple_of(base + (ctx >> 1) * 2 * HEAD_DIM, 2 * HEAD_DIM)
    wide = ref[:, pl.ds(first, 2 * HEAD_DIM)]
    low = lax.broadcasted_iota(jnp.int32, wide.shape, 1) < HEAD_DIM
    odd = (ctx & 1) == 1
    out = []
    for pair in range(heads // 2):
        parts = []
        for head in (2 * pair, 2 * pair + 1):
            first = pl.multiple_of(base + head * 4 * HEAD_DIM + (ctx >> 1) * 2 * HEAD_DIM, 2 * HEAD_DIM)
            parts.append(ref[:, pl.ds(first, 2 * HEAD_DIM)])
        even = jnp.where(low, parts[0], pltpu.roll(parts[1], HEAD_DIM, 1))
        other = jnp.where(low, pltpu.roll(parts[0], HEAD_DIM, 1), parts[1])
        out.append(jnp.where(odd, other, even))
    return out


def conv_back(size, width, grad, convsum_ref, convin_ref, conv_ref, ext_ref, seg, out_ref):
    sums = [[jnp.zeros((1, 128), F32)] * (CONV + 1) for _ in range(0, width, 128)]
    for first in range(0, size, 64):
        here = slice(first, first + 64)
        for strip, lane in enumerate(range(0, width, 128)):
            lanes = slice(lane, lane + 128)
            value = grad(here, lanes) * silu_grad(convsum_ref[here, lanes])
            ext_ref[here, lanes] = value
            sums[strip][CONV] = sums[strip][CONV] + jnp.sum(value, axis=0, keepdims=True)
    for first in range(0, size, 64):
        here = slice(first, first + 64)
        ids = seg(first, 64)
        same = [
            jnp.broadcast_to(seg(first + CONV - 1 - tap, 64) == ids, (64, 128)) for tap in range(CONV - 1)
        ]
        for strip, lane in enumerate(range(0, width, 128)):
            lanes = slice(lane, lane + 128)
            conv_in = convin_ref[here, lanes].astype(F32)
            back = jnp.zeros((64, 128), F32)
            for tap in range(CONV):
                at = first + CONV - 1 - tap
                term = ext_ref[at : at + 64, lanes]
                if tap < CONV - 1:
                    term = jnp.where(same[tap], term, 0.0)
                back = back + conv_ref[tap : tap + 1, lanes] * term
                sums[strip][tap] = sums[strip][tap] + jnp.sum(conv_in * term, axis=0, keepdims=True)
            out_ref[here, lanes] = back.astype(BF16)
    row = lax.broadcasted_iota(jnp.int32, (8, 128), 0)
    out = []
    for strip in sums:
        total = jnp.zeros((8, 128), F32)
        for at, value in enumerate(strip):
            total = jnp.where(row == at, value, total)
        out.append(total)
    return jnp.concatenate(out, axis=1)


def pack_kernel(near, here_ref, win_ref, wout_ref, dt_ref, conv_ref, gain_ref, w1_ref, wg_ref, wo_ref, tmp_ref):
    ctx = here_ref[2]
    rows = win_ref.shape[0]
    heads = HEADS // 4
    width = heads * HEAD_DIM
    copies = range(w1_ref.shape[0])
    for at, part in enumerate(pick_heads(win_ref, INNER, ctx, heads)):
        part = part.astype(BF16)
        for copy in copies:
            w1_ref[copy, 0:rows, at * 128 : (at + 1) * 128] = part
    part = win_ref[:, 2 * INNER :].astype(BF16)
    for copy in copies:
        w1_ref[copy, 0:rows, width:] = part
    tmp_ref[...] = jnp.zeros_like(tmp_ref)
    row = lax.broadcasted_iota(jnp.int32, (heads, HEADS), 0)
    col = lax.broadcasted_iota(jnp.int32, (heads, HEADS), 1)
    table = jnp.where(col == 4 * row + ctx, 1.0, 0.0).astype(BF16)
    tmp_ref[0:heads, 384 : 384 + dt_ref.shape[1]] = nn(table, dt_ref[...].astype(BF16))
    tmp_ref[8 : 8 + CONV + 1, 0 : conv_ref.shape[1]] = conv_ref[...]
    tmp_ref[8 + CONV + 1 : 8 + CONV + 2, 0 : gain_ref.shape[0]] = gain_ref[...].reshape(1, -1)
    for copy in copies:
        w1_ref[copy, rows : rows + 16, :] = tmp_ref[...].astype(BF16)
    for at, part in enumerate(pick_heads(win_ref, 0, ctx, heads)):
        part = part.astype(BF16)
        for copy in copies:
            wg_ref[copy, :, at * 128 : (at + 1) * 128] = part
    if near:
        mine = wout_ref[pl.ds(pl.multiple_of(ctx * HEAD_DIM, 8), HEAD_DIM), :].astype(BF16)
        for copy in copies:
            wo_ref[copy, :HEAD_DIM] = mine[:, :width]
            wo_ref[copy, HEAD_DIM:] = mine[:, width:]


def scan_forward_kernel(
    here_ref,
    at_ref,
    tok_pieces,
    w1_pieces,
    hrow_ref,
    hcol_ref,
    segc_ref,
    segr_ref,
    hid_ref,
    conv_ref,
    gpre_ref,
    gmine_ref,
    wdt_ref,
    w1_ref,
    mixed_ref,
    convin_ref,
    convsum_ref,
    inner_ref,
    raw_ref,
    stepc_ref,
    logc_ref,
    stepr_ref,
    logr_ref,
    start_ref,
    ext_ref,
    seg_ref,
    state_ref,
    small_ref,
    tok_ref,
    conv_all,
    gain_all,
    sems,
    tok_sems,
):
    step = pl.program_id(0)
    span, model = hid_ref.shape
    heads = wdt_ref.shape[0]
    width = heads * HEAD_DIM
    shards = small_ref.shape[0]
    rows = model // shards

    @pl.when(step == 0)
    def _():
        copies = place(
            w1_pieces,
            at_ref,
            len(w1_pieces),
            sems,
            [(0, rows, rows_of(w1_ref, rows)), (rows, 16, lambda at: small_ref.at[at])],
        )
        tokens = [
            pltpu.make_async_copy(piece, tok_ref.at[here_ref[2] ^ index], tok_sems.at[index])
            for index, piece in enumerate(tok_pieces)
        ]
        for copy in tokens:
            copy.start()
        ext_ref[0:8] = jnp.zeros((8, ext_ref.shape[1]), F32)
        state_ref[...] = jnp.zeros_like(state_ref)
        conv_all[...] = jnp.zeros_like(conv_all)
        for copy in copies:
            copy.wait()
        conv_cols = conv_all.shape[1] // shards
        gain_len = gain_all.shape[1] // shards
        for shard in range(shards):
            small = small_ref[shard].astype(F32)
            wdt_ref[:, shard * rows : (shard + 1) * rows] = small[0:8, 384 : 384 + rows].astype(BF16)
            conv_all[0 : CONV + 1, shard * conv_cols : (shard + 1) * conv_cols] = small[
                8 : 8 + CONV + 1, :conv_cols
            ]
            gain_all[:, shard * gain_len : (shard + 1) * gain_len] = small[13:14, :gain_len]
        for at, part in enumerate(pick_heads(conv_all, 0, here_ref[2], heads)):
            conv_ref[:, at * 128 : (at + 1) * 128] = part
        conv_ref[:, width:] = conv_all[:, INNER:]
        gpre_ref[...] = gain_all[:, :model]
        for at, part in enumerate(pick_heads(gain_all, model, here_ref[2], heads)):
            gmine_ref[:, at * 128 : (at + 1) * 128] = part
        for copy in tokens:
            copy.wait()

    for first in range(0, span, 32):
        tok = tok_ref[step, first : first + 32]
        scale = lax.rsqrt(jnp.mean(tok * tok, axis=-1, keepdims=True) + NORM_EPS)
        hid_ref[first : first + 32] = (tok * scale * gpre_ref[...]).astype(BF16)
    hid = hid_ref[...]
    proj = nn(hid, w1_ref[...]).astype(BF16)
    convin_ref[...] = proj
    ext_ref[8 : 8 + span] = proj.astype(F32)
    seg_ref[...] = segc_ref[pl.ds(pl.multiple_of(step * span, 8), span + 8), :]
    seg_here = seg_ref[8 : 8 + span]
    for first in range(0, span, 64):
        here = seg_ref[8 + first : 72 + first]
        starts = [8 - (CONV - 1) + tap + first for tap in range(CONV)]
        same = [jnp.broadcast_to(seg_ref[at : at + 64] == here, (64, 128)) for at in starts[:-1]]
        for lane in range(0, convin_ref.shape[1], 128):
            lanes = slice(lane, lane + 128)
            total = conv_ref[CONV : CONV + 1, lanes]
            for tap, at in enumerate(starts):
                term = ext_ref[at : at + 64, lanes]
                if tap < CONV - 1:
                    term = jnp.where(same[tap], term, 0.0)
                total = total + conv_ref[tap : tap + 1, lanes] * term
            convsum_ref[first : first + 64, lanes] = total
            mixed_ref[first : first + 64, lanes] = (total * sigmoid(total)).astype(BF16)
    ext_ref[0:8] = ext_ref[span : span + 8]

    raw_c = nt(hid, wdt_ref[...]) + hrow_ref[1:2]
    raw_r = nt(wdt_ref[...], hid) + hcol_ref[:, 1:2]
    step_c = softplus(raw_c)
    step_r = softplus(raw_r)
    log_c = nn(triangle(span, True), -step_c * jnp.exp(hrow_ref[0:1]), HIGHEST)
    log_r = nn(-step_r * jnp.exp(hcol_ref[:, 0:1]), triangle(span, False), HIGHEST)
    raw_ref[...] = raw_c
    stepc_ref[...] = step_c
    logc_ref[...] = log_c
    stepr_ref[...] = step_r
    logr_ref[...] = log_r

    low = lax.broadcasted_iota(jnp.int32, (SPAN, 2 * HEAD_DIM), 1) < HEAD_DIM
    earlier = lax.broadcasted_iota(jnp.int32, (SPAN, SPAN), 0) >= lax.broadcasted_iota(
        jnp.int32, (SPAN, SPAN), 1
    )
    skip_w = spread(hrow_ref[2:3] + jnp.zeros((8, heads), F32), width)[0:1]
    state = state_ref[...]
    for block in range(span // SPAN):
        here = slice(block * SPAN, (block + 1) * SPAN)
        values = mixed_ref[here, :width]
        write = mixed_ref[here, width : width + STATE]
        read = mixed_ref[here, width + STATE :]
        seg = seg_here[here]
        log = log_c[here]
        log_row = log_r[:, here]
        step_row = step_r[:, here]
        scores = jnp.where((seg == segr_ref[:, here]) & earlier, nt(read, write), 0.0)
        seg_prev = seg_ref[7 + block * SPAN : 8 + block * SPAN]
        seg_last = seg_ref[7 + (block + 1) * SPAN : 8 + (block + 1) * SPAN]
        last = log[SPAN - 1 : SPAN]
        enter = jnp.where(seg == seg_prev, jnp.exp(log), 0.0)
        tail = jnp.where(seg == seg_last, jnp.exp(last - log), 0.0) * step_c[here]
        keep = jnp.where(seg_last == seg_prev, jnp.exp(last), 0.0)
        start_ref[block] = state
        values_f = values.astype(F32)
        enter_w = spread(enter, width)
        inter = nn(read, state.astype(BF16))
        for pair in range(heads // 2):
            lanes = slice(pair * 2 * HEAD_DIM, (pair + 1) * 2 * HEAD_DIM)
            pieces = []
            for head in (2 * pair, 2 * pair + 1):
                gap = jnp.minimum(log[:, head : head + 1] - log_row[head : head + 1], 0.0)
                weights = scores * jnp.exp(gap) * step_row[head : head + 1]
                pieces.append(nn(weights.astype(BF16), values[:, lanes]))
            base = enter_w[:, lanes] * inter[:, lanes] + skip_w[:, lanes] * values_f[:, lanes]
            inner_ref[here, lanes] = base + jnp.where(low, pieces[0], pieces[1])
        moved = (spread(tail, width) * values_f).astype(BF16)
        keep_w = spread(keep + jnp.zeros((8, heads), F32), width)[0:1]
        state = keep_w * state + tn(write, moved)
    state_ref[...] = state


def row_stats(columns, at, stat_ref, before):
    value = jnp.concatenate(columns, axis=0)
    value = jnp.sum(jnp.where(diagonal(value.shape[0]), value, 0.0), axis=0, keepdims=True)
    row = lax.broadcasted_iota(jnp.int32, stat_ref.shape, 0)
    stat_ref[...] = jnp.where(row == at, value, before)


def gate_kernel(at_ref, hid_ref, wg_pieces, inner_ref, wg_ref, gate_ref, stat_ref, sems):
    rows = wg_pieces[0].shape[1]

    @pl.when(pl.program_id(0) == 0)
    def _():
        copies = place(wg_pieces, at_ref, len(wg_pieces), sems, [(0, rows, rows_of(wg_ref, rows))])
        for copy in copies:
            copy.wait()

    gate_ref[...] = nn(hid_ref[...], wg_ref[...]).astype(BF16)
    squares = []
    for first in range(0, gate_ref.shape[0], 32):
        here = slice(first, first + 32)
        gate = gate_ref[here].astype(F32)
        gated = inner_ref[here] * (gate * sigmoid(gate))
        squares.append(jnp.sum(gated * gated, axis=1, keepdims=True))
    row_stats(squares, 0, stat_ref, 0.0)


def normed_grad_kernel(
    here_ref,
    at_ref,
    wo_pieces,
    cot_pieces,
    inner_ref,
    gate_ref,
    before_ref,
    gain_ref,
    wout_ref,
    cot_ref,
    ng_ref,
    stat_ref,
    turned_ref,
    sems,
    cot_sems,
):
    step = pl.program_id(0)
    width = ng_ref.shape[1]

    @pl.when(step == 0)
    def _():
        some = rows_of(wout_ref, HEAD_DIM)
        copies = place(
            wo_pieces,
            at_ref,
            len(wo_pieces),
            sems,
            [
                (0, HEAD_DIM, lambda at: some(at).at[:, 0:width]),
                (HEAD_DIM, HEAD_DIM, lambda at: some(at).at[:, width : 2 * width]),
            ],
        )
        cots = [
            pltpu.make_async_copy(piece, cot_ref.at[here_ref[2] ^ index], cot_sems.at[index])
            for index, piece in enumerate(cot_pieces)
        ]
        for copy in cots:
            copy.start()
        for copy in copies + cots:
            copy.wait()
        turned_ref[...] = wout_ref[...].T

    ng_ref[...] = nn(cot_ref[step], turned_ref[...])
    crossed = []
    for first in range(0, ng_ref.shape[0], 32):
        here = slice(first, first + 32)
        gate = gate_ref[here].astype(F32)
        gated = inner_ref[here] * (gate * sigmoid(gate))
        crossed.append(jnp.sum(gated * (ng_ref[here] * gain_ref[...]), axis=1, keepdims=True))
    row_stats(crossed, 1, stat_ref, before_ref[...])


def norm_back_kernel(
    perm_ref,
    here_ref,
    hid_ref,
    inner_ref,
    gate_ref,
    ng_ref,
    stat_refs,
    gain_ref,
    mixed_ref,
    wout_ref,
    cot_ref,
    block_refs,
    keep_ref,
    send_ref,
    dy_ref,
    dgate_ref,
    sums_ref,
    outacc_ref,
    inacc_ref,
    normed_ref,
):
    step = pl.program_id(0)
    span, width = inner_ref.shape

    @pl.when(step == 0)
    def _():
        outacc_ref[...] = jnp.zeros_like(outacc_ref)
        inacc_ref[...] = jnp.zeros_like(inacc_ref)
        sums_ref[...] = jnp.zeros_like(sums_ref)

    same = diagonal(span)
    stats = sum(ref[...] for ref in stat_refs)
    squares = jnp.sum(jnp.where(same, stats[0:1], 0.0), axis=1, keepdims=True)
    cross = jnp.sum(jnp.where(same, stats[1:2], 0.0), axis=1, keepdims=True)
    inv = lax.rsqrt(squares * (1.0 / INNER) + NORM_EPS)
    gain_sum = jnp.zeros((1, width), F32)
    skip_sum = jnp.zeros((1, width), F32)
    for first in range(0, span, 32):
        here = slice(first, first + 32)
        gate = gate_ref[here].astype(F32)
        sig = sigmoid(gate)
        silu = gate * sig
        inner = inner_ref[here]
        scale = inv[here]
        unit = inner * silu * scale
        normed_ref[here] = (unit * gain_ref[...]).astype(BF16)
        grad = ng_ref[here]
        dgated = scale * (grad * gain_ref[...] - unit * (cross[here] * scale * (1.0 / INNER)))
        dy = dgated * silu
        dy_ref[here] = dy
        dgate_ref[here] = (dgated * inner * (sig * (1.0 + gate * (1.0 - sig)))).astype(BF16)
        gain_sum = gain_sum + jnp.sum(grad * unit, axis=0, keepdims=True)
        skip_sum = skip_sum + jnp.sum(dy * mixed_ref[here].astype(F32), axis=0, keepdims=True)
    normed = normed_ref[...]
    cot = cot_ref[perm_ref[step]]
    block = nn(normed, wout_ref[...]).astype(BF16)

    for at, block_ref in enumerate(block_refs):

        @pl.when(step == at)
        def _():
            block_ref[...] = block

    outacc_ref[...] += tn(normed, cot)
    inacc_ref[...] += tn(hid_ref[...], dgate_ref[...])
    at = lax.broadcasted_iota(jnp.int32, (8, width), 0)
    sums_ref[...] += jnp.where(at == 0, gain_sum, jnp.where(at == 1, skip_sum, 0.0))

    @pl.when(step == pl.num_programs(0) - 1)
    def _():
        own = here_ref[0]
        rows = inacc_ref.shape[0] // (2 * keep_ref.shape[0])
        part_of(lambda at: inacc_ref[at * rows : (at + 1) * rows], own, keep_ref, send_ref)
        outs = lambda at: outacc_ref[at * HEAD_DIM : (at + 1) * HEAD_DIM]
        part_of(lambda at: outs(at)[:, :width], own, keep_ref, send_ref, rows)
        part_of(lambda at: outs(at)[:, width:], own, keep_ref, send_ref, rows + HEAD_DIM)


def scan_back_kernel(
    perm_ref,
    here_ref,
    hid_ref,
    dy_ref,
    mixed_ref,
    convin_ref,
    convsum_ref,
    raw_ref,
    stepc_ref,
    logc_ref,
    stepr_ref,
    logr_ref,
    start_ref,
    conv_ref,
    hrow_ref,
    segc_ref,
    segr_ref,
    keep_ref,
    send_ref,
    dval_ref,
    dbc_ref,
    dstep_ref,
    convg_ref,
    dtg_ref,
    headg_ref,
    ext_ref,
    seg_ref,
    grad_ref,
    inacc_ref,
    dx_ref,
):
    step = pl.program_id(0)
    chunk = pl.num_programs(0) - 1 - step
    span = hid_ref.shape[0]
    heads = stepc_ref.shape[1]
    width = heads * HEAD_DIM

    @pl.when(step == 0)
    def _():
        ext_ref[span : span + 8] = jnp.zeros((8, width), F32)
        grad_ref[...] = jnp.zeros_like(grad_ref)
        inacc_ref[...] = jnp.zeros_like(inacc_ref)
        convg_ref[...] = jnp.zeros_like(convg_ref)
        dtg_ref[...] = jnp.zeros_like(dtg_ref)
        headg_ref[...] = jnp.zeros_like(headg_ref)

    seg_ref[...] = segc_ref[pl.ds(pl.multiple_of(chunk * span, 8), span + 16), :]
    seg_here = seg_ref[8 : 8 + span]
    low = lax.broadcasted_iota(jnp.int32, (SPAN, 2 * HEAD_DIM), 1) < HEAD_DIM
    earlier = lax.broadcasted_iota(jnp.int32, (SPAN, SPAN), 0) >= lax.broadcasted_iota(
        jnp.int32, (SPAN, SPAN), 1
    )
    head_at = lax.broadcasted_iota(jnp.int32, (heads, SPAN), 0)
    lane_at = lax.broadcasted_iota(jnp.int32, (SPAN, heads), 1)
    at_last = lax.broadcasted_iota(jnp.int32, (SPAN, heads), 0) == SPAN - 1
    skip_w = spread(hrow_ref[2:3] + jnp.zeros((8, heads), F32), width)[0:1]
    step_c = stepc_ref[...]
    step_r = stepr_ref[...]
    later = grad_ref[...]
    count = span // SPAN
    dlogs, dsteps_c, dsteps_r = [None] * count, [None] * count, [None] * count
    for block in reversed(range(count)):
        here = slice(block * SPAN, (block + 1) * SPAN)
        values = mixed_ref[here, :width]
        write = mixed_ref[here, width : width + STATE]
        read = mixed_ref[here, width + STATE :]
        values_f = values.astype(F32)
        seg = seg_here[here]
        seg_prev = seg_ref[7 + block * SPAN : 8 + block * SPAN]
        seg_last = seg_ref[7 + (block + 1) * SPAN : 8 + (block + 1) * SPAN]
        dy = dy_ref[here]
        dy_low = dy.astype(BF16)
        log = logc_ref[here]
        log_row = logr_ref[:, here]
        step_row = step_r[:, here]
        last = log[SPAN - 1 : SPAN]
        enter = jnp.where(seg == seg_prev, jnp.exp(log), 0.0)
        tail_raw = jnp.where(seg == seg_last, jnp.exp(last - log), 0.0)
        tail = tail_raw * step_c[here]
        keep = jnp.where(seg_last == seg_prev, jnp.exp(last), 0.0)
        enter_w = spread(enter, width)
        tail_w = spread(tail, width)
        keep_w = spread(keep + jnp.zeros((8, heads), F32), width)[0:1]
        state = start_ref[block]
        state_low = state.astype(BF16)
        later_low = later.astype(BF16)

        entered_low = (enter_w * dy).astype(BF16)
        inter = enter_w * nn(read, state_low)
        from_later = nn(write, later_low)
        moved_low = (tail_w * values_f).astype(BF16)
        dread = nt(entered_low, state_low)
        dwrite = nt(moved_low, later_low)
        tail_dot = gather_heads(values_f * from_later, heads)
        dlog = gather_heads(dy * inter, heads) - tail_dot * tail
        dsteps_c[block] = tail_dot * tail_raw
        carried = jnp.sum(later * state, axis=0, keepdims=True) + jnp.zeros((8, width), F32)
        carried = gather_heads(carried, heads)[0:1]
        dlog = dlog + jnp.where(
            at_last, jnp.sum(tail_dot * tail, axis=0, keepdims=True) + keep * carried, 0.0
        )
        later = keep_w * later + tn(read, entered_low)
        direct = tail_w * from_later + skip_w * dy

        visible = (seg == segr_ref[:, here]) & earlier
        scores = jnp.where(visible, nt(read, write), 0.0)
        dscores = jnp.zeros((SPAN, SPAN), F32)
        dstep = jnp.zeros((heads, SPAN), F32)
        for pair in range(heads // 2):
            lanes = slice(pair * 2 * HEAD_DIM, (pair + 1) * 2 * HEAD_DIM)
            dy_pair = dy_low[:, lanes]
            pieces = []
            for head in (2 * pair, 2 * pair + 1):
                mine = low if head % 2 == 0 else ~low
                gap = jnp.minimum(log[:, head : head + 1] - log_row[head : head + 1], 0.0)
                decay = jnp.exp(gap)
                outer = nt(jnp.where(mine, dy_pair, jnp.zeros_like(dy_pair)), values[:, lanes])
                fade = decay * step_row[head : head + 1]
                dscores = dscores + outer * fade
                weights = scores * fade
                flow = outer * scores
                dstep = dstep + jnp.where(
                    head_at == head, jnp.sum(flow * decay, axis=0, keepdims=True), 0.0
                )
                dlog = dlog + jnp.where(
                    lane_at == head, jnp.sum(outer * weights, axis=1, keepdims=True), 0.0
                )
                pieces.append(tn(weights.astype(BF16), dy_pair))
            dx_ref[here, lanes] = direct[:, lanes] + jnp.where(low, pieces[0], pieces[1])
        dscores = jnp.where(visible, dscores, 0.0).astype(BF16)
        dbc_ref[here, :STATE] = (dwrite + tn(dscores, read)).astype(BF16)
        dbc_ref[here, STATE:] = (dread + nn(dscores, write)).astype(BF16)
        dlogs[block], dsteps_r[block] = dlog, dstep
    grad_ref[...] = later
    dlog_c = jnp.concatenate(dlogs, axis=0)
    dstep_c = jnp.concatenate(dsteps_c, axis=0)
    dstep_r = jnp.concatenate(dsteps_r, axis=1)

    upper = triangle(span, False)
    eye = jnp.where(diagonal(span), 1.0, 0.0).astype(F32)
    dalpha = nn(upper, dlog_c, HIGHEST) - nt(upper, dstep_r * step_r, HIGHEST)
    dstep = dstep_c + nt(eye, dstep_r, HIGHEST)
    rate = jnp.exp(hrow_ref[0:1])
    draw = (dstep - rate * dalpha) * sigmoid(raw_ref[...])
    draw_low = draw.astype(BF16)
    dstep_ref[...] = draw_low
    hid = hid_ref[...]
    dtg_ref[...] += tn(draw_low, hid)
    rate_sum = jnp.sum(-dalpha * step_c * rate, axis=0, keepdims=True)
    bias_sum = jnp.sum(draw, axis=0, keepdims=True)
    at = lax.broadcasted_iota(jnp.int32, (8, heads), 0)
    headg_ref[...] += jnp.where(at == 0, rate_sum, jnp.where(at == 1, bias_sum, 0.0))

    convg_ref[...] += conv_back(
        span,
        width,
        lambda here, lanes: dx_ref[here, lanes],
        convsum_ref,
        convin_ref,
        conv_ref,
        ext_ref,
        lambda first, count: seg_ref[8 + first : 8 + first + count],
        dval_ref,
    )
    ext_ref[span : span + 8] = ext_ref[0:8]
    inacc_ref[...] += tn(hid, dval_ref[...])

    @pl.when(step == pl.num_programs(0) - 1)
    def _():
        rows = inacc_ref.shape[0] // (2 * keep_ref.shape[0])
        part_of(lambda at: inacc_ref[at * rows : (at + 1) * rows], here_ref[0], keep_ref, send_ref)


def hidden_back_kernel(
    perm_ref,
    dgate_ref,
    dval_ref,
    dstep_ref,
    wg_ref,
    wv_ref,
    wdt_ref,
    hid_ref,
    gain_ref,
    out_refs,
    gsum_ref,
    turned_ref,
):
    width = wg_ref.shape[1]

    @pl.when(pl.program_id(0) == 0)
    def _():
        gsum_ref[...] = jnp.zeros_like(gsum_ref)
        turned_ref[0:width] = wg_ref[...].T
        turned_ref[width:] = wv_ref[...].T

    total = nn(dgate_ref[...], turned_ref[0:width]) + nn(dval_ref[...], turned_ref[width:])
    total = total + nn(dstep_ref[...], wdt_ref[...])
    step = pl.program_id(0)

    for at, out_ref in enumerate(out_refs):

        @pl.when(step == at)
        def _():
            out_ref[...] = total.astype(BF16)

    gain_sum = jnp.zeros(gain_ref.shape, F32)
    for first in range(0, total.shape[0], 32):
        here = slice(first, first + 32)
        gain_sum = gain_sum + jnp.sum(total[here] * hid_ref[here].astype(F32), axis=0, keepdims=True)
    gsum_ref[...] += gain_sum / gain_ref[...] + jnp.zeros(gsum_ref.shape, F32)


def maps_back_kernel(
    here_ref,
    dbc_ref,
    dbcfar_ref,
    convsum_ref,
    convin_ref,
    conv_ref,
    segc_ref,
    hid_ref,
    w1_ref,
    gain_ref,
    convg_ref,
    sums_ref,
    headg_ref,
    dtg_ref,
    gall_ref,
    keep_ref,
    send_ref,
    own_ref,
    ext_ref,
    acc_ref,
    dmap_ref,
    small_ref,
):
    size, width = dmap_ref.shape
    ext_ref[size : size + 8] = jnp.zeros((8, width), F32)
    sums = conv_back(
        size,
        width,
        lambda here, lanes: dbc_ref[here, lanes].astype(F32) + dbcfar_ref[here, lanes].astype(F32),
        convsum_ref,
        convin_ref,
        conv_ref,
        ext_ref,
        lambda first, count: segc_ref[8 + first : 8 + first + count],
        dmap_ref,
    )
    ctx = here_ref[2]
    acc_ref[...] = tn(hid_ref[...], dmap_ref[...])
    span = own_ref.shape[0]
    own = pl.ds(pl.multiple_of(ctx * span, 16), span)
    grad = nt(dmap_ref[own, :], w1_ref[...])
    own_ref[...] = grad
    unit = hid_ref[own, :].astype(F32) / gain_ref[...]
    gain_sum = gall_ref[0:1] + jnp.sum(grad * unit, axis=0, keepdims=True)
    half = small_ref.shape[1]
    heads = headg_ref.shape[1]
    small_ref[...] = jnp.zeros_like(small_ref)
    small_ref[0 : CONV + 1] = convg_ref[0 : CONV + 1]
    small_ref[CONV + 1 : CONV + 3] = sums_ref[0:2]
    small_ref[7:8, 0:heads] = headg_ref[0:1]
    small_ref[7:8, 128 : 128 + heads] = headg_ref[1:2]
    small_ref[8 : 8 + CONV + 1, 0:width] = sums[0 : CONV + 1]
    small_ref[13:14] = gain_sum[:, :half]
    small_ref[14:15] = gain_sum[:, half:]
    small_ref[15:16] = small_ref[7:8] - small_ref[7:8].astype(BF16).astype(F32)
    small_ref[16:24] = dtg_ref[:, :half]
    small_ref[24:32] = dtg_ref[:, half:]
    small = small_ref[...].astype(BF16)
    count = keep_ref.shape[0] // 32 - 1
    block = acc_ref.shape[0] // (2 * count)
    some = block // 4
    keep_ref[0:32] = small
    send_ref[0:32] = small
    for at in range(count):
        start = pl.multiple_of(2 * at * block + ctx * some, 8)
        low = acc_ref[pl.ds(start, some), :].astype(BF16)
        start = pl.multiple_of((2 * at + 1) * block + ctx * some, 8)
        high = acc_ref[pl.ds(start, some), :].astype(BF16)
        keep_ref[32 + 32 * at : 64 + 32 * at, 0:width] = jnp.where(here_ref[0] == 0, low, high)
        send_ref[32 + 32 * at : 64 + 32 * at, 0:width] = jnp.where(here_ref[0] == 0, high, low)


def input_back_kernel(part_refs, own_ref, tok_ref, gain_ref, cot_ref, out_ref):
    for first in range(0, out_ref.shape[0], 32):
        here = slice(first, first + 32)
        grad = own_ref[here]
        for ref in part_refs:
            grad = grad + ref[here].astype(F32)
        tok = tok_ref[here]
        scale = lax.rsqrt(jnp.mean(tok * tok, axis=-1, keepdims=True) + NORM_EPS)
        unit = tok * scale
        scaled = grad * gain_ref[...]
        mean = jnp.mean(scaled * unit, axis=-1, keepdims=True)
        out_ref[here] = cot_ref[here] + scale * (scaled - unit * mean)


def with_rest(value, first):
    row = lax.broadcasted_iota(jnp.int32, value.shape, 0)
    head = value[first + 7 : first + 8] + value[first + 15 : first + 16]
    rest = head - head.astype(BF16).astype(F32)
    return jnp.where(row == first + 7, head, jnp.where(row == first + 15, rest, value))


def pair_sum_late_kernel(keep_ref, came_ref, mkeep_ref, mcame_ref, out_ref):
    count, rows, width = keep_ref.shape
    small = with_rest(mkeep_ref[0:32].astype(F32) + mcame_ref[0:32].astype(F32), 0).astype(BF16)
    for block in range(count):
        out_ref[block, 0:rows] = (keep_ref[block].astype(F32) + came_ref[block].astype(F32)).astype(BF16)
        out_ref[block, rows : rows + 32] = small
        at = slice(32 + 32 * block, 64 + 32 * block)
        out_ref[block, rows + 32 : rows + 64] = (
            mkeep_ref[at].astype(F32) + mcame_ref[at].astype(F32)
        ).astype(BF16)


def sum_late_kernel(parts_ref, out_ref):
    total = parts_ref[0].astype(F32)
    for at in range(1, parts_ref.shape[0]):
        total = total + parts_ref[at].astype(F32)
    out_ref[...] = with_rest(total, out_ref.shape[0] - 64).astype(BF16)


def adam_out_kernel(here_ref, weight_ref, first_ref, second_ref, early_refs, *rest):
    new_refs, early_ref = rest[:3], rest[3]
    step = pl.program_id(0)

    @pl.when(step == 0)
    def _():
        by_owner(early_refs, here_ref[2], early_ref)

    rows = weight_ref.shape[0]
    width = early_ref.shape[2]
    first = early_ref.shape[1] - 2 * rows
    for at in range(2):
        lanes = slice(at * width, (at + 1) * width)
        grad = early_ref[step, first + at * rows : first + (at + 1) * rows].astype(F32)
        news = adam_step(
            weight_ref[:, lanes], first_ref[:, lanes], second_ref[:, lanes], grad, 0.02, WEIGHT_DECAY
        )
        for ref, new in zip(new_refs, news):
            ref[:, lanes] = new


def by_owner(refs, ctx, natural_ref):
    for at, ref in enumerate(refs):
        natural_ref[pl.ds(ctx ^ at, 1)] = ref[...][None]


def adam_in_kernel(here_ref, weight_ref, first_ref, second_ref, early_refs, late_refs, *rest):
    new_refs, (early_ref, late_ref) = rest[:3], rest[3:]
    step = pl.program_id(0)
    pieces = len(early_refs)
    rows = weight_ref.shape[0]
    width = early_ref.shape[2]
    block = pieces * HEAD_DIM

    @pl.when(step == 0)
    def _():
        by_owner(early_refs, here_ref[2], early_ref)
        by_owner(late_refs, here_ref[2], late_ref)

    here = pl.ds(pl.multiple_of(step * rows, rows), rows)
    low = lax.broadcasted_iota(jnp.int32, (rows, 2 * HEAD_DIM), 1) < HEAD_DIM

    def update(lanes, grad):
        news = adam_step(
            weight_ref[:, lanes], first_ref[:, lanes], second_ref[:, lanes], grad, 0.03, WEIGHT_DECAY
        )
        for ref, new in zip(new_refs, news):
            ref[:, lanes] = new

    for base, ref in ((0, early_ref), (INNER, late_ref)):
        for pair in range(width // (2 * HEAD_DIM)):
            lanes = slice(pair * 2 * HEAD_DIM, (pair + 1) * 2 * HEAD_DIM)
            for at in range(0, pieces, 2):
                first = ref[at, here, lanes].astype(F32)
                second = ref[at + 1, here, lanes].astype(F32)
                start = base + 2 * pair * block + at * HEAD_DIM
                even = jnp.where(low, first, pltpu.roll(second, HEAD_DIM, 1))
                update(slice(start, start + 2 * HEAD_DIM), even)
                start = start + block
                odd = jnp.where(low, pltpu.roll(first, HEAD_DIM, 1), second)
                update(slice(start, start + 2 * HEAD_DIM), odd)
    some = 32 // rows
    first = pl.multiple_of(late_ref.shape[1] - 32 + (step % some) * rows, rows)
    grad = late_ref[step // some, pl.ds(first, rows), 0 : 2 * STATE].astype(F32)
    update(slice(2 * INNER, 2 * INNER + 2 * STATE), grad)


def swap(value, axis, bit):
    count = lax.axis_size(axis)
    return lax.ppermute(value, axis, [(at, at ^ bit) for at in range(count)])


def gather_ctx(value):
    far = swap(value, "ctx", 2)
    return [value, swap(value, "ctx", 1), far, swap(far, "ctx", 1)]


def high_all_to_all(value):
    count = lax.axis_size("dp")
    groups = [list(range(low, count, 2)) for low in range(2)]
    return lax.all_to_all(value, "dp", 0, 0, axis_index_groups=groups)


def from_owners(parts):
    count = len(parts)
    return [swap(parts[bit - 1], "ctx", bit) for bit in range(1, count)] + [parts[-1]]


def fan_ctx(value):
    return [value] + [swap(value, "ctx", bit) for bit in range(1, lax.axis_size("ctx"))]


def adam_step(weight, moment_one, second, gradient, step_rate, decay_rate):
    moment_new = BETA_ONE * moment_one + (1.0 - BETA_ONE) * gradient
    second_new = BETA_TWO * second + (1.0 - BETA_TWO) * gradient * gradient
    first_hat = moment_new / (1.0 - BETA_ONE**STEP)
    second_hat = second_new / (1.0 - BETA_TWO**STEP)
    weight_new = weight - step_rate * (
        first_hat / (jnp.sqrt(second_hat) + ADAM_EPS) + decay_rate * weight
    )
    return (weight_new, moment_new, second_new)


def full(shape):
    return pl.BlockSpec(shape, lambda *_: (0,) * len(shape))


def shape_of(*shape, dtype=F32):
    return jax.ShapeDtypeStruct(shape, dtype)


def shards(
    tokens,
    segment_ids,
    cotangent,
    in_weight,
    dt_weight,
    out_weight,
    conv_params,
    gains,
    head_params,
    in_first,
    in_second,
    dt_first,
    dt_second,
    out_first,
    out_second,
    conv_first,
    conv_second,
    gain_first,
    gain_second,
    head_first,
    head_second,
):
    _, span, model = tokens.shape
    length = segment_ids.shape[1]
    ndp, nctx = lax.axis_size("dp"), lax.axis_size("ctx")
    d, c = lax.axis_index("dp"), lax.axis_index("ctx")
    heads = HEADS // nctx
    width = INNER // nctx
    maps = 2 * STATE
    wide = width + maps
    chunks = nctx
    rows_in = in_weight.shape[0]
    conv_cols = conv_params.shape[1]
    gain_len = gains.shape[0]
    dt_cols = dt_weight.shape[1]
    near = ndp == heads
    high = heads // 2
    block_in = model // heads
    tok = tokens[0]
    bits = jnp.stack([d & 1, d >> 1, c] if near else [0 * d, 0 * d, c]).astype(jnp.int32)
    perm = c ^ jnp.asarray([1, 2, 3, 0], jnp.int32)
    smem = pl.BlockSpec(memory_space=pltpu.SMEM)
    vmem = pl.BlockSpec(memory_space=pltpu.VMEM)
    anywhere = lambda pieces: [pl.BlockSpec(memory_space=pl.ANY)] * len(pieces)

    w1, wg, wo = pl.pallas_call(
        functools.partial(pack_kernel, near),
        in_specs=[smem] + [vmem] * 5,
        out_shape=[
            shape_of(high if near else 1, rows_in + 16, wide, dtype=BF16),
            shape_of(high if near else 1, rows_in, width, dtype=BF16),
            shape_of(high if near else 1, 2 * HEAD_DIM, width, dtype=BF16),
        ],
        scratch_shapes=[pltpu.VMEM((16, wide), F32)],
        compiler_params=params(),
        name="pack",
    )(bits, in_weight, out_weight, dt_weight, conv_params, gains)
    ids = segment_ids[0]
    seg_col = jnp.pad(ids, (8, 8), constant_values=-1)[:, None]
    seg_row = segment_ids
    head_mine = lax.dynamic_index_in_dim(head_params.reshape(3, heads, nctx), c, 2, False)
    head_col = head_mine.T
    cot_low = cotangent[0].astype(BF16)
    if near:
        tok_far = swap(tok, "ctx", 2)
        tok_core = swap(tok, "ctx", 1)
        w1 = high_all_to_all(w1)
        at_rows = jnp.stack([d & 1, 1 - (d & 1)]).astype(jnp.int32)
        w1, wg, wo, cot_low, seg_col, head_mine, head_col, at_rows, perm = lax.optimization_barrier(
            (w1, wg, wo, cot_low, seg_col, head_mine, head_col, at_rows, perm)
        )
        w1_came = swap(w1, "dp", 1)
        wg = high_all_to_all(wg)
        wo = high_all_to_all(wo)
        w1, w1_came, tok_far = lax.optimization_barrier((w1, w1_came, tok_far))
        toks = [tok, tok_core, tok_far, swap(tok_far, "ctx", 1)]
        w1, w1_came, toks, wg, cot_low = lax.optimization_barrier((w1, w1_came, toks, wg, cot_low))
        w1 = [w1, w1_came]
        wg = [wg, swap(wg, "dp", 1)]
        cots = fan_ctx(cot_low)
    else:
        w1 = [lax.all_gather(w1[0], "dp", axis=0)]
        toks = gather_ctx(tok)
        cots = gather_ctx(cot_low)
        wg = [lax.all_gather(wg[0], "dp", axis=0, tiled=True).reshape(heads, block_in, width)]
        wo = lax.all_gather(out_weight.astype(BF16), "dp", axis=0, tiled=True)
        wo = lax.dynamic_index_in_dim(wo.reshape(heads, nctx, HEAD_DIM, model), c, 1, False)
        wo = [jnp.concatenate([wo[:, :, :width], wo[:, :, width:]], axis=1)]
        at_rows = jnp.zeros((1,), jnp.int32)

    rows = lambda cols: pl.BlockSpec((span, cols), lambda i, *_: (i, 0))
    row_of = pl.BlockSpec((heads, span), lambda i, *_: (0, i))
    rows_at = lambda cols: pl.BlockSpec((span, cols), lambda i, p, *_: (p[i], 0))
    whole = full((span, model))
    shards_in = sum(piece.shape[0] for piece in w1)

    (
        hid, conv_mine, gain_pre, gain_mine, dt_mine, w1, mixed, conv_in, conv_sum, inner, raw,
        step_c, log_c, step_r, log_r, starts,
    ) = pl.pallas_call(
        scan_forward_kernel,
        grid_spec=pltpu.PrefetchScalarGridSpec(
            num_scalar_prefetch=2,
            grid=(chunks,),
            in_specs=[
                anywhere(toks),
                anywhere(w1),
                full((3, heads)),
                full((heads, 3)),
                full((length + 16, 1)),
                pl.BlockSpec((1, span), lambda i, *_: (0, i)),
            ],
            out_specs=[
                rows(model),
                full((8, wide)),
                full((1, model)),
                full((1, width)),
                full((heads, model)),
                full((model, wide)),
                rows(wide),
                rows(wide),
                rows(wide),
                rows(width),
                rows(heads),
                rows(heads),
                rows(heads),
                row_of,
                row_of,
                pl.BlockSpec((span // SPAN, STATE, width), lambda i, *_: (i, 0, 0)),
            ],
            scratch_shapes=[
                pltpu.VMEM((span + 8, wide), F32),
                pltpu.VMEM((span + 8, 1), jnp.int32),
                pltpu.VMEM((STATE, width), F32),
                pltpu.VMEM((shards_in, 16, wide), BF16),
                pltpu.VMEM((nctx, span, model), F32),
                pltpu.VMEM((8, INNER + maps), F32),
                pltpu.VMEM((1, model + INNER), F32),
                pltpu.SemaphoreType.DMA((copies_of(w1, 2),)),
                pltpu.SemaphoreType.DMA((nctx,)),
            ],
        ),
        out_shape=[
            shape_of(length, model, dtype=BF16),
            shape_of(8, wide),
            shape_of(1, model),
            shape_of(1, width),
            shape_of(heads, model, dtype=BF16),
            shape_of(model, wide, dtype=BF16),
            shape_of(length, wide, dtype=BF16),
            shape_of(length, wide, dtype=BF16),
            shape_of(length, wide),
            shape_of(length, width),
            shape_of(length, heads),
            shape_of(length, heads),
            shape_of(length, heads),
            shape_of(heads, length),
            shape_of(heads, length),
            shape_of(length // SPAN, STATE, width),
        ],
        compiler_params=params("arbitrary"),
        name="scan_forward",
    )(bits, at_rows, toks, w1, head_mine, head_col, seg_col, seg_row)

    if near:
        wo, hid, cots = lax.optimization_barrier((wo, hid, cots))
        wo = [wo, swap(wo, "dp", 1)]
    stat_block = pl.BlockSpec((8, span), lambda i, *_: (0, i))
    wg, gate, squares = pl.pallas_call(
        gate_kernel,
        grid_spec=pltpu.PrefetchScalarGridSpec(
            num_scalar_prefetch=1,
            grid=(chunks,),
            in_specs=[rows(model), anywhere(wg), rows(width)],
            out_specs=[full((model, width)), rows(width), stat_block],
            scratch_shapes=[pltpu.SemaphoreType.DMA((copies_of(wg, 1),))],
        ),
        out_shape=[
            shape_of(model, width, dtype=BF16),
            shape_of(length, width, dtype=BF16),
            shape_of(8, length),
        ],
        compiler_params=params("arbitrary"),
        name="gate",
    )(at_rows, hid, wg, inner)
    if near:
        squares, wo = lax.optimization_barrier((squares, wo))
    wout, cot_all, normed_grad, stats = pl.pallas_call(
        normed_grad_kernel,
        grid_spec=pltpu.PrefetchScalarGridSpec(
            num_scalar_prefetch=2,
            grid=(chunks,),
            in_specs=[
                anywhere(wo),
                anywhere(cots),
                rows(width),
                rows(width),
                stat_block,
                full((1, width)),
            ],
            out_specs=[
                full((width, model)),
                full((nctx, span, model)),
                rows(width),
                stat_block,
            ],
            scratch_shapes=[
                pltpu.VMEM((model, width), BF16),
                pltpu.SemaphoreType.DMA((copies_of(wo, 2),)),
                pltpu.SemaphoreType.DMA((nctx,)),
            ],
        ),
        out_shape=[
            shape_of(width, model, dtype=BF16),
            shape_of(nctx, span, model, dtype=BF16),
            shape_of(length, width),
            shape_of(8, length),
        ],
        compiler_params=params("arbitrary"),
        name="normed_grad",
    )(bits, at_rows, wo, cots, inner, gate, squares, gain_mine)
    stats = fan_ctx(stats)

    early_rows = block_in + 2 * HEAD_DIM
    blocks_out, early_keep, early_send, dy, dgate, col_sums = pl.pallas_call(
        norm_back_kernel,
        grid_spec=pltpu.PrefetchScalarGridSpec(
            num_scalar_prefetch=2,
            grid=(chunks,),
            in_specs=[
                rows_at(model),
                rows_at(width),
                rows_at(width),
                rows_at(width),
                [pl.BlockSpec((8, span), lambda i, p, *_: (0, p[i]))] * nctx,
                full((1, width)),
                rows_at(width),
                full((width, model)),
                full((nctx, span, model)),
            ],
            out_specs=[
                [whole] * nctx,
                full((high, early_rows, width)),
                full((high, early_rows, width)),
                rows_at(width),
                rows_at(width),
                full((8, width)),
            ],
            scratch_shapes=[
                pltpu.VMEM((width, model), F32),
                pltpu.VMEM((model, width), F32),
                pltpu.VMEM((span, width), BF16),
            ],
        ),
        out_shape=[
            [shape_of(span, model, dtype=BF16)] * nctx,
            shape_of(high, early_rows, width, dtype=BF16),
            shape_of(high, early_rows, width, dtype=BF16),
            shape_of(length, width),
            shape_of(length, width, dtype=BF16),
            shape_of(8, width),
        ],
        compiler_params=params("arbitrary"),
        name="norm_back",
    )(perm, bits, hid, inner, gate, normed_grad, stats, gain_mine, mixed, wout, cot_all)
    blocks_out = from_owners(blocks_out)
    if near:
        early_came = swap(early_send, "dp", 1)

    back = lambda cols: pl.BlockSpec((span, cols), lambda i, *_: (chunks - 1 - i, 0))
    back_row = pl.BlockSpec((heads, span), lambda i, *_: (0, chunks - 1 - i))
    late_keep, late_send, dval, dbc, dstep, conv_grad, dt_grad, head_grad = pl.pallas_call(
        scan_back_kernel,
        grid_spec=pltpu.PrefetchScalarGridSpec(
            num_scalar_prefetch=2,
            grid=(chunks,),
            in_specs=[
                back(model),
                back(width),
                back(wide),
                back(width),
                back(width),
                back(heads),
                back(heads),
                back(heads),
                back_row,
                back_row,
                pl.BlockSpec((span // SPAN, STATE, width), lambda i, *_: (chunks - 1 - i, 0, 0)),
                full((8, width)),
                full((3, heads)),
                full((length + 16, 1)),
                pl.BlockSpec((1, span), lambda i, *_: (0, chunks - 1 - i)),
            ],
            out_specs=[
                full((high, block_in, width)),
                full((high, block_in, width)),
                back(width),
                back(maps),
                back(heads),
                full((8, width)),
                full((heads, model)),
                full((8, heads)),
            ],
            scratch_shapes=[
                pltpu.VMEM((span + 8, width), F32),
                pltpu.VMEM((span + 16, 1), jnp.int32),
                pltpu.VMEM((STATE, width), F32),
                pltpu.VMEM((model, width), F32),
                pltpu.VMEM((span, width), F32),
            ],
        ),
        out_shape=[
            shape_of(high, block_in, width, dtype=BF16),
            shape_of(high, block_in, width, dtype=BF16),
            shape_of(length, width, dtype=BF16),
            shape_of(length, maps, dtype=BF16),
            shape_of(length, heads, dtype=BF16),
            shape_of(8, width),
            shape_of(heads, model),
            shape_of(8, heads),
        ],
        compiler_params=params("arbitrary"),
        name="scan_back",
    )(
        perm, bits, hid, dy, mixed, conv_in, conv_sum, raw, step_c, log_c, step_r, log_r, starts,
        conv_mine, head_mine, seg_col, seg_row,
    )
    dbc_came = swap(dbc, "ctx", 1)
    if near:
        late_came = swap(late_send, "dp", 1)
        early_came, blocks_out, dval = lax.optimization_barrier((early_came, blocks_out, dval))
        early_parts = (early_keep.astype(F32) + early_came.astype(F32)).astype(BF16)
        early_parts = high_all_to_all(early_parts)
    dbc = (dbc.astype(F32) + dbc_came.astype(F32)).astype(BF16)
    dval, dbc = lax.optimization_barrier((dval, dbc))
    dbc_far = swap(dbc, "ctx", 2)

    hidden_out, gain_sum = pl.pallas_call(
        hidden_back_kernel,
        grid_spec=pltpu.PrefetchScalarGridSpec(
            num_scalar_prefetch=1,
            grid=(chunks,),
            in_specs=[
                rows_at(width),
                rows_at(width),
                rows_at(heads),
                full((model, width)),
                full((model, width)),
                full((heads, model)),
                rows_at(model),
                full((1, model)),
            ],
            out_specs=[[whole] * nctx, full((8, model))],
            scratch_shapes=[pltpu.VMEM((2 * width, model), BF16)],
        ),
        out_shape=[
            [shape_of(span, model, dtype=BF16)] * nctx,
            shape_of(8, model),
        ],
        compiler_params=params("arbitrary"),
        name="hidden_back",
    )(perm, dgate, dval, dstep, wg, w1, dt_mine, hid, gain_pre)
    hidden_out = from_owners(hidden_out)
    map_rows = 32 + 32 * high
    map_cols = lambda size: pl.BlockSpec((size, maps), lambda i: (0, width // maps))
    map_keep, map_send, hidden_own = pl.pallas_call(
        maps_back_kernel,
        grid=(1,),
        in_specs=[
            smem,
            full((length, maps)),
            full((length, maps)),
            map_cols(length),
            map_cols(length),
            map_cols(8),
            full((length + 16, 1)),
            full((length, model)),
            map_cols(model),
            full((1, model)),
            full((8, width)),
            full((8, width)),
            full((8, heads)),
            full((heads, model)),
            full((8, model)),
        ],
        out_specs=[full((map_rows, width)), full((map_rows, width)), full((span, model))],
        out_shape=[
            shape_of(map_rows, width, dtype=BF16),
            shape_of(map_rows, width, dtype=BF16),
            shape_of(span, model),
        ],
        scratch_shapes=[
            pltpu.VMEM((length + 8, maps), F32),
            pltpu.VMEM((model, maps), F32),
            pltpu.VMEM((length, maps), BF16),
            pltpu.VMEM((32, width), F32),
        ],
        compiler_params=params("arbitrary"),
        name="maps_back",
    )(
        bits,
        dbc,
        dbc_far,
        conv_sum,
        conv_in,
        conv_mine,
        seg_col,
        hid,
        w1,
        gain_pre,
        conv_grad,
        col_sums,
        head_grad,
        dt_grad,
        gain_sum,
    )

    block_output = tok + sum(part.astype(F32) for part in blocks_out)

    input_part = lambda parts, own: pl.pallas_call(
        input_back_kernel,
        in_specs=[[vmem] * nctx] + [vmem] * 4,
        out_shape=shape_of(span, model),
        compiler_params=params(),
        name="input_back",
    )(parts, own, tok, gain_pre, cotangent[0])

    late_rows = block_in + 64
    if near:
        early = jnp.sum(early_parts.astype(F32), axis=0).astype(BF16)
        map_came = swap(map_send, "dp", 1)
        map_came, block_output, early = lax.optimization_barrier((map_came, block_output, early))
        late_parts = pl.pallas_call(
            pair_sum_late_kernel,
            out_shape=shape_of(high, late_rows, width, dtype=BF16),
            compiler_params=params(),
            name="pair_sum_late",
        )(late_keep, late_came, map_keep, map_came)
        late_parts = high_all_to_all(late_parts)
        early = gather_ctx(early)
        row_block = lambda ref_rows, cols: pl.BlockSpec((ref_rows, cols), lambda i, *_: (i, 0))
        out_block = row_block(out_weight.shape[0] // nctx, model)
        early_spec = [full((early_rows, width))] * nctx
        early_scratch = pltpu.VMEM((nctx, early_rows, width), BF16)
        out_new = pl.pallas_call(
            adam_out_kernel,
            grid_spec=pltpu.PrefetchScalarGridSpec(
                num_scalar_prefetch=1,
                grid=(nctx,),
                in_specs=[out_block] * 3 + [early_spec],
                out_specs=[out_block] * 3,
                scratch_shapes=[early_scratch],
            ),
            out_shape=[shape_of(*out_weight.shape)] * 3,
            compiler_params=params("arbitrary"),
            name="adam_out",
        )(bits, out_weight, out_first, out_second, early)

        late_parts, out_new = lax.optimization_barrier((late_parts, out_new))
        late = pl.pallas_call(
            sum_late_kernel,
            out_shape=shape_of(late_rows, width, dtype=BF16),
            compiler_params=params(),
            name="sum_late",
        )(late_parts)
        late = fan_ctx(late)
        input_grad = input_part(hidden_out, hidden_own)
        late, input_grad = lax.optimization_barrier((late, input_grad))
        in_block = row_block(32, in_weight.shape[1])
        in_new = pl.pallas_call(
            adam_in_kernel,
            grid_spec=pltpu.PrefetchScalarGridSpec(
                num_scalar_prefetch=1,
                grid=(rows_in // 32,),
                in_specs=[in_block] * 3 + [early_spec, [full((late_rows, width))] * nctx],
                out_specs=[in_block] * 3,
                scratch_shapes=[early_scratch, pltpu.VMEM((nctx, late_rows, width), BF16)],
            ),
            out_shape=[shape_of(*in_weight.shape)] * 3,
            compiler_params=params("arbitrary"),
            name="adam_in",
        )(bits, in_weight, in_first, in_second, early, late)
        in_new, out_new = tuple(in_new), tuple(out_new)
        small = jnp.stack([part[block_in : block_in + 32] for part in late])[c ^ jnp.arange(nctx)]
        small = small.astype(F32)
    else:
        input_grad = input_part(hidden_out, hidden_own)
        blocks = lambda keep, send: jnp.stack([keep, send], axis=1).reshape((heads,) + keep.shape[1:])
        early = blocks(early_keep, early_send).astype(F32)
        late = blocks(late_keep, late_send).astype(F32)
        part = lambda value: value[32:].reshape(high, 32, width)[:, :, :maps]
        map_blocks = blocks(part(map_keep), part(map_send)).astype(F32)

        def total(value):
            return lax.psum_scatter(value, "dp", scatter_dimension=0, tiled=True)

        def spaced(value):
            place_at = (jnp.arange(nctx) == c).astype(F32).reshape((1, nctx, 1, 1))
            value = value[:, None] * place_at
            return lax.psum(total(value.reshape(-1, value.shape[-1])), "ctx")

        def by_head(value):
            value = lax.all_gather(total(value.reshape(model, width)), "ctx", axis=0)
            value = value.reshape(nctx, rows_in, heads, HEAD_DIM)
            return jnp.transpose(value, (1, 2, 0, 3)).reshape(rows_in, INNER)

        in_total = jnp.concatenate(
            [by_head(early[:, :block_in]), by_head(late), spaced(map_blocks)], axis=1
        )
        out_total = spaced(
            jnp.concatenate([early[:, block_in : block_in + HEAD_DIM], early[:, block_in + HEAD_DIM :]], axis=2)
        )
        in_new = adam_step(in_weight, in_first, in_second, in_total, 0.03, WEIGHT_DECAY)
        out_new = adam_step(out_weight, out_first, out_second, out_total, 0.02, WEIGHT_DECAY)
        small = lax.all_gather(lax.psum(map_keep[:32].astype(F32), "dp"), "ctx", axis=0)

    def in_order(value):
        return jnp.swapaxes(value.reshape(nctx, -1, heads, HEAD_DIM), 0, 1).swapaxes(1, 2).reshape(-1, INNER)

    columns = in_order(small[:, : CONV + 2])
    conv_total = jnp.concatenate([columns[: CONV + 1], small[0, 8 : 8 + CONV + 1, :maps]], axis=1)
    conv_total = lax.dynamic_slice_in_dim(conv_total, d * conv_cols, conv_cols, 1)
    dt_total = small[:, 16:32].reshape(nctx, 2, heads, width)
    dt_total = jnp.transpose(dt_total, (2, 0, 1, 3)).reshape(HEADS, model)
    dt_total = lax.dynamic_slice_in_dim(dt_total, d * dt_cols, dt_cols, 1)
    pre_total = jnp.sum(small[:, 13:15], axis=0).reshape(-1)
    gain_total = jnp.concatenate([pre_total, columns[CONV + 1]])
    gain_total = lax.dynamic_slice_in_dim(gain_total, d * gain_len, gain_len, 0)
    head_row = small[:, 7] + small[:, 15]
    head_total = jnp.stack(
        [
            head_row[:, :heads].T.reshape(-1),
            head_row[:, 128 : 128 + heads].T.reshape(-1),
            jnp.sum(small[:, CONV + 2].reshape(nctx, heads, HEAD_DIM), axis=2).T.reshape(-1),
        ]
    )

    dt_new = adam_step(dt_weight, dt_first, dt_second, dt_total, 0.03, WEIGHT_DECAY)
    conv_new = adam_step(conv_params, conv_first, conv_second, conv_total, 0.3, 0.0)
    gain_new = adam_step(gains, gain_first, gain_second, gain_total, 0.5, 0.0)
    head_new = adam_step(head_params, head_first, head_second, head_total, 2.0, 0.0)
    return (block_output[None], input_grad[None]) + in_new + dt_new + out_new + conv_new + gain_new + head_new


def solution(mesh):
    tokens, rows, cols = P("dp", "ctx", None), P("dp", None), P(None, "dp")
    return jax.shard_map(
        shards,
        mesh=mesh,
        in_specs=(tokens, rows, tokens, rows, cols, rows, cols, P("dp"), P())
        + (rows, rows, cols, cols, rows, rows, cols, cols, P("dp"), P("dp"), P(), P()),
        out_specs=(tokens, tokens)
        + (rows,) * 3
        + (cols,) * 3
        + (rows,) * 3
        + (cols,) * 3
        + (P("dp"),) * 3
        + (P(),) * 3,
        check_vma=False,
    )
```

```python
import functools

import jax
import jax.numpy as jnp
from jax import lax
from jax.experimental import pallas as pl
from jax.experimental.pallas import tpu as pltpu
from jax.sharding import PartitionSpec as P

INNER = 2048
HEADS = 32
HEAD_DIM = 64
STATE = 128
CONV = 4
STEP = 10
SPAN = 128

F32 = jnp.float32
BF16 = jnp.bfloat16
HIGHEST = lax.Precision.HIGHEST
NORM_EPS = 1e-05
BETA_ONE = 0.9
BETA_TWO = 0.95
ADAM_EPS = 1e-08
WEIGHT_DECAY = 0.1
VMEM_LIMIT = 56 * 1024 * 1024


def nn(a, b, precision=None):
    return lax.dot_general(
        a, b, (((1,), (0,)), ((), ())), precision=precision, preferred_element_type=F32
    )


def nt(a, b, precision=None):
    return lax.dot_general(
        a, b, (((1,), (1,)), ((), ())), precision=precision, preferred_element_type=F32
    )


def tn(a, b, precision=None):
    return lax.dot_general(
        a, b, (((0,), (0,)), ((), ())), precision=precision, preferred_element_type=F32
    )


def halves(value):
    high = value.astype(BF16)
    return high, (value - high.astype(F32)).astype(BF16)


def spread(value, width):
    heads = value.shape[1]
    row = lax.broadcasted_iota(jnp.int32, (heads, width), 0)
    col = lax.broadcasted_iota(jnp.int32, (heads, width), 1)
    table = jnp.where(col // HEAD_DIM == row, 1.0, 0.0).astype(BF16)
    high, low = halves(value)
    return nn(high, table) + nn(low, table)


def gather_heads(value, heads):
    width = value.shape[1]
    row = lax.broadcasted_iota(jnp.int32, (width, heads), 0)
    col = lax.broadcasted_iota(jnp.int32, (width, heads), 1)
    table = jnp.where(row // HEAD_DIM == col, 1.0, 0.0).astype(BF16)
    high, low = halves(value)
    return nn(high, table) + nn(low, table)


def softplus(value):
    return jnp.maximum(value, 0.0) + jnp.log1p(jnp.exp(-jnp.abs(value)))


def sigmoid(value):
    return 1.0 / (1.0 + jnp.exp(-value))


def silu_grad(value):
    sig = sigmoid(value)
    return sig * (1.0 + value * (1.0 - sig))


def diagonal(size):
    row = lax.broadcasted_iota(jnp.int32, (size, size), 0)
    return row == lax.broadcasted_iota(jnp.int32, (size, size), 1)


def triangle(size, lower):
    row = lax.broadcasted_iota(jnp.int32, (size, size), 0)
    col = lax.broadcasted_iota(jnp.int32, (size, size), 1)
    keep = (row >= col if lower else row <= col) & (row // SPAN == col // SPAN)
    return jnp.where(keep, 1.0, 0.0).astype(F32)


def params(*semantics):
    return pltpu.CompilerParams(
        dimension_semantics=semantics or None, vmem_limit_bytes=VMEM_LIMIT
    )


def place(pieces, at_ref, stride, sems, targets):
    copies = []
    for index, piece in enumerate(pieces):
        for block in range(piece.shape[0]):
            for first, rows, target in targets:
                copies.append(
                    pltpu.make_async_copy(
                        piece.at[block, first : first + rows],
                        target(at_ref[index] + stride * block),
                        sems.at[len(copies)],
                    )
                )
    for copy in copies:
        copy.start()
    return copies


def copies_of(pieces, targets):
    return sum(piece.shape[0] for piece in pieces) * targets


def rows_of(ref, rows):
    return lambda at: ref.at[pl.ds(pl.multiple_of(at * rows, 16), rows)]


def part_of(block, own_bit, keep_ref, send_ref, first=0):
    for at in range(keep_ref.shape[0]):
        low, high = block(2 * at).astype(BF16), block(2 * at + 1).astype(BF16)
        rows = slice(first, first + low.shape[0])
        keep_ref[at, rows] = jnp.where(own_bit == 0, low, high)
        send_ref[at, rows] = jnp.where(own_bit == 0, high, low)


def pick_heads(ref, base, ctx, heads):
    first = pl.multiple_of(base + (ctx >> 1) * 2 * HEAD_DIM, 2 * HEAD_DIM)
    wide = ref[:, pl.ds(first, 2 * HEAD_DIM)]
    low = lax.broadcasted_iota(jnp.int32, wide.shape, 1) < HEAD_DIM
    odd = (ctx & 1) == 1
    out = []
    for pair in range(heads // 2):
        parts = []
        for head in (2 * pair, 2 * pair + 1):
            first = pl.multiple_of(base + head * 4 * HEAD_DIM + (ctx >> 1) * 2 * HEAD_DIM, 2 * HEAD_DIM)
            parts.append(ref[:, pl.ds(first, 2 * HEAD_DIM)])
        even = jnp.where(low, parts[0], pltpu.roll(parts[1], HEAD_DIM, 1))
        other = jnp.where(low, pltpu.roll(parts[0], HEAD_DIM, 1), parts[1])
        out.append(jnp.where(odd, other, even))
    return out


def conv_back(size, width, grad, convsum_ref, convin_ref, conv_ref, ext_ref, seg, out_ref):
    sums = [[jnp.zeros((1, 128), F32)] * (CONV + 1) for _ in range(0, width, 128)]
    for first in range(0, size, 64):
        here = slice(first, first + 64)
        for strip, lane in enumerate(range(0, width, 128)):
            lanes = slice(lane, lane + 128)
            value = grad(here, lanes) * silu_grad(convsum_ref[here, lanes])
            ext_ref[here, lanes] = value
            sums[strip][CONV] = sums[strip][CONV] + jnp.sum(value, axis=0, keepdims=True)
    for first in range(0, size, 64):
        here = slice(first, first + 64)
        ids = seg(first, 64)
        same = [
            jnp.broadcast_to(seg(first + CONV - 1 - tap, 64) == ids, (64, 128)) for tap in range(CONV - 1)
        ]
        for strip, lane in enumerate(range(0, width, 128)):
            lanes = slice(lane, lane + 128)
            conv_in = convin_ref[here, lanes].astype(F32)
            back = jnp.zeros((64, 128), F32)
            for tap in range(CONV):
                at = first + CONV - 1 - tap
                term = ext_ref[at : at + 64, lanes]
                if tap < CONV - 1:
                    term = jnp.where(same[tap], term, 0.0)
                back = back + conv_ref[tap : tap + 1, lanes] * term
                sums[strip][tap] = sums[strip][tap] + jnp.sum(conv_in * term, axis=0, keepdims=True)
            out_ref[here, lanes] = back.astype(BF16)
    row = lax.broadcasted_iota(jnp.int32, (8, 128), 0)
    out = []
    for strip in sums:
        total = jnp.zeros((8, 128), F32)
        for at, value in enumerate(strip):
            total = jnp.where(row == at, value, total)
        out.append(total)
    return jnp.concatenate(out, axis=1)


def pack_kernel(here_ref, win_ref, wout_ref, dt_ref, conv_ref, gain_ref, w1_ref, g2_ref, tmp_ref):
    ctx = here_ref[2]
    rows = win_ref.shape[0]
    heads = HEADS // 4
    width = heads * HEAD_DIM
    copies = range(w1_ref.shape[0])
    for at, part in enumerate(pick_heads(win_ref, INNER, ctx, heads)):
        part = part.astype(BF16)
        for copy in copies:
            w1_ref[copy, 0:rows, at * 128 : (at + 1) * 128] = part
    part = win_ref[:, 2 * INNER :].astype(BF16)
    for copy in copies:
        w1_ref[copy, 0:rows, width:] = part
    tmp_ref[...] = jnp.zeros_like(tmp_ref)
    row = lax.broadcasted_iota(jnp.int32, (heads, HEADS), 0)
    col = lax.broadcasted_iota(jnp.int32, (heads, HEADS), 1)
    table = jnp.where(col == 4 * row + ctx, 1.0, 0.0).astype(BF16)
    tmp_ref[0:heads, 384 : 384 + dt_ref.shape[1]] = nn(table, dt_ref[...].astype(BF16))
    tmp_ref[8 : 8 + CONV + 1, 0 : conv_ref.shape[1]] = conv_ref[...]
    tmp_ref[8 + CONV + 1 : 8 + CONV + 2, 0 : gain_ref.shape[0]] = gain_ref[...].reshape(1, -1)
    for copy in copies:
        w1_ref[copy, rows : rows + 16, :] = tmp_ref[...].astype(BF16)
    copies = range(g2_ref.shape[0])
    for at, part in enumerate(pick_heads(win_ref, 0, ctx, heads)):
        part = part.astype(BF16)
        for copy in copies:
            g2_ref[copy, 0:rows, at * 128 : (at + 1) * 128] = part
    if g2_ref.shape[1] > rows:
        some = wout_ref.shape[0] // 4
        mine = wout_ref[pl.ds(pl.multiple_of(ctx * some, 8), some), :].astype(BF16)
        for copy in copies:
            g2_ref[copy, rows : rows + some] = mine[:, :width]
            g2_ref[copy, rows + some : rows + 2 * some] = mine[:, width:]


def scan_forward_kernel(
    here_ref,
    at_ref,
    tok_pieces,
    w1_pieces,
    hrow_ref,
    hcol_ref,
    segc_ref,
    segr_ref,
    hid_ref,
    conv_ref,
    gpre_ref,
    gmine_ref,
    wdt_ref,
    w1_ref,
    mixed_ref,
    convin_ref,
    convsum_ref,
    inner_ref,
    raw_ref,
    stepc_ref,
    logc_ref,
    stepr_ref,
    logr_ref,
    start_ref,
    ext_ref,
    seg_ref,
    state_ref,
    small_ref,
    tok_ref,
    conv_all,
    gain_all,
    sems,
    tok_sems,
):
    step = pl.program_id(0)
    span, model = hid_ref.shape
    heads = wdt_ref.shape[0]
    width = heads * HEAD_DIM
    shards = small_ref.shape[0]
    rows = model // shards

    @pl.when(step == 0)
    def _():
        copies = place(
            w1_pieces,
            at_ref,
            len(w1_pieces),
            sems,
            [(0, rows, rows_of(w1_ref, rows)), (rows, 16, lambda at: small_ref.at[at])],
        )
        tokens = [
            pltpu.make_async_copy(piece, tok_ref.at[here_ref[2] ^ index], tok_sems.at[index])
            for index, piece in enumerate(tok_pieces)
        ]
        for copy in tokens:
            copy.start()
        ext_ref[0:8] = jnp.zeros((8, ext_ref.shape[1]), F32)
        state_ref[...] = jnp.zeros_like(state_ref)
        conv_all[...] = jnp.zeros_like(conv_all)
        for copy in copies:
            copy.wait()
        conv_cols = conv_all.shape[1] // shards
        gain_len = gain_all.shape[1] // shards
        for shard in range(shards):
            small = small_ref[shard].astype(F32)
            wdt_ref[:, shard * rows : (shard + 1) * rows] = small[0:8, 384 : 384 + rows].astype(BF16)
            conv_all[0 : CONV + 1, shard * conv_cols : (shard + 1) * conv_cols] = small[
                8 : 8 + CONV + 1, :conv_cols
            ]
            gain_all[:, shard * gain_len : (shard + 1) * gain_len] = small[13:14, :gain_len]
        for at, part in enumerate(pick_heads(conv_all, 0, here_ref[2], heads)):
            conv_ref[:, at * 128 : (at + 1) * 128] = part
        conv_ref[:, width:] = conv_all[:, INNER:]
        gpre_ref[...] = gain_all[:, :model]
        for at, part in enumerate(pick_heads(gain_all, model, here_ref[2], heads)):
            gmine_ref[:, at * 128 : (at + 1) * 128] = part
        for copy in tokens:
            copy.wait()

    for first in range(0, span, 32):
        tok = tok_ref[step, first : first + 32]
        scale = lax.rsqrt(jnp.mean(tok * tok, axis=-1, keepdims=True) + NORM_EPS)
        hid_ref[first : first + 32] = (tok * scale * gpre_ref[...]).astype(BF16)
    hid = hid_ref[...]
    proj = nn(hid, w1_ref[...]).astype(BF16)
    convin_ref[...] = proj
    ext_ref[8 : 8 + span] = proj.astype(F32)
    seg_ref[...] = segc_ref[pl.ds(pl.multiple_of(step * span, 8), span + 8), :]
    seg_here = seg_ref[8 : 8 + span]
    for first in range(0, span, 64):
        here = seg_ref[8 + first : 72 + first]
        starts = [8 - (CONV - 1) + tap + first for tap in range(CONV)]
        same = [jnp.broadcast_to(seg_ref[at : at + 64] == here, (64, 128)) for at in starts[:-1]]
        for lane in range(0, convin_ref.shape[1], 128):
            lanes = slice(lane, lane + 128)
            total = conv_ref[CONV : CONV + 1, lanes]
            for tap, at in enumerate(starts):
                term = ext_ref[at : at + 64, lanes]
                if tap < CONV - 1:
                    term = jnp.where(same[tap], term, 0.0)
                total = total + conv_ref[tap : tap + 1, lanes] * term
            convsum_ref[first : first + 64, lanes] = total
            mixed_ref[first : first + 64, lanes] = (total * sigmoid(total)).astype(BF16)
    ext_ref[0:8] = ext_ref[span : span + 8]

    raw_c = nt(hid, wdt_ref[...]) + hrow_ref[1:2]
    raw_r = nt(wdt_ref[...], hid) + hcol_ref[:, 1:2]
    step_c = softplus(raw_c)
    step_r = softplus(raw_r)
    log_c = nn(triangle(span, True), -step_c * jnp.exp(hrow_ref[0:1]), HIGHEST)
    log_r = nn(-step_r * jnp.exp(hcol_ref[:, 0:1]), triangle(span, False), HIGHEST)
    raw_ref[...] = raw_c
    stepc_ref[...] = step_c
    logc_ref[...] = log_c
    stepr_ref[...] = step_r
    logr_ref[...] = log_r

    low = lax.broadcasted_iota(jnp.int32, (SPAN, 2 * HEAD_DIM), 1) < HEAD_DIM
    earlier = lax.broadcasted_iota(jnp.int32, (SPAN, SPAN), 0) >= lax.broadcasted_iota(
        jnp.int32, (SPAN, SPAN), 1
    )
    skip_w = spread(hrow_ref[2:3] + jnp.zeros((8, heads), F32), width)[0:1]
    state = state_ref[...]
    for block in range(span // SPAN):
        here = slice(block * SPAN, (block + 1) * SPAN)
        values = mixed_ref[here, :width]
        write = mixed_ref[here, width : width + STATE]
        read = mixed_ref[here, width + STATE :]
        seg = seg_here[here]
        log = log_c[here]
        log_row = log_r[:, here]
        step_row = step_r[:, here]
        scores = jnp.where((seg == segr_ref[:, here]) & earlier, nt(read, write), 0.0)
        seg_prev = seg_ref[7 + block * SPAN : 8 + block * SPAN]
        seg_last = seg_ref[7 + (block + 1) * SPAN : 8 + (block + 1) * SPAN]
        last = log[SPAN - 1 : SPAN]
        enter = jnp.where(seg == seg_prev, jnp.exp(log), 0.0)
        tail = jnp.where(seg == seg_last, jnp.exp(last - log), 0.0) * step_c[here]
        keep = jnp.where(seg_last == seg_prev, jnp.exp(last), 0.0)
        start_ref[block] = state
        values_f = values.astype(F32)
        enter_w = spread(enter, width)
        inter = nn(read, state.astype(BF16))
        for pair in range(heads // 2):
            lanes = slice(pair * 2 * HEAD_DIM, (pair + 1) * 2 * HEAD_DIM)
            pieces = []
            for head in (2 * pair, 2 * pair + 1):
                gap = jnp.minimum(log[:, head : head + 1] - log_row[head : head + 1], 0.0)
                weights = scores * jnp.exp(gap) * step_row[head : head + 1]
                pieces.append(nn(weights.astype(BF16), values[:, lanes]))
            base = enter_w[:, lanes] * inter[:, lanes] + skip_w[:, lanes] * values_f[:, lanes]
            inner_ref[here, lanes] = base + jnp.where(low, pieces[0], pieces[1])
        moved = (spread(tail, width) * values_f).astype(BF16)
        keep_w = spread(keep + jnp.zeros((8, heads), F32), width)[0:1]
        state = keep_w * state + tn(write, moved)
    state_ref[...] = state


def gate_kernel(
    here_ref,
    at_ref,
    hid_ref,
    g2_pieces,
    cot_pieces,
    inner_ref,
    gain_ref,
    wg_ref,
    wout_ref,
    cot_ref,
    gate_ref,
    ng_ref,
    stat_ref,
    turned_ref,
    sems,
    cot_sems,
):
    step = pl.program_id(0)
    rows = wg_ref.shape[0] // (wout_ref.shape[0] // HEAD_DIM)
    width = wg_ref.shape[1]

    @pl.when(step == 0)
    def _():
        some = rows_of(wout_ref, HEAD_DIM)
        copies = place(
            g2_pieces,
            at_ref,
            len(g2_pieces),
            sems,
            [
                (0, rows, rows_of(wg_ref, rows)),
                (rows, HEAD_DIM, lambda at: some(at).at[:, 0:width]),
                (rows + HEAD_DIM, HEAD_DIM, lambda at: some(at).at[:, width : 2 * width]),
            ],
        )
        cots = [
            pltpu.make_async_copy(piece, cot_ref.at[here_ref[2] ^ index], cot_sems.at[index])
            for index, piece in enumerate(cot_pieces)
        ]
        for copy in cots:
            copy.start()
        for copy in copies + cots:
            copy.wait()
        turned_ref[...] = wout_ref[...].T

    gate_ref[...] = nn(hid_ref[...], wg_ref[...]).astype(BF16)
    ng_ref[...] = nn(cot_ref[step], turned_ref[...])
    span = gate_ref.shape[0]
    squares, crossed = [], []
    for first in range(0, span, 32):
        here = slice(first, first + 32)
        gate = gate_ref[here].astype(F32)
        gated = inner_ref[here] * (gate * sigmoid(gate))
        squares.append(jnp.sum(gated * gated, axis=1, keepdims=True))
        crossed.append(jnp.sum(gated * (ng_ref[here] * gain_ref[...]), axis=1, keepdims=True))
    squares = jnp.concatenate(squares, axis=0)
    crossed = jnp.concatenate(crossed, axis=0)
    same = diagonal(span)
    squares = jnp.sum(jnp.where(same, squares, 0.0), axis=0, keepdims=True)
    crossed = jnp.sum(jnp.where(same, crossed, 0.0), axis=0, keepdims=True)
    at = lax.broadcasted_iota(jnp.int32, stat_ref.shape, 0)
    stat_ref[...] = jnp.where(at == 0, squares, crossed)


def norm_back_kernel(
    perm_ref,
    here_ref,
    hid_ref,
    inner_ref,
    gate_ref,
    ng_ref,
    stat_refs,
    gain_ref,
    mixed_ref,
    wout_ref,
    cot_ref,
    block_refs,
    keep_ref,
    send_ref,
    dy_ref,
    dgate_ref,
    sums_ref,
    outacc_ref,
    inacc_ref,
    normed_ref,
):
    step = pl.program_id(0)
    span, width = inner_ref.shape

    @pl.when(step == 0)
    def _():
        outacc_ref[...] = jnp.zeros_like(outacc_ref)
        inacc_ref[...] = jnp.zeros_like(inacc_ref)
        sums_ref[...] = jnp.zeros_like(sums_ref)

    same = diagonal(span)
    stats = sum(ref[...] for ref in stat_refs)
    squares = jnp.sum(jnp.where(same, stats[0:1], 0.0), axis=1, keepdims=True)
    cross = jnp.sum(jnp.where(same, stats[1:2], 0.0), axis=1, keepdims=True)
    inv = lax.rsqrt(squares * (1.0 / INNER) + NORM_EPS)
    gain_sum = jnp.zeros((1, width), F32)
    skip_sum = jnp.zeros((1, width), F32)
    for first in range(0, span, 32):
        here = slice(first, first + 32)
        gate = gate_ref[here].astype(F32)
        sig = sigmoid(gate)
        silu = gate * sig
        inner = inner_ref[here]
        scale = inv[here]
        unit = inner * silu * scale
        normed_ref[here] = (unit * gain_ref[...]).astype(BF16)
        grad = ng_ref[here]
        dgated = scale * (grad * gain_ref[...] - unit * (cross[here] * scale * (1.0 / INNER)))
        dy = dgated * silu
        dy_ref[here] = dy
        dgate_ref[here] = (dgated * inner * (sig * (1.0 + gate * (1.0 - sig)))).astype(BF16)
        gain_sum = gain_sum + jnp.sum(grad * unit, axis=0, keepdims=True)
        skip_sum = skip_sum + jnp.sum(dy * mixed_ref[here].astype(F32), axis=0, keepdims=True)
    normed = normed_ref[...]
    cot = cot_ref[perm_ref[step]]
    block = nn(normed, wout_ref[...]).astype(BF16)

    for at, block_ref in enumerate(block_refs):

        @pl.when(step == at)
        def _():
            block_ref[...] = block

    outacc_ref[...] += tn(normed, cot)
    inacc_ref[...] += tn(hid_ref[...], dgate_ref[...])
    at = lax.broadcasted_iota(jnp.int32, (8, width), 0)
    sums_ref[...] += jnp.where(at == 0, gain_sum, jnp.where(at == 1, skip_sum, 0.0))

    @pl.when(step == pl.num_programs(0) - 1)
    def _():
        own = here_ref[0]
        rows = inacc_ref.shape[0] // (2 * keep_ref.shape[0])
        part_of(lambda at: inacc_ref[at * rows : (at + 1) * rows], own, keep_ref, send_ref)
        outs = lambda at: outacc_ref[at * HEAD_DIM : (at + 1) * HEAD_DIM]
        part_of(lambda at: outs(at)[:, :width], own, keep_ref, send_ref, rows)
        part_of(lambda at: outs(at)[:, width:], own, keep_ref, send_ref, rows + HEAD_DIM)


def scan_back_kernel(
    perm_ref,
    here_ref,
    hid_ref,
    dy_ref,
    mixed_ref,
    convin_ref,
    convsum_ref,
    raw_ref,
    stepc_ref,
    logc_ref,
    stepr_ref,
    logr_ref,
    start_ref,
    conv_ref,
    hrow_ref,
    segc_ref,
    segr_ref,
    keep_ref,
    send_ref,
    dval_ref,
    dbc_ref,
    dstep_ref,
    convg_ref,
    dtg_ref,
    headg_ref,
    ext_ref,
    seg_ref,
    grad_ref,
    inacc_ref,
    dx_ref,
):
    step = pl.program_id(0)
    chunk = pl.num_programs(0) - 1 - step
    span = hid_ref.shape[0]
    heads = stepc_ref.shape[1]
    width = heads * HEAD_DIM

    @pl.when(step == 0)
    def _():
        ext_ref[span : span + 8] = jnp.zeros((8, width), F32)
        grad_ref[...] = jnp.zeros_like(grad_ref)
        inacc_ref[...] = jnp.zeros_like(inacc_ref)
        convg_ref[...] = jnp.zeros_like(convg_ref)
        dtg_ref[...] = jnp.zeros_like(dtg_ref)
        headg_ref[...] = jnp.zeros_like(headg_ref)

    seg_ref[...] = segc_ref[pl.ds(pl.multiple_of(chunk * span, 8), span + 16), :]
    seg_here = seg_ref[8 : 8 + span]
    low = lax.broadcasted_iota(jnp.int32, (SPAN, 2 * HEAD_DIM), 1) < HEAD_DIM
    earlier = lax.broadcasted_iota(jnp.int32, (SPAN, SPAN), 0) >= lax.broadcasted_iota(
        jnp.int32, (SPAN, SPAN), 1
    )
    head_at = lax.broadcasted_iota(jnp.int32, (heads, SPAN), 0)
    lane_at = lax.broadcasted_iota(jnp.int32, (SPAN, heads), 1)
    at_last = lax.broadcasted_iota(jnp.int32, (SPAN, heads), 0) == SPAN - 1
    skip_w = spread(hrow_ref[2:3] + jnp.zeros((8, heads), F32), width)[0:1]
    step_c = stepc_ref[...]
    step_r = stepr_ref[...]
    later = grad_ref[...]
    count = span // SPAN
    dlogs, dsteps_c, dsteps_r = [None] * count, [None] * count, [None] * count
    for block in reversed(range(count)):
        here = slice(block * SPAN, (block + 1) * SPAN)
        values = mixed_ref[here, :width]
        write = mixed_ref[here, width : width + STATE]
        read = mixed_ref[here, width + STATE :]
        values_f = values.astype(F32)
        seg = seg_here[here]
        seg_prev = seg_ref[7 + block * SPAN : 8 + block * SPAN]
        seg_last = seg_ref[7 + (block + 1) * SPAN : 8 + (block + 1) * SPAN]
        dy = dy_ref[here]
        dy_low = dy.astype(BF16)
        log = logc_ref[here]
        log_row = logr_ref[:, here]
        step_row = step_r[:, here]
        last = log[SPAN - 1 : SPAN]
        enter = jnp.where(seg == seg_prev, jnp.exp(log), 0.0)
        tail_raw = jnp.where(seg == seg_last, jnp.exp(last - log), 0.0)
        tail = tail_raw * step_c[here]
        keep = jnp.where(seg_last == seg_prev, jnp.exp(last), 0.0)
        enter_w = spread(enter, width)
        tail_w = spread(tail, width)
        keep_w = spread(keep + jnp.zeros((8, heads), F32), width)[0:1]
        state = start_ref[block]
        state_low = state.astype(BF16)
        later_low = later.astype(BF16)

        entered_low = (enter_w * dy).astype(BF16)
        inter = enter_w * nn(read, state_low)
        from_later = nn(write, later_low)
        moved_low = (tail_w * values_f).astype(BF16)
        dread = nt(entered_low, state_low)
        dwrite = nt(moved_low, later_low)
        tail_dot = gather_heads(values_f * from_later, heads)
        dlog = gather_heads(dy * inter, heads) - tail_dot * tail
        dsteps_c[block] = tail_dot * tail_raw
        carried = jnp.sum(later * state, axis=0, keepdims=True) + jnp.zeros((8, width), F32)
        carried = gather_heads(carried, heads)[0:1]
        dlog = dlog + jnp.where(
            at_last, jnp.sum(tail_dot * tail, axis=0, keepdims=True) + keep * carried, 0.0
        )
        later = keep_w * later + tn(read, entered_low)
        direct = tail_w * from_later + skip_w * dy

        visible = (seg == segr_ref[:, here]) & earlier
        scores = jnp.where(visible, nt(read, write), 0.0)
        dscores = jnp.zeros((SPAN, SPAN), F32)
        dstep = jnp.zeros((heads, SPAN), F32)
        for pair in range(heads // 2):
            lanes = slice(pair * 2 * HEAD_DIM, (pair + 1) * 2 * HEAD_DIM)
            dy_pair = dy_low[:, lanes]
            pieces = []
            for head in (2 * pair, 2 * pair + 1):
                mine = low if head % 2 == 0 else ~low
                gap = jnp.minimum(log[:, head : head + 1] - log_row[head : head + 1], 0.0)
                decay = jnp.exp(gap)
                outer = nt(jnp.where(mine, dy_pair, jnp.zeros_like(dy_pair)), values[:, lanes])
                fade = decay * step_row[head : head + 1]
                dscores = dscores + outer * fade
                weights = scores * fade
                flow = outer * scores
                dstep = dstep + jnp.where(
                    head_at == head, jnp.sum(flow * decay, axis=0, keepdims=True), 0.0
                )
                dlog = dlog + jnp.where(
                    lane_at == head, jnp.sum(outer * weights, axis=1, keepdims=True), 0.0
                )
                pieces.append(tn(weights.astype(BF16), dy_pair))
            dx_ref[here, lanes] = direct[:, lanes] + jnp.where(low, pieces[0], pieces[1])
        dscores = jnp.where(visible, dscores, 0.0).astype(BF16)
        dbc_ref[here, :STATE] = (dwrite + tn(dscores, read)).astype(BF16)
        dbc_ref[here, STATE:] = (dread + nn(dscores, write)).astype(BF16)
        dlogs[block], dsteps_r[block] = dlog, dstep
    grad_ref[...] = later
    dlog_c = jnp.concatenate(dlogs, axis=0)
    dstep_c = jnp.concatenate(dsteps_c, axis=0)
    dstep_r = jnp.concatenate(dsteps_r, axis=1)

    upper = triangle(span, False)
    eye = jnp.where(diagonal(span), 1.0, 0.0).astype(F32)
    dalpha = nn(upper, dlog_c, HIGHEST) - nt(upper, dstep_r * step_r, HIGHEST)
    dstep = dstep_c + nt(eye, dstep_r, HIGHEST)
    rate = jnp.exp(hrow_ref[0:1])
    draw = (dstep - rate * dalpha) * sigmoid(raw_ref[...])
    draw_low = draw.astype(BF16)
    dstep_ref[...] = draw_low
    hid = hid_ref[...]
    dtg_ref[...] += tn(draw_low, hid)
    rate_sum = jnp.sum(-dalpha * step_c * rate, axis=0, keepdims=True)
    bias_sum = jnp.sum(draw, axis=0, keepdims=True)
    at = lax.broadcasted_iota(jnp.int32, (8, heads), 0)
    headg_ref[...] += jnp.where(at == 0, rate_sum, jnp.where(at == 1, bias_sum, 0.0))

    convg_ref[...] += conv_back(
        span,
        width,
        lambda here, lanes: dx_ref[here, lanes],
        convsum_ref,
        convin_ref,
        conv_ref,
        ext_ref,
        lambda first, count: seg_ref[8 + first : 8 + first + count],
        dval_ref,
    )
    ext_ref[span : span + 8] = ext_ref[0:8]
    inacc_ref[...] += tn(hid, dval_ref[...])

    @pl.when(step == pl.num_programs(0) - 1)
    def _():
        rows = inacc_ref.shape[0] // (2 * keep_ref.shape[0])
        part_of(lambda at: inacc_ref[at * rows : (at + 1) * rows], here_ref[0], keep_ref, send_ref)


def hidden_back_kernel(
    perm_ref,
    dgate_ref,
    dval_ref,
    dstep_ref,
    wg_ref,
    wv_ref,
    wdt_ref,
    hid_ref,
    gain_ref,
    out_refs,
    gsum_ref,
    turned_ref,
):
    width = wg_ref.shape[1]

    @pl.when(pl.program_id(0) == 0)
    def _():
        gsum_ref[...] = jnp.zeros_like(gsum_ref)
        turned_ref[0:width] = wg_ref[...].T
        turned_ref[width:] = wv_ref[...].T

    total = nn(dgate_ref[...], turned_ref[0:width]) + nn(dval_ref[...], turned_ref[width:])
    total = total + nn(dstep_ref[...], wdt_ref[...])
    step = pl.program_id(0)

    for at, out_ref in enumerate(out_refs):

        @pl.when(step == at)
        def _():
            out_ref[...] = total.astype(BF16)

    gain_sum = jnp.zeros(gain_ref.shape, F32)
    for first in range(0, total.shape[0], 32):
        here = slice(first, first + 32)
        gain_sum = gain_sum + jnp.sum(total[here] * hid_ref[here].astype(F32), axis=0, keepdims=True)
    gsum_ref[...] += gain_sum / gain_ref[...] + jnp.zeros(gsum_ref.shape, F32)


def maps_back_kernel(
    here_ref,
    dbc_ref,
    dbcfar_ref,
    convsum_ref,
    convin_ref,
    conv_ref,
    segc_ref,
    hid_ref,
    w1_ref,
    gain_ref,
    convg_ref,
    sums_ref,
    headg_ref,
    dtg_ref,
    gall_ref,
    keep_ref,
    send_ref,
    own_ref,
    ext_ref,
    acc_ref,
    dmap_ref,
    small_ref,
):
    size, width = dmap_ref.shape
    ext_ref[size : size + 8] = jnp.zeros((8, width), F32)
    sums = conv_back(
        size,
        width,
        lambda here, lanes: dbc_ref[here, lanes].astype(F32) + dbcfar_ref[here, lanes].astype(F32),
        convsum_ref,
        convin_ref,
        conv_ref,
        ext_ref,
        lambda first, count: segc_ref[8 + first : 8 + first + count],
        dmap_ref,
    )
    ctx = here_ref[2]
    acc_ref[...] = tn(hid_ref[...], dmap_ref[...])
    span = own_ref.shape[0]
    own = pl.ds(pl.multiple_of(ctx * span, 16), span)
    grad = nt(dmap_ref[own, :], w1_ref[...])
    own_ref[...] = grad
    unit = hid_ref[own, :].astype(F32) / gain_ref[...]
    gain_sum = gall_ref[0:1] + jnp.sum(grad * unit, axis=0, keepdims=True)
    half = small_ref.shape[1]
    heads = headg_ref.shape[1]
    small_ref[...] = jnp.zeros_like(small_ref)
    small_ref[0 : CONV + 1] = convg_ref[0 : CONV + 1]
    small_ref[CONV + 1 : CONV + 3] = sums_ref[0:2]
    small_ref[7:8, 0:heads] = headg_ref[0:1]
    small_ref[7:8, 128 : 128 + heads] = headg_ref[1:2]
    small_ref[8 : 8 + CONV + 1, 0:width] = sums[0 : CONV + 1]
    small_ref[13:14] = gain_sum[:, :half]
    small_ref[14:15] = gain_sum[:, half:]
    small_ref[15:16] = small_ref[7:8] - small_ref[7:8].astype(BF16).astype(F32)
    small_ref[16:24] = dtg_ref[:, :half]
    small_ref[24:32] = dtg_ref[:, half:]
    small = small_ref[...].astype(BF16)
    count = keep_ref.shape[0] // 32 - 1
    block = acc_ref.shape[0] // (2 * count)
    some = block // 4
    keep_ref[0:32] = small
    send_ref[0:32] = small
    for at in range(count):
        start = pl.multiple_of(2 * at * block + ctx * some, 8)
        low = acc_ref[pl.ds(start, some), :].astype(BF16)
        start = pl.multiple_of((2 * at + 1) * block + ctx * some, 8)
        high = acc_ref[pl.ds(start, some), :].astype(BF16)
        keep_ref[32 + 32 * at : 64 + 32 * at, 0:width] = jnp.where(here_ref[0] == 0, low, high)
        send_ref[32 + 32 * at : 64 + 32 * at, 0:width] = jnp.where(here_ref[0] == 0, high, low)


def input_back_kernel(part_refs, own_ref, tok_ref, gain_ref, cot_ref, out_ref):
    for first in range(0, out_ref.shape[0], 32):
        here = slice(first, first + 32)
        grad = own_ref[here]
        for ref in part_refs:
            grad = grad + ref[here].astype(F32)
        tok = tok_ref[here]
        scale = lax.rsqrt(jnp.mean(tok * tok, axis=-1, keepdims=True) + NORM_EPS)
        unit = tok * scale
        scaled = grad * gain_ref[...]
        mean = jnp.mean(scaled * unit, axis=-1, keepdims=True)
        out_ref[here] = cot_ref[here] + scale * (scaled - unit * mean)


def with_rest(value, first):
    row = lax.broadcasted_iota(jnp.int32, value.shape, 0)
    head = value[first + 7 : first + 8] + value[first + 15 : first + 16]
    rest = head - head.astype(BF16).astype(F32)
    return jnp.where(row == first + 7, head, jnp.where(row == first + 15, rest, value))


def pair_sum_late_kernel(keep_ref, came_ref, mkeep_ref, mcame_ref, out_ref):
    count, rows, width = keep_ref.shape
    small = with_rest(mkeep_ref[0:32].astype(F32) + mcame_ref[0:32].astype(F32), 0).astype(BF16)
    for block in range(count):
        out_ref[block, 0:rows] = (keep_ref[block].astype(F32) + came_ref[block].astype(F32)).astype(BF16)
        out_ref[block, rows : rows + 32] = small
        at = slice(32 + 32 * block, 64 + 32 * block)
        out_ref[block, rows + 32 : rows + 64] = (
            mkeep_ref[at].astype(F32) + mcame_ref[at].astype(F32)
        ).astype(BF16)


def sum_late_kernel(parts_ref, out_ref):
    total = parts_ref[0].astype(F32)
    for at in range(1, parts_ref.shape[0]):
        total = total + parts_ref[at].astype(F32)
    out_ref[...] = with_rest(total, out_ref.shape[0] - 64).astype(BF16)


def adam_out_kernel(here_ref, weight_ref, first_ref, second_ref, early_refs, *rest):
    new_refs, early_ref = rest[:3], rest[3]
    step = pl.program_id(0)

    @pl.when(step == 0)
    def _():
        by_owner(early_refs, here_ref[2], early_ref)

    rows = weight_ref.shape[0]
    width = early_ref.shape[2]
    first = early_ref.shape[1] - 2 * rows
    for at in range(2):
        lanes = slice(at * width, (at + 1) * width)
        grad = early_ref[step, first + at * rows : first + (at + 1) * rows].astype(F32)
        news = adam_step(
            weight_ref[:, lanes], first_ref[:, lanes], second_ref[:, lanes], grad, 0.02, WEIGHT_DECAY
        )
        for ref, new in zip(new_refs, news):
            ref[:, lanes] = new


def by_owner(refs, ctx, natural_ref):
    for at, ref in enumerate(refs):
        natural_ref[pl.ds(ctx ^ at, 1)] = ref[...][None]


def adam_in_kernel(here_ref, weight_ref, first_ref, second_ref, early_refs, late_refs, *rest):
    new_refs, (early_ref, late_ref) = rest[:3], rest[3:]
    step = pl.program_id(0)
    pieces = len(early_refs)
    rows = weight_ref.shape[0]
    width = early_ref.shape[2]
    block = pieces * HEAD_DIM

    @pl.when(step == 0)
    def _():
        by_owner(early_refs, here_ref[2], early_ref)
        by_owner(late_refs, here_ref[2], late_ref)

    here = pl.ds(pl.multiple_of(step * rows, rows), rows)
    low = lax.broadcasted_iota(jnp.int32, (rows, 2 * HEAD_DIM), 1) < HEAD_DIM

    def update(lanes, grad):
        news = adam_step(
            weight_ref[:, lanes], first_ref[:, lanes], second_ref[:, lanes], grad, 0.03, WEIGHT_DECAY
        )
        for ref, new in zip(new_refs, news):
            ref[:, lanes] = new

    for base, ref in ((0, early_ref), (INNER, late_ref)):
        for pair in range(width // (2 * HEAD_DIM)):
            lanes = slice(pair * 2 * HEAD_DIM, (pair + 1) * 2 * HEAD_DIM)
            for at in range(0, pieces, 2):
                first = ref[at, here, lanes].astype(F32)
                second = ref[at + 1, here, lanes].astype(F32)
                start = base + 2 * pair * block + at * HEAD_DIM
                even = jnp.where(low, first, pltpu.roll(second, HEAD_DIM, 1))
                update(slice(start, start + 2 * HEAD_DIM), even)
                start = start + block
                odd = jnp.where(low, pltpu.roll(first, HEAD_DIM, 1), second)
                update(slice(start, start + 2 * HEAD_DIM), odd)
    some = 32 // rows
    first = pl.multiple_of(late_ref.shape[1] - 32 + (step % some) * rows, rows)
    grad = late_ref[step // some, pl.ds(first, rows), 0 : 2 * STATE].astype(F32)
    update(slice(2 * INNER, 2 * INNER + 2 * STATE), grad)


def swap(value, axis, bit):
    count = lax.axis_size(axis)
    return lax.ppermute(value, axis, [(at, at ^ bit) for at in range(count)])


def gather_ctx(value):
    far = swap(value, "ctx", 2)
    return [value, swap(value, "ctx", 1), far, swap(far, "ctx", 1)]


def high_all_to_all(value):
    count = lax.axis_size("dp")
    groups = [list(range(low, count, 2)) for low in range(2)]
    return lax.all_to_all(value, "dp", 0, 0, axis_index_groups=groups)


def from_owners(parts):
    count = len(parts)
    return [swap(parts[bit - 1], "ctx", bit) for bit in range(1, count)] + [parts[-1]]


def fan_ctx(value):
    return [value] + [swap(value, "ctx", bit) for bit in range(1, lax.axis_size("ctx"))]


def adam_step(weight, moment_one, second, gradient, step_rate, decay_rate):
    moment_new = BETA_ONE * moment_one + (1.0 - BETA_ONE) * gradient
    second_new = BETA_TWO * second + (1.0 - BETA_TWO) * gradient * gradient
    first_hat = moment_new / (1.0 - BETA_ONE**STEP)
    second_hat = second_new / (1.0 - BETA_TWO**STEP)
    weight_new = weight - step_rate * (
        first_hat / (jnp.sqrt(second_hat) + ADAM_EPS) + decay_rate * weight
    )
    return (weight_new, moment_new, second_new)


def full(shape):
    return pl.BlockSpec(shape, lambda *_: (0,) * len(shape))


def shape_of(*shape, dtype=F32):
    return jax.ShapeDtypeStruct(shape, dtype)


def shards(
    tokens,
    segment_ids,
    cotangent,
    in_weight,
    dt_weight,
    out_weight,
    conv_params,
    gains,
    head_params,
    in_first,
    in_second,
    dt_first,
    dt_second,
    out_first,
    out_second,
    conv_first,
    conv_second,
    gain_first,
    gain_second,
    head_first,
    head_second,
):
    _, span, model = tokens.shape
    length = segment_ids.shape[1]
    ndp, nctx = lax.axis_size("dp"), lax.axis_size("ctx")
    d, c = lax.axis_index("dp"), lax.axis_index("ctx")
    heads = HEADS // nctx
    width = INNER // nctx
    maps = 2 * STATE
    wide = width + maps
    chunks = nctx
    rows_in = in_weight.shape[0]
    conv_cols = conv_params.shape[1]
    gain_len = gains.shape[0]
    dt_cols = dt_weight.shape[1]
    near = ndp == heads
    high = heads // 2
    block_in = model // heads
    tok = tokens[0]
    bits = jnp.stack([d & 1, d >> 1, c] if near else [0 * d, 0 * d, c]).astype(jnp.int32)
    perm = c ^ jnp.asarray([1, 2, 3, 0], jnp.int32)
    smem = pl.BlockSpec(memory_space=pltpu.SMEM)
    vmem = pl.BlockSpec(memory_space=pltpu.VMEM)
    anywhere = lambda pieces: [pl.BlockSpec(memory_space=pl.ANY)] * len(pieces)

    w1, g2 = pl.pallas_call(
        pack_kernel,
        in_specs=[smem] + [vmem] * 5,
        out_shape=[
            shape_of(high if near else 1, rows_in + 16, wide, dtype=BF16),
            shape_of(high if near else 1, rows_in + (2 * HEAD_DIM if near else 0), width, dtype=BF16),
        ],
        scratch_shapes=[pltpu.VMEM((16, wide), F32)],
        compiler_params=params(),
        name="pack",
    )(bits, in_weight, out_weight, dt_weight, conv_params, gains)
    ids = segment_ids[0]
    seg_col = jnp.pad(ids, (8, 8), constant_values=-1)[:, None]
    seg_row = segment_ids
    head_mine = lax.dynamic_index_in_dim(head_params.reshape(3, heads, nctx), c, 2, False)
    head_col = head_mine.T
    cot_low = cotangent[0].astype(BF16)
    if near:
        tok_far = swap(tok, "ctx", 2)
        tok_core = swap(tok, "ctx", 1)
        w1 = high_all_to_all(w1)
        at_rows = jnp.stack([d & 1, 1 - (d & 1)]).astype(jnp.int32)
        w1, g2, cot_low, seg_col, head_mine, head_col, at_rows, perm = lax.optimization_barrier(
            (w1, g2, cot_low, seg_col, head_mine, head_col, at_rows, perm)
        )
        at_g2 = at_rows
        w1_came = swap(w1, "dp", 1)
        g2 = high_all_to_all(g2)
        w1, w1_came, tok_far = lax.optimization_barrier((w1, w1_came, tok_far))
        toks = [tok, tok_core, tok_far, swap(tok_far, "ctx", 1)]
        w1, w1_came, toks, g2, cot_low = lax.optimization_barrier((w1, w1_came, toks, g2, cot_low))
        w1 = [w1, w1_came]
        g2 = [g2, swap(g2, "dp", 1)]
        cots = fan_ctx(cot_low)
    else:
        w1 = [lax.all_gather(w1[0], "dp", axis=0)]
        toks = gather_ctx(tok)
        cots = gather_ctx(cot_low)
        wg = lax.all_gather(g2[0], "dp", axis=0, tiled=True).reshape(heads, block_in, width)
        wout = lax.all_gather(out_weight.astype(BF16), "dp", axis=0, tiled=True)
        wout = lax.dynamic_index_in_dim(wout.reshape(heads, nctx, HEAD_DIM, model), c, 1, False)
        g2 = [jnp.concatenate([wg, wout[:, :, :width], wout[:, :, width:]], axis=1)]
        at_rows = at_g2 = jnp.zeros((1,), jnp.int32)

    rows = lambda cols: pl.BlockSpec((span, cols), lambda i, *_: (i, 0))
    row_of = pl.BlockSpec((heads, span), lambda i, *_: (0, i))
    rows_at = lambda cols: pl.BlockSpec((span, cols), lambda i, p, *_: (p[i], 0))
    whole = full((span, model))
    shards_in = sum(piece.shape[0] for piece in w1)

    (
        hid, conv_mine, gain_pre, gain_mine, dt_mine, w1, mixed, conv_in, conv_sum, inner, raw,
        step_c, log_c, step_r, log_r, starts,
    ) = pl.pallas_call(
        scan_forward_kernel,
        grid_spec=pltpu.PrefetchScalarGridSpec(
            num_scalar_prefetch=2,
            grid=(chunks,),
            in_specs=[
                anywhere(toks),
                anywhere(w1),
                full((3, heads)),
                full((heads, 3)),
                full((length + 16, 1)),
                pl.BlockSpec((1, span), lambda i, *_: (0, i)),
            ],
            out_specs=[
                rows(model),
                full((8, wide)),
                full((1, model)),
                full((1, width)),
                full((heads, model)),
                full((model, wide)),
                rows(wide),
                rows(wide),
                rows(wide),
                rows(width),
                rows(heads),
                rows(heads),
                rows(heads),
                row_of,
                row_of,
                pl.BlockSpec((span // SPAN, STATE, width), lambda i, *_: (i, 0, 0)),
            ],
            scratch_shapes=[
                pltpu.VMEM((span + 8, wide), F32),
                pltpu.VMEM((span + 8, 1), jnp.int32),
                pltpu.VMEM((STATE, width), F32),
                pltpu.VMEM((shards_in, 16, wide), BF16),
                pltpu.VMEM((nctx, span, model), F32),
                pltpu.VMEM((8, INNER + maps), F32),
                pltpu.VMEM((1, model + INNER), F32),
                pltpu.SemaphoreType.DMA((copies_of(w1, 2),)),
                pltpu.SemaphoreType.DMA((nctx,)),
            ],
        ),
        out_shape=[
            shape_of(length, model, dtype=BF16),
            shape_of(8, wide),
            shape_of(1, model),
            shape_of(1, width),
            shape_of(heads, model, dtype=BF16),
            shape_of(model, wide, dtype=BF16),
            shape_of(length, wide, dtype=BF16),
            shape_of(length, wide, dtype=BF16),
            shape_of(length, wide),
            shape_of(length, width),
            shape_of(length, heads),
            shape_of(length, heads),
            shape_of(length, heads),
            shape_of(heads, length),
            shape_of(heads, length),
            shape_of(length // SPAN, STATE, width),
        ],
        compiler_params=params("arbitrary"),
        name="scan_forward",
    )(bits, at_rows, toks, w1, head_mine, head_col, seg_col, seg_row)

    wg, wout, cot_all, gate, normed_grad, stats = pl.pallas_call(
        gate_kernel,
        grid_spec=pltpu.PrefetchScalarGridSpec(
            num_scalar_prefetch=2,
            grid=(chunks,),
            in_specs=[rows(model), anywhere(g2), anywhere(cots), rows(width), full((1, width))],
            out_specs=[
                full((model, width)),
                full((width, model)),
                full((nctx, span, model)),
                rows(width),
                rows(width),
                pl.BlockSpec((8, span), lambda i, *_: (0, i)),
            ],
            scratch_shapes=[
                pltpu.VMEM((model, width), BF16),
                pltpu.SemaphoreType.DMA((copies_of(g2, 3),)),
                pltpu.SemaphoreType.DMA((nctx,)),
            ],
        ),
        out_shape=[
            shape_of(model, width, dtype=BF16),
            shape_of(width, model, dtype=BF16),
            shape_of(nctx, span, model, dtype=BF16),
            shape_of(length, width, dtype=BF16),
            shape_of(length, width),
            shape_of(8, length),
        ],
        compiler_params=params("arbitrary"),
        name="gate",
    )(bits, at_g2, hid, g2, cots, inner, gain_mine)
    stats = fan_ctx(stats)

    early_rows = block_in + 2 * HEAD_DIM
    blocks_out, early_keep, early_send, dy, dgate, col_sums = pl.pallas_call(
        norm_back_kernel,
        grid_spec=pltpu.PrefetchScalarGridSpec(
            num_scalar_prefetch=2,
            grid=(chunks,),
            in_specs=[
                rows_at(model),
                rows_at(width),
                rows_at(width),
                rows_at(width),
                [pl.BlockSpec((8, span), lambda i, p, *_: (0, p[i]))] * nctx,
                full((1, width)),
                rows_at(width),
                full((width, model)),
                full((nctx, span, model)),
            ],
            out_specs=[
                [whole] * nctx,
                full((high, early_rows, width)),
                full((high, early_rows, width)),
                rows_at(width),
                rows_at(width),
                full((8, width)),
            ],
            scratch_shapes=[
                pltpu.VMEM((width, model), F32),
                pltpu.VMEM((model, width), F32),
                pltpu.VMEM((span, width), BF16),
            ],
        ),
        out_shape=[
            [shape_of(span, model, dtype=BF16)] * nctx,
            shape_of(high, early_rows, width, dtype=BF16),
            shape_of(high, early_rows, width, dtype=BF16),
            shape_of(length, width),
            shape_of(length, width, dtype=BF16),
            shape_of(8, width),
        ],
        compiler_params=params("arbitrary"),
        name="norm_back",
    )(perm, bits, hid, inner, gate, normed_grad, stats, gain_mine, mixed, wout, cot_all)
    blocks_out = from_owners(blocks_out)
    if near:
        early_came = swap(early_send, "dp", 1)

    back = lambda cols: pl.BlockSpec((span, cols), lambda i, *_: (chunks - 1 - i, 0))
    back_row = pl.BlockSpec((heads, span), lambda i, *_: (0, chunks - 1 - i))
    late_keep, late_send, dval, dbc, dstep, conv_grad, dt_grad, head_grad = pl.pallas_call(
        scan_back_kernel,
        grid_spec=pltpu.PrefetchScalarGridSpec(
            num_scalar_prefetch=2,
            grid=(chunks,),
            in_specs=[
                back(model),
                back(width),
                back(wide),
                back(width),
                back(width),
                back(heads),
                back(heads),
                back(heads),
                back_row,
                back_row,
                pl.BlockSpec((span // SPAN, STATE, width), lambda i, *_: (chunks - 1 - i, 0, 0)),
                full((8, width)),
                full((3, heads)),
                full((length + 16, 1)),
                pl.BlockSpec((1, span), lambda i, *_: (0, chunks - 1 - i)),
            ],
            out_specs=[
                full((high, block_in, width)),
                full((high, block_in, width)),
                back(width),
                back(maps),
                back(heads),
                full((8, width)),
                full((heads, model)),
                full((8, heads)),
            ],
            scratch_shapes=[
                pltpu.VMEM((span + 8, width), F32),
                pltpu.VMEM((span + 16, 1), jnp.int32),
                pltpu.VMEM((STATE, width), F32),
                pltpu.VMEM((model, width), F32),
                pltpu.VMEM((span, width), F32),
            ],
        ),
        out_shape=[
            shape_of(high, block_in, width, dtype=BF16),
            shape_of(high, block_in, width, dtype=BF16),
            shape_of(length, width, dtype=BF16),
            shape_of(length, maps, dtype=BF16),
            shape_of(length, heads, dtype=BF16),
            shape_of(8, width),
            shape_of(heads, model),
            shape_of(8, heads),
        ],
        compiler_params=params("arbitrary"),
        name="scan_back",
    )(
        perm, bits, hid, dy, mixed, conv_in, conv_sum, raw, step_c, log_c, step_r, log_r, starts,
        conv_mine, head_mine, seg_col, seg_row,
    )
    dbc_came = swap(dbc, "ctx", 1)
    if near:
        late_came = swap(late_send, "dp", 1)
        early_came, blocks_out, dval = lax.optimization_barrier((early_came, blocks_out, dval))
        early_parts = (early_keep.astype(F32) + early_came.astype(F32)).astype(BF16)
        early_parts = high_all_to_all(early_parts)
    dbc = (dbc.astype(F32) + dbc_came.astype(F32)).astype(BF16)
    dval, dbc = lax.optimization_barrier((dval, dbc))
    dbc_far = swap(dbc, "ctx", 2)

    hidden_out, gain_sum = pl.pallas_call(
        hidden_back_kernel,
        grid_spec=pltpu.PrefetchScalarGridSpec(
            num_scalar_prefetch=1,
            grid=(chunks,),
            in_specs=[
                rows_at(width),
                rows_at(width),
                rows_at(heads),
                full((model, width)),
                full((model, width)),
                full((heads, model)),
                rows_at(model),
                full((1, model)),
            ],
            out_specs=[[whole] * nctx, full((8, model))],
            scratch_shapes=[pltpu.VMEM((2 * width, model), BF16)],
        ),
        out_shape=[
            [shape_of(span, model, dtype=BF16)] * nctx,
            shape_of(8, model),
        ],
        compiler_params=params("arbitrary"),
        name="hidden_back",
    )(perm, dgate, dval, dstep, wg, w1, dt_mine, hid, gain_pre)
    hidden_out = from_owners(hidden_out)
    map_rows = 32 + 32 * high
    map_cols = lambda size: pl.BlockSpec((size, maps), lambda i: (0, width // maps))
    map_keep, map_send, hidden_own = pl.pallas_call(
        maps_back_kernel,
        grid=(1,),
        in_specs=[
            smem,
            full((length, maps)),
            full((length, maps)),
            map_cols(length),
            map_cols(length),
            map_cols(8),
            full((length + 16, 1)),
            full((length, model)),
            map_cols(model),
            full((1, model)),
            full((8, width)),
            full((8, width)),
            full((8, heads)),
            full((heads, model)),
            full((8, model)),
        ],
        out_specs=[full((map_rows, width)), full((map_rows, width)), full((span, model))],
        out_shape=[
            shape_of(map_rows, width, dtype=BF16),
            shape_of(map_rows, width, dtype=BF16),
            shape_of(span, model),
        ],
        scratch_shapes=[
            pltpu.VMEM((length + 8, maps), F32),
            pltpu.VMEM((model, maps), F32),
            pltpu.VMEM((length, maps), BF16),
            pltpu.VMEM((32, width), F32),
        ],
        compiler_params=params("arbitrary"),
        name="maps_back",
    )(
        bits,
        dbc,
        dbc_far,
        conv_sum,
        conv_in,
        conv_mine,
        seg_col,
        hid,
        w1,
        gain_pre,
        conv_grad,
        col_sums,
        head_grad,
        dt_grad,
        gain_sum,
    )

    block_output = tok + sum(part.astype(F32) for part in blocks_out)

    input_part = lambda parts, own: pl.pallas_call(
        input_back_kernel,
        in_specs=[[vmem] * nctx] + [vmem] * 4,
        out_shape=shape_of(span, model),
        compiler_params=params(),
        name="input_back",
    )(parts, own, tok, gain_pre, cotangent[0])

    late_rows = block_in + 64
    if near:
        early = jnp.sum(early_parts.astype(F32), axis=0).astype(BF16)
        map_came = swap(map_send, "dp", 1)
        map_came, block_output, early, hidden_out = lax.optimization_barrier(
            (map_came, block_output, early, hidden_out)
        )
        late_parts = pl.pallas_call(
            pair_sum_late_kernel,
            out_shape=shape_of(high, late_rows, width, dtype=BF16),
            compiler_params=params(),
            name="pair_sum_late",
        )(late_keep, late_came, map_keep, map_came)
        late_parts = high_all_to_all(late_parts)
        early = gather_ctx(early)
        input_grad = input_part(hidden_out, hidden_own)
        row_block = lambda ref_rows, cols: pl.BlockSpec((ref_rows, cols), lambda i, *_: (i, 0))
        out_block = row_block(out_weight.shape[0] // nctx, model)
        early_spec = [full((early_rows, width))] * nctx
        early_scratch = pltpu.VMEM((nctx, early_rows, width), BF16)
        out_new = pl.pallas_call(
            adam_out_kernel,
            grid_spec=pltpu.PrefetchScalarGridSpec(
                num_scalar_prefetch=1,
                grid=(nctx,),
                in_specs=[out_block] * 3 + [early_spec],
                out_specs=[out_block] * 3,
                scratch_shapes=[early_scratch],
            ),
            out_shape=[shape_of(*out_weight.shape)] * 3,
            compiler_params=params("arbitrary"),
            name="adam_out",
        )(bits, out_weight, out_first, out_second, early)

        late_parts, input_grad, out_new = lax.optimization_barrier((late_parts, input_grad, out_new))
        late = pl.pallas_call(
            sum_late_kernel,
            out_shape=shape_of(late_rows, width, dtype=BF16),
            compiler_params=params(),
            name="sum_late",
        )(late_parts)
        late = fan_ctx(late)
        in_block = row_block(32, in_weight.shape[1])
        in_new = pl.pallas_call(
            adam_in_kernel,
            grid_spec=pltpu.PrefetchScalarGridSpec(
                num_scalar_prefetch=1,
                grid=(rows_in // 32,),
                in_specs=[in_block] * 3 + [early_spec, [full((late_rows, width))] * nctx],
                out_specs=[in_block] * 3,
                scratch_shapes=[early_scratch, pltpu.VMEM((nctx, late_rows, width), BF16)],
            ),
            out_shape=[shape_of(*in_weight.shape)] * 3,
            compiler_params=params("arbitrary"),
            name="adam_in",
        )(bits, in_weight, in_first, in_second, early, late)
        in_new, out_new = tuple(in_new), tuple(out_new)
        small = jnp.stack([part[block_in : block_in + 32] for part in late])[c ^ jnp.arange(nctx)]
        small = small.astype(F32)
    else:
        input_grad = input_part(hidden_out, hidden_own)
        blocks = lambda keep, send: jnp.stack([keep, send], axis=1).reshape((heads,) + keep.shape[1:])
        early = blocks(early_keep, early_send).astype(F32)
        late = blocks(late_keep, late_send).astype(F32)
        part = lambda value: value[32:].reshape(high, 32, width)[:, :, :maps]
        map_blocks = blocks(part(map_keep), part(map_send)).astype(F32)

        def total(value):
            return lax.psum_scatter(value, "dp", scatter_dimension=0, tiled=True)

        def spaced(value):
            place_at = (jnp.arange(nctx) == c).astype(F32).reshape((1, nctx, 1, 1))
            value = value[:, None] * place_at
            return lax.psum(total(value.reshape(-1, value.shape[-1])), "ctx")

        def by_head(value):
            value = lax.all_gather(total(value.reshape(model, width)), "ctx", axis=0)
            value = value.reshape(nctx, rows_in, heads, HEAD_DIM)
            return jnp.transpose(value, (1, 2, 0, 3)).reshape(rows_in, INNER)

        in_total = jnp.concatenate(
            [by_head(early[:, :block_in]), by_head(late), spaced(map_blocks)], axis=1
        )
        out_total = spaced(
            jnp.concatenate([early[:, block_in : block_in + HEAD_DIM], early[:, block_in + HEAD_DIM :]], axis=2)
        )
        in_new = adam_step(in_weight, in_first, in_second, in_total, 0.03, WEIGHT_DECAY)
        out_new = adam_step(out_weight, out_first, out_second, out_total, 0.02, WEIGHT_DECAY)
        small = lax.all_gather(lax.psum(map_keep[:32].astype(F32), "dp"), "ctx", axis=0)

    def in_order(value):
        return jnp.swapaxes(value.reshape(nctx, -1, heads, HEAD_DIM), 0, 1).swapaxes(1, 2).reshape(-1, INNER)

    columns = in_order(small[:, : CONV + 2])
    conv_total = jnp.concatenate([columns[: CONV + 1], small[0, 8 : 8 + CONV + 1, :maps]], axis=1)
    conv_total = lax.dynamic_slice_in_dim(conv_total, d * conv_cols, conv_cols, 1)
    dt_total = small[:, 16:32].reshape(nctx, 2, heads, width)
    dt_total = jnp.transpose(dt_total, (2, 0, 1, 3)).reshape(HEADS, model)
    dt_total = lax.dynamic_slice_in_dim(dt_total, d * dt_cols, dt_cols, 1)
    pre_total = jnp.sum(small[:, 13:15], axis=0).reshape(-1)
    gain_total = jnp.concatenate([pre_total, columns[CONV + 1]])
    gain_total = lax.dynamic_slice_in_dim(gain_total, d * gain_len, gain_len, 0)
    head_row = small[:, 7] + small[:, 15]
    head_total = jnp.stack(
        [
            head_row[:, :heads].T.reshape(-1),
            head_row[:, 128 : 128 + heads].T.reshape(-1),
            jnp.sum(small[:, CONV + 2].reshape(nctx, heads, HEAD_DIM), axis=2).T.reshape(-1),
        ]
    )

    dt_new = adam_step(dt_weight, dt_first, dt_second, dt_total, 0.03, WEIGHT_DECAY)
    conv_new = adam_step(conv_params, conv_first, conv_second, conv_total, 0.3, 0.0)
    gain_new = adam_step(gains, gain_first, gain_second, gain_total, 0.5, 0.0)
    head_new = adam_step(head_params, head_first, head_second, head_total, 2.0, 0.0)
    return (block_output[None], input_grad[None]) + in_new + dt_new + out_new + conv_new + gain_new + head_new


def solution(mesh):
    tokens, rows, cols = P("dp", "ctx", None), P("dp", None), P(None, "dp")
    return jax.shard_map(
        shards,
        mesh=mesh,
        in_specs=(tokens, rows, tokens, rows, cols, rows, cols, P("dp"), P())
        + (rows, rows, cols, cols, rows, rows, cols, cols, P("dp"), P("dp"), P(), P()),
        out_specs=(tokens, tokens)
        + (rows,) * 3
        + (cols,) * 3
        + (rows,) * 3
        + (cols,) * 3
        + (P("dp"),) * 3
        + (P(),) * 3,
        check_vma=False,
    )
```

```python
import functools

import jax
import jax.numpy as jnp
from jax import lax
from jax.experimental import pallas as pl
from jax.experimental.pallas import tpu as pltpu
from jax.sharding import PartitionSpec as P

INNER = 2048
HEADS = 32
HEAD_DIM = 64
STATE = 128
CONV = 4
STEP = 10
SPAN = 128

F32 = jnp.float32
BF16 = jnp.bfloat16
HIGHEST = lax.Precision.HIGHEST
NORM_EPS = 1e-05
BETA_ONE = 0.9
BETA_TWO = 0.95
ADAM_EPS = 1e-08
WEIGHT_DECAY = 0.1
VMEM_LIMIT = 56 * 1024 * 1024


def nn(a, b, precision=None):
    return lax.dot_general(
        a, b, (((1,), (0,)), ((), ())), precision=precision, preferred_element_type=F32
    )


def nt(a, b, precision=None):
    return lax.dot_general(
        a, b, (((1,), (1,)), ((), ())), precision=precision, preferred_element_type=F32
    )


def tn(a, b, precision=None):
    return lax.dot_general(
        a, b, (((0,), (0,)), ((), ())), precision=precision, preferred_element_type=F32
    )


def halves(value):
    high = value.astype(BF16)
    return high, (value - high.astype(F32)).astype(BF16)


def spread(value, width):
    heads = value.shape[1]
    row = lax.broadcasted_iota(jnp.int32, (heads, width), 0)
    col = lax.broadcasted_iota(jnp.int32, (heads, width), 1)
    table = jnp.where(col // HEAD_DIM == row, 1.0, 0.0).astype(BF16)
    high, low = halves(value)
    return nn(high, table) + nn(low, table)


def gather_heads(value, heads):
    width = value.shape[1]
    row = lax.broadcasted_iota(jnp.int32, (width, heads), 0)
    col = lax.broadcasted_iota(jnp.int32, (width, heads), 1)
    table = jnp.where(row // HEAD_DIM == col, 1.0, 0.0).astype(BF16)
    high, low = halves(value)
    return nn(high, table) + nn(low, table)


def softplus(value):
    return jnp.maximum(value, 0.0) + jnp.log1p(jnp.exp(-jnp.abs(value)))


def sigmoid(value):
    return 1.0 / (1.0 + jnp.exp(-value))


def silu_grad(value):
    sig = sigmoid(value)
    return sig * (1.0 + value * (1.0 - sig))


def diagonal(size):
    row = lax.broadcasted_iota(jnp.int32, (size, size), 0)
    return row == lax.broadcasted_iota(jnp.int32, (size, size), 1)


def triangle(size, lower):
    row = lax.broadcasted_iota(jnp.int32, (size, size), 0)
    col = lax.broadcasted_iota(jnp.int32, (size, size), 1)
    keep = (row >= col if lower else row <= col) & (row // SPAN == col // SPAN)
    return jnp.where(keep, 1.0, 0.0).astype(F32)


def params(*semantics):
    return pltpu.CompilerParams(
        dimension_semantics=semantics or None, vmem_limit_bytes=VMEM_LIMIT
    )


def place(pieces, at_ref, stride, sems, targets):
    copies = []
    for index, piece in enumerate(pieces):
        for block in range(piece.shape[0]):
            for first, rows, target in targets:
                copies.append(
                    pltpu.make_async_copy(
                        piece.at[block, first : first + rows],
                        target(at_ref[index] + stride * block),
                        sems.at[len(copies)],
                    )
                )
    for copy in copies:
        copy.start()
    return copies


def copies_of(pieces, targets):
    return sum(piece.shape[0] for piece in pieces) * targets


def rows_of(ref, rows):
    return lambda at: ref.at[pl.ds(pl.multiple_of(at * rows, 16), rows)]


def part_of(block, own_bit, keep_ref, send_ref, first=0):
    for at in range(keep_ref.shape[0]):
        low, high = block(2 * at).astype(BF16), block(2 * at + 1).astype(BF16)
        rows = slice(first, first + low.shape[0])
        keep_ref[at, rows] = jnp.where(own_bit == 0, low, high)
        send_ref[at, rows] = jnp.where(own_bit == 0, high, low)


def pick_heads(ref, base, ctx, heads):
    first = pl.multiple_of(base + (ctx >> 1) * 2 * HEAD_DIM, 2 * HEAD_DIM)
    wide = ref[:, pl.ds(first, 2 * HEAD_DIM)]
    low = lax.broadcasted_iota(jnp.int32, wide.shape, 1) < HEAD_DIM
    odd = (ctx & 1) == 1
    out = []
    for pair in range(heads // 2):
        parts = []
        for head in (2 * pair, 2 * pair + 1):
            first = pl.multiple_of(base + head * 4 * HEAD_DIM + (ctx >> 1) * 2 * HEAD_DIM, 2 * HEAD_DIM)
            parts.append(ref[:, pl.ds(first, 2 * HEAD_DIM)])
        even = jnp.where(low, parts[0], pltpu.roll(parts[1], HEAD_DIM, 1))
        other = jnp.where(low, pltpu.roll(parts[0], HEAD_DIM, 1), parts[1])
        out.append(jnp.where(odd, other, even))
    return out


def conv_back(size, width, grad, convsum_ref, convin_ref, conv_ref, ext_ref, seg, out_ref):
    sums = [[jnp.zeros((1, 128), F32)] * (CONV + 1) for _ in range(0, width, 128)]
    for first in range(0, size, 64):
        here = slice(first, first + 64)
        for strip, lane in enumerate(range(0, width, 128)):
            lanes = slice(lane, lane + 128)
            value = grad(here, lanes) * silu_grad(convsum_ref[here, lanes])
            ext_ref[here, lanes] = value
            sums[strip][CONV] = sums[strip][CONV] + jnp.sum(value, axis=0, keepdims=True)
    for first in range(0, size, 64):
        here = slice(first, first + 64)
        ids = seg(first, 64)
        same = [
            jnp.broadcast_to(seg(first + CONV - 1 - tap, 64) == ids, (64, 128)) for tap in range(CONV - 1)
        ]
        for strip, lane in enumerate(range(0, width, 128)):
            lanes = slice(lane, lane + 128)
            conv_in = convin_ref[here, lanes].astype(F32)
            back = jnp.zeros((64, 128), F32)
            for tap in range(CONV):
                at = first + CONV - 1 - tap
                term = ext_ref[at : at + 64, lanes]
                if tap < CONV - 1:
                    term = jnp.where(same[tap], term, 0.0)
                back = back + conv_ref[tap : tap + 1, lanes] * term
                sums[strip][tap] = sums[strip][tap] + jnp.sum(conv_in * term, axis=0, keepdims=True)
            out_ref[here, lanes] = back.astype(BF16)
    row = lax.broadcasted_iota(jnp.int32, (8, 128), 0)
    out = []
    for strip in sums:
        total = jnp.zeros((8, 128), F32)
        for at, value in enumerate(strip):
            total = jnp.where(row == at, value, total)
        out.append(total)
    return jnp.concatenate(out, axis=1)


def pack_kernel(here_ref, win_ref, wout_ref, dt_ref, conv_ref, gain_ref, w1_ref, g2_ref, tmp_ref):
    ctx = here_ref[2]
    rows = win_ref.shape[0]
    heads = HEADS // 4
    width = heads * HEAD_DIM
    copies = range(w1_ref.shape[0])
    for at, part in enumerate(pick_heads(win_ref, INNER, ctx, heads)):
        part = part.astype(BF16)
        for copy in copies:
            w1_ref[copy, 0:rows, at * 128 : (at + 1) * 128] = part
    part = win_ref[:, 2 * INNER :].astype(BF16)
    for copy in copies:
        w1_ref[copy, 0:rows, width:] = part
    tmp_ref[...] = jnp.zeros_like(tmp_ref)
    row = lax.broadcasted_iota(jnp.int32, (heads, HEADS), 0)
    col = lax.broadcasted_iota(jnp.int32, (heads, HEADS), 1)
    table = jnp.where(col == 4 * row + ctx, 1.0, 0.0).astype(BF16)
    tmp_ref[0:heads, 384 : 384 + dt_ref.shape[1]] = nn(table, dt_ref[...].astype(BF16))
    tmp_ref[8 : 8 + CONV + 1, 0 : conv_ref.shape[1]] = conv_ref[...]
    tmp_ref[8 + CONV + 1 : 8 + CONV + 2, 0 : gain_ref.shape[0]] = gain_ref[...].reshape(1, -1)
    for copy in copies:
        w1_ref[copy, rows : rows + 16, :] = tmp_ref[...].astype(BF16)
    copies = range(g2_ref.shape[0])
    for at, part in enumerate(pick_heads(win_ref, 0, ctx, heads)):
        part = part.astype(BF16)
        for copy in copies:
            g2_ref[copy, 0:rows, at * 128 : (at + 1) * 128] = part
    if g2_ref.shape[1] > rows:
        some = wout_ref.shape[0] // 4
        mine = wout_ref[pl.ds(pl.multiple_of(ctx * some, 8), some), :].astype(BF16)
        for copy in copies:
            g2_ref[copy, rows : rows + some] = mine[:, :width]
            g2_ref[copy, rows + some : rows + 2 * some] = mine[:, width:]


def scan_forward_kernel(
    here_ref,
    at_ref,
    tok_pieces,
    w1_pieces,
    hrow_ref,
    hcol_ref,
    segc_ref,
    segr_ref,
    hid_ref,
    conv_ref,
    gpre_ref,
    gmine_ref,
    wdt_ref,
    w1_ref,
    mixed_ref,
    convin_ref,
    convsum_ref,
    inner_ref,
    raw_ref,
    stepc_ref,
    logc_ref,
    stepr_ref,
    logr_ref,
    start_ref,
    ext_ref,
    seg_ref,
    state_ref,
    small_ref,
    tok_ref,
    conv_all,
    gain_all,
    sems,
    tok_sems,
):
    step = pl.program_id(0)
    span, model = hid_ref.shape
    heads = wdt_ref.shape[0]
    width = heads * HEAD_DIM
    shards = small_ref.shape[0]
    rows = model // shards

    @pl.when(step == 0)
    def _():
        copies = place(
            w1_pieces,
            at_ref,
            len(w1_pieces),
            sems,
            [(0, rows, rows_of(w1_ref, rows)), (rows, 16, lambda at: small_ref.at[at])],
        )
        tokens = [
            pltpu.make_async_copy(piece, tok_ref.at[here_ref[2] ^ index], tok_sems.at[index])
            for index, piece in enumerate(tok_pieces)
        ]
        for copy in tokens:
            copy.start()
        ext_ref[0:8] = jnp.zeros((8, ext_ref.shape[1]), F32)
        state_ref[...] = jnp.zeros_like(state_ref)
        conv_all[...] = jnp.zeros_like(conv_all)
        for copy in copies:
            copy.wait()
        conv_cols = conv_all.shape[1] // shards
        gain_len = gain_all.shape[1] // shards
        for shard in range(shards):
            small = small_ref[shard].astype(F32)
            wdt_ref[:, shard * rows : (shard + 1) * rows] = small[0:8, 384 : 384 + rows].astype(BF16)
            conv_all[0 : CONV + 1, shard * conv_cols : (shard + 1) * conv_cols] = small[
                8 : 8 + CONV + 1, :conv_cols
            ]
            gain_all[:, shard * gain_len : (shard + 1) * gain_len] = small[13:14, :gain_len]
        for at, part in enumerate(pick_heads(conv_all, 0, here_ref[2], heads)):
            conv_ref[:, at * 128 : (at + 1) * 128] = part
        conv_ref[:, width:] = conv_all[:, INNER:]
        gpre_ref[...] = gain_all[:, :model]
        for at, part in enumerate(pick_heads(gain_all, model, here_ref[2], heads)):
            gmine_ref[:, at * 128 : (at + 1) * 128] = part
        for copy in tokens:
            copy.wait()

    for first in range(0, span, 32):
        tok = tok_ref[step, first : first + 32]
        scale = lax.rsqrt(jnp.mean(tok * tok, axis=-1, keepdims=True) + NORM_EPS)
        hid_ref[first : first + 32] = (tok * scale * gpre_ref[...]).astype(BF16)
    hid = hid_ref[...]
    proj = nn(hid, w1_ref[...]).astype(BF16)
    convin_ref[...] = proj
    ext_ref[8 : 8 + span] = proj.astype(F32)
    seg_ref[...] = segc_ref[pl.ds(pl.multiple_of(step * span, 8), span + 8), :]
    seg_here = seg_ref[8 : 8 + span]
    for first in range(0, span, 64):
        here = seg_ref[8 + first : 72 + first]
        starts = [8 - (CONV - 1) + tap + first for tap in range(CONV)]
        same = [jnp.broadcast_to(seg_ref[at : at + 64] == here, (64, 128)) for at in starts[:-1]]
        for lane in range(0, convin_ref.shape[1], 128):
            lanes = slice(lane, lane + 128)
            total = conv_ref[CONV : CONV + 1, lanes]
            for tap, at in enumerate(starts):
                term = ext_ref[at : at + 64, lanes]
                if tap < CONV - 1:
                    term = jnp.where(same[tap], term, 0.0)
                total = total + conv_ref[tap : tap + 1, lanes] * term
            convsum_ref[first : first + 64, lanes] = total
            mixed_ref[first : first + 64, lanes] = (total * sigmoid(total)).astype(BF16)
    ext_ref[0:8] = ext_ref[span : span + 8]

    raw_c = nt(hid, wdt_ref[...]) + hrow_ref[1:2]
    raw_r = nt(wdt_ref[...], hid) + hcol_ref[:, 1:2]
    step_c = softplus(raw_c)
    step_r = softplus(raw_r)
    log_c = nn(triangle(span, True), -step_c * jnp.exp(hrow_ref[0:1]), HIGHEST)
    log_r = nn(-step_r * jnp.exp(hcol_ref[:, 0:1]), triangle(span, False), HIGHEST)
    raw_ref[...] = raw_c
    stepc_ref[...] = step_c
    logc_ref[...] = log_c
    stepr_ref[...] = step_r
    logr_ref[...] = log_r

    low = lax.broadcasted_iota(jnp.int32, (SPAN, 2 * HEAD_DIM), 1) < HEAD_DIM
    earlier = lax.broadcasted_iota(jnp.int32, (SPAN, SPAN), 0) >= lax.broadcasted_iota(
        jnp.int32, (SPAN, SPAN), 1
    )
    skip_w = spread(hrow_ref[2:3] + jnp.zeros((8, heads), F32), width)[0:1]
    state = state_ref[...]
    for block in range(span // SPAN):
        here = slice(block * SPAN, (block + 1) * SPAN)
        values = mixed_ref[here, :width]
        write = mixed_ref[here, width : width + STATE]
        read = mixed_ref[here, width + STATE :]
        seg = seg_here[here]
        log = log_c[here]
        log_row = log_r[:, here]
        step_row = step_r[:, here]
        scores = jnp.where((seg == segr_ref[:, here]) & earlier, nt(read, write), 0.0)
        seg_prev = seg_ref[7 + block * SPAN : 8 + block * SPAN]
        seg_last = seg_ref[7 + (block + 1) * SPAN : 8 + (block + 1) * SPAN]
        last = log[SPAN - 1 : SPAN]
        enter = jnp.where(seg == seg_prev, jnp.exp(log), 0.0)
        tail = jnp.where(seg == seg_last, jnp.exp(last - log), 0.0) * step_c[here]
        keep = jnp.where(seg_last == seg_prev, jnp.exp(last), 0.0)
        start_ref[block] = state
        values_f = values.astype(F32)
        enter_w = spread(enter, width)
        inter = nn(read, state.astype(BF16))
        for pair in range(heads // 2):
            lanes = slice(pair * 2 * HEAD_DIM, (pair + 1) * 2 * HEAD_DIM)
            pieces = []
            for head in (2 * pair, 2 * pair + 1):
                gap = jnp.minimum(log[:, head : head + 1] - log_row[head : head + 1], 0.0)
                weights = scores * jnp.exp(gap) * step_row[head : head + 1]
                pieces.append(nn(weights.astype(BF16), values[:, lanes]))
            base = enter_w[:, lanes] * inter[:, lanes] + skip_w[:, lanes] * values_f[:, lanes]
            inner_ref[here, lanes] = base + jnp.where(low, pieces[0], pieces[1])
        moved = (spread(tail, width) * values_f).astype(BF16)
        keep_w = spread(keep + jnp.zeros((8, heads), F32), width)[0:1]
        state = keep_w * state + tn(write, moved)
    state_ref[...] = state


def gate_kernel(
    here_ref,
    at_ref,
    hid_ref,
    g2_pieces,
    cot_pieces,
    inner_ref,
    gain_ref,
    wg_ref,
    wout_ref,
    cot_ref,
    gate_ref,
    ng_ref,
    stat_ref,
    turned_ref,
    sems,
    cot_sems,
):
    step = pl.program_id(0)
    rows = wg_ref.shape[0] // (wout_ref.shape[0] // HEAD_DIM)
    width = wg_ref.shape[1]

    @pl.when(step == 0)
    def _():
        some = rows_of(wout_ref, HEAD_DIM)
        copies = place(
            g2_pieces,
            at_ref,
            len(g2_pieces),
            sems,
            [
                (0, rows, rows_of(wg_ref, rows)),
                (rows, HEAD_DIM, lambda at: some(at).at[:, 0:width]),
                (rows + HEAD_DIM, HEAD_DIM, lambda at: some(at).at[:, width : 2 * width]),
            ],
        )
        cots = [
            pltpu.make_async_copy(piece, cot_ref.at[here_ref[2] ^ index], cot_sems.at[index])
            for index, piece in enumerate(cot_pieces)
        ]
        for copy in cots:
            copy.start()
        for copy in copies + cots:
            copy.wait()
        turned_ref[...] = wout_ref[...].T

    gate_ref[...] = nn(hid_ref[...], wg_ref[...]).astype(BF16)
    ng_ref[...] = nn(cot_ref[step], turned_ref[...])
    span = gate_ref.shape[0]
    squares, crossed = [], []
    for first in range(0, span, 32):
        here = slice(first, first + 32)
        gate = gate_ref[here].astype(F32)
        gated = inner_ref[here] * (gate * sigmoid(gate))
        squares.append(jnp.sum(gated * gated, axis=1, keepdims=True))
        crossed.append(jnp.sum(gated * (ng_ref[here] * gain_ref[...]), axis=1, keepdims=True))
    squares = jnp.concatenate(squares, axis=0)
    crossed = jnp.concatenate(crossed, axis=0)
    same = diagonal(span)
    squares = jnp.sum(jnp.where(same, squares, 0.0), axis=0, keepdims=True)
    crossed = jnp.sum(jnp.where(same, crossed, 0.0), axis=0, keepdims=True)
    at = lax.broadcasted_iota(jnp.int32, stat_ref.shape, 0)
    stat_ref[...] = jnp.where(at == 0, squares, crossed)


def norm_back_kernel(
    perm_ref,
    here_ref,
    hid_ref,
    inner_ref,
    gate_ref,
    ng_ref,
    stat_refs,
    gain_ref,
    mixed_ref,
    wout_ref,
    cot_ref,
    block_refs,
    keep_ref,
    send_ref,
    dy_ref,
    dgate_ref,
    sums_ref,
    outacc_ref,
    inacc_ref,
    normed_ref,
):
    step = pl.program_id(0)
    span, width = inner_ref.shape

    @pl.when(step == 0)
    def _():
        outacc_ref[...] = jnp.zeros_like(outacc_ref)
        inacc_ref[...] = jnp.zeros_like(inacc_ref)
        sums_ref[...] = jnp.zeros_like(sums_ref)

    same = diagonal(span)
    stats = sum(ref[...] for ref in stat_refs)
    squares = jnp.sum(jnp.where(same, stats[0:1], 0.0), axis=1, keepdims=True)
    cross = jnp.sum(jnp.where(same, stats[1:2], 0.0), axis=1, keepdims=True)
    inv = lax.rsqrt(squares * (1.0 / INNER) + NORM_EPS)
    gain_sum = jnp.zeros((1, width), F32)
    skip_sum = jnp.zeros((1, width), F32)
    for first in range(0, span, 32):
        here = slice(first, first + 32)
        gate = gate_ref[here].astype(F32)
        sig = sigmoid(gate)
        silu = gate * sig
        inner = inner_ref[here]
        scale = inv[here]
        unit = inner * silu * scale
        normed_ref[here] = (unit * gain_ref[...]).astype(BF16)
        grad = ng_ref[here]
        dgated = scale * (grad * gain_ref[...] - unit * (cross[here] * scale * (1.0 / INNER)))
        dy = dgated * silu
        dy_ref[here] = dy
        dgate_ref[here] = (dgated * inner * (sig * (1.0 + gate * (1.0 - sig)))).astype(BF16)
        gain_sum = gain_sum + jnp.sum(grad * unit, axis=0, keepdims=True)
        skip_sum = skip_sum + jnp.sum(dy * mixed_ref[here].astype(F32), axis=0, keepdims=True)
    normed = normed_ref[...]
    cot = cot_ref[perm_ref[step]]
    block = nn(normed, wout_ref[...]).astype(BF16)

    for at, block_ref in enumerate(block_refs):

        @pl.when(step == at)
        def _():
            block_ref[...] = block

    outacc_ref[...] += tn(normed, cot)
    inacc_ref[...] += tn(hid_ref[...], dgate_ref[...])
    at = lax.broadcasted_iota(jnp.int32, (8, width), 0)
    sums_ref[...] += jnp.where(at == 0, gain_sum, jnp.where(at == 1, skip_sum, 0.0))

    @pl.when(step == pl.num_programs(0) - 1)
    def _():
        own = here_ref[0]
        rows = inacc_ref.shape[0] // (2 * keep_ref.shape[0])
        part_of(lambda at: inacc_ref[at * rows : (at + 1) * rows], own, keep_ref, send_ref)
        outs = lambda at: outacc_ref[at * HEAD_DIM : (at + 1) * HEAD_DIM]
        part_of(lambda at: outs(at)[:, :width], own, keep_ref, send_ref, rows)
        part_of(lambda at: outs(at)[:, width:], own, keep_ref, send_ref, rows + HEAD_DIM)


def scan_back_kernel(
    perm_ref,
    here_ref,
    hid_ref,
    dy_ref,
    mixed_ref,
    convin_ref,
    convsum_ref,
    raw_ref,
    stepc_ref,
    logc_ref,
    stepr_ref,
    logr_ref,
    start_ref,
    conv_ref,
    hrow_ref,
    segc_ref,
    segr_ref,
    keep_ref,
    send_ref,
    dval_ref,
    dbc_ref,
    dstep_ref,
    convg_ref,
    dtg_ref,
    headg_ref,
    ext_ref,
    seg_ref,
    grad_ref,
    inacc_ref,
    dx_ref,
):
    step = pl.program_id(0)
    chunk = pl.num_programs(0) - 1 - step
    span = hid_ref.shape[0]
    heads = stepc_ref.shape[1]
    width = heads * HEAD_DIM

    @pl.when(step == 0)
    def _():
        ext_ref[span : span + 8] = jnp.zeros((8, width), F32)
        grad_ref[...] = jnp.zeros_like(grad_ref)
        inacc_ref[...] = jnp.zeros_like(inacc_ref)
        convg_ref[...] = jnp.zeros_like(convg_ref)
        dtg_ref[...] = jnp.zeros_like(dtg_ref)
        headg_ref[...] = jnp.zeros_like(headg_ref)

    seg_ref[...] = segc_ref[pl.ds(pl.multiple_of(chunk * span, 8), span + 16), :]
    seg_here = seg_ref[8 : 8 + span]
    low = lax.broadcasted_iota(jnp.int32, (SPAN, 2 * HEAD_DIM), 1) < HEAD_DIM
    earlier = lax.broadcasted_iota(jnp.int32, (SPAN, SPAN), 0) >= lax.broadcasted_iota(
        jnp.int32, (SPAN, SPAN), 1
    )
    head_at = lax.broadcasted_iota(jnp.int32, (heads, SPAN), 0)
    lane_at = lax.broadcasted_iota(jnp.int32, (SPAN, heads), 1)
    at_last = lax.broadcasted_iota(jnp.int32, (SPAN, heads), 0) == SPAN - 1
    skip_w = spread(hrow_ref[2:3] + jnp.zeros((8, heads), F32), width)[0:1]
    step_c = stepc_ref[...]
    step_r = stepr_ref[...]
    later = grad_ref[...]
    count = span // SPAN
    dlogs, dsteps_c, dsteps_r = [None] * count, [None] * count, [None] * count
    for block in reversed(range(count)):
        here = slice(block * SPAN, (block + 1) * SPAN)
        values = mixed_ref[here, :width]
        write = mixed_ref[here, width : width + STATE]
        read = mixed_ref[here, width + STATE :]
        values_f = values.astype(F32)
        seg = seg_here[here]
        seg_prev = seg_ref[7 + block * SPAN : 8 + block * SPAN]
        seg_last = seg_ref[7 + (block + 1) * SPAN : 8 + (block + 1) * SPAN]
        dy = dy_ref[here]
        dy_low = dy.astype(BF16)
        log = logc_ref[here]
        log_row = logr_ref[:, here]
        step_row = step_r[:, here]
        last = log[SPAN - 1 : SPAN]
        enter = jnp.where(seg == seg_prev, jnp.exp(log), 0.0)
        tail_raw = jnp.where(seg == seg_last, jnp.exp(last - log), 0.0)
        tail = tail_raw * step_c[here]
        keep = jnp.where(seg_last == seg_prev, jnp.exp(last), 0.0)
        enter_w = spread(enter, width)
        tail_w = spread(tail, width)
        keep_w = spread(keep + jnp.zeros((8, heads), F32), width)[0:1]
        state = start_ref[block]
        state_low = state.astype(BF16)
        later_low = later.astype(BF16)

        entered_low = (enter_w * dy).astype(BF16)
        inter = enter_w * nn(read, state_low)
        from_later = nn(write, later_low)
        moved_low = (tail_w * values_f).astype(BF16)
        dread = nt(entered_low, state_low)
        dwrite = nt(moved_low, later_low)
        tail_dot = gather_heads(values_f * from_later, heads)
        dlog = gather_heads(dy * inter, heads) - tail_dot * tail
        dsteps_c[block] = tail_dot * tail_raw
        carried = jnp.sum(later * state, axis=0, keepdims=True) + jnp.zeros((8, width), F32)
        carried = gather_heads(carried, heads)[0:1]
        dlog = dlog + jnp.where(
            at_last, jnp.sum(tail_dot * tail, axis=0, keepdims=True) + keep * carried, 0.0
        )
        later = keep_w * later + tn(read, entered_low)
        direct = tail_w * from_later + skip_w * dy

        visible = (seg == segr_ref[:, here]) & earlier
        scores = jnp.where(visible, nt(read, write), 0.0)
        dscores = jnp.zeros((SPAN, SPAN), F32)
        dstep = jnp.zeros((heads, SPAN), F32)
        for pair in range(heads // 2):
            lanes = slice(pair * 2 * HEAD_DIM, (pair + 1) * 2 * HEAD_DIM)
            dy_pair = dy_low[:, lanes]
            pieces = []
            for head in (2 * pair, 2 * pair + 1):
                mine = low if head % 2 == 0 else ~low
                gap = jnp.minimum(log[:, head : head + 1] - log_row[head : head + 1], 0.0)
                decay = jnp.exp(gap)
                outer = nt(jnp.where(mine, dy_pair, jnp.zeros_like(dy_pair)), values[:, lanes])
                fade = decay * step_row[head : head + 1]
                dscores = dscores + outer * fade
                weights = scores * fade
                flow = outer * scores
                dstep = dstep + jnp.where(
                    head_at == head, jnp.sum(flow * decay, axis=0, keepdims=True), 0.0
                )
                dlog = dlog + jnp.where(
                    lane_at == head, jnp.sum(outer * weights, axis=1, keepdims=True), 0.0
                )
                pieces.append(tn(weights.astype(BF16), dy_pair))
            dx_ref[here, lanes] = direct[:, lanes] + jnp.where(low, pieces[0], pieces[1])
        dscores = jnp.where(visible, dscores, 0.0).astype(BF16)
        dbc_ref[here, :STATE] = (dwrite + tn(dscores, read)).astype(BF16)
        dbc_ref[here, STATE:] = (dread + nn(dscores, write)).astype(BF16)
        dlogs[block], dsteps_r[block] = dlog, dstep
    grad_ref[...] = later
    dlog_c = jnp.concatenate(dlogs, axis=0)
    dstep_c = jnp.concatenate(dsteps_c, axis=0)
    dstep_r = jnp.concatenate(dsteps_r, axis=1)

    upper = triangle(span, False)
    eye = jnp.where(diagonal(span), 1.0, 0.0).astype(F32)
    dalpha = nn(upper, dlog_c, HIGHEST) - nt(upper, dstep_r * step_r, HIGHEST)
    dstep = dstep_c + nt(eye, dstep_r, HIGHEST)
    rate = jnp.exp(hrow_ref[0:1])
    draw = (dstep - rate * dalpha) * sigmoid(raw_ref[...])
    draw_low = draw.astype(BF16)
    dstep_ref[...] = draw_low
    hid = hid_ref[...]
    dtg_ref[...] += tn(draw_low, hid)
    rate_sum = jnp.sum(-dalpha * step_c * rate, axis=0, keepdims=True)
    bias_sum = jnp.sum(draw, axis=0, keepdims=True)
    at = lax.broadcasted_iota(jnp.int32, (8, heads), 0)
    headg_ref[...] += jnp.where(at == 0, rate_sum, jnp.where(at == 1, bias_sum, 0.0))

    convg_ref[...] += conv_back(
        span,
        width,
        lambda here, lanes: dx_ref[here, lanes],
        convsum_ref,
        convin_ref,
        conv_ref,
        ext_ref,
        lambda first, count: seg_ref[8 + first : 8 + first + count],
        dval_ref,
    )
    ext_ref[span : span + 8] = ext_ref[0:8]
    inacc_ref[...] += tn(hid, dval_ref[...])

    @pl.when(step == pl.num_programs(0) - 1)
    def _():
        rows = inacc_ref.shape[0] // (2 * keep_ref.shape[0])
        part_of(lambda at: inacc_ref[at * rows : (at + 1) * rows], here_ref[0], keep_ref, send_ref)


def hidden_back_kernel(
    perm_ref,
    dgate_ref,
    dval_ref,
    dstep_ref,
    wg_ref,
    wv_ref,
    wdt_ref,
    hid_ref,
    gain_ref,
    out_refs,
    gsum_ref,
    turned_ref,
):
    width = wg_ref.shape[1]

    @pl.when(pl.program_id(0) == 0)
    def _():
        gsum_ref[...] = jnp.zeros_like(gsum_ref)
        turned_ref[0:width] = wg_ref[...].T
        turned_ref[width:] = wv_ref[...].T

    total = nn(dgate_ref[...], turned_ref[0:width]) + nn(dval_ref[...], turned_ref[width:])
    total = total + nn(dstep_ref[...], wdt_ref[...])
    step = pl.program_id(0)

    for at, out_ref in enumerate(out_refs):

        @pl.when(step == at)
        def _():
            out_ref[...] = total.astype(BF16)

    gain_sum = jnp.zeros(gain_ref.shape, F32)
    for first in range(0, total.shape[0], 32):
        here = slice(first, first + 32)
        gain_sum = gain_sum + jnp.sum(total[here] * hid_ref[here].astype(F32), axis=0, keepdims=True)
    gsum_ref[...] += gain_sum / gain_ref[...] + jnp.zeros(gsum_ref.shape, F32)


def maps_back_kernel(
    here_ref,
    dbc_ref,
    dbcfar_ref,
    convsum_ref,
    convin_ref,
    conv_ref,
    segc_ref,
    hid_ref,
    w1_ref,
    gain_ref,
    convg_ref,
    sums_ref,
    headg_ref,
    dtg_ref,
    gall_ref,
    keep_ref,
    send_ref,
    own_ref,
    ext_ref,
    acc_ref,
    dmap_ref,
    small_ref,
):
    size, width = dmap_ref.shape
    ext_ref[size : size + 8] = jnp.zeros((8, width), F32)
    sums = conv_back(
        size,
        width,
        lambda here, lanes: dbc_ref[here, lanes].astype(F32) + dbcfar_ref[here, lanes].astype(F32),
        convsum_ref,
        convin_ref,
        conv_ref,
        ext_ref,
        lambda first, count: segc_ref[8 + first : 8 + first + count],
        dmap_ref,
    )
    ctx = here_ref[2]
    acc_ref[...] = tn(hid_ref[...], dmap_ref[...])
    span = own_ref.shape[0]
    own = pl.ds(pl.multiple_of(ctx * span, 16), span)
    grad = nt(dmap_ref[own, :], w1_ref[...])
    own_ref[...] = grad
    unit = hid_ref[own, :].astype(F32) / gain_ref[...]
    gain_sum = gall_ref[0:1] + jnp.sum(grad * unit, axis=0, keepdims=True)
    half = small_ref.shape[1]
    heads = headg_ref.shape[1]
    small_ref[...] = jnp.zeros_like(small_ref)
    small_ref[0 : CONV + 1] = convg_ref[0 : CONV + 1]
    small_ref[CONV + 1 : CONV + 3] = sums_ref[0:2]
    small_ref[7:8, 0:heads] = headg_ref[0:1]
    small_ref[7:8, 128 : 128 + heads] = headg_ref[1:2]
    small_ref[8 : 8 + CONV + 1, 0:width] = sums[0 : CONV + 1]
    small_ref[13:14] = gain_sum[:, :half]
    small_ref[14:15] = gain_sum[:, half:]
    small_ref[15:16] = small_ref[7:8] - small_ref[7:8].astype(BF16).astype(F32)
    small_ref[16:24] = dtg_ref[:, :half]
    small_ref[24:32] = dtg_ref[:, half:]
    small = small_ref[...].astype(BF16)
    count = keep_ref.shape[0] // 32 - 1
    block = acc_ref.shape[0] // (2 * count)
    some = block // 4
    keep_ref[0:32] = small
    send_ref[0:32] = small
    for at in range(count):
        start = pl.multiple_of(2 * at * block + ctx * some, 8)
        low = acc_ref[pl.ds(start, some), :].astype(BF16)
        start = pl.multiple_of((2 * at + 1) * block + ctx * some, 8)
        high = acc_ref[pl.ds(start, some), :].astype(BF16)
        keep_ref[32 + 32 * at : 64 + 32 * at, 0:width] = jnp.where(here_ref[0] == 0, low, high)
        send_ref[32 + 32 * at : 64 + 32 * at, 0:width] = jnp.where(here_ref[0] == 0, high, low)


def input_back_kernel(part_refs, own_ref, tok_ref, gain_ref, cot_ref, out_ref):
    for first in range(0, out_ref.shape[0], 32):
        here = slice(first, first + 32)
        grad = own_ref[here]
        for ref in part_refs:
            grad = grad + ref[here].astype(F32)
        tok = tok_ref[here]
        scale = lax.rsqrt(jnp.mean(tok * tok, axis=-1, keepdims=True) + NORM_EPS)
        unit = tok * scale
        scaled = grad * gain_ref[...]
        mean = jnp.mean(scaled * unit, axis=-1, keepdims=True)
        out_ref[here] = cot_ref[here] + scale * (scaled - unit * mean)


def with_rest(value, first):
    row = lax.broadcasted_iota(jnp.int32, value.shape, 0)
    head = value[first + 7 : first + 8] + value[first + 15 : first + 16]
    rest = head - head.astype(BF16).astype(F32)
    return jnp.where(row == first + 7, head, jnp.where(row == first + 15, rest, value))


def pair_sum_late_kernel(keep_ref, came_ref, mkeep_ref, mcame_ref, out_ref):
    count, rows, width = keep_ref.shape
    small = with_rest(mkeep_ref[0:32].astype(F32) + mcame_ref[0:32].astype(F32), 0).astype(BF16)
    for block in range(count):
        out_ref[block, 0:rows] = (keep_ref[block].astype(F32) + came_ref[block].astype(F32)).astype(BF16)
        out_ref[block, rows : rows + 32] = small
        at = slice(32 + 32 * block, 64 + 32 * block)
        out_ref[block, rows + 32 : rows + 64] = (
            mkeep_ref[at].astype(F32) + mcame_ref[at].astype(F32)
        ).astype(BF16)


def sum_late_kernel(parts_ref, out_ref):
    total = parts_ref[0].astype(F32)
    for at in range(1, parts_ref.shape[0]):
        total = total + parts_ref[at].astype(F32)
    out_ref[...] = with_rest(total, out_ref.shape[0] - 64).astype(BF16)


def adam_out_kernel(here_ref, weight_ref, first_ref, second_ref, early_refs, *rest):
    new_refs, early_ref = rest[:3], rest[3]
    step = pl.program_id(0)

    @pl.when(step == 0)
    def _():
        by_owner(early_refs, here_ref[2], early_ref)

    rows = weight_ref.shape[0]
    width = early_ref.shape[2]
    first = early_ref.shape[1] - 2 * rows
    for at in range(2):
        lanes = slice(at * width, (at + 1) * width)
        grad = early_ref[step, first + at * rows : first + (at + 1) * rows].astype(F32)
        news = adam_step(
            weight_ref[:, lanes], first_ref[:, lanes], second_ref[:, lanes], grad, 0.02, WEIGHT_DECAY
        )
        for ref, new in zip(new_refs, news):
            ref[:, lanes] = new


def by_owner(refs, ctx, natural_ref):
    for at, ref in enumerate(refs):
        natural_ref[pl.ds(ctx ^ at, 1)] = ref[...][None]


def adam_in_kernel(here_ref, weight_ref, first_ref, second_ref, early_refs, late_refs, *rest):
    new_refs, (early_ref, late_ref) = rest[:3], rest[3:]
    step = pl.program_id(0)
    pieces = len(early_refs)
    rows = weight_ref.shape[0]
    width = early_ref.shape[2]
    block = pieces * HEAD_DIM

    @pl.when(step == 0)
    def _():
        by_owner(early_refs, here_ref[2], early_ref)
        by_owner(late_refs, here_ref[2], late_ref)

    here = pl.ds(pl.multiple_of(step * rows, rows), rows)
    low = lax.broadcasted_iota(jnp.int32, (rows, 2 * HEAD_DIM), 1) < HEAD_DIM

    def update(lanes, grad):
        news = adam_step(
            weight_ref[:, lanes], first_ref[:, lanes], second_ref[:, lanes], grad, 0.03, WEIGHT_DECAY
        )
        for ref, new in zip(new_refs, news):
            ref[:, lanes] = new

    for base, ref in ((0, early_ref), (INNER, late_ref)):
        for pair in range(width // (2 * HEAD_DIM)):
            lanes = slice(pair * 2 * HEAD_DIM, (pair + 1) * 2 * HEAD_DIM)
            for at in range(0, pieces, 2):
                first = ref[at, here, lanes].astype(F32)
                second = ref[at + 1, here, lanes].astype(F32)
                start = base + 2 * pair * block + at * HEAD_DIM
                even = jnp.where(low, first, pltpu.roll(second, HEAD_DIM, 1))
                update(slice(start, start + 2 * HEAD_DIM), even)
                start = start + block
                odd = jnp.where(low, pltpu.roll(first, HEAD_DIM, 1), second)
                update(slice(start, start + 2 * HEAD_DIM), odd)
    some = 32 // rows
    first = pl.multiple_of(late_ref.shape[1] - 32 + (step % some) * rows, rows)
    grad = late_ref[step // some, pl.ds(first, rows), 0 : 2 * STATE].astype(F32)
    update(slice(2 * INNER, 2 * INNER + 2 * STATE), grad)


def swap(value, axis, bit):
    count = lax.axis_size(axis)
    return lax.ppermute(value, axis, [(at, at ^ bit) for at in range(count)])


def gather_ctx(value):
    far = swap(value, "ctx", 2)
    return [value, swap(value, "ctx", 1), far, swap(far, "ctx", 1)]


def high_all_to_all(value):
    count = lax.axis_size("dp")
    groups = [list(range(low, count, 2)) for low in range(2)]
    return lax.all_to_all(value, "dp", 0, 0, axis_index_groups=groups)


def from_owners(parts):
    count = len(parts)
    return [swap(parts[bit - 1], "ctx", bit) for bit in range(1, count)] + [parts[-1]]


def fan_ctx(value):
    return [value] + [swap(value, "ctx", bit) for bit in range(1, lax.axis_size("ctx"))]


def adam_step(weight, moment_one, second, gradient, step_rate, decay_rate):
    moment_new = BETA_ONE * moment_one + (1.0 - BETA_ONE) * gradient
    second_new = BETA_TWO * second + (1.0 - BETA_TWO) * gradient * gradient
    first_hat = moment_new / (1.0 - BETA_ONE**STEP)
    second_hat = second_new / (1.0 - BETA_TWO**STEP)
    weight_new = weight - step_rate * (
        first_hat / (jnp.sqrt(second_hat) + ADAM_EPS) + decay_rate * weight
    )
    return (weight_new, moment_new, second_new)


def full(shape):
    return pl.BlockSpec(shape, lambda *_: (0,) * len(shape))


def shape_of(*shape, dtype=F32):
    return jax.ShapeDtypeStruct(shape, dtype)


def shards(
    tokens,
    segment_ids,
    cotangent,
    in_weight,
    dt_weight,
    out_weight,
    conv_params,
    gains,
    head_params,
    in_first,
    in_second,
    dt_first,
    dt_second,
    out_first,
    out_second,
    conv_first,
    conv_second,
    gain_first,
    gain_second,
    head_first,
    head_second,
):
    _, span, model = tokens.shape
    length = segment_ids.shape[1]
    ndp, nctx = lax.axis_size("dp"), lax.axis_size("ctx")
    d, c = lax.axis_index("dp"), lax.axis_index("ctx")
    heads = HEADS // nctx
    width = INNER // nctx
    maps = 2 * STATE
    wide = width + maps
    chunks = nctx
    rows_in = in_weight.shape[0]
    conv_cols = conv_params.shape[1]
    gain_len = gains.shape[0]
    dt_cols = dt_weight.shape[1]
    near = ndp == heads
    high = heads // 2
    block_in = model // heads
    tok = tokens[0]
    bits = jnp.stack([d & 1, d >> 1, c] if near else [0 * d, 0 * d, c]).astype(jnp.int32)
    perm = c ^ jnp.asarray([1, 2, 3, 0], jnp.int32)
    smem = pl.BlockSpec(memory_space=pltpu.SMEM)
    vmem = pl.BlockSpec(memory_space=pltpu.VMEM)
    anywhere = lambda pieces: [pl.BlockSpec(memory_space=pl.ANY)] * len(pieces)

    w1, g2 = pl.pallas_call(
        pack_kernel,
        in_specs=[smem] + [vmem] * 5,
        out_shape=[
            shape_of(high if near else 1, rows_in + 16, wide, dtype=BF16),
            shape_of(high if near else 1, rows_in + (2 * HEAD_DIM if near else 0), width, dtype=BF16),
        ],
        scratch_shapes=[pltpu.VMEM((16, wide), F32)],
        compiler_params=params(),
        name="pack",
    )(bits, in_weight, out_weight, dt_weight, conv_params, gains)
    ids = segment_ids[0]
    seg_col = jnp.pad(ids, (8, 8), constant_values=-1)[:, None]
    seg_row = segment_ids
    head_mine = lax.dynamic_index_in_dim(head_params.reshape(3, heads, nctx), c, 2, False)
    head_col = head_mine.T
    cot_low = cotangent[0].astype(BF16)
    if near:
        tok_far = swap(tok, "ctx", 2)
        tok_core = swap(tok, "ctx", 1)
        w1 = high_all_to_all(w1)
        at_rows = jnp.stack([d & 1, 1 - (d & 1)]).astype(jnp.int32)
        w1, g2, cot_low, seg_col, head_mine, head_col, at_rows, perm = lax.optimization_barrier(
            (w1, g2, cot_low, seg_col, head_mine, head_col, at_rows, perm)
        )
        at_g2 = at_rows
        w1_came = swap(w1, "dp", 1)
        g2 = high_all_to_all(g2)
        w1, w1_came, tok_far = lax.optimization_barrier((w1, w1_came, tok_far))
        toks = [tok, tok_core, tok_far, swap(tok_far, "ctx", 1)]
        w1, w1_came, toks, g2, cot_low = lax.optimization_barrier((w1, w1_came, toks, g2, cot_low))
        w1 = [w1, w1_came]
        g2 = [g2, swap(g2, "dp", 1)]
        cots = fan_ctx(cot_low)
    else:
        w1 = [lax.all_gather(w1[0], "dp", axis=0)]
        toks = gather_ctx(tok)
        cots = gather_ctx(cot_low)
        wg = lax.all_gather(g2[0], "dp", axis=0, tiled=True).reshape(heads, block_in, width)
        wout = lax.all_gather(out_weight.astype(BF16), "dp", axis=0, tiled=True)
        wout = lax.dynamic_index_in_dim(wout.reshape(heads, nctx, HEAD_DIM, model), c, 1, False)
        g2 = [jnp.concatenate([wg, wout[:, :, :width], wout[:, :, width:]], axis=1)]
        at_rows = at_g2 = jnp.zeros((1,), jnp.int32)

    rows = lambda cols: pl.BlockSpec((span, cols), lambda i, *_: (i, 0))
    row_of = pl.BlockSpec((heads, span), lambda i, *_: (0, i))
    rows_at = lambda cols: pl.BlockSpec((span, cols), lambda i, p, *_: (p[i], 0))
    whole = full((span, model))
    shards_in = sum(piece.shape[0] for piece in w1)

    (
        hid, conv_mine, gain_pre, gain_mine, dt_mine, w1, mixed, conv_in, conv_sum, inner, raw,
        step_c, log_c, step_r, log_r, starts,
    ) = pl.pallas_call(
        scan_forward_kernel,
        grid_spec=pltpu.PrefetchScalarGridSpec(
            num_scalar_prefetch=2,
            grid=(chunks,),
            in_specs=[
                anywhere(toks),
                anywhere(w1),
                full((3, heads)),
                full((heads, 3)),
                full((length + 16, 1)),
                pl.BlockSpec((1, span), lambda i, *_: (0, i)),
            ],
            out_specs=[
                rows(model),
                full((8, wide)),
                full((1, model)),
                full((1, width)),
                full((heads, model)),
                full((model, wide)),
                rows(wide),
                rows(wide),
                rows(wide),
                rows(width),
                rows(heads),
                rows(heads),
                rows(heads),
                row_of,
                row_of,
                pl.BlockSpec((span // SPAN, STATE, width), lambda i, *_: (i, 0, 0)),
            ],
            scratch_shapes=[
                pltpu.VMEM((span + 8, wide), F32),
                pltpu.VMEM((span + 8, 1), jnp.int32),
                pltpu.VMEM((STATE, width), F32),
                pltpu.VMEM((shards_in, 16, wide), BF16),
                pltpu.VMEM((nctx, span, model), F32),
                pltpu.VMEM((8, INNER + maps), F32),
                pltpu.VMEM((1, model + INNER), F32),
                pltpu.SemaphoreType.DMA((copies_of(w1, 2),)),
                pltpu.SemaphoreType.DMA((nctx,)),
            ],
        ),
        out_shape=[
            shape_of(length, model, dtype=BF16),
            shape_of(8, wide),
            shape_of(1, model),
            shape_of(1, width),
            shape_of(heads, model, dtype=BF16),
            shape_of(model, wide, dtype=BF16),
            shape_of(length, wide, dtype=BF16),
            shape_of(length, wide, dtype=BF16),
            shape_of(length, wide),
            shape_of(length, width),
            shape_of(length, heads),
            shape_of(length, heads),
            shape_of(length, heads),
            shape_of(heads, length),
            shape_of(heads, length),
            shape_of(length // SPAN, STATE, width),
        ],
        compiler_params=params("arbitrary"),
        name="scan_forward",
    )(bits, at_rows, toks, w1, head_mine, head_col, seg_col, seg_row)

    wg, wout, cot_all, gate, normed_grad, stats = pl.pallas_call(
        gate_kernel,
        grid_spec=pltpu.PrefetchScalarGridSpec(
            num_scalar_prefetch=2,
            grid=(chunks,),
            in_specs=[rows(model), anywhere(g2), anywhere(cots), rows(width), full((1, width))],
            out_specs=[
                full((model, width)),
                full((width, model)),
                full((nctx, span, model)),
                rows(width),
                rows(width),
                pl.BlockSpec((8, span), lambda i, *_: (0, i)),
            ],
            scratch_shapes=[
                pltpu.VMEM((model, width), BF16),
                pltpu.SemaphoreType.DMA((copies_of(g2, 3),)),
                pltpu.SemaphoreType.DMA((nctx,)),
            ],
        ),
        out_shape=[
            shape_of(model, width, dtype=BF16),
            shape_of(width, model, dtype=BF16),
            shape_of(nctx, span, model, dtype=BF16),
            shape_of(length, width, dtype=BF16),
            shape_of(length, width),
            shape_of(8, length),
        ],
        compiler_params=params("arbitrary"),
        name="gate",
    )(bits, at_g2, hid, g2, cots, inner, gain_mine)
    stats = fan_ctx(stats)

    early_rows = block_in + 2 * HEAD_DIM
    blocks_out, early_keep, early_send, dy, dgate, col_sums = pl.pallas_call(
        norm_back_kernel,
        grid_spec=pltpu.PrefetchScalarGridSpec(
            num_scalar_prefetch=2,
            grid=(chunks,),
            in_specs=[
                rows_at(model),
                rows_at(width),
                rows_at(width),
                rows_at(width),
                [pl.BlockSpec((8, span), lambda i, p, *_: (0, p[i]))] * nctx,
                full((1, width)),
                rows_at(width),
                full((width, model)),
                full((nctx, span, model)),
            ],
            out_specs=[
                [whole] * nctx,
                full((high, early_rows, width)),
                full((high, early_rows, width)),
                rows_at(width),
                rows_at(width),
                full((8, width)),
            ],
            scratch_shapes=[
                pltpu.VMEM((width, model), F32),
                pltpu.VMEM((model, width), F32),
                pltpu.VMEM((span, width), BF16),
            ],
        ),
        out_shape=[
            [shape_of(span, model, dtype=BF16)] * nctx,
            shape_of(high, early_rows, width, dtype=BF16),
            shape_of(high, early_rows, width, dtype=BF16),
            shape_of(length, width),
            shape_of(length, width, dtype=BF16),
            shape_of(8, width),
        ],
        compiler_params=params("arbitrary"),
        name="norm_back",
    )(perm, bits, hid, inner, gate, normed_grad, stats, gain_mine, mixed, wout, cot_all)
    blocks_out = from_owners(blocks_out)
    if near:
        early_came = swap(early_send, "dp", 1)

    back = lambda cols: pl.BlockSpec((span, cols), lambda i, *_: (chunks - 1 - i, 0))
    back_row = pl.BlockSpec((heads, span), lambda i, *_: (0, chunks - 1 - i))
    late_keep, late_send, dval, dbc, dstep, conv_grad, dt_grad, head_grad = pl.pallas_call(
        scan_back_kernel,
        grid_spec=pltpu.PrefetchScalarGridSpec(
            num_scalar_prefetch=2,
            grid=(chunks,),
            in_specs=[
                back(model),
                back(width),
                back(wide),
                back(width),
                back(width),
                back(heads),
                back(heads),
                back(heads),
                back_row,
                back_row,
                pl.BlockSpec((span // SPAN, STATE, width), lambda i, *_: (chunks - 1 - i, 0, 0)),
                full((8, width)),
                full((3, heads)),
                full((length + 16, 1)),
                pl.BlockSpec((1, span), lambda i, *_: (0, chunks - 1 - i)),
            ],
            out_specs=[
                full((high, block_in, width)),
                full((high, block_in, width)),
                back(width),
                back(maps),
                back(heads),
                full((8, width)),
                full((heads, model)),
                full((8, heads)),
            ],
            scratch_shapes=[
                pltpu.VMEM((span + 8, width), F32),
                pltpu.VMEM((span + 16, 1), jnp.int32),
                pltpu.VMEM((STATE, width), F32),
                pltpu.VMEM((model, width), F32),
                pltpu.VMEM((span, width), F32),
            ],
        ),
        out_shape=[
            shape_of(high, block_in, width, dtype=BF16),
            shape_of(high, block_in, width, dtype=BF16),
            shape_of(length, width, dtype=BF16),
            shape_of(length, maps, dtype=BF16),
            shape_of(length, heads, dtype=BF16),
            shape_of(8, width),
            shape_of(heads, model),
            shape_of(8, heads),
        ],
        compiler_params=params("arbitrary"),
        name="scan_back",
    )(
        perm, bits, hid, dy, mixed, conv_in, conv_sum, raw, step_c, log_c, step_r, log_r, starts,
        conv_mine, head_mine, seg_col, seg_row,
    )
    dbc_came = swap(dbc, "ctx", 1)
    if near:
        late_came = swap(late_send, "dp", 1)
        early_came, blocks_out, dval = lax.optimization_barrier((early_came, blocks_out, dval))
        early_parts = (early_keep.astype(F32) + early_came.astype(F32)).astype(BF16)
        early_parts = high_all_to_all(early_parts)
    dbc = (dbc.astype(F32) + dbc_came.astype(F32)).astype(BF16)
    dval, dbc = lax.optimization_barrier((dval, dbc))
    dbc_far = swap(dbc, "ctx", 2)

    hidden_out, gain_sum = pl.pallas_call(
        hidden_back_kernel,
        grid_spec=pltpu.PrefetchScalarGridSpec(
            num_scalar_prefetch=1,
            grid=(chunks,),
            in_specs=[
                rows_at(width),
                rows_at(width),
                rows_at(heads),
                full((model, width)),
                full((model, width)),
                full((heads, model)),
                rows_at(model),
                full((1, model)),
            ],
            out_specs=[[whole] * nctx, full((8, model))],
            scratch_shapes=[pltpu.VMEM((2 * width, model), BF16)],
        ),
        out_shape=[
            [shape_of(span, model, dtype=BF16)] * nctx,
            shape_of(8, model),
        ],
        compiler_params=params("arbitrary"),
        name="hidden_back",
    )(perm, dgate, dval, dstep, wg, w1, dt_mine, hid, gain_pre)
    hidden_near = swap(hidden_out[0], "ctx", 1)
    hidden_far = (hidden_out[1].astype(F32) + swap(hidden_out[2], "ctx", 1).astype(F32)).astype(BF16)
    hidden_out = [hidden_out[3], hidden_near]
    map_rows = 32 + 32 * high
    map_cols = lambda size: pl.BlockSpec((size, maps), lambda i: (0, width // maps))
    map_keep, map_send, hidden_own = pl.pallas_call(
        maps_back_kernel,
        grid=(1,),
        in_specs=[
            smem,
            full((length, maps)),
            full((length, maps)),
            map_cols(length),
            map_cols(length),
            map_cols(8),
            full((length + 16, 1)),
            full((length, model)),
            map_cols(model),
            full((1, model)),
            full((8, width)),
            full((8, width)),
            full((8, heads)),
            full((heads, model)),
            full((8, model)),
        ],
        out_specs=[full((map_rows, width)), full((map_rows, width)), full((span, model))],
        out_shape=[
            shape_of(map_rows, width, dtype=BF16),
            shape_of(map_rows, width, dtype=BF16),
            shape_of(span, model),
        ],
        scratch_shapes=[
            pltpu.VMEM((length + 8, maps), F32),
            pltpu.VMEM((model, maps), F32),
            pltpu.VMEM((length, maps), BF16),
            pltpu.VMEM((32, width), F32),
        ],
        compiler_params=params("arbitrary"),
        name="maps_back",
    )(
        bits,
        dbc,
        dbc_far,
        conv_sum,
        conv_in,
        conv_mine,
        seg_col,
        hid,
        w1,
        gain_pre,
        conv_grad,
        col_sums,
        head_grad,
        dt_grad,
        gain_sum,
    )

    block_output = tok + sum(part.astype(F32) for part in blocks_out)

    input_part = lambda parts, own: pl.pallas_call(
        input_back_kernel,
        in_specs=[[vmem] * (nctx - 1)] + [vmem] * 4,
        out_shape=shape_of(span, model),
        compiler_params=params(),
        name="input_back",
    )(parts, own, tok, gain_pre, cotangent[0])

    late_rows = block_in + 64
    if near:
        early = jnp.sum(early_parts.astype(F32), axis=0).astype(BF16)
        map_came = swap(map_send, "dp", 1)
        map_came, block_output, early, hidden_far = lax.optimization_barrier(
            (map_came, block_output, early, hidden_far)
        )
    hidden_out = hidden_out + [swap(hidden_far, "ctx", 2)]
    if near:
        late_parts = pl.pallas_call(
            pair_sum_late_kernel,
            out_shape=shape_of(high, late_rows, width, dtype=BF16),
            compiler_params=params(),
            name="pair_sum_late",
        )(late_keep, late_came, map_keep, map_came)
        late_parts = high_all_to_all(late_parts)
        early = gather_ctx(early)
        row_block = lambda ref_rows, cols: pl.BlockSpec((ref_rows, cols), lambda i, *_: (i, 0))
        out_block = row_block(out_weight.shape[0] // nctx, model)
        early_spec = [full((early_rows, width))] * nctx
        early_scratch = pltpu.VMEM((nctx, early_rows, width), BF16)
        out_new = pl.pallas_call(
            adam_out_kernel,
            grid_spec=pltpu.PrefetchScalarGridSpec(
                num_scalar_prefetch=1,
                grid=(nctx,),
                in_specs=[out_block] * 3 + [early_spec],
                out_specs=[out_block] * 3,
                scratch_shapes=[early_scratch],
            ),
            out_shape=[shape_of(*out_weight.shape)] * 3,
            compiler_params=params("arbitrary"),
            name="adam_out",
        )(bits, out_weight, out_first, out_second, early)

        late_parts, out_new = lax.optimization_barrier((late_parts, out_new))
        late = pl.pallas_call(
            sum_late_kernel,
            out_shape=shape_of(late_rows, width, dtype=BF16),
            compiler_params=params(),
            name="sum_late",
        )(late_parts)
        late = fan_ctx(late)
        input_grad = input_part(hidden_out, hidden_own)
        late, input_grad = lax.optimization_barrier((late, input_grad))
        in_block = row_block(32, in_weight.shape[1])
        in_new = pl.pallas_call(
            adam_in_kernel,
            grid_spec=pltpu.PrefetchScalarGridSpec(
                num_scalar_prefetch=1,
                grid=(rows_in // 32,),
                in_specs=[in_block] * 3 + [early_spec, [full((late_rows, width))] * nctx],
                out_specs=[in_block] * 3,
                scratch_shapes=[early_scratch, pltpu.VMEM((nctx, late_rows, width), BF16)],
            ),
            out_shape=[shape_of(*in_weight.shape)] * 3,
            compiler_params=params("arbitrary"),
            name="adam_in",
        )(bits, in_weight, in_first, in_second, early, late)
        in_new, out_new = tuple(in_new), tuple(out_new)
        small = jnp.stack([part[block_in : block_in + 32] for part in late])[c ^ jnp.arange(nctx)]
        small = small.astype(F32)
    else:
        input_grad = input_part(hidden_out, hidden_own)
        blocks = lambda keep, send: jnp.stack([keep, send], axis=1).reshape((heads,) + keep.shape[1:])
        early = blocks(early_keep, early_send).astype(F32)
        late = blocks(late_keep, late_send).astype(F32)
        part = lambda value: value[32:].reshape(high, 32, width)[:, :, :maps]
        map_blocks = blocks(part(map_keep), part(map_send)).astype(F32)

        def total(value):
            return lax.psum_scatter(value, "dp", scatter_dimension=0, tiled=True)

        def spaced(value):
            place_at = (jnp.arange(nctx) == c).astype(F32).reshape((1, nctx, 1, 1))
            value = value[:, None] * place_at
            return lax.psum(total(value.reshape(-1, value.shape[-1])), "ctx")

        def by_head(value):
            value = lax.all_gather(total(value.reshape(model, width)), "ctx", axis=0)
            value = value.reshape(nctx, rows_in, heads, HEAD_DIM)
            return jnp.transpose(value, (1, 2, 0, 3)).reshape(rows_in, INNER)

        in_total = jnp.concatenate(
            [by_head(early[:, :block_in]), by_head(late), spaced(map_blocks)], axis=1
        )
        out_total = spaced(
            jnp.concatenate([early[:, block_in : block_in + HEAD_DIM], early[:, block_in + HEAD_DIM :]], axis=2)
        )
        in_new = adam_step(in_weight, in_first, in_second, in_total, 0.03, WEIGHT_DECAY)
        out_new = adam_step(out_weight, out_first, out_second, out_total, 0.02, WEIGHT_DECAY)
        small = lax.all_gather(lax.psum(map_keep[:32].astype(F32), "dp"), "ctx", axis=0)

    def in_order(value):
        return jnp.swapaxes(value.reshape(nctx, -1, heads, HEAD_DIM), 0, 1).swapaxes(1, 2).reshape(-1, INNER)

    columns = in_order(small[:, : CONV + 2])
    conv_total = jnp.concatenate([columns[: CONV + 1], small[0, 8 : 8 + CONV + 1, :maps]], axis=1)
    conv_total = lax.dynamic_slice_in_dim(conv_total, d * conv_cols, conv_cols, 1)
    dt_total = small[:, 16:32].reshape(nctx, 2, heads, width)
    dt_total = jnp.transpose(dt_total, (2, 0, 1, 3)).reshape(HEADS, model)
    dt_total = lax.dynamic_slice_in_dim(dt_total, d * dt_cols, dt_cols, 1)
    pre_total = jnp.sum(small[:, 13:15], axis=0).reshape(-1)
    gain_total = jnp.concatenate([pre_total, columns[CONV + 1]])
    gain_total = lax.dynamic_slice_in_dim(gain_total, d * gain_len, gain_len, 0)
    head_row = small[:, 7] + small[:, 15]
    head_total = jnp.stack(
        [
            head_row[:, :heads].T.reshape(-1),
            head_row[:, 128 : 128 + heads].T.reshape(-1),
            jnp.sum(small[:, CONV + 2].reshape(nctx, heads, HEAD_DIM), axis=2).T.reshape(-1),
        ]
    )

    dt_new = adam_step(dt_weight, dt_first, dt_second, dt_total, 0.03, WEIGHT_DECAY)
    conv_new = adam_step(conv_params, conv_first, conv_second, conv_total, 0.3, 0.0)
    gain_new = adam_step(gains, gain_first, gain_second, gain_total, 0.5, 0.0)
    head_new = adam_step(head_params, head_first, head_second, head_total, 2.0, 0.0)
    return (block_output[None], input_grad[None]) + in_new + dt_new + out_new + conv_new + gain_new + head_new


def solution(mesh):
    tokens, rows, cols = P("dp", "ctx", None), P("dp", None), P(None, "dp")
    return jax.shard_map(
        shards,
        mesh=mesh,
        in_specs=(tokens, rows, tokens, rows, cols, rows, cols, P("dp"), P())
        + (rows, rows, cols, cols, rows, rows, cols, cols, P("dp"), P("dp"), P(), P()),
        out_specs=(tokens, tokens)
        + (rows,) * 3
        + (cols,) * 3
        + (rows,) * 3
        + (cols,) * 3
        + (P("dp"),) * 3
        + (P(),) * 3,
        check_vma=False,
    )
```
